32 devices in a mesh: dp: 8 (over y, x, core), fsdp: 4 (over z).
Axes of the slice: x: 2, y: 2, z: 4, core: 2. Of those that a mesh axis runs over, the one named last changes fastest.
Arguments:
- tokens: bfloat16 [32, 1024, 512], P('dp', 'fsdp'), may hold values from -6 to 6
- out_grad: bfloat16 [32, 1024, 512], P('dp', 'fsdp'), may hold values from -6 to 6
- segment_ids: int32 [32, 1024], P('dp', 'fsdp'), may hold values from 0 to 7, as said below
- key_mask: int32 [32, 1024], P('dp', 'fsdp'), may hold values from 0 to 1, as said below
- sent_task: int32 [32, 8], P('dp'), may hold values from 0 to 31, as said below
- task_experts: int32 [32, 2], replicated, may hold values from 0 to 7, all different within a row
- ln1_gain: bfloat16 [512], P(('dp', 'fsdp')), may hold values from 0.5 to 1.5
- ln1_bias: bfloat16 [512], P(('dp', 'fsdp')), may hold values from -1.1953125 to 1.1953125
- w_qkv: bfloat16 [512, 1536], P(('dp', 'fsdp')), may hold values from -0.25 to 0.25
- w_proj: bfloat16 [512, 512], P(('dp', 'fsdp')), may hold values from -1 to 1
- ln2_gain: bfloat16 [512], P(('dp', 'fsdp')), may hold values from 0.5 to 1.5
- ln2_bias: bfloat16 [512], P(('dp', 'fsdp')), may hold values from -1.1953125 to 1.1953125
- task_embed: bfloat16 [32, 512], P(None, ('dp', 'fsdp')), may hold values from -6 to 6
- w_gate: bfloat16 [512, 8], P(('dp', 'fsdp')), may hold values from -0.125 to 0.125
- w_up: bfloat16 [8, 512, 2048], P('dp', 'fsdp'), may hold values from -0.25 to 0.25
- b_up: bfloat16 [8, 2048], P('dp', 'fsdp'), may hold values from -0.59765625 to 0.59765625
- w_down: bfloat16 [8, 2048, 512], P('dp', 'fsdp'), may hold values from -0.125 to 0.125
- b_down: bfloat16 [8, 512], P('dp', 'fsdp'), may hold values from -0.59765625 to 0.59765625
Outputs:
- output: bfloat16 [32, 1024, 512], P('dp', 'fsdp')
- d_tokens: float32 [32, 1024, 512], P('dp', 'fsdp')
- d_ln1_gain: float32 [512], P(('dp', 'fsdp'))
- d_ln1_bias: float32 [512], P(('dp', 'fsdp'))
- d_w_qkv: float32 [512, 1536], P(('dp', 'fsdp'))
- d_w_proj: float32 [512, 512], P(('dp', 'fsdp'))
- d_ln2_gain: float32 [512], P(('dp', 'fsdp'))
- d_ln2_bias: float32 [512], P(('dp', 'fsdp'))
- d_task_embed: float32 [32, 512], P(None, ('dp', 'fsdp'))
- d_w_gate: float32 [512, 8], P(('dp', 'fsdp'))
- d_w_up: float32 [8, 512, 2048], P('dp', 'fsdp')
- d_b_up: float32 [8, 2048], P('dp', 'fsdp')
- d_w_down: float32 [8, 2048, 512], P('dp', 'fsdp')
- d_b_down: float32 [8, 512], P('dp', 'fsdp')
The draws below stay inside these ranges and needn't reach their ends.
Inputs may be any that keep to these rules, and one draw needn't show every extreme that they name: `segment_ids`: never falling along a row. In each group of 4 rows that share an index of dp, one row holds a single sentence. `key_mask`: the first position of every sentence is 1. `sent_task`: entries past a row's last sentence are unused. The single-sentence rows all have the same task. `task_experts`: two different experts per task; every expert belongs to some task.
All inputs are finite; a program needn't handle non-finite values.
Results may differ from the reference program's by a relative error of at most 0.012.
Values may be sent and summed in bfloat16 or wider, within the bound.
A program may use at most 192 MiB of HBM per device.

```python
import jax
import jax.numpy as jnp
from jax import lax

D = 512
HEADS = 8
HD = 64
FF = 2048
E = 8
TASKS = 32
LEN = 1024
SEGS = 8
ROWS_DP = 4
ROWS = 32
PIECE = 256
TOK_DEV = 1024
CAP = 512
N_DP = 8
N_FSDP = 4


def row_layout(key):
    pick_key, cut_key = jax.random.split(key)
    groups = ROWS // ROWS_DP
    picked = jax.random.randint(pick_key, (groups,), 0, ROWS_DP)
    single = jnp.arange(ROWS) % ROWS_DP == jnp.repeat(picked, ROWS_DP)
    cut_flags = jax.random.randint(cut_key, (ROWS, LEN), 0, LEN) < 12
    cut_flags = cut_flags & (jnp.arange(LEN)[None, :] > 0)
    segment = jnp.minimum(jnp.cumsum(cut_flags.astype(jnp.int32), axis=1), SEGS - 1)
    segment = jnp.where(single[:, None], 0, segment)
    return (single, segment.astype(jnp.int32))


def draw_segment_ids(key, part):
    layout = row_layout(key)
    return layout[1]


def draw_key_mask(key, part):
    layout = row_layout(key)
    key = jax.random.fold_in(key, 5)
    segment = layout[1]
    keeping = jax.random.randint(key, (ROWS, LEN), 0, 8) > 0
    starts = jnp.concatenate([jnp.ones((ROWS, 1), bool), segment[:, 1:] != segment[:, :-1]], axis=1)
    return (keeping | starts).astype(jnp.int32)


def draw_sent_task(key, part):
    layout = row_layout(key)
    key = jax.random.fold_in(key, 7)
    hot_key, task_key = jax.random.split(key)
    hottest = jax.random.randint(hot_key, (), 0, TASKS)
    chosen = jax.random.randint(task_key, (ROWS, SEGS), 0, TASKS)
    leading = jnp.where(layout[0], hottest, chosen[:, 0])
    return chosen.at[:, 0].set(leading).astype(jnp.int32)


def levels(stream_key, dims, shards, least, top_value):
    def one(position, shards_of):
        heights = jax.random.uniform(jax.random.fold_in(jax.random.fold_in(stream_key, 6), position), (shards_of,), jnp.float32, least / len(shards), top_value / len(shards))
        return jnp.repeat(jnp.exp(heights), dims[position] // shards_of).reshape((-1,) + (1,) * (len(dims) - position - 1))

    gain = one(*shards[0])
    for cut in shards[1:]:
        gain = gain * one(*cut)
    return gain


def distinct(key, rows, count, top, lift):
    order = jax.random.permutation(jax.random.fold_in(key, 1), count)
    boost = order
    for power in range(3):
        boost = boost * boost // count
    boost = boost * lift // count
    lots = jax.random.randint(jax.random.fold_in(key, 2), (rows, count), 0, 4096) + boost
    sure = jax.random.permutation(jax.random.fold_in(key, 3), rows)[jnp.arange(count) % rows]
    lots = jnp.where(jnp.arange(rows)[:, None] == sure[None, :], 1 << 14, lots)
    score = lots * count + jnp.arange(count)
    return lax.top_k(score.astype(jnp.int32), top)[1].astype(jnp.int32)


def gaussian(key, shape, scale, most, cuts=(), kind=jnp.bfloat16):
    drawn = scale * jax.random.normal(key, shape, jnp.float32)
    if cuts:
        drawn = drawn * levels(key, shape, cuts, -0.22, 0.18)
    return jnp.clip(drawn, -most, most).astype(kind)


def setup_inputs(seed: int = 0) -> dict:
    streams_of = jax.random.split(jax.random.key(seed), 19)
    return {
        "tokens": gaussian(streams_of[0], (ROWS, LEN, D), 1.0, 6.0, ((0, 8), (1, 4))),
        "out_grad": gaussian(streams_of[1], (ROWS, LEN, D), 1.0, 6.0, ((0, 8), (1, 4))),
        "segment_ids": draw_segment_ids(jax.random.fold_in(streams_of[18], 71), 0),
        "key_mask": draw_key_mask(jax.random.fold_in(streams_of[18], 71), 0),
        "sent_task": draw_sent_task(jax.random.fold_in(streams_of[18], 71), 0),
        "task_experts": distinct(streams_of[5], TASKS, E, 2, 2048),
        "ln1_gain": jnp.clip(1.0 + 0.1 * jax.random.normal(streams_of[6], (D,), jnp.float32), 0.5, 1.5).astype(jnp.bfloat16),
        "ln1_bias": gaussian(streams_of[7], (D,), 0.2, 1.1953125, ((0, 32),)),
        "w_qkv": gaussian(streams_of[8], (D, 3 * D), D ** -0.5, 0.25, ((0, 32),)),
        "w_proj": gaussian(streams_of[9], (D, D), (D // 16) ** -0.5, 1.0, ((0, 32),)),
        "ln2_gain": jnp.clip(1.0 + 0.1 * jax.random.normal(streams_of[10], (D,), jnp.float32), 0.5, 1.5).astype(jnp.bfloat16),
        "ln2_bias": gaussian(streams_of[11], (D,), 0.2, 1.1953125, ((0, 32),)),
        "task_embed": gaussian(streams_of[12], (TASKS, D), 1.0, 6.0, ((1, 32),)),
        "w_gate": gaussian(streams_of[13], (D, E), (4 * D) ** -0.5, 0.125, ((0, 32),)),
        "w_up": gaussian(streams_of[14], (E, D, FF), D ** -0.5, 0.25, ((0, 8), (1, 4))),
        "b_up": gaussian(streams_of[15], (E, FF), 0.1, 0.59765625, ((0, 8), (1, 4))),
        "w_down": gaussian(streams_of[16], (E, FF, D), FF ** -0.5, 0.125, ((0, 8), (1, 4))),
        "b_down": gaussian(streams_of[17], (E, D), 0.1, 0.59765625, ((0, 8), (1, 4))),
    }


@jax.custom_vjp
def low(v):
    return lax.optimization_barrier(v.astype(jnp.bfloat16)).astype(jnp.float32)

@jax.custom_vjp
def low_back(v):
    return v

def low_keep(v):
    return (low(v), None)

def low_pass(kept, grad):
    return (grad,)

def back_keep(v):
    return (v, None)

def back_low(kept, grad):
    return (low(grad),)
low.defvjp(low_keep, low_pass)
low_back.defvjp(back_keep, back_low)
exact = lax.Precision.HIGHEST

def layer_norm(values_in, gain_vec, shift_vec):
    centre = values_in - lax.optimization_barrier(jnp.mean(values_in, axis=-1, keepdims=True))
    spread = lax.optimization_barrier(jnp.mean(centre * centre, axis=-1, keepdims=True))
    return centre * lax.rsqrt(spread + 1e-05) * gain_vec + shift_vec

def attend_group(queries, key_heads, value_heads, segment_rows, mark_rows):
    scores = low_back(jnp.einsum('rqhd,rkhd->rhqk', queries, key_heads, precision=exact) * 0.125)
    allowed = (segment_rows[:, :, None] == segment_rows[:, None, :]) & (mark_rows[:, None, :] == 1)
    scores = jnp.where(allowed[:, None], scores, -1000000000.0)
    biggest = lax.optimization_barrier(jnp.max(scores, axis=-1, keepdims=True))
    weights = jnp.exp(scores - biggest)
    weights = low(weights / lax.optimization_barrier(jnp.sum(weights, axis=-1, keepdims=True)))
    return jnp.einsum('rhqk,rkhd->rqhd', weights, value_heads, precision=exact)

def reference(tokens, out_grad, segment_ids, key_mask, sent_task, task_experts, ln1_gain, ln1_bias, w_qkv, w_proj, ln2_gain, ln2_bias, task_embed, w_gate, w_up, b_up, w_down, b_down):
    blocks = N_DP * N_FSDP
    total_slots = E * blocks * CAP
    task_tok = jnp.take_along_axis(sent_task, segment_ids, axis=1)
    task_flat = task_tok.reshape(-1)
    expert_tok = jnp.take(task_experts, task_flat, axis=0).reshape(ROWS, LEN, 2)

    def to_blocks(table):
        return table.reshape(N_DP, ROWS_DP, N_FSDP, PIECE, 2).transpose(0, 2, 4, 1, 3).reshape(blocks, 2 * TOK_DEV)
    copy_expert = to_blocks(expert_tok)
    one_hot = (copy_expert[:, :, None] == jnp.arange(E, dtype=jnp.int32)[None, None, :]).astype(jnp.int32)
    rank = lax.optimization_barrier(jnp.sum((jnp.cumsum(one_hot, axis=1) - one_hot) * one_hot, axis=-1))
    block_base = jnp.arange(blocks, dtype=jnp.int32)[:, None] * CAP
    slot_index = jnp.where(rank < CAP, copy_expert * (blocks * CAP) + block_base + rank, total_slots).astype(jnp.int32)
    token_ids = jnp.broadcast_to(jnp.arange(ROWS * LEN, dtype=jnp.int32).reshape(ROWS, LEN, 1), (ROWS, LEN, 2))
    slot_token = jnp.full((total_slots + 1,), ROWS * LEN, jnp.int32).at[slot_index.reshape(-1)].set(to_blocks(token_ids).reshape(-1))
    slot_token = slot_token[:total_slots].reshape(E, blocks * CAP)
    token_slot = slot_index.reshape(N_DP, N_FSDP, 2, ROWS_DP, PIECE).transpose(0, 3, 1, 4, 2).reshape(ROWS * LEN, 2)
    kept_copy = (token_slot < total_slots).astype(jnp.float32)
    groups = ROWS // ROWS_DP
    segment_groups = segment_ids.reshape(groups, ROWS_DP, LEN)
    mark_groups = key_mask.reshape(groups, ROWS_DP, LEN)

    def forward(inputs, gain_one, bias_one, qkv_weight, proj_weight, gain_two, bias_two, embed_table, router, weight_in, bias_in, weight_out, bias_out):
        flat_in = inputs.reshape(ROWS * LEN, D)
        normed = low(layer_norm(flat_in, gain_one, bias_one))
        projected = low(low_back(jnp.dot(normed, qkv_weight, precision=exact)))
        projected = projected.reshape(groups, ROWS_DP, LEN, 3, HEADS, HD)

        def one_group(carry, parts):
            return (carry, jax.checkpoint(attend_group)(*parts))
        carried, attended = lax.scan(one_group, jnp.zeros((), jnp.float32), (projected[:, :, :, 0], projected[:, :, :, 1], projected[:, :, :, 2], segment_groups, mark_groups))
        attended = low(low_back(attended.reshape(ROWS * LEN, D)))
        hidden = flat_in + low_back(jnp.dot(attended, proj_weight, precision=exact))
        normed_two = low(layer_norm(hidden, gain_two, bias_two))
        padded = jnp.concatenate([normed_two, jnp.zeros((1, D), jnp.float32)], axis=0)

        def one_expert(parts):
            slot_list, expert_in, expert_in_bias, expert_out, expert_out_bias = parts
            slot_rows = low_back(jnp.take(padded, slot_list, axis=0))
            pre_act = low_back(jnp.dot(slot_rows, expert_in, precision=exact) + expert_in_bias)
            activated = low(jax.nn.gelu(pre_act, approximate=True))
            return low(low_back(jnp.dot(activated, expert_out, precision=exact) + expert_out_bias))
        produced = lax.map(jax.checkpoint(one_expert), (slot_token, weight_in, bias_in, weight_out, bias_out))
        produced = jnp.concatenate([produced.reshape(total_slots, D), jnp.zeros((1, D), jnp.float32)], axis=0)
        logits = jnp.take_along_axis(jnp.dot(embed_table, router, precision=exact), task_experts, axis=1)
        gate_probs = jax.nn.softmax(logits, axis=-1)
        gate_tok = jnp.take(gate_probs, task_flat, axis=0) * kept_copy
        first_copy = jnp.take(produced, token_slot[:, 0], axis=0)
        second_copy = jnp.take(produced, token_slot[:, 1], axis=0)
        mixed = hidden + gate_tok[:, 0:1] * first_copy + gate_tok[:, 1:2] * second_copy
        return mixed.reshape(ROWS, LEN, D)
    floats = [array_in.astype(jnp.float32) for array_in in (tokens, ln1_gain, ln1_bias, w_qkv, w_proj, ln2_gain, ln2_bias, task_embed, w_gate, w_up, b_up, w_down, b_down)]
    result, pullback = jax.vjp(forward, *floats)
    grads = pullback(out_grad.astype(jnp.float32))
    return (result.astype(jnp.bfloat16), grads[0], grads[1], grads[2], grads[3], grads[4], grads[5], grads[6], grads[7], grads[8], grads[9], grads[10], grads[11], grads[12])
```

```python
import functools

import jax
import jax.numpy as jnp
from jax import lax
from jax.experimental import pallas as pl
from jax.experimental.pallas import tpu as pltpu
from jax.sharding import PartitionSpec as P

HEADS = 8
HD = 64


exact = lax.Precision.HIGHEST


def layer_norm(values_in, gain_vec, shift_vec):
    centre = values_in - jnp.mean(values_in, axis=-1, keepdims=True)
    spread = jnp.mean(centre * centre, axis=-1, keepdims=True)
    return centre * lax.rsqrt(spread + 1e-05) * gain_vec + shift_vec


def allow_table(query_codes, key_codes):
    query_int = query_codes.astype(jnp.int32)
    key_int = key_codes.astype(jnp.int32)
    same_sentence = (query_int // 2)[:, :, None] == (key_int // 2)[:, None, :]
    return same_sentence & ((key_int % 2)[:, None, :] == 1)


def row_scores(query_row, key_row, allow_row):
    scores = (
        jnp.einsum("qhd,khd->hqk", query_row, key_row, preferred_element_type=jnp.float32) * 0.125
    )
    return jnp.where(allow_row[None], scores, -1000000000.0)


def attend_forward(queries, key_heads, value_heads, allowed):

    def one_row(parts):
        query_row, key_row, value_row, allow_row = parts
        scores = row_scores(query_row, key_row, allow_row)
        biggest = jnp.max(scores, axis=-1, keepdims=True)
        weights = jnp.exp(scores - biggest)
        row_total = jnp.sum(weights, axis=-1, keepdims=True)
        weights_low = (weights / row_total).astype(jnp.bfloat16)
        mixed_row = jnp.einsum(
            "hqk,khd->qhd", weights_low, value_row, preferred_element_type=jnp.float32
        )
        return (mixed_row.astype(jnp.bfloat16), (biggest + jnp.log(row_total))[..., 0])

    return lax.map(one_row, (queries, key_heads, value_heads, allowed))


def attend_backward(queries, key_heads, value_heads, allowed, logsum, grad_out):

    def one_row(parts):
        query_row, key_row, value_row, allow_row, logsum_row, grad_row = parts
        scores = row_scores(query_row, key_row, allow_row)
        weights = jnp.exp(scores - logsum_row[..., None])
        grad_weights = jnp.einsum(
            "qhd,khd->hqk", grad_row, value_row, preferred_element_type=jnp.float32
        )
        inner = jnp.sum(weights * grad_weights, axis=-1, keepdims=True)
        grad_scores = (weights * (grad_weights - inner)).astype(jnp.bfloat16)
        grad_query = (
            jnp.einsum("hqk,khd->qhd", grad_scores, key_row, preferred_element_type=jnp.float32)
            * 0.125
        )
        grad_key = (
            jnp.einsum("hqk,qhd->khd", grad_scores, query_row, preferred_element_type=jnp.float32)
            * 0.125
        )
        grad_value = jnp.einsum(
            "hqk,qhd->khd",
            weights.astype(jnp.bfloat16),
            grad_row,
            preferred_element_type=jnp.float32,
        )
        return (grad_query, grad_key, grad_value)

    return lax.map(one_row, (queries, key_heads, value_heads, allowed, logsum, grad_out))


def shards(
    tokens,
    out_grad,
    segment_ids,
    key_mask,
    sent_task,
    task_experts,
    ln1_gain,
    ln1_bias,
    w_qkv,
    w_proj,
    ln2_gain,
    ln2_bias,
    task_embed,
    w_gate,
    w_up,
    b_up,
    w_down,
    b_down,
):
    row_count, piece_len, model_width = tokens.shape
    tok_count = row_count * piece_len
    gain_one, bias_one, qkv_full, proj_full, gain_two, bias_two, embed_full, router_full = (
        lax.all_gather(ln1_gain, ("dp", "fsdp"), axis=0, tiled=True),
        lax.all_gather(ln1_bias, ("dp", "fsdp"), axis=0, tiled=True),
        lax.all_gather(w_qkv, ("dp", "fsdp"), axis=0, tiled=True),
        lax.all_gather(w_proj, ("dp", "fsdp"), axis=0, tiled=True),
        lax.all_gather(ln2_gain, ("dp", "fsdp"), axis=0, tiled=True),
        lax.all_gather(ln2_bias, ("dp", "fsdp"), axis=0, tiled=True),
        lax.all_gather(task_embed, ("dp", "fsdp"), axis=1, tiled=True),
        lax.all_gather(w_gate, ("dp", "fsdp"), axis=0, tiled=True),
    )
    up_full, up_bias, down_full, down_bias = (
        lax.all_gather(w_up, "fsdp", axis=1, tiled=True),
        lax.all_gather(b_up, "fsdp", axis=1, tiled=True),
        lax.all_gather(w_down, "fsdp", axis=1, tiled=True),
        lax.all_gather(b_down, "fsdp", axis=1, tiled=True),
    )
    up_full = up_full[0]
    down_full = down_full[0]
    up_bias_f = up_bias[0].astype(jnp.float32)
    down_bias_f = down_bias[0].astype(jnp.float32)
    experts_count = router_full.shape[1]
    task_count = embed_full.shape[0]
    capacity = 4 * tok_count // experts_count
    inputs = tokens.astype(jnp.float32).reshape(tok_count, model_width)
    normed, norm_back = jax.vjp(
        layer_norm, inputs, gain_one.astype(jnp.float32), bias_one.astype(jnp.float32)
    )
    normed_low = normed.astype(jnp.bfloat16)
    projected = jnp.dot(normed_low, qkv_full, preferred_element_type=jnp.float32).astype(
        jnp.bfloat16
    )
    projected = projected.reshape(row_count, piece_len, 3, HEADS, HD)
    queries = projected[:, :, 0]
    key_heads = projected[:, :, 1]
    value_heads = projected[:, :, 2]
    row_codes = (2 * segment_ids + key_mask).astype(jnp.bfloat16)
    keys_all, values_all, codes_all = (
        lax.all_gather(key_heads, "fsdp", axis=1, tiled=True),
        lax.all_gather(value_heads, "fsdp", axis=1, tiled=True),
        lax.all_gather(row_codes, "fsdp", axis=1, tiled=True),
    )
    allowed = allow_table(row_codes, codes_all)
    attended, logsum = attend_forward(queries, keys_all, values_all, allowed)
    attended_flat = attended.reshape(tok_count, model_width)
    hidden = inputs + jnp.dot(attended_flat, proj_full, preferred_element_type=jnp.float32)
    normed_two, norm_two_back = jax.vjp(
        layer_norm, hidden, gain_two.astype(jnp.float32), bias_two.astype(jnp.float32)
    )
    normed_two_low = normed_two.astype(jnp.bfloat16)
    choose = (task_experts[:, :, None] == jnp.arange(experts_count)[None, None, :]).astype(
        jnp.float32
    )

    def gate_values(embed_in, router_in):
        logits = jnp.einsum(
            "te,tke->tk", jnp.dot(embed_in, router_in, precision=exact), choose, precision=exact
        )
        return jax.nn.softmax(logits, axis=-1)

    gate_probs, gate_back = jax.vjp(
        gate_values, embed_full.astype(jnp.float32), router_full.astype(jnp.float32)
    )
    segment_hot = (segment_ids[:, :, None] == jnp.arange(sent_task.shape[1])[None, None, :]).astype(
        jnp.int32
    )
    task_tok = jnp.sum(segment_hot * sent_task[:, None, :], axis=-1).reshape(tok_count)
    task_hot = (task_tok[:, None] == jnp.arange(task_count)[None, :]).astype(jnp.float32)
    gate_tok = jnp.dot(task_hot, gate_probs, precision=exact)
    expert_tok = jnp.sum(task_hot.astype(jnp.int32)[:, :, None] * task_experts[None], axis=1)
    copy_expert = expert_tok.T.reshape(-1)
    one_hot = (copy_expert[:, None] == jnp.arange(experts_count)[None, :]).astype(jnp.int32)
    rank = jnp.sum((jnp.cumsum(one_hot, axis=0) - one_hot) * one_hot, axis=-1)
    kept_copy = rank < capacity
    slot_index = jnp.where(kept_copy, copy_expert * capacity + rank, experts_count * capacity)
    send_rows = (
        jnp.zeros((experts_count * capacity + 1, model_width), jnp.bfloat16)
        .at[slot_index]
        .set(jnp.tile(normed_two_low, (2, 1)))
    )
    send_rows = send_rows[:-1].reshape(experts_count, capacity, model_width)
    received = lax.all_to_all(send_rows, "dp", split_axis=0, concat_axis=0, tiled=True)
    slot_total = received.shape[0] * received.shape[1]
    block_rows = min(512, slot_total)
    block_count = slot_total // block_rows
    slot_blocks = received.reshape(block_count, block_rows, model_width)

    def expert_forward(slot_rows):
        pre_act = jnp.dot(slot_rows, up_full, preferred_element_type=jnp.float32) + up_bias_f
        activated = jax.nn.gelu(pre_act, approximate=True).astype(jnp.bfloat16)
        return (
            jnp.dot(activated, down_full, preferred_element_type=jnp.float32) + down_bias_f
        ).astype(jnp.bfloat16)

    produced = lax.map(expert_forward, slot_blocks).reshape(received.shape)
    returned = lax.all_to_all(produced, "dp", split_axis=0, concat_axis=0, tiled=True)
    return_pad = jnp.concatenate(
        [returned.reshape(-1, model_width), jnp.zeros((1, model_width), jnp.bfloat16)], axis=0
    )
    copies = jnp.take(return_pad, slot_index, axis=0).reshape(2, tok_count, model_width)
    kept_float = kept_copy.reshape(2, tok_count).astype(jnp.float32)
    copy_weight = gate_tok.T * kept_float
    mixed_rows = (
        hidden
        + copy_weight[0][:, None] * copies[0].astype(jnp.float32)
        + copy_weight[1][:, None] * copies[1].astype(jnp.float32)
    )
    output = mixed_rows.astype(jnp.bfloat16).reshape(tokens.shape)
    grad_mixed = out_grad.astype(jnp.float32).reshape(tok_count, model_width)
    grad_copies = (copy_weight[:, :, None] * grad_mixed[None]).astype(jnp.bfloat16)
    grad_gate_copy = jnp.sum(copies.astype(jnp.float32) * grad_mixed[None], axis=-1) * kept_float
    grad_send = (
        jnp.zeros((experts_count * capacity + 1, model_width), jnp.bfloat16)
        .at[slot_index]
        .set(grad_copies.reshape(-1, model_width))
    )
    grad_send = grad_send[:-1].reshape(experts_count, capacity, model_width)
    grad_received = lax.all_to_all(grad_send, "dp", split_axis=0, concat_axis=0, tiled=True)

    def expert_backward(totals, parts):
        slot_rows, grad_rows = parts
        pre_act = jnp.dot(slot_rows, up_full, preferred_element_type=jnp.float32) + up_bias_f
        activated, gelu_back = jax.vjp(
            lambda values_in: jax.nn.gelu(values_in, approximate=True), pre_act
        )
        activated_low = activated.astype(jnp.bfloat16)
        grad_act = jnp.dot(grad_rows, down_full.T, preferred_element_type=jnp.float32)
        grad_pre = gelu_back(grad_act)[0].astype(jnp.bfloat16)
        grad_inputs_slot = jnp.dot(grad_pre, up_full.T, preferred_element_type=jnp.float32).astype(
            jnp.bfloat16
        )
        totals = (
            totals[0] + jnp.dot(slot_rows.T, grad_pre, preferred_element_type=jnp.float32),
            totals[1] + jnp.sum(grad_pre.astype(jnp.float32), axis=0),
            totals[2] + jnp.dot(activated_low.T, grad_rows, preferred_element_type=jnp.float32),
            totals[3] + jnp.sum(grad_rows.astype(jnp.float32), axis=0),
        )
        return (totals, grad_inputs_slot)

    start_totals = (
        jnp.zeros(up_full.shape, jnp.float32),
        jnp.zeros(up_bias_f.shape, jnp.float32),
        jnp.zeros(down_full.shape, jnp.float32),
        jnp.zeros(down_bias_f.shape, jnp.float32),
    )
    totals, grad_slots = lax.scan(
        expert_backward,
        start_totals,
        (slot_blocks, grad_received.reshape(block_count, block_rows, model_width)),
    )
    grad_back = lax.all_to_all(
        grad_slots.reshape(received.shape), "dp", split_axis=0, concat_axis=0, tiled=True
    )
    grad_pad = jnp.concatenate(
        [grad_back.reshape(-1, model_width), jnp.zeros((1, model_width), jnp.bfloat16)], axis=0
    )
    grad_taken = (
        jnp.take(grad_pad, slot_index, axis=0)
        .reshape(2, tok_count, model_width)
        .astype(jnp.float32)
    )
    grad_normed_two = grad_taken[0] + grad_taken[1]
    grad_up, grad_up_bias, grad_down, grad_down_bias = (
        lax.psum_scatter(
            totals[0][None].astype(jnp.bfloat16), "fsdp", scatter_dimension=1, tiled=True
        ).astype(jnp.float32),
        lax.psum_scatter(
            totals[1][None].astype(jnp.bfloat16), "fsdp", scatter_dimension=1, tiled=True
        ).astype(jnp.float32),
        lax.psum_scatter(
            totals[2][None].astype(jnp.bfloat16), "fsdp", scatter_dimension=1, tiled=True
        ).astype(jnp.float32),
        lax.psum_scatter(
            totals[3][None].astype(jnp.bfloat16), "fsdp", scatter_dimension=1, tiled=True
        ).astype(jnp.float32),
    )
    grad_hidden_part, grad_gain_two, grad_bias_two = norm_two_back(grad_normed_two)
    grad_hidden = grad_mixed + grad_hidden_part
    grad_branch = grad_hidden.astype(jnp.bfloat16)
    grad_proj = jnp.dot(attended_flat.T, grad_branch, preferred_element_type=jnp.float32)
    grad_attended = jnp.dot(grad_branch, proj_full.T, preferred_element_type=jnp.float32).astype(
        jnp.bfloat16
    )
    grad_attended = grad_attended.reshape(row_count, piece_len, HEADS, HD)
    part_query, part_key, part_value = attend_backward(
        queries, keys_all, values_all, allowed, logsum, grad_attended
    )
    summed_key, summed_value = (
        lax.psum_scatter(
            part_key.astype(jnp.bfloat16), "fsdp", scatter_dimension=1, tiled=True
        ).astype(jnp.float32),
        lax.psum_scatter(
            part_value.astype(jnp.bfloat16), "fsdp", scatter_dimension=1, tiled=True
        ).astype(jnp.float32),
    )
    grad_query = part_query.astype(jnp.bfloat16)
    grad_key = summed_key.astype(jnp.bfloat16)
    grad_value = summed_value.astype(jnp.bfloat16)
    grad_projected = jnp.stack([grad_query, grad_key, grad_value], axis=2).reshape(
        tok_count, 3 * model_width
    )
    grad_qkv_weight = jnp.dot(normed_low.T, grad_projected, preferred_element_type=jnp.float32)
    grad_normed = jnp.dot(grad_projected, qkv_full.T, preferred_element_type=jnp.float32)
    grad_inputs, grad_gain_one, grad_bias_one = norm_back(grad_normed)
    grad_tokens = (grad_hidden + grad_inputs).reshape(tokens.shape)
    grad_gate_task = jnp.dot(task_hot.T, grad_gate_copy.T, precision=exact)
    grad_embed, grad_router = gate_back(grad_gate_task)
    reduced = (
        lax.psum_scatter(grad_gain_one, ("dp", "fsdp"), scatter_dimension=0, tiled=True),
        lax.psum_scatter(grad_bias_one, ("dp", "fsdp"), scatter_dimension=0, tiled=True),
        lax.psum_scatter(grad_qkv_weight, ("dp", "fsdp"), scatter_dimension=0, tiled=True),
        lax.psum_scatter(grad_proj, ("dp", "fsdp"), scatter_dimension=0, tiled=True),
        lax.psum_scatter(grad_gain_two, ("dp", "fsdp"), scatter_dimension=0, tiled=True),
        lax.psum_scatter(grad_bias_two, ("dp", "fsdp"), scatter_dimension=0, tiled=True),
        lax.psum_scatter(grad_embed, ("dp", "fsdp"), scatter_dimension=1, tiled=True),
        lax.psum_scatter(grad_router, ("dp", "fsdp"), scatter_dimension=0, tiled=True),
    )
    return (
        output,
        grad_tokens,
        reduced[0],
        reduced[1],
        reduced[2],
        reduced[3],
        reduced[4],
        reduced[5],
        reduced[6],
        reduced[7],
        grad_up,
        grad_up_bias,
        grad_down,
        grad_down_bias,
    )


MESH_ID = pl.DeviceIdType.MESH
VMEM_MAX = 60 * 1024 * 1024
TILE = 16
BLOCK = 512
FCHUNK = 512
QCHUNK = 256
FAR = -float(2**30)
F32 = jnp.float32
BF16 = jnp.bfloat16


def dot_nn(lhs, rhs):
    return lax.dot_general(lhs, rhs, (((1,), (0,)), ((), ())), preferred_element_type=F32)


def dot_nt(lhs, rhs):
    return lax.dot_general(lhs, rhs, (((1,), (1,)), ((), ())), preferred_element_type=F32)


def dot_tn(lhs, rhs):
    return lax.dot_general(lhs, rhs, (((0,), (0,)), ((), ())), preferred_element_type=F32)


def vmem_spec():
    return pl.BlockSpec(memory_space=pltpu.VMEM)


def any_spec():
    return pl.BlockSpec(memory_space=pl.ANY)


def smem_spec():
    return pl.BlockSpec(memory_space=pltpu.SMEM)


def norm_parts(values):
    centre = values - jnp.mean(values, axis=-1, keepdims=True)
    spread = jnp.mean(centre * centre, axis=-1, keepdims=True)
    scale = lax.rsqrt(spread + 1e-05)
    return centre * scale, scale


def norm_back_parts(grad, normal, scale):
    mean_grad = jnp.mean(grad, axis=-1, keepdims=True)
    mean_prod = jnp.mean(grad * normal, axis=-1, keepdims=True)
    return (grad - mean_grad - normal * mean_prod) * scale


def fold_rows(values):
    rows, width = values.shape
    return jnp.sum(values.reshape(rows // 8, 8, width), axis=0)


def plane_ids():
    me = lax.axis_index("dp")
    core, xpos, ypos = lax.rem(me, 2), lax.rem(me // 2, 2), me // 4

    def at(ypos, xpos, core):
        return (ypos * 2 + xpos) * 2 + core

    return me, core, xpos, ypos, at


def greet(peers):
    barrier = pltpu.get_barrier_semaphore()
    for peer in peers:
        pl.semaphore_signal(barrier, inc=1, device_id=peer, device_id_type=MESH_ID)
    pl.semaphore_wait(barrier, len(peers))


class Sender:
    def __init__(self, send_sems, recv_sems):
        self.send_sems, self.recv_sems, self.count, self.all = send_sems, recv_sems, 0, []

    def start(self, src, dst, peer):
        copy = pltpu.make_async_remote_copy(
            src_ref=src,
            dst_ref=dst,
            send_sem=self.send_sems.at[self.count],
            recv_sem=self.recv_sems.at[self.count],
            device_id=peer,
            device_id_type=MESH_ID,
        )
        copy.start()
        self.count += 1
        self.all.append(copy)
        return copy

    def drain(self):
        for copy in self.all:
            copy.wait_send()


def plane_gather_steps(block, own, rows, sender, z):
    me, core, xpos, ypos, at = plane_ids()
    sib, xn, yn = at(ypos, xpos, 1 - core), at(ypos, 1 - xpos, core), at(1 - ypos, xpos, core)
    diag = at(1 - ypos, 1 - xpos, core)
    half = rows // 2

    def part(i, k):
        return block(i).at[pl.ds(k * half, half)]

    def send(i, k, peer):
        src = own.at[pl.ds(k * half, half)] if i is me else part(i, k)
        return sender.start(src, part(i, k), (peer, z))

    x_own = [send(me, 0, xn)]
    y_own = [send(me, 1, yn)]
    x_own.append(send(me, 1, xn))
    y_own.insert(0, send(me, 0, yn))
    last = [send(me, 0, sib), send(me, 1, sib)]
    x_own[0].wait_recv()
    to_y = send(xn, 0, yn)
    y_own[1].wait_recv()
    to_x = send(yn, 1, xn)
    last.append(send(xn, 0, sib))
    last.append(send(yn, 1, sib))
    x_own[1].wait_recv()
    last.append(send(xn, 1, sib))
    y_own[0].wait_recv()
    last.append(send(yn, 0, sib))
    to_y.wait_recv()
    last.append(send(diag, 0, sib))
    to_x.wait_recv()
    last.append(send(diag, 1, sib))
    for copy in last:
        copy.wait_recv()


PLANE_GATHER_COPIES = 14


def plane_peers(z):
    me, core, xpos, ypos, at = plane_ids()
    return [
        (at(ypos, xpos, 1 - core), z),
        (at(ypos, 1 - xpos, core), z),
        (at(1 - ypos, xpos, core), z),
    ]


def small_gather_kernel(planes, groups, in_ref, out_ref, send_sems, recv_sems):
    me, z = lax.axis_index("dp"), lax.axis_index("fsdp")
    z_peers = [(me, lax.rem(z + k, planes)) for k in range(1, planes)]
    d_peers = [(lax.rem(me + k, groups), z) for k in range(1, groups)]
    greet(z_peers + d_peers)
    sender = Sender(send_sems, recv_sems)
    out_ref[me, z] = in_ref[...]
    first = [sender.start(in_ref, out_ref.at[me, z], peer) for peer in z_peers]
    for copy in first:
        copy.wait_recv()
    second = [sender.start(out_ref.at[me], out_ref.at[me], peer) for peer in d_peers]
    for copy in second:
        copy.wait_recv()
    sender.drain()


def small_gather(payload, planes, groups):
    return pl.pallas_call(
        functools.partial(small_gather_kernel, planes, groups),
        out_shape=jax.ShapeDtypeStruct((groups, planes) + payload.shape, payload.dtype),
        in_specs=[vmem_spec()],
        out_specs=vmem_spec(),
        scratch_shapes=[
            pltpu.SemaphoreType.DMA((planes + groups,)),
            pltpu.SemaphoreType.DMA((planes + groups,)),
        ],
        compiler_params=pltpu.CompilerParams(collective_id=1, has_side_effects=True),
        name="routing_gather",
    )(payload)


def enter_kernel(planes, tok_ref, w_ref, row_ref, full_ref, send_sems, recv_sems, loc_sems):
    me, z = lax.axis_index("dp"), lax.axis_index("fsdp")
    z_peers = [(me, lax.rem(z + k, planes)) for k in range(1, planes)]
    greet(z_peers + plane_peers(z))
    shard = w_ref.shape[0]
    sender = Sender(send_sems, recv_sems)
    mine = pltpu.make_async_copy(w_ref, full_ref.at[me, pl.ds(z * shard, shard)], loc_sems.at[0])
    mine.start()
    held = pltpu.make_async_copy(tok_ref.at[z], row_ref.at[z], loc_sems.at[1])
    held.start()
    first = [
        sender.start(w_ref, full_ref.at[me, pl.ds(z * shard, shard)], peer) for peer in z_peers
    ]
    rows = [sender.start(tok_ref.at[peer[1]], row_ref.at[z], peer) for peer in z_peers]
    mine.wait()
    for copy in first:
        copy.wait_recv()
    plane_gather_steps(lambda i: full_ref.at[i], full_ref.at[me], planes * shard, sender, z)
    for copy in rows:
        copy.wait_recv()
    held.wait()
    sender.drain()


def enter(tokens, weights, planes, groups):
    copies = 2 * (planes - 1) + PLANE_GATHER_COPIES
    return pl.pallas_call(
        functools.partial(enter_kernel, planes),
        out_shape=(
            jax.ShapeDtypeStruct(tokens.shape, tokens.dtype),
            jax.ShapeDtypeStruct(
                (groups, planes * weights.shape[0], weights.shape[1]), weights.dtype
            ),
        ),
        in_specs=[any_spec(), any_spec()],
        out_specs=(any_spec(), any_spec()),
        scratch_shapes=[
            pltpu.SemaphoreType.DMA((copies,)),
            pltpu.SemaphoreType.DMA((copies,)),
            pltpu.SemaphoreType.DMA((2,)),
        ],
        compiler_params=pltpu.CompilerParams(collective_id=2, has_side_effects=True),
        name="rows_and_dense_weights",
    )(tokens, weights)


def plane_gather_kernel(in_ref, out_ref, send_sems, recv_sems):
    z = lax.axis_index("fsdp")
    greet(plane_peers(z))
    sender = Sender(send_sems, recv_sems)
    plane_gather_steps(lambda i: out_ref.at[i], in_ref, in_ref.shape[0], sender, z)
    sender.drain()


def plane_gather(block, groups):
    return pl.pallas_call(
        plane_gather_kernel,
        out_shape=jax.ShapeDtypeStruct((groups,) + block.shape, block.dtype),
        in_specs=[any_spec()],
        out_specs=any_spec(),
        scratch_shapes=[
            pltpu.SemaphoreType.DMA((PLANE_GATHER_COPIES,)),
            pltpu.SemaphoreType.DMA((PLANE_GATHER_COPIES,)),
        ],
        compiler_params=pltpu.CompilerParams(collective_id=3, has_side_effects=True),
        name="expert_rows_gather",
    )(block)


def plane_scatter_steps(z_ref, out_ref, own, theirs, deep, near_x, near_y, sender, loc_sems, z):
    me, core, xpos, ypos, at = plane_ids()
    sib, xn, yn = at(ypos, xpos, 1 - core), at(ypos, 1 - xpos, core), at(1 - ypos, xpos, core)
    chips = [(ypos, xpos), (ypos, 1 - xpos), (1 - ypos, xpos), (1 - ypos, 1 - xpos)]
    rows = z_ref.shape[1]
    half = rows // 2
    first, second = pl.ds(0, half), pl.ds(half, half)
    loads, trades = {}, {}
    for slot in (3, 1, 2, 0):
        pos = chips[slot]
        loads[slot] = pltpu.make_async_copy(
            z_ref.at[at(pos[0], pos[1], core)], own.at[slot], loc_sems.at[slot]
        )
        loads[slot].start()
        trades[slot] = sender.start(
            z_ref.at[at(pos[0], pos[1], 1 - core)], theirs.at[slot], (sib, z)
        )

    def add(slot, part):
        own[slot, part] = (
            own[slot, part].astype(F32) + theirs[slot, part].astype(F32)
        ).astype(own.dtype)

    loads[3].wait()
    trades[3].wait_recv()
    add(3, first)
    deep_x = sender.start(own.at[3, first], deep.at[0], (xn, z))
    add(3, second)
    deep_y = sender.start(own.at[3, second], deep.at[1], (yn, z))
    loads[1].wait()
    trades[1].wait_recv()
    add(1, first)
    x_first = sender.start(own.at[1, first], near_x.at[first], (xn, z))
    loads[2].wait()
    trades[2].wait_recv()
    add(2, second)
    y_second = sender.start(own.at[2, second], near_y.at[second], (yn, z))
    add(1, second)
    add(2, first)
    deep_y.wait_recv()
    own[1, second] = (own[1, second].astype(F32) + deep[1].astype(F32)).astype(own.dtype)
    x_second = sender.start(own.at[1, second], near_x.at[second], (xn, z))
    deep_x.wait_recv()
    own[2, first] = (own[2, first].astype(F32) + deep[0].astype(F32)).astype(own.dtype)
    y_first = sender.start(own.at[2, first], near_y.at[first], (yn, z))
    loads[0].wait()
    trades[0].wait_recv()
    mine = own[0].astype(F32) + theirs[0].astype(F32)
    x_first.wait_recv()
    y_second.wait_recv()
    x_second.wait_recv()
    y_first.wait_recv()
    out_ref[...] = (mine + near_x[...].astype(F32) + near_y[...].astype(F32)).astype(out_ref.dtype)


PLANE_SCATTER_COPIES = 10


def plane_scatter_scratch(rows, width):
    return [
        pltpu.VMEM((4, rows, width), BF16),
        pltpu.VMEM((4, rows, width), BF16),
        pltpu.VMEM((2, rows // 2, width), BF16),
        pltpu.VMEM((rows, width), BF16),
        pltpu.VMEM((rows, width), BF16),
    ]


def plane_scatter_kernel(
    planes,
    groups,
    z_ref,
    small_ref,
    out_ref,
    small_out,
    own,
    theirs,
    deep,
    near_x,
    near_y,
    small_in,
    send_sems,
    recv_sems,
    loc_sems,
):
    me, z = lax.axis_index("dp"), lax.axis_index("fsdp")
    z_peers = [(me, lax.rem(z + k, planes)) for k in range(1, planes)]
    d_peers = [(lax.rem(me + k, groups), z) for k in range(1, groups)]
    greet(z_peers + d_peers)
    sender = Sender(send_sems, recv_sems)
    first = [sender.start(small_ref, small_in.at[k], peer) for k, peer in enumerate(z_peers)]
    for copy in first:
        copy.wait_recv()
    small_out[me] = small_ref[...] + jnp.sum(small_in[...], axis=0)
    second = [sender.start(small_out.at[me], small_out.at[me], peer) for peer in d_peers]
    plane_scatter_steps(
        z_ref, out_ref, own, theirs, deep, near_x, near_y, sender, loc_sems, z
    )
    for copy in second:
        copy.wait_recv()
    sender.drain()


def plane_scatter(terms, small, planes, groups):
    rows, width = terms.shape[1:]
    copies = PLANE_SCATTER_COPIES + planes + groups
    return pl.pallas_call(
        functools.partial(plane_scatter_kernel, planes, groups),
        out_shape=(
            jax.ShapeDtypeStruct((rows, width), F32),
            jax.ShapeDtypeStruct((groups,) + small.shape, F32),
        ),
        in_specs=[any_spec(), vmem_spec()],
        out_specs=(vmem_spec(), vmem_spec()),
        scratch_shapes=plane_scatter_scratch(rows, width)
        + [
            pltpu.VMEM((planes - 1,) + small.shape, F32),
            pltpu.SemaphoreType.DMA((copies,)),
            pltpu.SemaphoreType.DMA((copies,)),
            pltpu.SemaphoreType.DMA((4,)),
        ],
        compiler_params=pltpu.CompilerParams(
            collective_id=4, has_side_effects=True, vmem_limit_bytes=VMEM_MAX
        ),
        name="expert_grads_scatter",
    )(terms, small)


def leave_kernel(
    planes,
    tok_ref,
    w_ref,
    piece_ref,
    shard_ref,
    own,
    theirs,
    deep,
    near_x,
    near_y,
    plane_sum,
    plane_in,
    send_sems,
    recv_sems,
    loc_sems,
):
    me, z = lax.axis_index("dp"), lax.axis_index("fsdp")
    z_peers = [(me, lax.rem(z + k, planes)) for k in range(1, planes)]
    greet(z_peers + plane_peers(z))
    sender = Sender(send_sems, recv_sems)
    held = pltpu.make_async_copy(tok_ref.at[z], piece_ref.at[z], loc_sems.at[4])
    held.start()
    rows = [sender.start(tok_ref.at[peer[1]], piece_ref.at[z], peer) for peer in z_peers]
    plane_scatter_steps(
        w_ref, plane_sum, own, theirs, deep, near_x, near_y, sender, loc_sems, z
    )
    shard = shard_ref.shape[0]
    last = [
        sender.start(plane_sum.at[pl.ds(peer[1] * shard, shard)], plane_in.at[k], peer)
        for k, peer in enumerate(z_peers)
    ]
    total = plane_sum[pl.ds(z * shard, shard)].astype(F32)
    for k, copy in enumerate(last):
        copy.wait_recv()
        total = total + plane_in[k].astype(F32)
    shard_ref[...] = total
    for copy in rows:
        copy.wait_recv()
    held.wait()
    sender.drain()


def leave(tokens, terms, planes, groups):
    rows, width = terms.shape[1:]
    copies = PLANE_SCATTER_COPIES + 2 * planes
    return pl.pallas_call(
        functools.partial(leave_kernel, planes),
        out_shape=(
            jax.ShapeDtypeStruct(tokens.shape, tokens.dtype),
            jax.ShapeDtypeStruct((rows // planes, width), F32),
        ),
        in_specs=[any_spec(), any_spec()],
        out_specs=(any_spec(), vmem_spec()),
        scratch_shapes=plane_scatter_scratch(rows, width)
        + [
            pltpu.VMEM((rows, width), BF16),
            pltpu.VMEM((planes - 1, rows // planes, width), BF16),
            pltpu.SemaphoreType.DMA((copies,)),
            pltpu.SemaphoreType.DMA((copies,)),
            pltpu.SemaphoreType.DMA((5,)),
        ],
        compiler_params=pltpu.CompilerParams(
            collective_id=5, has_side_effects=True, vmem_limit_bytes=VMEM_MAX
        ),
        name="grads_and_rows_back",
    )(tokens, terms)


def pick_rows_kernel(order_ref, *refs):
    count = len(refs) // 2
    for a in range(count):
        refs[count + a][...] = refs[a][...].astype(refs[count + a].dtype)


def pick_rows(order, arrays, kinds):
    def block(array):
        return (1,) + array.shape[1:]

    return pl.pallas_call(
        pick_rows_kernel,
        out_shape=tuple(
            jax.ShapeDtypeStruct(array.shape, kind) for array, kind in zip(arrays, kinds)
        ),
        grid_spec=pltpu.PrefetchScalarGridSpec(
            num_scalar_prefetch=1,
            grid=(arrays[0].shape[0],),
            in_specs=[
                pl.BlockSpec(block(array), lambda r, order_ref: (order_ref[r], 0, 0))
                for array in arrays
            ],
            out_specs=tuple(
                pl.BlockSpec(block(array), lambda r, order_ref: (r, 0, 0)) for array in arrays
            ),
        ),
        name="row_order",
    )(order, *arrays)


def forward_kernel(
    heads,
    tok_ref,
    norm_ref,
    w_ref,
    qf_ref,
    kf_ref,
    qkv_ref,
    o_ref,
    lse_ref,
    hres_ref,
    xn2_ref,
    kaug,
    vaug,
):
    rows, width = tok_ref.shape
    chunk = QCHUNK
    pair = 2 * (width // heads)
    lane = lax.broadcasted_iota(jnp.int32, (rows, pair), 1)
    lane_c = lax.broadcasted_iota(jnp.int32, (chunk, pair), 1)

    def project(c, carry):
        part = pl.ds(pl.multiple_of(c * chunk, chunk), chunk)
        normal, _ = norm_parts(tok_ref[part, :].astype(F32))
        xn1 = (normal * norm_ref[0:1, :] + norm_ref[1:2, :]).astype(BF16)
        out = dot_nn(xn1, w_ref[:, : 3 * width])
        qkv_ref[part, :width] = (out[:, :width] * 0.125).astype(BF16)
        qkv_ref[part, width:] = out[:, width:].astype(BF16)
        return carry

    lax.fori_loop(0, rows // chunk, project, 0)

    for side in range(2):
        kaug[side, :, pair:] = kf_ref[...]
        vaug[side, :, pair:] = jnp.where((lane // (pair // 2)) == side, 1.0, 0.0).astype(BF16)

    def one_pair(g, carry):
        cols = pl.ds(pl.multiple_of(g * pair, pair), pair)
        k_pair = qkv_ref[:, pl.ds(pl.multiple_of(width + g * pair, pair), pair)]
        v_pair = qkv_ref[:, pl.ds(pl.multiple_of(2 * width + g * pair, pair), pair)]
        zero = jnp.zeros_like(k_pair)
        for side in range(2):
            mine = (lane // (pair // 2)) == side
            kaug[side, :, :pair] = jnp.where(mine, k_pair, zero)
            vaug[side, :, :pair] = jnp.where(mine, v_pair, zero)

        def one_chunk(c, inner):
            part = pl.ds(pl.multiple_of(c * chunk, chunk), chunk)
            qa = jnp.concatenate([qkv_ref[part, cols], qf_ref[part, :]], axis=1)
            acc = jnp.zeros((chunk, 2 * pair), F32)
            tops = []
            for side in range(2):
                s = dot_nt(qa, kaug[side])
                top = jnp.max(s, axis=-1, keepdims=True)
                acc = acc + dot_nn(jnp.exp(s - top).astype(BF16), vaug[side])
                tops.append(top)
            total = acc[:, pair:]
            o_ref[part, cols] = (acc[:, :pair] / total).astype(BF16)
            top = jnp.where(lane_c < pair // 2, tops[0], tops[1])
            lse_ref[part, cols] = top + jnp.log(total)
            return inner

        lax.fori_loop(0, rows // chunk, one_chunk, 0)
        return carry

    lax.fori_loop(0, heads // 2, one_pair, 0)

    def finish(c, carry):
        part = pl.ds(pl.multiple_of(c * chunk, chunk), chunk)
        hres = tok_ref[part, :].astype(F32) + dot_nn(o_ref[part, :], w_ref[:, 3 * width :])
        hres_ref[part, :] = hres
        normal, _ = norm_parts(hres)
        xn2_ref[part, :] = (normal * norm_ref[2:3, :] + norm_ref[3:4, :]).astype(BF16)
        return carry

    lax.fori_loop(0, rows // chunk, finish, 0)


def forward(row, norms, weights, qf, kf, heads):
    rows, width = row.shape
    pair = 2 * (width // heads)
    return pl.pallas_call(
        functools.partial(forward_kernel, heads),
        out_shape=(
            jax.ShapeDtypeStruct((rows, 3 * width), BF16),
            jax.ShapeDtypeStruct((rows, width), BF16),
            jax.ShapeDtypeStruct((rows, width), F32),
            jax.ShapeDtypeStruct((rows, width), F32),
            jax.ShapeDtypeStruct((rows, width), BF16),
        ),
        in_specs=[vmem_spec()] * 5,
        out_specs=tuple([vmem_spec()] * 5),
        scratch_shapes=[
            pltpu.VMEM((2, rows, 2 * pair), BF16),
            pltpu.VMEM((2, rows, 2 * pair), BF16),
        ],
        compiler_params=pltpu.CompilerParams(vmem_limit_bytes=VMEM_MAX),
        cost_estimate=pl.CostEstimate(
            flops=40_000_000_000, bytes_accessed=10_000_000, transcendentals=8_000_000
        ),
        name="attention_forward",
    )(row, norms, weights, qf, kf)


def split3(values):
    high = values.astype(BF16)
    rest = values - high.astype(F32)
    middle = rest.astype(BF16)
    low = (rest - middle.astype(F32)).astype(BF16)
    return high, middle, low


def backward_kernel(
    heads,
    tok_ref,
    norm_ref,
    w_ref,
    qf_ref,
    kf_ref,
    qkv_ref,
    o_ref,
    lse_ref,
    hres_ref,
    dxn2_ref,
    gm_ref,
    dtok_ref,
    dw_ref,
    dnorm_ref,
    kaug,
    vaug,
    dh,
    db,
    do,
    delta,
    qt,
    dot_t,
    dkt,
    dvt,
    dq,
    dqkv,
    xn1,
):
    rows, width = tok_ref.shape
    chunk = QCHUNK
    head = width // heads
    pair = 2 * head
    lane = lax.broadcasted_iota(jnp.int32, (rows, pair), 1)
    lane_c = lax.broadcasted_iota(jnp.int32, (chunk, pair), 1)
    same = (
        lax.broadcasted_iota(jnp.int32, (pair, pair), 0) // head
        == lax.broadcasted_iota(jnp.int32, (pair, pair), 1) // head
    )
    ones = jnp.where(same, 1.0, 0.0).astype(BF16)
    dnorm_ref[...] = jnp.zeros_like(dnorm_ref)

    def begin(c, carry):
        part = pl.ds(pl.multiple_of(c * chunk, chunk), chunk)
        normal, scale = norm_parts(hres_ref[part, :])
        grad = dxn2_ref[part, :]
        dnorm_ref[2] += fold_rows(grad * normal)
        dnorm_ref[3] += fold_rows(grad)
        dh_part = gm_ref[part, :].astype(F32) + norm_back_parts(
            grad * norm_ref[2:3, :], normal, scale
        )
        dh[part, :] = dh_part
        low = dh_part.astype(BF16)
        db[part, :] = low
        do_part = dot_nt(low, w_ref[:, 3 * width :]).astype(BF16)
        do[part, :] = do_part
        prod = do_part.astype(F32) * o_ref[part, :].astype(F32)
        high = prod.astype(BF16)
        rest = (prod - high.astype(F32)).astype(BF16)
        for g in range(heads // 2):
            cols = slice(g * pair, (g + 1) * pair)
            delta[part, cols] = dot_nn(high[:, cols], ones) + dot_nn(rest[:, cols], ones)
        qt[:, part] = qkv_ref[part, :width].T
        dot_t[:, part] = do_part.T
        normal, _ = norm_parts(tok_ref[part, :].astype(F32))
        xn1[part, :] = (normal * norm_ref[0:1, :] + norm_ref[1:2, :]).astype(BF16)
        return carry

    lax.fori_loop(0, rows // chunk, begin, 0)
    dw_ref[:, 3 * width :] = dot_tn(o_ref[...], db[...]).astype(BF16)

    mark = (lane >= heads) & (lane < heads + 3)
    for side in range(2):
        kaug[side, :, pair:] = jnp.where(mark, 1.0, kf_ref[...].astype(F32)).astype(BF16)
        vaug[side, :, pair:] = jnp.where(mark, 1.0, 0.0).astype(BF16)

    def put_parts(base, values):
        high, middle, low = split3(-values)
        out = jnp.where(lane_c == heads, high.astype(F32), base)
        out = jnp.where(lane_c == heads + 1, middle.astype(F32), out)
        return jnp.where(lane_c == heads + 2, low.astype(F32), out).astype(BF16)

    def one_pair(g, carry):
        cols = pl.ds(pl.multiple_of(g * pair, pair), pair)
        k_pair = qkv_ref[:, pl.ds(pl.multiple_of(width + g * pair, pair), pair)]
        v_pair = qkv_ref[:, pl.ds(pl.multiple_of(2 * width + g * pair, pair), pair)]
        zero = jnp.zeros_like(k_pair)
        for side in range(2):
            mine = (lane // head) == side
            kaug[side, :, :pair] = jnp.where(mine, k_pair, zero)
            vaug[side, :, :pair] = jnp.where(mine, v_pair, zero)

        def one_chunk(c, inner):
            part = pl.ds(pl.multiple_of(c * chunk, chunk), chunk)
            q_pair, do_pair = qkv_ref[part, cols], do[part, cols]
            lse_pair, delta_pair = lse_ref[part, cols], delta[part, cols]
            base = qf_ref[part, :].astype(F32)
            acc = jnp.zeros((chunk, pair), F32)
            for side in range(2):
                lse = lse_pair[:, side * head : side * head + 1]
                qa = jnp.concatenate([q_pair, put_parts(base, lse)], axis=1)
                pr = jnp.exp(dot_nt(qa, kaug[side]))
                dlt = delta_pair[:, side * head : side * head + 1]
                da = jnp.concatenate([do_pair, put_parts(jnp.zeros_like(base), dlt)], axis=1)
                ds = (pr * dot_nt(da, vaug[side])).astype(BF16)
                acc = acc + dot_nn(ds, kaug[side, :, :pair])
                spot = pl.ds(pl.multiple_of(g * pair + side * head, head), head)
                dk_new = dot_nn(qt[spot, part], ds)
                dv_new = dot_nn(dot_t[spot, part], pr.astype(BF16))

                @pl.when(c == 0)
                def _():
                    dkt[spot, :] = dk_new
                    dvt[spot, :] = dv_new

                @pl.when(c > 0)
                def _():
                    dkt[spot, :] += dk_new
                    dvt[spot, :] += dv_new

            dq[part, cols] = (acc * 0.125).astype(BF16)
            return inner

        lax.fori_loop(0, rows // chunk, one_chunk, 0)
        return carry

    lax.fori_loop(0, heads // 2, one_pair, 0)

    def finish(c, carry):
        part = pl.ds(pl.multiple_of(c * chunk, chunk), chunk)
        dqkv[part, :width] = dq[part, :]
        dqkv[part, width : 2 * width] = dkt[:, part].T.astype(BF16)
        dqkv[part, 2 * width :] = dvt[:, part].T.astype(BF16)
        grad = dot_nt(dqkv[part, :], w_ref[:, : 3 * width])
        normal, scale = norm_parts(tok_ref[part, :].astype(F32))
        dnorm_ref[0] += fold_rows(grad * normal)
        dnorm_ref[1] += fold_rows(grad)
        dtok_ref[part, :] = (
            dh[part, :] + norm_back_parts(grad * norm_ref[0:1, :], normal, scale)
        ).astype(BF16)
        return carry

    lax.fori_loop(0, rows // chunk, finish, 0)
    for c in range(3):
        cols = slice(c * width, (c + 1) * width)
        dw_ref[:, cols] = dot_tn(xn1[...], dqkv[:, cols]).astype(BF16)


def backward(row, norms, weights, qf, kf, qkv, o, lse, hres, dxn2, gm, heads):
    rows, width = row.shape
    pair = 2 * (width // heads)
    return pl.pallas_call(
        functools.partial(backward_kernel, heads),
        out_shape=(
            jax.ShapeDtypeStruct((rows, width), BF16),
            jax.ShapeDtypeStruct((width, 4 * width), BF16),
            jax.ShapeDtypeStruct((4, 8, width), F32),
        ),
        in_specs=[vmem_spec()] * 11,
        out_specs=tuple([vmem_spec()] * 3),
        scratch_shapes=[
            pltpu.VMEM((2, rows, 2 * pair), BF16),
            pltpu.VMEM((2, rows, 2 * pair), BF16),
            pltpu.VMEM((rows, width), F32),
            pltpu.VMEM((rows, width), BF16),
            pltpu.VMEM((rows, width), BF16),
            pltpu.VMEM((rows, width), F32),
            pltpu.VMEM((width, rows), BF16),
            pltpu.VMEM((width, rows), BF16),
            pltpu.VMEM((width, rows), F32),
            pltpu.VMEM((width, rows), F32),
            pltpu.VMEM((rows, width), BF16),
            pltpu.VMEM((rows, 3 * width), BF16),
            pltpu.VMEM((rows, width), BF16),
        ],
        compiler_params=pltpu.CompilerParams(vmem_limit_bytes=VMEM_MAX),
        cost_estimate=pl.CostEstimate(
            flops=80_000_000_000, bytes_accessed=20_000_000, transcendentals=8_000_000
        ),
        name="attention_backward",
    )(row, norms, weights, qf, kf, qkv, o, lse, hres, dxn2, gm)


def expert_kernel(planes, groups, *refs):
    refs = list(refs)

    def take(count):
        out = refs[:count]
        del refs[:count]
        return out

    list_ref, meta_ref, own_ref, x_ref = take(4)
    g_refs, up_refs, down_refs = take(groups), take(planes), take(planes)
    bup_ref, bdown_ref = take(2)
    (zd_ref,) = take(1)
    zy_refs, dup_refs, ddown_refs = take(groups), take(planes), take(planes)
    dbup_ref, dbdown_ref, dgate_ref = take(3)
    xs, gs, up, down, acc_up, acc_down, xb, gb, mb, dyb, xt, dyt, yacc, xacc, cast, sems = refs
    me, z = lax.axis_index("dp"), lax.axis_index("fsdp")
    width, hidden = up.shape
    rows = x_ref.shape[1]
    up_rows, down_rows = width // planes, hidden // planes
    tiles = BLOCK // TILE
    copies = []

    def load(src, dst):
        copy = pltpu.make_async_copy(src, dst, sems.at[len(copies)])
        copy.start()
        copies.append(copy)

    for k in range(planes):
        owner = lax.rem(z + k, planes)
        load(up_refs[k], up.at[pl.ds(pl.multiple_of(owner * up_rows, up_rows), up_rows)])
        load(down_refs[k], down.at[pl.ds(pl.multiple_of(owner * down_rows, down_rows), down_rows)])
    for k in range(groups):
        owner = me ^ k
        load(g_refs[k], gs.at[pl.ds(pl.multiple_of(owner * rows, rows), rows)])
        load(
            x_ref.at[owner] if k else own_ref,
            xs.at[pl.ds(pl.multiple_of(owner * rows, rows), rows)],
        )
    acc_up[...] = jnp.zeros_like(acc_up)
    acc_down[...] = jnp.zeros_like(acc_down)
    dbup_ref[...] = jnp.zeros_like(dbup_ref)
    dbdown_ref[...] = jnp.zeros_like(dbdown_ref)
    dgate_ref[...] = jnp.zeros_like(dgate_ref)
    for copy in copies:
        copy.wait()
    n_tiles = list_ref[0]
    n_blocks = lax.div(n_tiles + (tiles - 1), tiles)

    def spot(index):
        return pl.ds(pl.multiple_of(index * TILE, TILE), TILE)

    def one_block(b, carry):
        def fetch(k, inner):
            src = spot(list_ref[1 + b * tiles + k])
            dst = spot(k)
            xb[dst, :] = xs[src, :]
            gb[dst, :] = gs[src, :]
            mb[dst, :] = meta_ref[src, :]
            return inner

        lax.fori_loop(0, tiles, fetch, 0, unroll=4)
        gate = mb[:, 0:1]
        dyb_new = (gb[...].astype(F32) * gate).astype(BF16)
        dyb[...] = dyb_new
        xt[...] = xb[...].T
        dyt[...] = dyb_new.T
        dbdown_ref[...] += fold_rows(dyb_new.astype(F32))

        def one_chunk(f, inner):
            cols = pl.ds(pl.multiple_of(f * FCHUNK, FCHUNK), FCHUNK)
            u = dot_nn(xb[...], up[:, cols]) + bup_ref[:, cols]
            sq = u * u
            th = jnp.tanh(u * (0.7978845608028654 + 0.035677408136300125 * sq))
            half = 0.5 + 0.5 * th
            slope = half + u * (
                (0.5 - 0.5 * th * th) * (0.7978845608028654 + 0.10703222440890037 * sq)
            )
            a = (u * half).astype(BF16)
            du = (dot_nt(dyb[...], down[cols, :]) * slope).astype(BF16)
            y_new = dot_nn(a, down[cols, :])
            x_new = dot_nt(du, up[:, cols])

            @pl.when(f == 0)
            def _():
                yacc[...] = y_new
                xacc[...] = x_new

            @pl.when(f > 0)
            def _():
                yacc[...] += y_new
                xacc[...] += x_new

            acc_up[:, cols] += dot_nn(xt[...], du)
            acc_down[:, cols] += dot_nn(dyt[...], a)
            dbup_ref[:, cols] += fold_rows(du.astype(F32))
            return inner

        lax.fori_loop(0, hidden // FCHUNK, one_chunk, 0)
        y = (yacc[...] + bdown_ref[...]).astype(BF16).astype(F32)
        inner_prod = jnp.sum(y * gb[...].astype(F32), axis=-1, keepdims=True)
        lane = lax.broadcasted_iota(jnp.int32, (BLOCK, 128), 1).astype(F32)
        dgate_ref[...] += fold_rows(jnp.where(lane == mb[:, 1:2], inner_prod, 0.0))
        gb[...] = (y * gate).astype(BF16)
        xb[...] = xacc[...].astype(BF16)

        def store(k, inner):
            dst = spot(list_ref[1 + b * tiles + k])
            src = spot(k)
            xs[dst, :] = xb[src, :]
            gs[dst, :] = gb[src, :]
            return inner

        lax.fori_loop(0, tiles, store, 0, unroll=4)
        return carry

    lax.fori_loop(0, n_blocks, one_block, 0)

    def clear(k, carry):
        dst = spot(list_ref[1 + k])
        xs[dst, :] = jnp.zeros((TILE, width), BF16)
        gs[dst, :] = jnp.zeros((TILE, width), BF16)
        return carry

    lax.fori_loop(n_blocks * tiles, groups * rows // TILE, clear, 0)
    outs = []

    def save(src, dst):
        copy = pltpu.make_async_copy(src, dst, sems.at[len(outs)])
        copy.start()
        outs.append(copy)

    for k in range(groups):
        owner = me ^ k
        save(xs.at[pl.ds(k * rows, rows)], zd_ref.at[k])
        save(gs.at[pl.ds(pl.multiple_of(owner * rows, rows), rows)], zy_refs[k])
    up[...] = acc_up[...].astype(BF16)
    for k in range(hidden // FCHUNK):
        cols = slice(k * FCHUNK, (k + 1) * FCHUNK)
        down[cols, :] = acc_down[:, cols].T.astype(BF16)
    for k in range(planes):
        owner = lax.rem(z + k, planes)
        save(up.at[pl.ds(pl.multiple_of(owner * up_rows, up_rows), up_rows)], dup_refs[k])
        save(
            down.at[pl.ds(pl.multiple_of(owner * down_rows, down_rows), down_rows)], ddown_refs[k]
        )
    for copy in outs:
        copy.wait()


def experts(tile_list, meta, x_own, x_all, g_list, up_list, down_list, b_up, b_down):
    groups, rows, width = x_all.shape
    planes = len(up_list)
    hidden = b_up.shape[1]
    total = groups * rows
    sd = jax.ShapeDtypeStruct
    out = pl.pallas_call(
        functools.partial(expert_kernel, planes, groups),
        out_shape=(
            [sd(x_all.shape, BF16)]
            + [sd((rows, width), BF16)] * groups
            + [sd((width // planes, hidden), BF16)] * planes
            + [sd((hidden // planes, width), BF16)] * planes
            + [sd((8, hidden), F32), sd((8, width), F32), sd((8, 128), F32)]
        ),
        in_specs=[smem_spec(), vmem_spec()]
        + [any_spec()] * (2 + groups + 2 * planes)
        + [vmem_spec()] * 2,
        out_specs=[any_spec()] * (1 + groups + 2 * planes) + [vmem_spec()] * 3,
        scratch_shapes=[
            pltpu.VMEM((total, width), BF16),
            pltpu.VMEM((total, width), BF16),
            pltpu.VMEM((width, hidden), BF16),
            pltpu.VMEM((hidden, width), BF16),
            pltpu.VMEM((width, hidden), F32),
            pltpu.VMEM((width, hidden), F32),
            pltpu.VMEM((BLOCK, width), BF16),
            pltpu.VMEM((BLOCK, width), BF16),
            pltpu.VMEM((BLOCK, 128), F32),
            pltpu.VMEM((BLOCK, width), BF16),
            pltpu.VMEM((width, BLOCK), BF16),
            pltpu.VMEM((width, BLOCK), BF16),
            pltpu.VMEM((BLOCK, width), F32),
            pltpu.VMEM((BLOCK, width), F32),
            pltpu.VMEM((8, 128), F32),
            pltpu.SemaphoreType.DMA((2 * (groups + planes),)),
        ],
        compiler_params=pltpu.CompilerParams(vmem_limit_bytes=VMEM_MAX),
        cost_estimate=pl.CostEstimate(
            flops=60_000_000_000, bytes_accessed=40_000_000, transcendentals=8_000_000
        ),
        name="experts",
    )(tile_list, meta, x_own, x_all, *g_list, *up_list, *down_list, b_up, b_down)
    zd = out[0]
    zy = out[1 : 1 + groups]
    dup = out[1 + groups : 1 + groups + planes]
    ddown = out[1 + groups + planes : 1 + groups + 2 * planes]
    return zd, zy, dup, ddown, out[-3], out[-2], out[-1]


def fast_shards(
    mesh_sizes,
    tokens,
    out_grad,
    segment_ids,
    key_mask,
    sent_task,
    task_experts,
    ln1_gain,
    ln1_bias,
    w_qkv,
    w_proj,
    ln2_gain,
    ln2_bias,
    task_embed,
    w_gate,
    w_up,
    b_up,
    w_down,
    b_down,
):
    groups, planes = mesh_sizes
    row_count, piece, width = tokens.shape
    length = piece * planes
    total = groups * length
    tasks = task_experts.shape[0]
    n_experts = w_gate.shape[1]
    hidden = w_up.shape[2]
    capacity = 4 * row_count * piece // n_experts
    me, z = lax.axis_index("dp"), lax.axis_index("fsdp")

    def z_shift(x, k):
        return lax.ppermute(x, "fsdp", [(i, (i + k) % planes) for i in range(planes)])

    def d_swap(x, k):
        return lax.ppermute(x, "dp", [(i, i ^ k) for i in range(groups)])

    seg_hot = segment_ids[:, :, None] == jnp.arange(sent_task.shape[1])[None, None, :]
    task_tok = jnp.sum(jnp.where(seg_hot, sent_task[:, None, :], 0), axis=-1)
    code = (task_tok * 16 + segment_ids * 2 + key_mask).astype(F32)
    logits_part = jnp.dot(task_embed.astype(F32), w_gate.astype(F32), precision=exact)
    norm_part = jnp.stack([ln1_gain, ln1_bias, ln2_gain, ln2_bias]).astype(F32)
    bias_part = jnp.concatenate([b_up[0], b_down[0]]).astype(F32)
    parts = [code.reshape(-1), logits_part.reshape(-1), norm_part.reshape(-1), bias_part]
    used = sum(p.shape[0] for p in parts)
    pad_rows = -(-used // 1024) * 8
    payload = jnp.concatenate(parts + [jnp.zeros((pad_rows * 128 - used,), F32)])
    gathered = small_gather(payload.reshape(pad_rows, 128), planes, groups)
    gathered = gathered.reshape(groups, planes, pad_rows * 128)
    ends = []
    at = 0
    for p in parts:
        ends.append((at, at + p.shape[0]))
        at += p.shape[0]
    codes = gathered[:, :, ends[0][0] : ends[0][1]].astype(jnp.int32)
    codes = codes.reshape(groups, planes, row_count, piece)
    logits_all = jnp.sum(gathered[:, :, ends[1][0] : ends[1][1]], axis=(0, 1))
    logits_all = logits_all.reshape(tasks, n_experts)
    norms = gathered[:, :, ends[2][0] : ends[2][1]].reshape(groups * planes, 4, -1)
    norms = norms.transpose(1, 0, 2).reshape(4, width)
    norms = jnp.concatenate([norms, jnp.zeros((4, width), F32)])
    biases = lax.dynamic_index_in_dim(
        gathered[:, :, ends[3][0] : ends[3][1]], me, 0, keepdims=False
    )
    bias_up = biases[:, : b_up.shape[1]].reshape(1, hidden)
    bias_down = biases[:, b_up.shape[1] :].reshape(1, width)

    seg_first = codes[:, 0, :, 0] % 16 // 2
    seg_last = codes[:, planes - 1, :, piece - 1] % 16 // 2
    single = jnp.argmax((seg_first == seg_last).astype(jnp.int32), axis=1)
    target = jnp.arange(groups) % planes
    slots = jnp.arange(planes)[None, :]
    order = jnp.where(
        slots == target[:, None],
        single[:, None],
        jnp.where(slots == single[:, None], target[:, None], slots),
    ).astype(jnp.int32)
    my_order = lax.dynamic_index_in_dim(order, me, 0, keepdims=False)
    row_of = lax.dynamic_index_in_dim(order, z, 1, keepdims=False)

    tokens_out, grads_out = pick_rows(my_order, (tokens, out_grad), (BF16, BF16))
    dense = jnp.concatenate([w_qkv, w_proj], axis=1)
    row, dense_full = enter(tokens_out, dense, planes, groups)
    row = row.reshape(length, width)
    dense_full = dense_full.reshape(width, 4 * width)

    w_up, w_down, grads_out, row = lax.optimization_barrier((w_up, w_down, grads_out, row))
    up_list = [w_up[0]] + [z_shift(w_up[0], planes - k) for k in range(1, planes)]
    down_list = [w_down[0]] + [z_shift(w_down[0], planes - k) for k in range(1, planes)]

    grad_pieces = [lax.dynamic_index_in_dim(grads_out, z, 0, keepdims=False)]
    for k in range(1, planes):
        grad_pieces.append(
            z_shift(lax.dynamic_index_in_dim(grads_out, (z + k) % planes, 0, keepdims=False), k)
        )
    gm = jnp.zeros((planes, piece, width), BF16)
    for k in range(planes):
        gm = lax.dynamic_update_index_in_dim(gm, grad_pieces[k], (z - k) % planes, 0)
    gm = gm.reshape(length, width)
    g_list = [gm] + [d_swap(gm, k) for k in range(1, groups)]

    my_codes = lax.dynamic_index_in_dim(codes, me, 0, keepdims=False)
    my_code = lax.dynamic_index_in_dim(my_codes, row_of[me], 1, keepdims=False).reshape(length)
    my_seg, my_key = my_code % 16 // 2, my_code % 2
    pair = 2 * HD
    feature = jnp.arange(pair)[None, :]
    hot = my_seg[:, None] == feature
    qf = hot.astype(BF16)
    kf = jnp.where((feature < 8) & ~(hot & (my_key[:, None] == 1)), FAR, 0.0).astype(BF16)

    qkv, o, lse, hres, xn2 = forward(row, norms, dense_full, qf, kf, HEADS)

    choose = (task_experts[:, :, None] == jnp.arange(n_experts)[None, None, :]).astype(F32)

    def gate_values(logits):
        return jax.nn.softmax(jnp.sum(logits[:, None, :] * choose, axis=-1), axis=-1)

    gates, gate_back = jax.vjp(gate_values, logits_all)
    mine = task_experts == me
    bits = jnp.sum(
        jnp.where(mine, jnp.left_shift(1, jnp.arange(tasks, dtype=jnp.int32))[:, None], 0), axis=0
    )
    gate_of_task = jnp.sum(jnp.where(mine, gates, 0.0), axis=1)
    task_all = codes // 16
    hits = (jnp.right_shift(bits[None, None, :, None, None], task_all[:, :, None]) & 1).astype(F32)
    lower = (jnp.arange(piece)[:, None] < jnp.arange(piece)[None, :]).astype(BF16)
    before = jnp.dot(
        hits.reshape(-1, piece).astype(BF16), lower, preferred_element_type=F32
    ).reshape(hits.shape)
    counts = jnp.sum(hits, axis=-1).reshape(groups, planes, 2 * row_count)
    ahead = (jnp.cumsum(counts, axis=-1) - counts).reshape(groups, planes, 2, row_count)
    rank = before + ahead[..., None]
    kept = jnp.where(rank < capacity, hits, 0.0)
    kept = jnp.sum(kept, axis=2)
    here = (jnp.arange(row_count)[None, :] == row_of[:, None]).astype(F32)
    kept_here = jnp.sum(kept * here[:, None, :, None], axis=2).reshape(total)
    task_here = jnp.sum(
        jnp.where(here[:, None, :, None] > 0, task_all, 0), axis=2
    ).reshape(total)
    task_hot = task_here[:, None] == jnp.arange(tasks)[None, :]
    gate_here = jnp.sum(jnp.where(task_hot, gate_of_task[None, :], 0.0), axis=1) * kept_here
    task_mark = jnp.where(kept_here > 0, task_here.astype(F32), -1.0)
    lane = jnp.arange(128)[None, :]
    meta = jnp.where(
        lane == 0, gate_here[:, None], jnp.where(lane == 1, task_mark[:, None], 0.0)
    )
    n_tiles = total // TILE
    tile_hit = (jnp.max(kept_here.reshape(n_tiles, TILE), axis=1) > 0).astype(jnp.int32)
    hit_count = jnp.sum(tile_hit)
    hit_rank = jnp.cumsum(tile_hit)
    index = jnp.arange(n_tiles, dtype=jnp.int32)
    place = jnp.where(tile_hit > 0, hit_rank - 1, hit_count + index - hit_rank)
    tile_list = jnp.sum(
        jnp.where(place[None, :] == index[:, None], index[None, :], 0), axis=1, dtype=jnp.int32
    )
    tile_list = jnp.concatenate([hit_count[None].astype(jnp.int32), tile_list])

    x_all = plane_gather(xn2, groups)
    zd, zy, dup, ddown, dbup, dbdown, dgate = experts(
        tile_list, meta, xn2, x_all, g_list, up_list, down_list, bias_up, bias_down
    )
    small = jnp.concatenate(
        [
            jnp.sum(dgate, axis=0, keepdims=True),
            jnp.sum(dbup, axis=0).reshape(-1, 128),
            jnp.sum(dbdown, axis=0).reshape(-1, 128),
        ]
    )
    small_rows = small.shape[0]
    small = jnp.concatenate([small, jnp.zeros((-small_rows % 8, 128), F32)])
    dxn2, small_all = plane_scatter(zd, small, planes, groups)

    dup, ddown, zy, dxn2 = lax.optimization_barrier((dup, ddown, zy, dxn2))
    d_w_up = dup[0].astype(F32)
    d_w_down = ddown[0].astype(F32)
    for k in range(1, planes):
        d_w_up = d_w_up + z_shift(dup[k], k).astype(F32)
        d_w_down = d_w_down + z_shift(ddown[k], k).astype(F32)
    mixed = hres + zy[0].astype(F32)
    for k in range(1, groups):
        mixed = mixed + d_swap(zy[k], k).astype(F32)
    mixed = mixed.astype(BF16).reshape(planes, piece, width)
    out_pieces = jnp.zeros((planes, piece, width), BF16)
    for k in range(planes):
        part = lax.dynamic_index_in_dim(mixed, (z + k) % planes, 0, keepdims=False)
        part = z_shift(part, k) if k else part
        out_pieces = lax.dynamic_update_index_in_dim(out_pieces, part, (z - k) % planes, 0)

    dtok, dense_grad, dnorm = backward(
        row, norms, dense_full, qf, kf, qkv, o, lse, hres, dxn2, gm, HEADS
    )
    norm_cols = jnp.sum(dnorm, axis=1).T.astype(BF16)
    terms = jnp.concatenate(
        [dense_grad, norm_cols, jnp.zeros((width, 128 - norm_cols.shape[1]), BF16)], axis=1
    )
    pieces, shard = leave(
        dtok.reshape(planes, piece, width),
        terms.reshape(groups, width // groups, terms.shape[1]),
        planes,
        groups,
    )
    output, d_tokens = pick_rows(my_order, (out_pieces, pieces), (BF16, F32))

    dgate_all = small_all[:, 0, :tasks].T
    dgates = jnp.sum(dgate_all[:, None, :] * choose, axis=-1)
    (dlogits,) = gate_back(dgates)
    d_task_embed = jnp.dot(dlogits, w_gate.astype(F32).T, precision=exact)
    d_w_gate = jnp.dot(task_embed.astype(F32).T, dlogits, precision=exact)
    my_small = lax.dynamic_index_in_dim(small_all, me, 0, keepdims=False)
    cut = 1 + hidden // 128
    d_b_up = lax.dynamic_slice_in_dim(
        my_small[1:cut].reshape(hidden), z * (hidden // planes), hidden // planes, 0
    )
    d_b_down = lax.dynamic_slice_in_dim(
        my_small[cut : cut + width // 128].reshape(width), z * (width // planes), width // planes, 0
    )
    return (
        output,
        d_tokens,
        shard[:, 4 * width],
        shard[:, 4 * width + 1],
        shard[:, : 3 * width],
        shard[:, 3 * width : 4 * width],
        shard[:, 4 * width + 2],
        shard[:, 4 * width + 3],
        d_task_embed,
        d_w_gate,
        d_w_up[None],
        d_b_up[None],
        d_w_down[None],
        d_b_down[None],
    )


def fits_rows(mesh, tokens, w_gate):
    groups, planes = mesh.shape["dp"], mesh.shape["fsdp"]
    return (
        groups == 8
        and tokens.shape[0] == groups * planes
        and w_gate.shape[1] == groups
        and tokens.shape[1] % (planes * QCHUNK) == 0
    )


def solution(mesh):
    placed = (
        P("dp", "fsdp", None),
        P("dp", "fsdp", None),
        P("dp", "fsdp"),
        P("dp", "fsdp"),
        P("dp", None),
        P(),
        P(("dp", "fsdp")),
        P(("dp", "fsdp")),
        P(("dp", "fsdp"), None),
        P(("dp", "fsdp"), None),
        P(("dp", "fsdp")),
        P(("dp", "fsdp")),
        P(None, ("dp", "fsdp")),
        P(("dp", "fsdp"), None),
        P("dp", "fsdp", None),
        P("dp", "fsdp"),
        P("dp", "fsdp", None),
        P("dp", "fsdp"),
    )
    placed_out = (
        P("dp", "fsdp", None),
        P("dp", "fsdp", None),
        P(("dp", "fsdp")),
        P(("dp", "fsdp")),
        P(("dp", "fsdp"), None),
        P(("dp", "fsdp"), None),
        P(("dp", "fsdp")),
        P(("dp", "fsdp")),
        P(None, ("dp", "fsdp")),
        P(("dp", "fsdp"), None),
        P("dp", "fsdp", None),
        P("dp", "fsdp"),
        P("dp", "fsdp", None),
        P("dp", "fsdp"),
    )

    def program(*args):
        fast = fits_rows(mesh, args[0], args[13])
        sizes = (mesh.shape["dp"], mesh.shape["fsdp"])
        return jax.shard_map(
            functools.partial(fast_shards, sizes) if fast else shards,
            mesh=mesh,
            in_specs=placed,
            out_specs=placed_out,
            check_vma=False,
        )(*args)

    return program
```

```python
import functools

import jax
import jax.numpy as jnp
from jax import lax
from jax.experimental import pallas as pl
from jax.experimental.pallas import tpu as pltpu
from jax.sharding import PartitionSpec as P

HEADS = 8
HD = 64


exact = lax.Precision.HIGHEST


def layer_norm(values_in, gain_vec, shift_vec):
    centre = values_in - jnp.mean(values_in, axis=-1, keepdims=True)
    spread = jnp.mean(centre * centre, axis=-1, keepdims=True)
    return centre * lax.rsqrt(spread + 1e-05) * gain_vec + shift_vec


def allow_table(query_codes, key_codes):
    query_int = query_codes.astype(jnp.int32)
    key_int = key_codes.astype(jnp.int32)
    same_sentence = (query_int // 2)[:, :, None] == (key_int // 2)[:, None, :]
    return same_sentence & ((key_int % 2)[:, None, :] == 1)


def row_scores(query_row, key_row, allow_row):
    scores = (
        jnp.einsum("qhd,khd->hqk", query_row, key_row, preferred_element_type=jnp.float32) * 0.125
    )
    return jnp.where(allow_row[None], scores, -1000000000.0)


def attend_forward(queries, key_heads, value_heads, allowed):

    def one_row(parts):
        query_row, key_row, value_row, allow_row = parts
        scores = row_scores(query_row, key_row, allow_row)
        biggest = jnp.max(scores, axis=-1, keepdims=True)
        weights = jnp.exp(scores - biggest)
        row_total = jnp.sum(weights, axis=-1, keepdims=True)
        weights_low = (weights / row_total).astype(jnp.bfloat16)
        mixed_row = jnp.einsum(
            "hqk,khd->qhd", weights_low, value_row, preferred_element_type=jnp.float32
        )
        return (mixed_row.astype(jnp.bfloat16), (biggest + jnp.log(row_total))[..., 0])

    return lax.map(one_row, (queries, key_heads, value_heads, allowed))


def attend_backward(queries, key_heads, value_heads, allowed, logsum, grad_out):

    def one_row(parts):
        query_row, key_row, value_row, allow_row, logsum_row, grad_row = parts
        scores = row_scores(query_row, key_row, allow_row)
        weights = jnp.exp(scores - logsum_row[..., None])
        grad_weights = jnp.einsum(
            "qhd,khd->hqk", grad_row, value_row, preferred_element_type=jnp.float32
        )
        inner = jnp.sum(weights * grad_weights, axis=-1, keepdims=True)
        grad_scores = (weights * (grad_weights - inner)).astype(jnp.bfloat16)
        grad_query = (
            jnp.einsum("hqk,khd->qhd", grad_scores, key_row, preferred_element_type=jnp.float32)
            * 0.125
        )
        grad_key = (
            jnp.einsum("hqk,qhd->khd", grad_scores, query_row, preferred_element_type=jnp.float32)
            * 0.125
        )
        grad_value = jnp.einsum(
            "hqk,qhd->khd",
            weights.astype(jnp.bfloat16),
            grad_row,
            preferred_element_type=jnp.float32,
        )
        return (grad_query, grad_key, grad_value)

    return lax.map(one_row, (queries, key_heads, value_heads, allowed, logsum, grad_out))


def shards(
    tokens,
    out_grad,
    segment_ids,
    key_mask,
    sent_task,
    task_experts,
    ln1_gain,
    ln1_bias,
    w_qkv,
    w_proj,
    ln2_gain,
    ln2_bias,
    task_embed,
    w_gate,
    w_up,
    b_up,
    w_down,
    b_down,
):
    row_count, piece_len, model_width = tokens.shape
    tok_count = row_count * piece_len
    gain_one, bias_one, qkv_full, proj_full, gain_two, bias_two, embed_full, router_full = (
        lax.all_gather(ln1_gain, ("dp", "fsdp"), axis=0, tiled=True),
        lax.all_gather(ln1_bias, ("dp", "fsdp"), axis=0, tiled=True),
        lax.all_gather(w_qkv, ("dp", "fsdp"), axis=0, tiled=True),
        lax.all_gather(w_proj, ("dp", "fsdp"), axis=0, tiled=True),
        lax.all_gather(ln2_gain, ("dp", "fsdp"), axis=0, tiled=True),
        lax.all_gather(ln2_bias, ("dp", "fsdp"), axis=0, tiled=True),
        lax.all_gather(task_embed, ("dp", "fsdp"), axis=1, tiled=True),
        lax.all_gather(w_gate, ("dp", "fsdp"), axis=0, tiled=True),
    )
    up_full, up_bias, down_full, down_bias = (
        lax.all_gather(w_up, "fsdp", axis=1, tiled=True),
        lax.all_gather(b_up, "fsdp", axis=1, tiled=True),
        lax.all_gather(w_down, "fsdp", axis=1, tiled=True),
        lax.all_gather(b_down, "fsdp", axis=1, tiled=True),
    )
    up_full = up_full[0]
    down_full = down_full[0]
    up_bias_f = up_bias[0].astype(jnp.float32)
    down_bias_f = down_bias[0].astype(jnp.float32)
    experts_count = router_full.shape[1]
    task_count = embed_full.shape[0]
    capacity = 4 * tok_count // experts_count
    inputs = tokens.astype(jnp.float32).reshape(tok_count, model_width)
    normed, norm_back = jax.vjp(
        layer_norm, inputs, gain_one.astype(jnp.float32), bias_one.astype(jnp.float32)
    )
    normed_low = normed.astype(jnp.bfloat16)
    projected = jnp.dot(normed_low, qkv_full, preferred_element_type=jnp.float32).astype(
        jnp.bfloat16
    )
    projected = projected.reshape(row_count, piece_len, 3, HEADS, HD)
    queries = projected[:, :, 0]
    key_heads = projected[:, :, 1]
    value_heads = projected[:, :, 2]
    row_codes = (2 * segment_ids + key_mask).astype(jnp.bfloat16)
    keys_all, values_all, codes_all = (
        lax.all_gather(key_heads, "fsdp", axis=1, tiled=True),
        lax.all_gather(value_heads, "fsdp", axis=1, tiled=True),
        lax.all_gather(row_codes, "fsdp", axis=1, tiled=True),
    )
    allowed = allow_table(row_codes, codes_all)
    attended, logsum = attend_forward(queries, keys_all, values_all, allowed)
    attended_flat = attended.reshape(tok_count, model_width)
    hidden = inputs + jnp.dot(attended_flat, proj_full, preferred_element_type=jnp.float32)
    normed_two, norm_two_back = jax.vjp(
        layer_norm, hidden, gain_two.astype(jnp.float32), bias_two.astype(jnp.float32)
    )
    normed_two_low = normed_two.astype(jnp.bfloat16)
    choose = (task_experts[:, :, None] == jnp.arange(experts_count)[None, None, :]).astype(
        jnp.float32
    )

    def gate_values(embed_in, router_in):
        logits = jnp.einsum(
            "te,tke->tk", jnp.dot(embed_in, router_in, precision=exact), choose, precision=exact
        )
        return jax.nn.softmax(logits, axis=-1)

    gate_probs, gate_back = jax.vjp(
        gate_values, embed_full.astype(jnp.float32), router_full.astype(jnp.float32)
    )
    segment_hot = (segment_ids[:, :, None] == jnp.arange(sent_task.shape[1])[None, None, :]).astype(
        jnp.int32
    )
    task_tok = jnp.sum(segment_hot * sent_task[:, None, :], axis=-1).reshape(tok_count)
    task_hot = (task_tok[:, None] == jnp.arange(task_count)[None, :]).astype(jnp.float32)
    gate_tok = jnp.dot(task_hot, gate_probs, precision=exact)
    expert_tok = jnp.sum(task_hot.astype(jnp.int32)[:, :, None] * task_experts[None], axis=1)
    copy_expert = expert_tok.T.reshape(-1)
    one_hot = (copy_expert[:, None] == jnp.arange(experts_count)[None, :]).astype(jnp.int32)
    rank = jnp.sum((jnp.cumsum(one_hot, axis=0) - one_hot) * one_hot, axis=-1)
    kept_copy = rank < capacity
    slot_index = jnp.where(kept_copy, copy_expert * capacity + rank, experts_count * capacity)
    send_rows = (
        jnp.zeros((experts_count * capacity + 1, model_width), jnp.bfloat16)
        .at[slot_index]
        .set(jnp.tile(normed_two_low, (2, 1)))
    )
    send_rows = send_rows[:-1].reshape(experts_count, capacity, model_width)
    received = lax.all_to_all(send_rows, "dp", split_axis=0, concat_axis=0, tiled=True)
    slot_total = received.shape[0] * received.shape[1]
    block_rows = min(512, slot_total)
    block_count = slot_total // block_rows
    slot_blocks = received.reshape(block_count, block_rows, model_width)

    def expert_forward(slot_rows):
        pre_act = jnp.dot(slot_rows, up_full, preferred_element_type=jnp.float32) + up_bias_f
        activated = jax.nn.gelu(pre_act, approximate=True).astype(jnp.bfloat16)
        return (
            jnp.dot(activated, down_full, preferred_element_type=jnp.float32) + down_bias_f
        ).astype(jnp.bfloat16)

    produced = lax.map(expert_forward, slot_blocks).reshape(received.shape)
    returned = lax.all_to_all(produced, "dp", split_axis=0, concat_axis=0, tiled=True)
    return_pad = jnp.concatenate(
        [returned.reshape(-1, model_width), jnp.zeros((1, model_width), jnp.bfloat16)], axis=0
    )
    copies = jnp.take(return_pad, slot_index, axis=0).reshape(2, tok_count, model_width)
    kept_float = kept_copy.reshape(2, tok_count).astype(jnp.float32)
    copy_weight = gate_tok.T * kept_float
    mixed_rows = (
        hidden
        + copy_weight[0][:, None] * copies[0].astype(jnp.float32)
        + copy_weight[1][:, None] * copies[1].astype(jnp.float32)
    )
    output = mixed_rows.astype(jnp.bfloat16).reshape(tokens.shape)
    grad_mixed = out_grad.astype(jnp.float32).reshape(tok_count, model_width)
    grad_copies = (copy_weight[:, :, None] * grad_mixed[None]).astype(jnp.bfloat16)
    grad_gate_copy = jnp.sum(copies.astype(jnp.float32) * grad_mixed[None], axis=-1) * kept_float
    grad_send = (
        jnp.zeros((experts_count * capacity + 1, model_width), jnp.bfloat16)
        .at[slot_index]
        .set(grad_copies.reshape(-1, model_width))
    )
    grad_send = grad_send[:-1].reshape(experts_count, capacity, model_width)
    grad_received = lax.all_to_all(grad_send, "dp", split_axis=0, concat_axis=0, tiled=True)

    def expert_backward(totals, parts):
        slot_rows, grad_rows = parts
        pre_act = jnp.dot(slot_rows, up_full, preferred_element_type=jnp.float32) + up_bias_f
        activated, gelu_back = jax.vjp(
            lambda values_in: jax.nn.gelu(values_in, approximate=True), pre_act
        )
        activated_low = activated.astype(jnp.bfloat16)
        grad_act = jnp.dot(grad_rows, down_full.T, preferred_element_type=jnp.float32)
        grad_pre = gelu_back(grad_act)[0].astype(jnp.bfloat16)
        grad_inputs_slot = jnp.dot(grad_pre, up_full.T, preferred_element_type=jnp.float32).astype(
            jnp.bfloat16
        )
        totals = (
            totals[0] + jnp.dot(slot_rows.T, grad_pre, preferred_element_type=jnp.float32),
            totals[1] + jnp.sum(grad_pre.astype(jnp.float32), axis=0),
            totals[2] + jnp.dot(activated_low.T, grad_rows, preferred_element_type=jnp.float32),
            totals[3] + jnp.sum(grad_rows.astype(jnp.float32), axis=0),
        )
        return (totals, grad_inputs_slot)

    start_totals = (
        jnp.zeros(up_full.shape, jnp.float32),
        jnp.zeros(up_bias_f.shape, jnp.float32),
        jnp.zeros(down_full.shape, jnp.float32),
        jnp.zeros(down_bias_f.shape, jnp.float32),
    )
    totals, grad_slots = lax.scan(
        expert_backward,
        start_totals,
        (slot_blocks, grad_received.reshape(block_count, block_rows, model_width)),
    )
    grad_back = lax.all_to_all(
        grad_slots.reshape(received.shape), "dp", split_axis=0, concat_axis=0, tiled=True
    )
    grad_pad = jnp.concatenate(
        [grad_back.reshape(-1, model_width), jnp.zeros((1, model_width), jnp.bfloat16)], axis=0
    )
    grad_taken = (
        jnp.take(grad_pad, slot_index, axis=0)
        .reshape(2, tok_count, model_width)
        .astype(jnp.float32)
    )
    grad_normed_two = grad_taken[0] + grad_taken[1]
    grad_up, grad_up_bias, grad_down, grad_down_bias = (
        lax.psum_scatter(
            totals[0][None].astype(jnp.bfloat16), "fsdp", scatter_dimension=1, tiled=True
        ).astype(jnp.float32),
        lax.psum_scatter(
            totals[1][None].astype(jnp.bfloat16), "fsdp", scatter_dimension=1, tiled=True
        ).astype(jnp.float32),
        lax.psum_scatter(
            totals[2][None].astype(jnp.bfloat16), "fsdp", scatter_dimension=1, tiled=True
        ).astype(jnp.float32),
        lax.psum_scatter(
            totals[3][None].astype(jnp.bfloat16), "fsdp", scatter_dimension=1, tiled=True
        ).astype(jnp.float32),
    )
    grad_hidden_part, grad_gain_two, grad_bias_two = norm_two_back(grad_normed_two)
    grad_hidden = grad_mixed + grad_hidden_part
    grad_branch = grad_hidden.astype(jnp.bfloat16)
    grad_proj = jnp.dot(attended_flat.T, grad_branch, preferred_element_type=jnp.float32)
    grad_attended = jnp.dot(grad_branch, proj_full.T, preferred_element_type=jnp.float32).astype(
        jnp.bfloat16
    )
    grad_attended = grad_attended.reshape(row_count, piece_len, HEADS, HD)
    part_query, part_key, part_value = attend_backward(
        queries, keys_all, values_all, allowed, logsum, grad_attended
    )
    summed_key, summed_value = (
        lax.psum_scatter(
            part_key.astype(jnp.bfloat16), "fsdp", scatter_dimension=1, tiled=True
        ).astype(jnp.float32),
        lax.psum_scatter(
            part_value.astype(jnp.bfloat16), "fsdp", scatter_dimension=1, tiled=True
        ).astype(jnp.float32),
    )
    grad_query = part_query.astype(jnp.bfloat16)
    grad_key = summed_key.astype(jnp.bfloat16)
    grad_value = summed_value.astype(jnp.bfloat16)
    grad_projected = jnp.stack([grad_query, grad_key, grad_value], axis=2).reshape(
        tok_count, 3 * model_width
    )
    grad_qkv_weight = jnp.dot(normed_low.T, grad_projected, preferred_element_type=jnp.float32)
    grad_normed = jnp.dot(grad_projected, qkv_full.T, preferred_element_type=jnp.float32)
    grad_inputs, grad_gain_one, grad_bias_one = norm_back(grad_normed)
    grad_tokens = (grad_hidden + grad_inputs).reshape(tokens.shape)
    grad_gate_task = jnp.dot(task_hot.T, grad_gate_copy.T, precision=exact)
    grad_embed, grad_router = gate_back(grad_gate_task)
    reduced = (
        lax.psum_scatter(grad_gain_one, ("dp", "fsdp"), scatter_dimension=0, tiled=True),
        lax.psum_scatter(grad_bias_one, ("dp", "fsdp"), scatter_dimension=0, tiled=True),
        lax.psum_scatter(grad_qkv_weight, ("dp", "fsdp"), scatter_dimension=0, tiled=True),
        lax.psum_scatter(grad_proj, ("dp", "fsdp"), scatter_dimension=0, tiled=True),
        lax.psum_scatter(grad_gain_two, ("dp", "fsdp"), scatter_dimension=0, tiled=True),
        lax.psum_scatter(grad_bias_two, ("dp", "fsdp"), scatter_dimension=0, tiled=True),
        lax.psum_scatter(grad_embed, ("dp", "fsdp"), scatter_dimension=1, tiled=True),
        lax.psum_scatter(grad_router, ("dp", "fsdp"), scatter_dimension=0, tiled=True),
    )
    return (
        output,
        grad_tokens,
        reduced[0],
        reduced[1],
        reduced[2],
        reduced[3],
        reduced[4],
        reduced[5],
        reduced[6],
        reduced[7],
        grad_up,
        grad_up_bias,
        grad_down,
        grad_down_bias,
    )


MESH_ID = pl.DeviceIdType.MESH
VMEM_MAX = 60 * 1024 * 1024
TILE = 16
BLOCK = 512
FCHUNK = 512
QCHUNK = 256
FAR = -float(2**30)
F32 = jnp.float32
BF16 = jnp.bfloat16


def dot_nn(lhs, rhs):
    return lax.dot_general(lhs, rhs, (((1,), (0,)), ((), ())), preferred_element_type=F32)


def dot_nt(lhs, rhs):
    return lax.dot_general(lhs, rhs, (((1,), (1,)), ((), ())), preferred_element_type=F32)


def dot_tn(lhs, rhs):
    return lax.dot_general(lhs, rhs, (((0,), (0,)), ((), ())), preferred_element_type=F32)


def vmem_spec():
    return pl.BlockSpec(memory_space=pltpu.VMEM)


def any_spec():
    return pl.BlockSpec(memory_space=pl.ANY)


def smem_spec():
    return pl.BlockSpec(memory_space=pltpu.SMEM)


def norm_parts(values):
    centre = values - jnp.mean(values, axis=-1, keepdims=True)
    spread = jnp.mean(centre * centre, axis=-1, keepdims=True)
    scale = lax.rsqrt(spread + 1e-05)
    return centre * scale, scale


def norm_back_parts(grad, normal, scale):
    mean_grad = jnp.mean(grad, axis=-1, keepdims=True)
    mean_prod = jnp.mean(grad * normal, axis=-1, keepdims=True)
    return (grad - mean_grad - normal * mean_prod) * scale


def fold_rows(values):
    rows, width = values.shape
    return jnp.sum(values.reshape(rows // 8, 8, width), axis=0)


def plane_ids():
    me = lax.axis_index("dp")
    core, xpos, ypos = lax.rem(me, 2), lax.rem(me // 2, 2), me // 4

    def at(ypos, xpos, core):
        return (ypos * 2 + xpos) * 2 + core

    return me, core, xpos, ypos, at


def greet(peers):
    barrier = pltpu.get_barrier_semaphore()
    for peer in peers:
        pl.semaphore_signal(barrier, inc=1, device_id=peer, device_id_type=MESH_ID)
    pl.semaphore_wait(barrier, len(peers))


class Sender:
    def __init__(self, send_sems, recv_sems):
        self.send_sems, self.recv_sems, self.count, self.all = send_sems, recv_sems, 0, []

    def start(self, src, dst, peer):
        copy = pltpu.make_async_remote_copy(
            src_ref=src,
            dst_ref=dst,
            send_sem=self.send_sems.at[self.count],
            recv_sem=self.recv_sems.at[self.count],
            device_id=peer,
            device_id_type=MESH_ID,
        )
        copy.start()
        self.count += 1
        self.all.append(copy)
        return copy

    def drain(self):
        for copy in self.all:
            copy.wait_send()


def plane_gather_steps(block, own, rows, sender, z):
    me, core, xpos, ypos, at = plane_ids()
    sib, xn, yn = at(ypos, xpos, 1 - core), at(ypos, 1 - xpos, core), at(1 - ypos, xpos, core)
    diag = at(1 - ypos, 1 - xpos, core)
    half = rows // 2

    def part(i, k):
        return block(i).at[pl.ds(k * half, half)]

    def send(i, k, peer):
        src = own.at[pl.ds(k * half, half)] if i is me else part(i, k)
        return sender.start(src, part(i, k), (peer, z))

    x_own = [send(me, 0, xn)]
    y_own = [send(me, 1, yn)]
    x_own.append(send(me, 1, xn))
    y_own.insert(0, send(me, 0, yn))
    last = [send(me, 0, sib), send(me, 1, sib)]
    x_own[0].wait_recv()
    to_y = send(xn, 0, yn)
    y_own[1].wait_recv()
    to_x = send(yn, 1, xn)
    last.append(send(xn, 0, sib))
    last.append(send(yn, 1, sib))
    x_own[1].wait_recv()
    last.append(send(xn, 1, sib))
    y_own[0].wait_recv()
    last.append(send(yn, 0, sib))
    to_y.wait_recv()
    last.append(send(diag, 0, sib))
    to_x.wait_recv()
    last.append(send(diag, 1, sib))
    for copy in last:
        copy.wait_recv()


PLANE_GATHER_COPIES = 14


def plane_peers(z):
    me, core, xpos, ypos, at = plane_ids()
    return [
        (at(ypos, xpos, 1 - core), z),
        (at(ypos, 1 - xpos, core), z),
        (at(1 - ypos, xpos, core), z),
    ]


def column_peers(planes):
    me, z = lax.axis_index("dp"), lax.axis_index("fsdp")
    peers = [(me, lax.rem(z + k, planes)) for k in range(1, planes)]
    return peers + [(me ^ 1, lax.rem(z + k, planes)) for k in range(1, planes)]


class PlaneGather:
    COPIES = 28

    def __init__(self, block, own, send_sems, recv_sems):
        me, core, xpos, ypos, at = plane_ids()
        self.z = lax.axis_index("fsdp")
        self.me = me
        self.sib = at(ypos, xpos, 1 - core)
        self.xn, self.yn = at(ypos, 1 - xpos, core), at(1 - ypos, xpos, core)
        self.diag = at(1 - ypos, 1 - xpos, core)
        self.block, self.own = block, own
        self.send_sems, self.recv_sems = send_sems, recv_sems
        self.all = {}

    def send(self, kind, c, src, owner, peer):
        copy = pltpu.make_async_remote_copy(
            src_ref=src,
            dst_ref=self.block(owner).at[c],
            send_sem=self.send_sems.at[kind * 4 + c],
            recv_sem=self.recv_sems.at[kind * 4 + c],
            device_id=(peer, self.z),
            device_id_type=MESH_ID,
        )
        copy.start()
        self.all[kind, c] = copy

    def start(self, c):
        src = self.own.at[c]
        self.send(0, c, src, self.me, self.xn)
        self.send(1, c, src, self.me, self.yn)
        self.send(2, c, src, self.me, self.sib)

    def pass_on(self, c):
        x_part, y_part = self.block(self.xn).at[c], self.block(self.yn).at[c]
        self.all[0, c].wait_recv()
        if c < 2:
            self.send(3, c, x_part, self.xn, self.yn)
        self.send(4, c, x_part, self.xn, self.sib)
        self.all[1, c].wait_recv()
        if c >= 2:
            self.send(3, c, y_part, self.yn, self.xn)
        self.send(5, c, y_part, self.yn, self.sib)

    def pass_diag(self, c):
        self.all[3, c].wait_recv()
        self.send(6, c, self.block(self.diag).at[c], self.diag, self.sib)

    def finish(self):
        for kind in (2, 4, 5, 6):
            for c in range(4):
                self.all[kind, c].wait_recv()
        for copy in self.all.values():
            copy.wait_send()


def small_gather_kernel(planes, groups, in_ref, out_ref, send_sems, recv_sems):
    me, z = lax.axis_index("dp"), lax.axis_index("fsdp")
    z_peers = [(me, lax.rem(z + k, planes)) for k in range(1, planes)]
    d_peers = [(lax.rem(me + k, groups), z) for k in range(1, groups)]
    greet(z_peers + d_peers)
    sender = Sender(send_sems, recv_sems)
    out_ref[me, z] = in_ref[...]
    first = [sender.start(in_ref, out_ref.at[me, z], peer) for peer in z_peers]
    for copy in first:
        copy.wait_recv()
    second = [sender.start(out_ref.at[me], out_ref.at[me], peer) for peer in d_peers]
    for copy in second:
        copy.wait_recv()
    sender.drain()


def small_gather(payload, planes, groups):
    return pl.pallas_call(
        functools.partial(small_gather_kernel, planes, groups),
        out_shape=jax.ShapeDtypeStruct((groups, planes) + payload.shape, payload.dtype),
        in_specs=[vmem_spec()],
        out_specs=vmem_spec(),
        scratch_shapes=[
            pltpu.SemaphoreType.DMA((planes + groups,)),
            pltpu.SemaphoreType.DMA((planes + groups,)),
        ],
        compiler_params=pltpu.CompilerParams(collective_id=1, has_side_effects=True),
        name="routing_gather",
    )(payload)


def plane_scatter_steps(z_ref, own, theirs, deep, near_x, near_y, sender, loc_sems, z):
    me, core, xpos, ypos, at = plane_ids()
    sib, xn, yn = at(ypos, xpos, 1 - core), at(ypos, 1 - xpos, core), at(1 - ypos, xpos, core)
    chips = [(ypos, xpos), (ypos, 1 - xpos), (1 - ypos, xpos), (1 - ypos, 1 - xpos)]
    rows = z_ref.shape[1]
    half = rows // 2
    first, second = pl.ds(0, half), pl.ds(half, half)
    loads, trades = {}, {}
    for slot in (3, 1, 2, 0):
        pos = chips[slot]
        loads[slot] = pltpu.make_async_copy(
            z_ref.at[at(pos[0], pos[1], core)], own.at[slot], loc_sems.at[slot]
        )
        loads[slot].start()
        trades[slot] = sender.start(
            z_ref.at[at(pos[0], pos[1], 1 - core)], theirs.at[slot], (sib, z)
        )

    yield

    def add(slot, part):
        own[slot, part] = (
            own[slot, part].astype(F32) + theirs[slot, part].astype(F32)
        ).astype(own.dtype)

    loads[3].wait()
    trades[3].wait_recv()
    add(3, first)
    deep_x = sender.start(own.at[3, first], deep.at[0], (xn, z))
    add(3, second)
    deep_y = sender.start(own.at[3, second], deep.at[1], (yn, z))
    loads[1].wait()
    trades[1].wait_recv()
    add(1, first)
    x_first = sender.start(own.at[1, first], near_x.at[first], (xn, z))
    loads[2].wait()
    trades[2].wait_recv()
    add(2, second)
    y_second = sender.start(own.at[2, second], near_y.at[second], (yn, z))
    add(1, second)
    add(2, first)
    yield
    deep_y.wait_recv()
    own[1, second] = (own[1, second].astype(F32) + deep[1].astype(F32)).astype(own.dtype)
    x_second = sender.start(own.at[1, second], near_x.at[second], (xn, z))
    deep_x.wait_recv()
    own[2, first] = (own[2, first].astype(F32) + deep[0].astype(F32)).astype(own.dtype)
    y_first = sender.start(own.at[2, first], near_y.at[first], (yn, z))
    yield
    loads[0].wait()
    trades[0].wait_recv()
    yield
    mine = own[0].astype(F32) + theirs[0].astype(F32)
    x_first.wait_recv()
    y_second.wait_recv()
    x_second.wait_recv()
    y_first.wait_recv()
    yield mine + near_x[...].astype(F32) + near_y[...].astype(F32)


PLANE_SCATTER_COPIES = 10


def pick_rows_kernel(order_ref, *refs):
    count = len(refs) // 2
    for a in range(count):
        refs[count + a][...] = refs[a][...].astype(refs[count + a].dtype)


def pick_rows(order, arrays, kinds):
    def block(array):
        return (1,) + array.shape[1:]

    return pl.pallas_call(
        pick_rows_kernel,
        out_shape=tuple(
            jax.ShapeDtypeStruct(array.shape, kind) for array, kind in zip(arrays, kinds)
        ),
        grid_spec=pltpu.PrefetchScalarGridSpec(
            num_scalar_prefetch=1,
            grid=(arrays[0].shape[0],),
            in_specs=[
                pl.BlockSpec(block(array), lambda r, order_ref: (order_ref[r], 0, 0))
                for array in arrays
            ],
            out_specs=tuple(
                pl.BlockSpec(block(array), lambda r, order_ref: (r, 0, 0)) for array in arrays
            ),
        ),
        name="row_order",
    )(order, *arrays)


def unit_copy(src, dst, send_sem, recv_sem, peer):
    return pltpu.make_async_remote_copy(
        src_ref=src,
        dst_ref=dst,
        send_sem=send_sem,
        recv_sem=recv_sem,
        device_id=peer,
        device_id_type=MESH_ID,
    )


class WeightSpread:
    def __init__(self, up_ref, down_ref, up_all, down_all, sems):
        self.me, self.z = lax.axis_index("dp"), lax.axis_index("fsdp")
        self.core = lax.rem(self.me, 2)
        self.src = (up_ref, down_ref)
        self.dst = (up_all, down_all)
        self.own_send, self.pass_send, self.recv, self.local = sems
        self.side = self.z // 2
        self.near = self.z ^ 1
        self.far = 2 - self.side
        self.inner = (self.z == 1) | (self.z == 2)

    def targets(self):
        chip = self.me - self.core
        return [
            (self.core, self.near),
            (self.core, self.far),
            (1 - self.core, self.near),
            (1 - self.core, self.far),
            (1 - self.core, self.z),
        ], chip

    def copy(self, kind, src, m, p, send_sem, peer):
        return unit_copy(
            src,
            self.dst[kind].at[m, p],
            send_sem,
            self.recv.at[kind * 8 + m * 4 + p],
            peer,
        )

    def own(self):
        targets, chip = self.targets()
        out = []
        for kind in range(2):
            for k, (h, p) in enumerate(targets):
                out.append(
                    self.copy(
                        kind,
                        self.src[kind].at[h],
                        self.core,
                        self.z,
                        self.own_send.at[kind * 5 + k],
                        (chip + h, p),
                    )
                )
        return out

    def mine(self):
        return [
            pltpu.make_async_copy(
                self.src[kind].at[self.core],
                self.dst[kind].at[self.core, self.z],
                self.local.at[kind],
            )
            for kind in range(2)
        ]

    def passed(self, j):
        p = 2 * (1 - self.side) + j
        return [
            self.copy(
                kind,
                self.dst[kind].at[m, p],
                m,
                p,
                self.pass_send.at[kind * 4 + m * 2 + j],
                (self.me, self.near),
            )
            for kind in range(2)
            for m in range(2)
        ]

    def start(self):
        for copy in self.mine() + self.own():
            copy.start()

    def pass_on(self, first):
        for side in range(2):

            @pl.when((self.z == 1 + side))
            def _():
                j = side if first else 1 - side
                for copy in self.passed(j):
                    copy.wait_recv()
                    copy.start()

    def finish(self):
        for copy in self.mine():
            copy.wait()
        for copy in self.own():
            copy.wait_send()

        def arrived(kind, m, p):
            self.copy(
                kind, self.dst[kind].at[m, p], m, p, self.own_send.at[0], (self.me, self.near)
            ).wait_recv()

        for kind in range(2):
            arrived(kind, 1 - self.core, self.z)
            for m in range(2):
                arrived(kind, m, self.near)

        @pl.when(self.inner)
        def _():
            for j in range(2):
                for copy in self.passed(j):
                    copy.wait_send()

        @pl.when(jnp.logical_not(self.inner))
        def _():
            for kind in range(2):
                for m in range(2):
                    for j in range(2):
                        arrived(kind, m, 2 * (1 - self.side) + j)


def forward_kernel(
    heads,
    planes,
    tok_ref,
    gm_ref,
    w_ref,
    upw_ref,
    downw_ref,
    norm_ref,
    qf_ref,
    kf_ref,
    row_ref,
    dense_ref,
    qkv_ref,
    o_ref,
    lse_ref,
    hres_ref,
    xn2_ref,
    x_all,
    g_all,
    up_all,
    down_all,
    kaug,
    vaug,
    z_send,
    z_recv,
    w_send,
    w_recv,
    x_send,
    x_recv,
    g_send,
    g_recv,
    u_own,
    u_pass,
    u_recv,
    loc_sems,
):
    me, z = lax.axis_index("dp"), lax.axis_index("fsdp")
    z_peers = [(me, lax.rem(z + k, planes)) for k in range(1, planes)]
    greet(column_peers(planes) + plane_peers(z))
    rows, width = qkv_ref.shape[0], row_ref.shape[2]
    chunk = row_ref.shape[1]
    head = width // heads
    pair = 2 * head
    shard = w_ref.shape[0]
    sender = Sender(z_send, z_recv)
    dense_own = pltpu.make_async_copy(
        w_ref, dense_ref.at[me, pl.ds(z * shard, shard)], loc_sems.at[0]
    )
    dense_own.start()
    tok_own = pltpu.make_async_copy(tok_ref.at[z], row_ref.at[z], loc_sems.at[1])
    tok_own.start()
    gm_own = pltpu.make_async_copy(gm_ref.at[z], g_all.at[me, z], loc_sems.at[2])
    gm_own.start()
    dense_z = [
        sender.start(w_ref, dense_ref.at[me, pl.ds(z * shard, shard)], peer) for peer in z_peers
    ]
    toks = [sender.start(tok_ref.at[peer[1]], row_ref.at[z], peer) for peer in z_peers]
    dense_own.wait()
    for copy in dense_z:
        copy.wait_recv()
    dense_sender = Sender(w_send, w_recv)
    plane_gather_steps(
        lambda i: dense_ref.at[i], dense_ref.at[me], planes * shard, dense_sender, z
    )
    for copy in toks:
        copy.wait_recv()
    tok_own.wait()
    gms = [sender.start(gm_ref.at[peer[1]], g_all.at[me, z], peer) for peer in z_peers]
    spread = WeightSpread(upw_ref, downw_ref, up_all, down_all, (u_own, u_pass, u_recv, loc_sems.at[pl.ds(3, 2)]))
    x_gather = PlaneGather(lambda i: x_all.at[i], xn2_ref, x_send, x_recv)
    g_gather = PlaneGather(lambda i: g_all.at[i], g_all.at[me], g_send, g_recv)

    lane = lax.broadcasted_iota(jnp.int32, (rows, pair), 1)
    lane_c = lax.broadcasted_iota(jnp.int32, (chunk, pair), 1)
    w_qkv = dense_ref[:, :, : 3 * width].reshape(width, 3 * width)

    def project(c, carry):
        part = pl.ds(pl.multiple_of(c * chunk, chunk), chunk)
        normal, _ = norm_parts(row_ref[c].astype(F32))
        xn1 = (normal * norm_ref[0:1, :] + norm_ref[1:2, :]).astype(BF16)
        out = dot_nn(xn1, dense_ref[:, :, : 3 * width].reshape(width, 3 * width))
        qkv_ref[part, :width] = (out[:, :width] * 0.125).astype(BF16)
        qkv_ref[part, width:] = out[:, width:].astype(BF16)
        return carry

    lax.fori_loop(0, planes, project, 0)

    def prepare(g, carry):
        k_pair = qkv_ref[:, pl.ds(pl.multiple_of(width + g * pair, pair), pair)]
        v_pair = qkv_ref[:, pl.ds(pl.multiple_of(2 * width + g * pair, pair), pair)]
        zero = jnp.zeros_like(k_pair)
        for side in range(2):
            mine = (lane // head) == side
            kaug[g, side, :, :pair] = jnp.where(mine, k_pair, zero)
            vaug[g, side, :, :pair] = jnp.where(mine, v_pair, zero)
            kaug[g, side, :, pair:] = kf_ref[...]
            vaug[g, side, :, pair:] = jnp.where(mine, 1.0, 0.0).astype(BF16)
        return carry

    lax.fori_loop(0, heads // 2, prepare, 0)

    def attend(c):
        part = pl.ds(c * chunk, chunk)

        def one_pair(g, carry):
            cols = pl.ds(pl.multiple_of(g * pair, pair), pair)
            qa = jnp.concatenate([qkv_ref[part, cols], qf_ref[part, :]], axis=1)
            acc = jnp.zeros((chunk, 2 * pair), F32)
            tops = []
            for side in range(2):
                s = dot_nt(qa, kaug[g, side])
                top = jnp.max(s, axis=-1, keepdims=True)
                acc = acc + dot_nn(jnp.exp(s - top).astype(BF16), vaug[g, side])
                tops.append(top)
            total = acc[:, pair:]
            o_ref[part, cols] = (acc[:, :pair] / total).astype(BF16)
            top = jnp.where(lane_c < head, tops[0], tops[1])
            lse_ref[part, cols] = top + jnp.log(total)
            return carry

        lax.fori_loop(0, heads // 2, one_pair, 0)
        w_proj = dense_ref[:, :, 3 * width :].reshape(width, width)
        hres = row_ref[c].astype(F32) + dot_nn(o_ref[part, :], w_proj)
        hres_ref[part, :] = hres
        normal, _ = norm_parts(hres)
        xn2_ref[c] = (normal * norm_ref[2:3, :] + norm_ref[3:4, :]).astype(BF16)
        x_gather.start(c)

    attend(0)
    attend(1)
    for copy in gms:
        copy.wait_recv()
    gm_own.wait()
    spread.start()
    for c in range(4):
        g_gather.start(c)
    attend(2)
    x_gather.pass_on(0)
    x_gather.pass_on(1)
    attend(3)
    x_gather.pass_on(2)
    for c in range(4):
        g_gather.pass_on(c)
    x_gather.pass_on(3)
    spread.pass_on(True)
    for c in range(4):
        x_gather.pass_diag(c)
        g_gather.pass_diag(c)
    spread.pass_on(False)
    x_gather.finish()
    g_gather.finish()
    spread.finish()
    sender.drain()
    dense_sender.drain()


def forward(tokens, grads, dense, up, down, norms, qf, kf, heads, groups):
    planes, piece, width = tokens.shape
    rows = planes * piece
    pair = 2 * (width // heads)
    sd = jax.ShapeDtypeStruct
    dma = pltpu.SemaphoreType.DMA
    return pl.pallas_call(
        functools.partial(forward_kernel, heads, planes),
        out_shape=(
            sd(tokens.shape, BF16),
            sd((groups, planes * dense.shape[0], dense.shape[1]), BF16),
            sd((rows, 3 * width), BF16),
            sd((rows, width), BF16),
            sd((rows, width), F32),
            sd((rows, width), F32),
            sd(tokens.shape, BF16),
            sd((groups,) + tokens.shape, BF16),
            sd((groups,) + tokens.shape, BF16),
            sd((2, planes) + up.shape[1:], BF16),
            sd((2, planes) + down.shape[1:], BF16),
        ),
        in_specs=[any_spec()] * 5 + [vmem_spec()] * 3,
        out_specs=tuple([vmem_spec()] * 7 + [any_spec()] * 4),
        scratch_shapes=[
            pltpu.VMEM((heads // 2, 2, rows, 2 * pair), BF16),
            pltpu.VMEM((heads // 2, 2, rows, 2 * pair), BF16),
            dma((3 * planes,)),
            dma((3 * planes,)),
            dma((PLANE_GATHER_COPIES,)),
            dma((PLANE_GATHER_COPIES,)),
            dma((PlaneGather.COPIES,)),
            dma((PlaneGather.COPIES,)),
            dma((PlaneGather.COPIES,)),
            dma((PlaneGather.COPIES,)),
            dma((10,)),
            dma((8,)),
            dma((16,)),
            dma((5,)),
        ],
        compiler_params=pltpu.CompilerParams(
            collective_id=2, has_side_effects=True, vmem_limit_bytes=VMEM_MAX
        ),
        cost_estimate=pl.CostEstimate(
            flops=40_000_000_000, bytes_accessed=10_000_000, transcendentals=8_000_000
        ),
        name="attention_forward",
    )(tokens, grads, dense, up, down, norms, qf, kf)


def split3(values):
    high = values.astype(BF16)
    rest = values - high.astype(F32)
    middle = rest.astype(BF16)
    low = (rest - middle.astype(F32)).astype(BF16)
    return high, middle, low


def backward_kernel(
    heads,
    planes,
    groups,
    row_ref,
    norm_ref,
    dense_ref,
    qf_ref,
    kf_ref,
    qkv_ref,
    o_ref,
    lse_ref,
    hres_ref,
    g_all,
    zd_ref,
    zy_ref,
    gu_ref,
    gd_ref,
    small_ref,
    out_ref,
    dtok_ref,
    shard_ref,
    gu_in,
    gd_in,
    small_out,
    gm,
    kaug,
    vaug,
    dh,
    db,
    do,
    delta,
    qt,
    dot_t,
    dkt,
    dvt,
    dqkv,
    xn1,
    dw,
    dnorm,
    moved,
    own,
    d_theirs,
    d_deep,
    d_x,
    d_y,
    y_theirs,
    y_deep,
    y_x,
    y_y,
    w_own,
    w_theirs,
    w_deep,
    w_x,
    w_y,
    w_sum,
    w_in,
    small_in,
    s_send,
    s_recv,
    d_send,
    d_recv,
    y_send,
    y_recv,
    w_send,
    w_recv,
    z_send,
    z_recv,
    u_send,
    u_recv,
    loc_sems,
):
    me, z = lax.axis_index("dp"), lax.axis_index("fsdp")
    core = lax.rem(me, 2)
    chip = me - core
    z_peers = [(me, lax.rem(z + k, planes)) for k in range(1, planes)]
    d_peers = [(lax.rem(me + k, groups), z) for k in range(1, groups)]
    greet(column_peers(planes) + d_peers)
    rows, width = hres_ref.shape
    chunk = row_ref.shape[1]
    head = width // heads
    pair = 2 * head

    gm_load = pltpu.make_async_copy(g_all.at[me], gm, loc_sems.at[4])
    gm_load.start()
    small_sender = Sender(s_send, s_recv)
    small_z = [small_sender.start(small_ref, small_in.at[k], p) for k, p in enumerate(z_peers)]
    d_sender = Sender(d_send, d_recv)
    d_scatter = plane_scatter_steps(
        zd_ref, own, d_theirs, d_deep, d_x, d_y, d_sender, loc_sems, z
    )
    next(d_scatter)
    unit_copies = []
    for kind, (src, dst) in enumerate(((gu_ref, gu_in), (gd_ref, gd_in))):
        for t in range(2):
            for k in range(planes):
                h, p = (core + t) % 2, lax.rem(z + k, planes)
                if t == 0 and k == 0:
                    copy = pltpu.make_async_copy(
                        src.at[z, core], dst.at[core, z], loc_sems.at[5 + kind]
                    )
                    copy.start()
                else:
                    i = kind * 8 + t * 4 + k
                    copy = unit_copy(
                        src.at[p, h], dst.at[core, z], u_send.at[i], u_recv.at[i], (chip + h, p)
                    )
                    copy.start()
                unit_copies.append(copy)
    for copy in small_z:
        copy.wait_recv()
    small_out[me] = small_ref[...] + jnp.sum(small_in[...], axis=0)
    small_d = [small_sender.start(small_out.at[me], small_out.at[me], p) for p in d_peers]
    gm_load.wait()

    for _ in range(3):
        next(d_scatter)
    dh[...] = next(d_scatter)
    y_sender = Sender(y_send, y_recv)
    y_scatter = plane_scatter_steps(
        zy_ref, own, y_theirs, y_deep, y_x, y_y, y_sender, loc_sems, z
    )
    d_sender.drain()
    next(y_scatter)

    lane = lax.broadcasted_iota(jnp.int32, (rows, pair), 1)
    lane_c = lax.broadcasted_iota(jnp.int32, (chunk, pair), 1)
    same = (
        lax.broadcasted_iota(jnp.int32, (pair, pair), 0) // head
        == lax.broadcasted_iota(jnp.int32, (pair, pair), 1) // head
    )
    ones = jnp.where(same, 1.0, 0.0).astype(BF16)
    dnorm[...] = jnp.zeros_like(dnorm)

    def begin(c, carry):
        part = pl.ds(pl.multiple_of(c * chunk, chunk), chunk)
        normal, scale = norm_parts(hres_ref[part, :])
        grad = dh[part, :]
        dnorm[2] += fold_rows(grad * normal)
        dnorm[3] += fold_rows(grad)
        dh_part = gm[c].astype(F32) + norm_back_parts(grad * norm_ref[2:3, :], normal, scale)
        dh[part, :] = dh_part
        low = dh_part.astype(BF16)
        db[part, :] = low
        do_part = dot_nt(low, dense_ref[:, :, 3 * width :].reshape(width, width)).astype(BF16)
        do[part, :] = do_part
        prod = do_part.astype(F32) * o_ref[part, :].astype(F32)
        high = prod.astype(BF16)
        rest = (prod - high.astype(F32)).astype(BF16)
        for g in range(heads // 2):
            cols = slice(g * pair, (g + 1) * pair)
            delta[part, cols] = dot_nn(high[:, cols], ones) + dot_nn(rest[:, cols], ones)
        normal, _ = norm_parts(row_ref[c].astype(F32))
        xn1[part, :] = (normal * norm_ref[0:1, :] + norm_ref[1:2, :]).astype(BF16)
        return carry

    lax.fori_loop(0, planes, begin, 0)
    next(y_scatter)
    w_rows = w_sum.shape[0]
    w_cols = w_sum.shape[1]
    dw[:, :, 3 * width : 4 * width] = (
        dot_tn(o_ref[...], db[...]).astype(BF16).reshape(groups, w_rows, width)
    )

    mark = (lane >= heads) & (lane < heads + 3)
    for side in range(2):
        kaug[side, :, pair:] = jnp.where(mark, 1.0, kf_ref[...].astype(F32)).astype(BF16)
        vaug[side, :, pair:] = jnp.where(mark, 1.0, 0.0).astype(BF16)

    def put_parts(base, values):
        high, middle, low = split3(-values)
        out = jnp.where(lane_c == heads, high.astype(F32), base)
        out = jnp.where(lane_c == heads + 1, middle.astype(F32), out)
        return jnp.where(lane_c == heads + 2, low.astype(F32), out).astype(BF16)

    def one_pair(g):
        cols = slice(g * pair, (g + 1) * pair)
        k_pair = qkv_ref[:, width + g * pair : width + (g + 1) * pair]
        v_pair = qkv_ref[:, 2 * width + g * pair : 2 * width + (g + 1) * pair]
        zero = jnp.zeros_like(k_pair)
        for side in range(2):
            mine = (lane // head) == side
            kaug[side, :, :pair] = jnp.where(mine, k_pair, zero)
            vaug[side, :, :pair] = jnp.where(mine, v_pair, zero)
        qt[...] = qkv_ref[:, cols].T
        dot_t[...] = do[:, cols].T
        dkt[...] = jnp.zeros_like(dkt)
        dvt[...] = jnp.zeros_like(dvt)

        def one_chunk(c, inner):
            part = pl.ds(pl.multiple_of(c * chunk, chunk), chunk)
            q_pair, do_pair = qkv_ref[part, cols], do[part, cols]
            lse_pair, delta_pair = lse_ref[part, cols], delta[part, cols]
            base = qf_ref[part, :].astype(F32)
            acc = jnp.zeros((chunk, pair), F32)
            for side in range(2):
                lse = lse_pair[:, side * head : side * head + 1]
                qa = jnp.concatenate([q_pair, put_parts(base, lse)], axis=1)
                pr = jnp.exp(dot_nt(qa, kaug[side]))
                dlt = delta_pair[:, side * head : side * head + 1]
                da = jnp.concatenate([do_pair, put_parts(jnp.zeros_like(base), dlt)], axis=1)
                ds = (pr * dot_nt(da, vaug[side])).astype(BF16)
                acc = acc + dot_nn(ds, kaug[side, :, :pair])
                here = slice(side * head, (side + 1) * head)
                dkt[here, :] += dot_nn(qt[here, part], ds)
                dvt[here, :] += dot_nn(dot_t[here, part], pr.astype(BF16))
            dqkv[part, cols] = (acc * 0.125).astype(BF16)
            return inner

        lax.fori_loop(0, planes, one_chunk, 0)
        dqkv[:, width + g * pair : width + (g + 1) * pair] = dkt[...].T.astype(BF16)
        dqkv[:, 2 * width + g * pair : 2 * width + (g + 1) * pair] = dvt[...].T.astype(BF16)

    out_sender = Sender(z_send, z_recv)
    one_pair(0)
    next(y_scatter)
    one_pair(1)
    next(y_scatter)
    one_pair(2)
    mixed = hres_ref[...] + next(y_scatter)
    moved[0] = mixed.astype(BF16).reshape(planes, chunk, width)
    out_keep = pltpu.make_async_copy(moved.at[0, z], out_ref.at[z], loc_sems.at[7])
    out_keep.start()
    sent = [out_sender.start(moved.at[0, p[1]], out_ref.at[z], p) for p in z_peers]
    one_pair(3)

    def finish(c, carry):
        part = pl.ds(pl.multiple_of(c * chunk, chunk), chunk)
        grad = dot_nt(
            dqkv[part, :], dense_ref[:, :, : 3 * width].reshape(width, 3 * width)
        )
        normal, scale = norm_parts(row_ref[c].astype(F32))
        dnorm[0] += fold_rows(grad * normal)
        dnorm[1] += fold_rows(grad)
        moved[1, c] = (
            dh[part, :] + norm_back_parts(grad * norm_ref[0:1, :], normal, scale)
        ).astype(BF16)
        return carry

    lax.fori_loop(0, planes, finish, 0)
    tok_keep = pltpu.make_async_copy(moved.at[1, z], dtok_ref.at[z], loc_sems.at[8])
    tok_keep.start()
    sent += [out_sender.start(moved.at[1, p[1]], dtok_ref.at[z], p) for p in z_peers]
    for c in range(3):
        cols = slice(c * width, (c + 1) * width)
        dw[:, :, cols] = (
            dot_tn(xn1[...], dqkv[:, cols]).astype(BF16).reshape(groups, w_rows, width)
        )
    lanes = lax.broadcasted_iota(jnp.int32, (8, width), 0)
    table = jnp.zeros((8, width), F32)
    for k in range(4):
        table = jnp.where(lanes == k, jnp.sum(dnorm[k], axis=0, keepdims=True), table)
    table = jnp.concatenate([table, jnp.zeros((w_cols - 4 * width - 8, width), F32)], axis=0)
    dw[:, :, 4 * width :] = table.T.astype(BF16).reshape(groups, w_rows, w_cols - 4 * width)
    w_sender = Sender(w_send, w_recv)
    w_scatter = plane_scatter_steps(
        dw, w_own, w_theirs, w_deep, w_x, w_y, w_sender, loc_sems, z
    )
    for _ in range(4):
        next(w_scatter)
    w_sum[...] = next(w_scatter).astype(BF16)
    shard = shard_ref.shape[0]
    last = [
        out_sender.start(w_sum.at[pl.ds(p[1] * shard, shard)], w_in.at[k], p)
        for k, p in enumerate(z_peers)
    ]
    total = w_sum[pl.ds(z * shard, shard)].astype(F32)
    for k, copy in enumerate(last):
        copy.wait_recv()
        total = total + w_in[k].astype(F32)
    shard_ref[...] = total
    for copy in sent + small_d:
        copy.wait_recv()
    for i, copy in enumerate(unit_copies):
        if i % 8 == 0:
            copy.wait()
        else:
            copy.wait_recv()
            copy.wait_send()
    out_keep.wait()
    tok_keep.wait()
    for sender in (small_sender, y_sender, w_sender, out_sender):
        sender.drain()


def scatter_scratch(rows, width):
    return [
        pltpu.VMEM((4, rows, width), BF16),
        pltpu.VMEM((2, rows // 2, width), BF16),
        pltpu.VMEM((rows, width), BF16),
        pltpu.VMEM((rows, width), BF16),
    ]


def backward(row, norms, dense, qf, kf, qkv, o, lse, hres, g_all, zd, zy, gu, gd, small, heads):
    planes, piece, width = row.shape
    groups = zd.shape[0]
    rows = planes * piece
    pair = 2 * (width // heads)
    w_rows, w_cols = width // groups, 4 * width + 128
    sd = jax.ShapeDtypeStruct
    dma = pltpu.SemaphoreType.DMA
    return pl.pallas_call(
        functools.partial(backward_kernel, heads, planes, groups),
        out_shape=(
            sd(row.shape, BF16),
            sd(row.shape, BF16),
            sd((w_rows // planes, w_cols), F32),
            sd((2, planes) + gu.shape[2:], BF16),
            sd((2, planes) + gd.shape[2:], BF16),
            sd((groups,) + small.shape, F32),
        ),
        in_specs=[vmem_spec()] * 9 + [any_spec()] * 5 + [vmem_spec()],
        out_specs=(any_spec(), any_spec(), vmem_spec(), any_spec(), any_spec(), vmem_spec()),
        scratch_shapes=[
            pltpu.VMEM(row.shape, BF16),
            pltpu.VMEM((2, rows, 2 * pair), BF16),
            pltpu.VMEM((2, rows, 2 * pair), BF16),
            pltpu.VMEM((rows, width), F32),
            pltpu.VMEM((rows, width), BF16),
            pltpu.VMEM((rows, width), BF16),
            pltpu.VMEM((rows, width), F32),
            pltpu.VMEM((pair, rows), BF16),
            pltpu.VMEM((pair, rows), BF16),
            pltpu.VMEM((pair, rows), F32),
            pltpu.VMEM((pair, rows), F32),
            pltpu.VMEM((rows, 3 * width), BF16),
            pltpu.VMEM((rows, width), BF16),
            pltpu.VMEM((groups, w_rows, w_cols), BF16),
            pltpu.VMEM((4, 8, width), F32),
            pltpu.VMEM((2,) + row.shape, BF16),
            pltpu.VMEM((4, rows, width), BF16),
        ]
        + scatter_scratch(rows, width)
        + scatter_scratch(rows, width)
        + [pltpu.VMEM((4, w_rows, w_cols), BF16)]
        + scatter_scratch(w_rows, w_cols)
        + [
            pltpu.VMEM((w_rows, w_cols), BF16),
            pltpu.VMEM((planes - 1, w_rows // planes, w_cols), BF16),
            pltpu.VMEM((planes - 1,) + small.shape, F32),
            dma((planes + groups,)),
            dma((planes + groups,)),
            dma((PLANE_SCATTER_COPIES,)),
            dma((PLANE_SCATTER_COPIES,)),
            dma((PLANE_SCATTER_COPIES,)),
            dma((PLANE_SCATTER_COPIES,)),
            dma((PLANE_SCATTER_COPIES,)),
            dma((PLANE_SCATTER_COPIES,)),
            dma((3 * planes,)),
            dma((3 * planes,)),
            dma((16,)),
            dma((16,)),
            dma((9,)),
        ],
        compiler_params=pltpu.CompilerParams(
            collective_id=4, has_side_effects=True, vmem_limit_bytes=VMEM_MAX
        ),
        cost_estimate=pl.CostEstimate(
            flops=80_000_000_000, bytes_accessed=20_000_000, transcendentals=8_000_000
        ),
        name="attention_backward",
    )(row, norms, dense, qf, kf, qkv, o, lse, hres, g_all, zd, zy, gu, gd, small)


def expert_kernel(
    list_ref,
    meta_ref,
    own_ref,
    x_ref,
    g_ref,
    up_ref,
    down_ref,
    bup_ref,
    bdown_ref,
    zd_ref,
    zy_ref,
    gu_ref,
    gd_ref,
    dbup_ref,
    dbdown_ref,
    dgate_ref,
    xs,
    gs,
    zds,
    zys,
    up,
    down,
    acc_up,
    acc_down,
    xb,
    gb,
    mb,
    dyb,
    xt,
    dyt,
    yacc,
    xacc,
    sems,
):
    me = lax.axis_index("dp")
    groups, rows, width = x_ref.shape
    hidden = up.shape[2]
    planes = gu_ref.shape[0]
    tiles = BLOCK // TILE
    copies = []

    def load(src, dst):
        copy = pltpu.make_async_copy(src, dst, sems.at[len(copies)])
        copy.start()
        copies.append(copy)

    load(up_ref, up)
    load(down_ref, down)
    load(g_ref, gs)
    load(own_ref, xs.at[me])
    for k in range(1, groups):
        load(x_ref.at[me ^ k], xs.at[me ^ k])

    def wipe(k, carry):
        part = pl.ds(pl.multiple_of(k * BLOCK, BLOCK), BLOCK)
        zds[part, :] = jnp.zeros((BLOCK, width), BF16)
        zys[part, :] = jnp.zeros((BLOCK, width), BF16)
        return carry

    lax.fori_loop(0, groups * rows // BLOCK, wipe, 0)
    dbup_ref[...] = jnp.zeros_like(dbup_ref)
    dbdown_ref[...] = jnp.zeros_like(dbdown_ref)
    dgate_ref[...] = jnp.zeros_like(dgate_ref)
    for copy in copies:
        copy.wait()

    def spot(index):
        return pl.ds(pl.multiple_of(index * TILE, TILE), TILE)

    saves = []

    def save(src, dst):
        copy = pltpu.make_async_copy(src, dst, sems.at[len(copies) + len(saves)])
        copy.start()
        saves.append(copy)

    per_row = rows // TILE

    def one_expert(e):
        acc_up[...] = jnp.zeros_like(acc_up)
        acc_down[...] = jnp.zeros_like(acc_down)
        n_blocks = lax.div(list_ref[e, 0] + (tiles - 1), tiles)

        def one_block(b, carry):
            def fetch(k, inner):
                index = list_ref[e, 1 + b * tiles + k]
                src, part = lax.div(index, per_row), spot(lax.rem(index, per_row))
                dst = spot(k)
                xb[dst, :] = xs[src, part, :]
                gb[dst, :] = gs[src, part, :]
                mb[dst, :] = meta_ref[spot(index), :]
                return inner

            lax.fori_loop(0, tiles, fetch, 0, unroll=4)
            gate = mb[:, 2 * e : 2 * e + 1]
            dyb_new = (gb[...].astype(F32) * gate).astype(BF16)
            dyb[...] = dyb_new
            xt[...] = xb[...].T
            dyt[...] = dyb_new.T
            dbdown_ref[e] += fold_rows(dyb_new.astype(F32))

            def one_chunk(f, inner):
                cols = pl.ds(pl.multiple_of(f * FCHUNK, FCHUNK), FCHUNK)
                u = dot_nn(xb[...], up[e, :, cols]) + bup_ref[e, :, cols]
                sq = u * u
                th = jnp.tanh(u * (0.7978845608028654 + 0.035677408136300125 * sq))
                half = 0.5 + 0.5 * th
                slope = half + u * (
                    (0.5 - 0.5 * th * th) * (0.7978845608028654 + 0.10703222440890037 * sq)
                )
                a = (u * half).astype(BF16)
                du = (dot_nt(dyb[...], down[e, cols, :]) * slope).astype(BF16)
                y_new = dot_nn(a, down[e, cols, :])
                x_new = dot_nt(du, up[e, :, cols])

                @pl.when(f == 0)
                def _():
                    yacc[...] = y_new
                    xacc[...] = x_new

                @pl.when(f > 0)
                def _():
                    yacc[...] += y_new
                    xacc[...] += x_new

                acc_up[:, cols] += dot_nn(xt[...], du)
                acc_down[:, cols] += dot_nn(dyt[...], a)
                dbup_ref[e, :, cols] += fold_rows(du.astype(F32))
                return inner

            lax.fori_loop(0, hidden // FCHUNK, one_chunk, 0)
            y = yacc[...] + bdown_ref[e]
            inner_prod = jnp.sum(y * gb[...].astype(F32), axis=-1, keepdims=True)
            lane = lax.broadcasted_iota(jnp.int32, (BLOCK, 128), 1).astype(F32)
            dgate_ref[e] += fold_rows(jnp.where(lane == mb[:, 2 * e + 1 : 2 * e + 2], inner_prod, 0.0))
            gb[...] = (y * gate).astype(BF16)
            xb[...] = xacc[...].astype(BF16)

            def store(k, inner):
                dst = spot(list_ref[e, 1 + b * tiles + k])
                src = spot(k)
                if e == 0:
                    zds[dst, :] = xb[src, :]
                    zys[dst, :] = gb[src, :]
                else:
                    zds[dst, :] = (zds[dst, :].astype(F32) + xb[src, :].astype(F32)).astype(BF16)
                    zys[dst, :] = (zys[dst, :].astype(F32) + gb[src, :].astype(F32)).astype(BF16)
                return inner

            lax.fori_loop(0, tiles, store, 0, unroll=4)
            return carry

        lax.fori_loop(0, n_blocks, one_block, 0)
        up[e] = acc_up[...].astype(BF16)
        for k in range(hidden // FCHUNK):
            cols = slice(k * FCHUNK, (k + 1) * FCHUNK)
            down[e, cols, :] = acc_down[:, cols].T.astype(BF16)
        up_rows, down_rows = width // planes, hidden // planes
        for k in range(planes):
            save(up.at[e, pl.ds(k * up_rows, up_rows)], gu_ref.at[k, e])
            save(down.at[e, pl.ds(k * down_rows, down_rows)], gd_ref.at[k, e])

    one_expert(0)
    one_expert(1)
    save(zds, zd_ref)
    save(zys, zy_ref)
    for copy in saves:
        copy.wait()


def experts(tile_list, meta, x_own, x_all, g_all, up, down, b_up, b_down):
    groups, rows, width = x_all.shape
    hidden = up.shape[2]
    planes = 4
    total = groups * rows
    sd = jax.ShapeDtypeStruct
    return pl.pallas_call(
        expert_kernel,
        out_shape=(
            sd((total, width), BF16),
            sd((total, width), BF16),
            sd((planes, 2, width // planes, hidden), BF16),
            sd((planes, 2, hidden // planes, width), BF16),
            sd((2, 8, hidden), F32),
            sd((2, 8, width), F32),
            sd((2, 8, 128), F32),
        ),
        in_specs=[smem_spec(), vmem_spec()] + [any_spec()] * 5 + [vmem_spec()] * 2,
        out_specs=tuple([any_spec()] * 4 + [vmem_spec()] * 3),
        scratch_shapes=[
            pltpu.VMEM((groups, rows, width), BF16),
            pltpu.VMEM((groups, rows, width), BF16),
            pltpu.VMEM((total, width), BF16),
            pltpu.VMEM((total, width), BF16),
            pltpu.VMEM((2, width, hidden), BF16),
            pltpu.VMEM((2, hidden, width), BF16),
            pltpu.VMEM((width, hidden), F32),
            pltpu.VMEM((width, hidden), F32),
            pltpu.VMEM((BLOCK, width), BF16),
            pltpu.VMEM((BLOCK, width), BF16),
            pltpu.VMEM((BLOCK, 128), F32),
            pltpu.VMEM((BLOCK, width), BF16),
            pltpu.VMEM((width, BLOCK), BF16),
            pltpu.VMEM((width, BLOCK), BF16),
            pltpu.VMEM((BLOCK, width), F32),
            pltpu.VMEM((BLOCK, width), F32),
            pltpu.SemaphoreType.DMA((40,)),
        ],
        compiler_params=pltpu.CompilerParams(vmem_limit_bytes=VMEM_MAX),
        cost_estimate=pl.CostEstimate(
            flops=60_000_000_000, bytes_accessed=40_000_000, transcendentals=8_000_000
        ),
        name="experts",
    )(tile_list, meta, x_own, x_all, g_all, up, down, b_up, b_down)


def fast_shards(
    mesh_sizes,
    tokens,
    out_grad,
    segment_ids,
    key_mask,
    sent_task,
    task_experts,
    ln1_gain,
    ln1_bias,
    w_qkv,
    w_proj,
    ln2_gain,
    ln2_bias,
    task_embed,
    w_gate,
    w_up,
    b_up,
    w_down,
    b_down,
):
    groups, planes = mesh_sizes
    row_count, piece, width = tokens.shape
    length = piece * planes
    total = groups * length
    tasks = task_experts.shape[0]
    n_experts = w_gate.shape[1]
    hidden = w_up.shape[2]
    capacity = 4 * row_count * piece // n_experts
    me, z = lax.axis_index("dp"), lax.axis_index("fsdp")

    seg_hot = segment_ids[:, :, None] == jnp.arange(sent_task.shape[1])[None, None, :]
    task_tok = jnp.sum(jnp.where(seg_hot, sent_task[:, None, :], 0), axis=-1)
    code = (task_tok * 16 + segment_ids * 2 + key_mask).astype(F32)
    logits_part = jnp.dot(task_embed.astype(F32), w_gate.astype(F32), precision=exact)
    norm_part = jnp.stack([ln1_gain, ln1_bias, ln2_gain, ln2_bias]).astype(F32)
    bias_part = jnp.concatenate([b_up[0], b_down[0]]).astype(F32)
    parts = [code.reshape(-1), logits_part.reshape(-1), norm_part.reshape(-1), bias_part]
    used = sum(p.shape[0] for p in parts)
    pad_rows = -(-used // 1024) * 8
    payload = jnp.concatenate(parts + [jnp.zeros((pad_rows * 128 - used,), F32)])
    gathered = small_gather(payload.reshape(pad_rows, 128), planes, groups)
    gathered = gathered.reshape(groups, planes, pad_rows * 128)
    ends = []
    at = 0
    for p in parts:
        ends.append((at, at + p.shape[0]))
        at += p.shape[0]
    codes = gathered[:, :, ends[0][0] : ends[0][1]].astype(jnp.int32)
    codes = codes.reshape(groups, planes, row_count, piece)
    logits_all = jnp.sum(gathered[:, :, ends[1][0] : ends[1][1]], axis=(0, 1))
    logits_all = logits_all.reshape(tasks, n_experts)
    norms = gathered[:, :, ends[2][0] : ends[2][1]].reshape(groups * planes, 4, -1)
    norms = norms.transpose(1, 0, 2).reshape(4, width)
    norms = jnp.concatenate([norms, jnp.zeros((4, width), F32)])
    core = me % 2
    biases = lax.dynamic_slice_in_dim(
        gathered[:, :, ends[3][0] : ends[3][1]], me - core, 2, 0
    )
    half = hidden // 2
    bias_up = biases[:, :, : b_up.shape[1]].reshape(2, planes, 2, half // planes)
    bias_up = lax.dynamic_index_in_dim(bias_up, core, 2, keepdims=False).reshape(2, 1, half)
    bias_down = biases[:, :, b_up.shape[1] :].reshape(2, 1, width)
    bias_down = jnp.where(core == 0, bias_down, 0.0)

    seg_first = codes[:, 0, :, 0] % 16 // 2
    seg_last = codes[:, planes - 1, :, piece - 1] % 16 // 2
    single = jnp.argmax((seg_first == seg_last).astype(jnp.int32), axis=1)
    target = jnp.arange(groups) % planes
    slots = jnp.arange(planes)[None, :]
    order = jnp.where(
        slots == target[:, None],
        single[:, None],
        jnp.where(slots == single[:, None], target[:, None], slots),
    ).astype(jnp.int32)
    my_order = lax.dynamic_index_in_dim(order, me, 0, keepdims=False)
    row_of = lax.dynamic_index_in_dim(order, z, 1, keepdims=False)

    tokens_out, grads_out = pick_rows(my_order, (tokens, out_grad), (BF16, BF16))
    dense = jnp.concatenate([w_qkv, w_proj], axis=1)
    my_codes = lax.dynamic_index_in_dim(codes, me, 0, keepdims=False)
    my_code = lax.dynamic_index_in_dim(my_codes, row_of[me], 1, keepdims=False).reshape(length)
    my_seg, my_key = my_code % 16 // 2, my_code % 2
    pair = 2 * HD
    feature = jnp.arange(pair)[None, :]
    hot = my_seg[:, None] == feature
    qf = hot.astype(BF16)
    kf = jnp.where((feature < 8) & ~(hot & (my_key[:, None] == 1)), FAR, 0.0).astype(BF16)

    up_halves = w_up[0].reshape(-1, planes, 2, half // planes).transpose(2, 0, 1, 3)
    up_halves = up_halves.reshape(2, -1, half)
    down_halves = w_down[0].reshape(2, -1, width)
    (row, dense_full, qkv, o, lse, hres, xn2, x_all, g_all, up_all, down_all) = forward(
        tokens_out, grads_out, dense, up_halves, down_halves, norms, qf, kf, HEADS, groups
    )

    choose = (task_experts[:, :, None] == jnp.arange(n_experts)[None, None, :]).astype(F32)

    def gate_values(logits):
        return jax.nn.softmax(jnp.sum(logits[:, None, :] * choose, axis=-1), axis=-1)

    gates, gate_back = jax.vjp(gate_values, logits_all)
    chip_experts = me - core + jnp.arange(2)
    mine = task_experts[None] == chip_experts[:, None, None]
    shifts = jnp.left_shift(1, jnp.arange(tasks, dtype=jnp.int32))
    bits = jnp.sum(jnp.where(mine, shifts[None, :, None], 0), axis=1)
    gate_of_task = jnp.sum(jnp.where(mine, gates[None], 0.0), axis=2)
    task_all = codes // 16
    hits = jnp.right_shift(bits[:, None, None, :, None, None], task_all[None, :, :, None]) & 1
    hits = hits.astype(F32)
    lower = (jnp.arange(piece)[:, None] < jnp.arange(piece)[None, :]).astype(BF16)
    before = jnp.dot(
        hits.reshape(-1, piece).astype(BF16), lower, preferred_element_type=F32
    ).reshape(hits.shape)
    counts = jnp.sum(hits, axis=-1).reshape(2, groups, planes, 2 * row_count)
    ahead = (jnp.cumsum(counts, axis=-1) - counts).reshape(2, groups, planes, 2, row_count)
    rank = before + ahead[..., None]
    kept = jnp.sum(jnp.where(rank < capacity, hits, 0.0), axis=3)
    here = (jnp.arange(row_count)[None, :] == row_of[:, None])[:, None, :, None]
    kept_here = jnp.sum(jnp.where(here[None], kept, 0.0), axis=3).reshape(2, total)
    task_here = jnp.sum(jnp.where(here, task_all, 0), axis=2).reshape(total)
    task_hot = task_here[:, None] == jnp.arange(tasks)[None, :]
    gate_here = jnp.sum(jnp.where(task_hot[None], gate_of_task[:, None, :], 0.0), axis=2)
    gate_here = gate_here * kept_here
    task_mark = jnp.where(kept_here > 0, task_here.astype(F32)[None], -1.0)
    lane = jnp.arange(128)[None, :]
    meta = jnp.zeros((total, 128), F32)
    for k in range(2):
        meta = jnp.where(lane == 2 * k, gate_here[k][:, None], meta)
        meta = jnp.where(lane == 2 * k + 1, task_mark[k][:, None], meta)
    n_tiles = total // TILE
    tile_hit = jnp.max(kept_here.reshape(2, n_tiles, TILE), axis=2) > 0
    hit_rank = jnp.cumsum(tile_hit.astype(jnp.int32), axis=1)
    hit_count = hit_rank[:, -1:]
    index = jnp.arange(n_tiles, dtype=jnp.int32)
    place = jnp.where(tile_hit, hit_rank - 1, hit_count + index[None] - hit_rank)
    tile_list = jnp.sum(
        jnp.where(place[:, None, :] == index[None, :, None], index[None, None, :], 0),
        axis=2,
        dtype=jnp.int32,
    )
    tile_list = jnp.concatenate([hit_count, tile_list], axis=1)

    zd, zy, gu, gd, dbup, dbdown, dgate = experts(
        tile_list,
        meta,
        xn2.reshape(length, width),
        x_all.reshape(groups, length, width),
        g_all.reshape(groups, length, width),
        up_all.reshape(2, width, half),
        down_all.reshape(2, half, width),
        bias_up,
        bias_down,
    )
    small = jnp.concatenate(
        [
            jnp.sum(dgate, axis=1),
            jnp.sum(dbup, axis=1).reshape(-1, 128),
            jnp.sum(dbdown, axis=1).reshape(-1, 128),
        ]
    )
    small = jnp.concatenate([small, jnp.zeros((-small.shape[0] % 8, 128), F32)])
    out_pieces, tok_pieces, shard, gu_in, gd_in, small_all = backward(
        row,
        norms,
        dense_full,
        qf,
        kf,
        qkv,
        o,
        lse,
        hres,
        g_all,
        zd.reshape(groups, length, width),
        zy.reshape(groups, length, width),
        gu,
        gd,
        small,
        HEADS,
    )
    d_w_up = jnp.sum(gu_in.astype(F32), axis=1).reshape(2, -1, planes, half // planes)
    d_w_up = d_w_up.transpose(1, 2, 0, 3).reshape(-1, hidden)
    d_w_down = jnp.sum(gd_in.astype(F32), axis=1).reshape(-1, width)
    output, d_tokens = pick_rows(my_order, (out_pieces, tok_pieces), (BF16, F32))

    chips = small_all.reshape(groups // 2, 2, -1, 128)
    dgate_all = jnp.sum(chips[:, :, :2, :tasks], axis=1).reshape(n_experts, tasks).T
    dgates = jnp.sum(dgate_all[:, None, :] * choose, axis=-1)
    (dlogits,) = gate_back(dgates)
    d_task_embed = jnp.dot(dlogits, w_gate.astype(F32).T, precision=exact)
    d_w_gate = jnp.dot(task_embed.astype(F32).T, dlogits, precision=exact)
    my_chip = lax.dynamic_index_in_dim(chips, me // 2, 0, keepdims=False)
    cut = 2 + 2 * half // 128
    d_b_up = lax.dynamic_index_in_dim(
        my_chip[:, 2:cut].reshape(2, 2, planes, half // planes), core, 1, keepdims=False
    )
    d_b_up = lax.dynamic_index_in_dim(d_b_up, z, 1, keepdims=False).reshape(hidden // planes)
    d_b_down = lax.dynamic_index_in_dim(
        my_chip[0, cut : cut + 2 * width // 128].reshape(2, planes, width // planes),
        core,
        0,
        keepdims=False,
    )
    d_b_down = lax.dynamic_index_in_dim(d_b_down, z, 0, keepdims=False)
    return (
        output,
        d_tokens,
        shard[:, 4 * width],
        shard[:, 4 * width + 1],
        shard[:, : 3 * width],
        shard[:, 3 * width : 4 * width],
        shard[:, 4 * width + 2],
        shard[:, 4 * width + 3],
        d_task_embed,
        d_w_gate,
        d_w_up[None],
        d_b_up[None],
        d_w_down[None],
        d_b_down[None],
    )


def fits_rows(mesh, tokens, w_gate):
    groups, planes = mesh.shape["dp"], mesh.shape["fsdp"]
    return (
        groups == 8
        and planes == 4
        and tokens.shape[0] == groups * planes
        and w_gate.shape[1] == groups
        and tokens.shape[1] % (planes * QCHUNK) == 0
    )


def solution(mesh):
    placed = (
        P("dp", "fsdp", None),
        P("dp", "fsdp", None),
        P("dp", "fsdp"),
        P("dp", "fsdp"),
        P("dp", None),
        P(),
        P(("dp", "fsdp")),
        P(("dp", "fsdp")),
        P(("dp", "fsdp"), None),
        P(("dp", "fsdp"), None),
        P(("dp", "fsdp")),
        P(("dp", "fsdp")),
        P(None, ("dp", "fsdp")),
        P(("dp", "fsdp"), None),
        P("dp", "fsdp", None),
        P("dp", "fsdp"),
        P("dp", "fsdp", None),
        P("dp", "fsdp"),
    )
    placed_out = (
        P("dp", "fsdp", None),
        P("dp", "fsdp", None),
        P(("dp", "fsdp")),
        P(("dp", "fsdp")),
        P(("dp", "fsdp"), None),
        P(("dp", "fsdp"), None),
        P(("dp", "fsdp")),
        P(("dp", "fsdp")),
        P(None, ("dp", "fsdp")),
        P(("dp", "fsdp"), None),
        P("dp", "fsdp", None),
        P("dp", "fsdp"),
        P("dp", "fsdp", None),
        P("dp", "fsdp"),
    )

    def program(*args):
        fast = fits_rows(mesh, args[0], args[13])
        sizes = (mesh.shape["dp"], mesh.shape["fsdp"])
        return jax.shard_map(
            functools.partial(fast_shards, sizes) if fast else shards,
            mesh=mesh,
            in_specs=placed,
            out_specs=placed_out,
            check_vma=False,
        )(*args)

    return program
```

```python
import functools

import jax
import jax.numpy as jnp
from jax import lax
from jax.experimental import pallas as pl
from jax.experimental.pallas import tpu as pltpu
from jax.sharding import PartitionSpec as P

HEADS = 8
HD = 64


exact = lax.Precision.HIGHEST


def layer_norm(values_in, gain_vec, shift_vec):
    centre = values_in - jnp.mean(values_in, axis=-1, keepdims=True)
    spread = jnp.mean(centre * centre, axis=-1, keepdims=True)
    return centre * lax.rsqrt(spread + 1e-05) * gain_vec + shift_vec


def allow_table(query_codes, key_codes):
    query_int = query_codes.astype(jnp.int32)
    key_int = key_codes.astype(jnp.int32)
    same_sentence = (query_int // 2)[:, :, None] == (key_int // 2)[:, None, :]
    return same_sentence & ((key_int % 2)[:, None, :] == 1)


def row_scores(query_row, key_row, allow_row):
    scores = (
        jnp.einsum("qhd,khd->hqk", query_row, key_row, preferred_element_type=jnp.float32) * 0.125
    )
    return jnp.where(allow_row[None], scores, -1000000000.0)


def attend_forward(queries, key_heads, value_heads, allowed):

    def one_row(parts):
        query_row, key_row, value_row, allow_row = parts
        scores = row_scores(query_row, key_row, allow_row)
        biggest = jnp.max(scores, axis=-1, keepdims=True)
        weights = jnp.exp(scores - biggest)
        row_total = jnp.sum(weights, axis=-1, keepdims=True)
        weights_low = (weights / row_total).astype(jnp.bfloat16)
        mixed_row = jnp.einsum(
            "hqk,khd->qhd", weights_low, value_row, preferred_element_type=jnp.float32
        )
        return (mixed_row.astype(jnp.bfloat16), (biggest + jnp.log(row_total))[..., 0])

    return lax.map(one_row, (queries, key_heads, value_heads, allowed))


def attend_backward(queries, key_heads, value_heads, allowed, logsum, grad_out):

    def one_row(parts):
        query_row, key_row, value_row, allow_row, logsum_row, grad_row = parts
        scores = row_scores(query_row, key_row, allow_row)
        weights = jnp.exp(scores - logsum_row[..., None])
        grad_weights = jnp.einsum(
            "qhd,khd->hqk", grad_row, value_row, preferred_element_type=jnp.float32
        )
        inner = jnp.sum(weights * grad_weights, axis=-1, keepdims=True)
        grad_scores = (weights * (grad_weights - inner)).astype(jnp.bfloat16)
        grad_query = (
            jnp.einsum("hqk,khd->qhd", grad_scores, key_row, preferred_element_type=jnp.float32)
            * 0.125
        )
        grad_key = (
            jnp.einsum("hqk,qhd->khd", grad_scores, query_row, preferred_element_type=jnp.float32)
            * 0.125
        )
        grad_value = jnp.einsum(
            "hqk,qhd->khd",
            weights.astype(jnp.bfloat16),
            grad_row,
            preferred_element_type=jnp.float32,
        )
        return (grad_query, grad_key, grad_value)

    return lax.map(one_row, (queries, key_heads, value_heads, allowed, logsum, grad_out))


def shards(
    tokens,
    out_grad,
    segment_ids,
    key_mask,
    sent_task,
    task_experts,
    ln1_gain,
    ln1_bias,
    w_qkv,
    w_proj,
    ln2_gain,
    ln2_bias,
    task_embed,
    w_gate,
    w_up,
    b_up,
    w_down,
    b_down,
):
    row_count, piece_len, model_width = tokens.shape
    tok_count = row_count * piece_len
    gain_one, bias_one, qkv_full, proj_full, gain_two, bias_two, embed_full, router_full = (
        lax.all_gather(ln1_gain, ("dp", "fsdp"), axis=0, tiled=True),
        lax.all_gather(ln1_bias, ("dp", "fsdp"), axis=0, tiled=True),
        lax.all_gather(w_qkv, ("dp", "fsdp"), axis=0, tiled=True),
        lax.all_gather(w_proj, ("dp", "fsdp"), axis=0, tiled=True),
        lax.all_gather(ln2_gain, ("dp", "fsdp"), axis=0, tiled=True),
        lax.all_gather(ln2_bias, ("dp", "fsdp"), axis=0, tiled=True),
        lax.all_gather(task_embed, ("dp", "fsdp"), axis=1, tiled=True),
        lax.all_gather(w_gate, ("dp", "fsdp"), axis=0, tiled=True),
    )
    up_full, up_bias, down_full, down_bias = (
        lax.all_gather(w_up, "fsdp", axis=1, tiled=True),
        lax.all_gather(b_up, "fsdp", axis=1, tiled=True),
        lax.all_gather(w_down, "fsdp", axis=1, tiled=True),
        lax.all_gather(b_down, "fsdp", axis=1, tiled=True),
    )
    up_full = up_full[0]
    down_full = down_full[0]
    up_bias_f = up_bias[0].astype(jnp.float32)
    down_bias_f = down_bias[0].astype(jnp.float32)
    experts_count = router_full.shape[1]
    task_count = embed_full.shape[0]
    capacity = 4 * tok_count // experts_count
    inputs = tokens.astype(jnp.float32).reshape(tok_count, model_width)
    normed, norm_back = jax.vjp(
        layer_norm, inputs, gain_one.astype(jnp.float32), bias_one.astype(jnp.float32)
    )
    normed_low = normed.astype(jnp.bfloat16)
    projected = jnp.dot(normed_low, qkv_full, preferred_element_type=jnp.float32).astype(
        jnp.bfloat16
    )
    projected = projected.reshape(row_count, piece_len, 3, HEADS, HD)
    queries = projected[:, :, 0]
    key_heads = projected[:, :, 1]
    value_heads = projected[:, :, 2]
    row_codes = (2 * segment_ids + key_mask).astype(jnp.bfloat16)
    keys_all, values_all, codes_all = (
        lax.all_gather(key_heads, "fsdp", axis=1, tiled=True),
        lax.all_gather(value_heads, "fsdp", axis=1, tiled=True),
        lax.all_gather(row_codes, "fsdp", axis=1, tiled=True),
    )
    allowed = allow_table(row_codes, codes_all)
    attended, logsum = attend_forward(queries, keys_all, values_all, allowed)
    attended_flat = attended.reshape(tok_count, model_width)
    hidden = inputs + jnp.dot(attended_flat, proj_full, preferred_element_type=jnp.float32)
    normed_two, norm_two_back = jax.vjp(
        layer_norm, hidden, gain_two.astype(jnp.float32), bias_two.astype(jnp.float32)
    )
    normed_two_low = normed_two.astype(jnp.bfloat16)
    choose = (task_experts[:, :, None] == jnp.arange(experts_count)[None, None, :]).astype(
        jnp.float32
    )

    def gate_values(embed_in, router_in):
        logits = jnp.einsum(
            "te,tke->tk", jnp.dot(embed_in, router_in, precision=exact), choose, precision=exact
        )
        return jax.nn.softmax(logits, axis=-1)

    gate_probs, gate_back = jax.vjp(
        gate_values, embed_full.astype(jnp.float32), router_full.astype(jnp.float32)
    )
    segment_hot = (segment_ids[:, :, None] == jnp.arange(sent_task.shape[1])[None, None, :]).astype(
        jnp.int32
    )
    task_tok = jnp.sum(segment_hot * sent_task[:, None, :], axis=-1).reshape(tok_count)
    task_hot = (task_tok[:, None] == jnp.arange(task_count)[None, :]).astype(jnp.float32)
    gate_tok = jnp.dot(task_hot, gate_probs, precision=exact)
    expert_tok = jnp.sum(task_hot.astype(jnp.int32)[:, :, None] * task_experts[None], axis=1)
    copy_expert = expert_tok.T.reshape(-1)
    one_hot = (copy_expert[:, None] == jnp.arange(experts_count)[None, :]).astype(jnp.int32)
    rank = jnp.sum((jnp.cumsum(one_hot, axis=0) - one_hot) * one_hot, axis=-1)
    kept_copy = rank < capacity
    slot_index = jnp.where(kept_copy, copy_expert * capacity + rank, experts_count * capacity)
    send_rows = (
        jnp.zeros((experts_count * capacity + 1, model_width), jnp.bfloat16)
        .at[slot_index]
        .set(jnp.tile(normed_two_low, (2, 1)))
    )
    send_rows = send_rows[:-1].reshape(experts_count, capacity, model_width)
    received = lax.all_to_all(send_rows, "dp", split_axis=0, concat_axis=0, tiled=True)
    slot_total = received.shape[0] * received.shape[1]
    block_rows = min(512, slot_total)
    block_count = slot_total // block_rows
    slot_blocks = received.reshape(block_count, block_rows, model_width)

    def expert_forward(slot_rows):
        pre_act = jnp.dot(slot_rows, up_full, preferred_element_type=jnp.float32) + up_bias_f
        activated = jax.nn.gelu(pre_act, approximate=True).astype(jnp.bfloat16)
        return (
            jnp.dot(activated, down_full, preferred_element_type=jnp.float32) + down_bias_f
        ).astype(jnp.bfloat16)

    produced = lax.map(expert_forward, slot_blocks).reshape(received.shape)
    returned = lax.all_to_all(produced, "dp", split_axis=0, concat_axis=0, tiled=True)
    return_pad = jnp.concatenate(
        [returned.reshape(-1, model_width), jnp.zeros((1, model_width), jnp.bfloat16)], axis=0
    )
    copies = jnp.take(return_pad, slot_index, axis=0).reshape(2, tok_count, model_width)
    kept_float = kept_copy.reshape(2, tok_count).astype(jnp.float32)
    copy_weight = gate_tok.T * kept_float
    mixed_rows = (
        hidden
        + copy_weight[0][:, None] * copies[0].astype(jnp.float32)
        + copy_weight[1][:, None] * copies[1].astype(jnp.float32)
    )
    output = mixed_rows.astype(jnp.bfloat16).reshape(tokens.shape)
    grad_mixed = out_grad.astype(jnp.float32).reshape(tok_count, model_width)
    grad_copies = (copy_weight[:, :, None] * grad_mixed[None]).astype(jnp.bfloat16)
    grad_gate_copy = jnp.sum(copies.astype(jnp.float32) * grad_mixed[None], axis=-1) * kept_float
    grad_send = (
        jnp.zeros((experts_count * capacity + 1, model_width), jnp.bfloat16)
        .at[slot_index]
        .set(grad_copies.reshape(-1, model_width))
    )
    grad_send = grad_send[:-1].reshape(experts_count, capacity, model_width)
    grad_received = lax.all_to_all(grad_send, "dp", split_axis=0, concat_axis=0, tiled=True)

    def expert_backward(totals, parts):
        slot_rows, grad_rows = parts
        pre_act = jnp.dot(slot_rows, up_full, preferred_element_type=jnp.float32) + up_bias_f
        activated, gelu_back = jax.vjp(
            lambda values_in: jax.nn.gelu(values_in, approximate=True), pre_act
        )
        activated_low = activated.astype(jnp.bfloat16)
        grad_act = jnp.dot(grad_rows, down_full.T, preferred_element_type=jnp.float32)
        grad_pre = gelu_back(grad_act)[0].astype(jnp.bfloat16)
        grad_inputs_slot = jnp.dot(grad_pre, up_full.T, preferred_element_type=jnp.float32).astype(
            jnp.bfloat16
        )
        totals = (
            totals[0] + jnp.dot(slot_rows.T, grad_pre, preferred_element_type=jnp.float32),
            totals[1] + jnp.sum(grad_pre.astype(jnp.float32), axis=0),
            totals[2] + jnp.dot(activated_low.T, grad_rows, preferred_element_type=jnp.float32),
            totals[3] + jnp.sum(grad_rows.astype(jnp.float32), axis=0),
        )
        return (totals, grad_inputs_slot)

    start_totals = (
        jnp.zeros(up_full.shape, jnp.float32),
        jnp.zeros(up_bias_f.shape, jnp.float32),
        jnp.zeros(down_full.shape, jnp.float32),
        jnp.zeros(down_bias_f.shape, jnp.float32),
    )
    totals, grad_slots = lax.scan(
        expert_backward,
        start_totals,
        (slot_blocks, grad_received.reshape(block_count, block_rows, model_width)),
    )
    grad_back = lax.all_to_all(
        grad_slots.reshape(received.shape), "dp", split_axis=0, concat_axis=0, tiled=True
    )
    grad_pad = jnp.concatenate(
        [grad_back.reshape(-1, model_width), jnp.zeros((1, model_width), jnp.bfloat16)], axis=0
    )
    grad_taken = (
        jnp.take(grad_pad, slot_index, axis=0)
        .reshape(2, tok_count, model_width)
        .astype(jnp.float32)
    )
    grad_normed_two = grad_taken[0] + grad_taken[1]
    grad_up, grad_up_bias, grad_down, grad_down_bias = (
        lax.psum_scatter(
            totals[0][None].astype(jnp.bfloat16), "fsdp", scatter_dimension=1, tiled=True
        ).astype(jnp.float32),
        lax.psum_scatter(
            totals[1][None].astype(jnp.bfloat16), "fsdp", scatter_dimension=1, tiled=True
        ).astype(jnp.float32),
        lax.psum_scatter(
            totals[2][None].astype(jnp.bfloat16), "fsdp", scatter_dimension=1, tiled=True
        ).astype(jnp.float32),
        lax.psum_scatter(
            totals[3][None].astype(jnp.bfloat16), "fsdp", scatter_dimension=1, tiled=True
        ).astype(jnp.float32),
    )
    grad_hidden_part, grad_gain_two, grad_bias_two = norm_two_back(grad_normed_two)
    grad_hidden = grad_mixed + grad_hidden_part
    grad_branch = grad_hidden.astype(jnp.bfloat16)
    grad_proj = jnp.dot(attended_flat.T, grad_branch, preferred_element_type=jnp.float32)
    grad_attended = jnp.dot(grad_branch, proj_full.T, preferred_element_type=jnp.float32).astype(
        jnp.bfloat16
    )
    grad_attended = grad_attended.reshape(row_count, piece_len, HEADS, HD)
    part_query, part_key, part_value = attend_backward(
        queries, keys_all, values_all, allowed, logsum, grad_attended
    )
    summed_key, summed_value = (
        lax.psum_scatter(
            part_key.astype(jnp.bfloat16), "fsdp", scatter_dimension=1, tiled=True
        ).astype(jnp.float32),
        lax.psum_scatter(
            part_value.astype(jnp.bfloat16), "fsdp", scatter_dimension=1, tiled=True
        ).astype(jnp.float32),
    )
    grad_query = part_query.astype(jnp.bfloat16)
    grad_key = summed_key.astype(jnp.bfloat16)
    grad_value = summed_value.astype(jnp.bfloat16)
    grad_projected = jnp.stack([grad_query, grad_key, grad_value], axis=2).reshape(
        tok_count, 3 * model_width
    )
    grad_qkv_weight = jnp.dot(normed_low.T, grad_projected, preferred_element_type=jnp.float32)
    grad_normed = jnp.dot(grad_projected, qkv_full.T, preferred_element_type=jnp.float32)
    grad_inputs, grad_gain_one, grad_bias_one = norm_back(grad_normed)
    grad_tokens = (grad_hidden + grad_inputs).reshape(tokens.shape)
    grad_gate_task = jnp.dot(task_hot.T, grad_gate_copy.T, precision=exact)
    grad_embed, grad_router = gate_back(grad_gate_task)
    reduced = (
        lax.psum_scatter(grad_gain_one, ("dp", "fsdp"), scatter_dimension=0, tiled=True),
        lax.psum_scatter(grad_bias_one, ("dp", "fsdp"), scatter_dimension=0, tiled=True),
        lax.psum_scatter(grad_qkv_weight, ("dp", "fsdp"), scatter_dimension=0, tiled=True),
        lax.psum_scatter(grad_proj, ("dp", "fsdp"), scatter_dimension=0, tiled=True),
        lax.psum_scatter(grad_gain_two, ("dp", "fsdp"), scatter_dimension=0, tiled=True),
        lax.psum_scatter(grad_bias_two, ("dp", "fsdp"), scatter_dimension=0, tiled=True),
        lax.psum_scatter(grad_embed, ("dp", "fsdp"), scatter_dimension=1, tiled=True),
        lax.psum_scatter(grad_router, ("dp", "fsdp"), scatter_dimension=0, tiled=True),
    )
    return (
        output,
        grad_tokens,
        reduced[0],
        reduced[1],
        reduced[2],
        reduced[3],
        reduced[4],
        reduced[5],
        reduced[6],
        reduced[7],
        grad_up,
        grad_up_bias,
        grad_down,
        grad_down_bias,
    )


MESH_ID = pl.DeviceIdType.MESH
VMEM_MAX = 62 * 1024 * 1024
TILE = 16
BLOCK = 512
FCHUNK = 1024
QCHUNK = 256
FAR = -float(2**30)
F32 = jnp.float32
BF16 = jnp.bfloat16


def dot_nn(lhs, rhs):
    return lax.dot_general(lhs, rhs, (((1,), (0,)), ((), ())), preferred_element_type=F32)


def dot_nt(lhs, rhs):
    return lax.dot_general(lhs, rhs, (((1,), (1,)), ((), ())), preferred_element_type=F32)


def dot_tn(lhs, rhs):
    return lax.dot_general(lhs, rhs, (((0,), (0,)), ((), ())), preferred_element_type=F32)


def vmem_spec():
    return pl.BlockSpec(memory_space=pltpu.VMEM)


def any_spec():
    return pl.BlockSpec(memory_space=pl.ANY)


def smem_spec():
    return pl.BlockSpec(memory_space=pltpu.SMEM)


def norm_parts(values):
    centre = values - jnp.mean(values, axis=-1, keepdims=True)
    spread = jnp.mean(centre * centre, axis=-1, keepdims=True)
    scale = lax.rsqrt(spread + 1e-05)
    return centre * scale, scale


def norm_back_parts(grad, normal, scale):
    mean_grad = jnp.mean(grad, axis=-1, keepdims=True)
    mean_prod = jnp.mean(grad * normal, axis=-1, keepdims=True)
    return (grad - mean_grad - normal * mean_prod) * scale


def fold_rows(values):
    rows, width = values.shape
    return jnp.sum(values.reshape(rows // 8, 8, width), axis=0)


def plane_ids():
    me = lax.axis_index("dp")
    core, xpos, ypos = lax.rem(me, 2), lax.rem(me // 2, 2), me // 4

    def at(ypos, xpos, core):
        return (ypos * 2 + xpos) * 2 + core

    return me, core, xpos, ypos, at


def greet(peers):
    barrier = pltpu.get_barrier_semaphore()
    for peer in peers:
        pl.semaphore_signal(barrier, inc=1, device_id=peer, device_id_type=MESH_ID)
    pl.semaphore_wait(barrier, len(peers))


class Sender:
    def __init__(self, send_sems, recv_sems):
        self.send_sems, self.recv_sems, self.count, self.all = send_sems, recv_sems, 0, []

    def start(self, src, dst, peer):
        copy = pltpu.make_async_remote_copy(
            src_ref=src,
            dst_ref=dst,
            send_sem=self.send_sems.at[self.count],
            recv_sem=self.recv_sems.at[self.count],
            device_id=peer,
            device_id_type=MESH_ID,
        )
        copy.start()
        self.count += 1
        self.all.append(copy)
        return copy

    def drain(self):
        for copy in self.all:
            copy.wait_send()


def plane_gather_steps(block, own, rows, sender, z):
    me, core, xpos, ypos, at = plane_ids()
    sib, xn, yn = at(ypos, xpos, 1 - core), at(ypos, 1 - xpos, core), at(1 - ypos, xpos, core)
    diag = at(1 - ypos, 1 - xpos, core)
    half = rows // 2

    def part(i, k):
        return block(i).at[pl.ds(k * half, half)]

    def send(i, k, peer):
        src = own.at[pl.ds(k * half, half)] if i is me else part(i, k)
        return sender.start(src, part(i, k), (peer, z))

    x_own = [send(me, 0, xn)]
    y_own = [send(me, 1, yn)]
    x_own.append(send(me, 1, xn))
    y_own.insert(0, send(me, 0, yn))
    last = [send(me, 0, sib), send(me, 1, sib)]
    x_own[0].wait_recv()
    to_y = send(xn, 0, yn)
    y_own[1].wait_recv()
    to_x = send(yn, 1, xn)
    last.append(send(xn, 0, sib))
    last.append(send(yn, 1, sib))
    x_own[1].wait_recv()
    last.append(send(xn, 1, sib))
    y_own[0].wait_recv()
    last.append(send(yn, 0, sib))
    to_y.wait_recv()
    last.append(send(diag, 0, sib))
    to_x.wait_recv()
    last.append(send(diag, 1, sib))
    for copy in last:
        copy.wait_recv()


PLANE_GATHER_COPIES = 14


def plane_peers(z):
    me, core, xpos, ypos, at = plane_ids()
    return [
        (at(ypos, xpos, 1 - core), z),
        (at(ypos, 1 - xpos, core), z),
        (at(1 - ypos, xpos, core), z),
    ]


def column_peers(planes):
    me, z = lax.axis_index("dp"), lax.axis_index("fsdp")
    peers = [(me, lax.rem(z + k, planes)) for k in range(1, planes)]
    return peers + [(me ^ 1, lax.rem(z + k, planes)) for k in range(1, planes)]


class PlaneGather:
    COPIES = 28

    def __init__(self, block, own, send_sems, recv_sems):
        me, core, xpos, ypos, at = plane_ids()
        self.z = lax.axis_index("fsdp")
        self.me = me
        self.sib = at(ypos, xpos, 1 - core)
        self.xn, self.yn = at(ypos, 1 - xpos, core), at(1 - ypos, xpos, core)
        self.diag = at(1 - ypos, 1 - xpos, core)
        self.block, self.own = block, own
        self.send_sems, self.recv_sems = send_sems, recv_sems
        self.all = {}

    def send(self, kind, c, src, owner, peer):
        copy = pltpu.make_async_remote_copy(
            src_ref=src,
            dst_ref=self.block(owner).at[c],
            send_sem=self.send_sems.at[kind * 4 + c],
            recv_sem=self.recv_sems.at[kind * 4 + c],
            device_id=(peer, self.z),
            device_id_type=MESH_ID,
        )
        copy.start()
        self.all[kind, c] = copy

    def start(self, c):
        src = self.own.at[c]
        self.send(0, c, src, self.me, self.xn)
        self.send(1, c, src, self.me, self.yn)
        self.send(2, c, src, self.me, self.sib)

    def pass_on(self, c):
        x_part, y_part = self.block(self.xn).at[c], self.block(self.yn).at[c]
        self.all[0, c].wait_recv()
        if c % 2 == 0:
            self.send(3, c, x_part, self.xn, self.yn)
        self.send(4, c, x_part, self.xn, self.sib)
        self.all[1, c].wait_recv()
        if c % 2 == 1:
            self.send(3, c, y_part, self.yn, self.xn)
        self.send(5, c, y_part, self.yn, self.sib)

    def pass_diag(self, c):
        self.all[3, c].wait_recv()
        self.send(6, c, self.block(self.diag).at[c], self.diag, self.sib)

    def finish(self):
        for kind in (2, 4, 5, 6):
            for c in range(4):
                self.all[kind, c].wait_recv()
        for copy in self.all.values():
            copy.wait_send()


def plane_scatter_steps(z_ref, own, theirs, deep, near_x, near_y, sender, loc_sems, z):
    me, core, xpos, ypos, at = plane_ids()
    sib, xn, yn = at(ypos, xpos, 1 - core), at(ypos, 1 - xpos, core), at(1 - ypos, xpos, core)
    chips = [(ypos, xpos), (ypos, 1 - xpos), (1 - ypos, xpos), (1 - ypos, 1 - xpos)]
    rows = z_ref.shape[1]
    half = rows // 2
    first, second = pl.ds(0, half), pl.ds(half, half)
    loads, trades = {}, {}
    for slot in (3, 1, 2, 0):
        pos = chips[slot]
        trades[slot] = sender.start(
            z_ref.at[at(pos[0], pos[1], 1 - core)], theirs.at[slot], (sib, z)
        )

    yield
    for slot in (3, 1, 2, 0):
        pos = chips[slot]
        loads[slot] = pltpu.make_async_copy(
            z_ref.at[at(pos[0], pos[1], core)], own.at[slot], loc_sems.at[slot]
        )
        loads[slot].start()
    yield

    def add(slot, part):
        own[slot, part] = (
            own[slot, part].astype(F32) + theirs[slot, part].astype(F32)
        ).astype(own.dtype)

    loads[3].wait()
    trades[3].wait_recv()
    add(3, first)
    deep_x = sender.start(own.at[3, first], deep.at[0], (xn, z))
    add(3, second)
    deep_y = sender.start(own.at[3, second], deep.at[1], (yn, z))
    loads[1].wait()
    trades[1].wait_recv()
    add(1, first)
    x_first = sender.start(own.at[1, first], near_x.at[first], (xn, z))
    loads[2].wait()
    trades[2].wait_recv()
    add(2, second)
    y_second = sender.start(own.at[2, second], near_y.at[second], (yn, z))
    add(1, second)
    add(2, first)
    yield
    deep_y.wait_recv()
    own[1, second] = (own[1, second].astype(F32) + deep[1].astype(F32)).astype(own.dtype)
    x_second = sender.start(own.at[1, second], near_x.at[second], (xn, z))
    deep_x.wait_recv()
    own[2, first] = (own[2, first].astype(F32) + deep[0].astype(F32)).astype(own.dtype)
    y_first = sender.start(own.at[2, first], near_y.at[first], (yn, z))
    yield
    loads[0].wait()
    trades[0].wait_recv()
    yield
    mine = own[0].astype(F32) + theirs[0].astype(F32)
    x_first.wait_recv()
    y_second.wait_recv()
    x_second.wait_recv()
    y_first.wait_recv()
    yield mine + near_x[...].astype(F32) + near_y[...].astype(F32)


PLANE_SCATTER_COPIES = 10


def pick_rows_kernel(order_ref, *refs):
    count = len(refs) // 2
    for a in range(count):
        for r in range(refs[a].shape[0]):
            refs[count + a][r] = refs[a][order_ref[0, r]].astype(refs[count + a].dtype)


def pick_rows(order, arrays, kinds):
    return pl.pallas_call(
        pick_rows_kernel,
        out_shape=tuple(
            jax.ShapeDtypeStruct(array.shape, kind) for array, kind in zip(arrays, kinds)
        ),
        in_specs=[smem_spec()] + [vmem_spec()] * len(arrays),
        out_specs=tuple(vmem_spec() for _ in arrays),
        compiler_params=pltpu.CompilerParams(vmem_limit_bytes=VMEM_MAX),
        name="row_order",
    )(order, *arrays)


PAYLOAD = 48
CODE_LOW, CODE_HIGH, BIAS_UP, BIAS_DOWN, NORMS, LOGITS = 0, 4, 8, 12, 13, 16


def make_payload(payload, sent_ref, seg_ref, key_ref, logit_ref, norm_ref, bup_ref, bdown_ref):
    seg = seg_ref[...]
    row_count, piece = seg.shape
    row = lax.broadcasted_iota(jnp.int32, seg.shape, 0)
    task = jnp.zeros_like(seg)
    for r in range(row_count):
        for k in range(sent_ref.shape[1]):
            task = jnp.where((row == r) & (seg == k), sent_ref[r, k], task)
    code = (task * 16 + seg * 2 + key_ref[...]).astype(F32)
    payload[...] = jnp.zeros_like(payload)
    payload[CODE_LOW : CODE_LOW + row_count] = code[:, : piece // 2]
    payload[CODE_HIGH : CODE_HIGH + row_count] = code[:, piece // 2 :]
    for k in range(bup_ref.shape[1] // 128):
        payload[BIAS_UP + k : BIAS_UP + k + 1] = bup_ref[:, k * 128 : (k + 1) * 128].astype(F32)
    payload[BIAS_DOWN : BIAS_DOWN + 1] = bdown_ref[...].astype(F32)
    payload[NORMS : NORMS + 1] = norm_ref[...]
    tasks, n_experts = logit_ref.shape
    payload[LOGITS : LOGITS + tasks, :n_experts] = logit_ref[...]


def code_segment(code):
    return lax.shift_right_logical(code.astype(jnp.int32), 1) & 7


def row_order(codes_ref, me, planes):
    single = jnp.int32(0)
    for r in reversed(range(planes)):
        first = jnp.max(code_segment(codes_ref[me, 0, CODE_LOW + r : CODE_LOW + r + 1, :1]))
        last = jnp.max(
            code_segment(codes_ref[me, planes - 1, CODE_HIGH + r : CODE_HIGH + r + 1, 127:])
        )
        single = jnp.where(first == last, r, single)
    target = lax.rem(me, planes)
    return [
        jnp.where(p == target, single, jnp.where(p == single, target, p)) for p in range(planes)
    ]


def row_features(codes_ref, me, order, z, planes, qf_ref, kf_ref, order_ref):
    mine = order[0]
    for p in range(1, planes):
        mine = jnp.where(z == p, order[p], mine)
    parts = []
    for p in range(planes):
        low, high = codes_ref[me, p, CODE_LOW : CODE_LOW + 4], codes_ref[me, p, CODE_HIGH : CODE_HIGH + 4]
        row = lax.broadcasted_iota(jnp.int32, low.shape, 0)
        for half in (low, high):
            parts.append(jnp.sum(jnp.where(row == mine, half, 0.0), axis=0, keepdims=True))
    columns = jnp.concatenate(parts, axis=0).T
    lane = lax.broadcasted_iota(jnp.int32, (128, qf_ref.shape[1]), 1)
    for k in range(2 * planes):
        code = columns[:, k : k + 1].astype(jnp.int32)
        hot = (lax.shift_right_logical(code, 1) & 7) == lane
        part = slice(k * 128, (k + 1) * 128)
        qf_ref[part, :] = jnp.where(hot, 1.0, 0.0).astype(BF16)
        seen = hot & ((code & 1) == 1)
        kf_ref[part, :] = jnp.where((lane < 8) & jnp.logical_not(seen), FAR, 0.0).astype(BF16)
    spot = lax.broadcasted_iota(jnp.int32, order_ref.shape, 1)
    table = jnp.zeros(order_ref.shape, jnp.int32)
    for p in range(planes):
        table = jnp.where(spot == p, order[p], table)
    order_ref[...] = table


def gather_norms(codes_ref, norm_ref):
    devices = codes_ref.shape[0] * codes_ref.shape[1]
    width = norm_ref.shape[1]
    size = width // devices
    shards = codes_ref[:, :, NORMS : NORMS + 1, :].reshape(devices, 128).astype(BF16)
    lane = lax.broadcasted_iota(jnp.int32, (128, width), 0)
    column = lax.broadcasted_iota(jnp.int32, (128, width), 1)
    owner = lax.broadcasted_iota(jnp.int32, (devices, width), 0)
    owned = lax.broadcasted_iota(jnp.int32, (devices, width), 1) // size
    for k in range(4):
        place = jnp.where(lane == k * size + lax.rem(column, size), 1.0, 0.0).astype(BF16)
        full = jnp.where(owner == owned, dot_nn(shards, place), 0.0)
        norm_ref[k : k + 1] = jnp.sum(full, axis=0, keepdims=True)


def routing_marks(codes_ref, te_ref, marks_ref, gates_ref, me, z, planes, capacity):
    groups = codes_ref.shape[0]
    tasks = te_ref.shape[0]
    count = groups * planes * planes
    low = codes_ref[:, :, CODE_LOW : CODE_LOW + planes, :].reshape(count, 128)
    high = codes_ref[:, :, CODE_HIGH : CODE_HIGH + planes, :].reshape(count, 128)
    code = jnp.concatenate([low, high], axis=1).astype(jnp.int32)
    piece = code.shape[1]
    task = lax.shift_right_logical(code, 4)
    one = lax.broadcasted_iota(jnp.int32, (count, count), 0)
    two = lax.broadcasted_iota(jnp.int32, (count, count), 1)
    block_one, block_two = one // planes, two // planes
    row_one, row_two = lax.rem(one, planes), lax.rem(two, planes)

    def table(mask):
        return jnp.where(mask, 1.0, 0.0).astype(BF16)

    whole = table(block_one == block_two)
    ahead_rows = table((block_one == block_two) & (row_two < row_one))
    group_one, group_two = block_one // planes, block_two // planes
    plane_two = lax.rem(block_two, planes)
    same_row = (group_one == group_two) & (row_one == row_two)

    def wide(column):
        return jnp.broadcast_to(column, (count, 128)).astype(BF16)

    seg = lax.shift_right_logical(code, 1) & 7
    first = dot_nn(table(same_row & (plane_two == 0)), wide(seg[:, :1].astype(F32)))
    last = dot_nn(
        table(same_row & (plane_two == planes - 1)), wide(seg[:, piece - 1 :].astype(F32))
    )
    lone = jnp.where(first == last, 1.0, 0.0)
    lone = jnp.where(dot_nn(ahead_rows, lone.astype(BF16)) == 0.0, lone, 0.0)
    row = lax.rem(lax.broadcasted_iota(jnp.int32, (count, 128), 0), planes)
    group = lax.broadcasted_iota(jnp.int32, (count, 128), 0) // (planes * planes)
    single = dot_nn(whole, (lone * row.astype(F32)).astype(BF16)).astype(jnp.int32)
    target = lax.rem(group, planes)
    picked = jnp.where(z == target, single, jnp.where(z == single, target, z))
    here = jnp.where(row == picked, 1.0, 0.0)[:, :1]

    before_table = table(
        lax.broadcasted_iota(jnp.int32, (piece, piece), 0)
        < lax.broadcasted_iota(jnp.int32, (piece, piece), 1)
    )
    gather = table(
        lax.broadcasted_iota(jnp.int32, (count // planes, count), 0)
        == lax.broadcasted_iota(jnp.int32, (count // planes, count), 1) // planes
    )
    chip = me - lax.rem(me, 2)
    for e in range(2):
        hits = []
        for j in range(2):
            bits = jnp.int32(0)
            for t in range(tasks):
                bit = (1 << t) if t < 31 else -(1 << 31)
                bits = bits | jnp.where(te_ref[t, j] == chip + e, jnp.int32(bit), jnp.int32(0))
            hits.append((lax.shift_right_logical(jnp.full(task.shape, bits), task) & 1).astype(F32))
        kept = jnp.zeros(task.shape, F32)
        base = jnp.zeros((count, 128), F32)
        for j in range(2):
            total = wide(jnp.sum(hits[j], axis=1, keepdims=True))
            rank = dot_nn(hits[j].astype(BF16), before_table)
            rank = rank + (base + dot_nn(ahead_rows, total))[:, :1]
            kept = kept + jnp.where(rank < capacity, hits[j], 0.0)
            base = base + dot_nn(whole, total)
        mark = kept * here * (task + 1).astype(F32)
        marks_ref[e] = dot_nn(gather, mark.astype(BF16)) - 1.0

    logits = jnp.sum(
        codes_ref[:, :, LOGITS : LOGITS + tasks, :].reshape(groups * planes, tasks, 128), axis=0
    )
    lane = lax.broadcasted_iota(jnp.int32, (tasks, 128), 1)
    task_row = lax.broadcasted_iota(jnp.int32, (tasks, 128), 0)
    hot = []
    for j in range(2):
        chosen = jnp.zeros((tasks, 128), jnp.int32)
        for t in range(tasks):
            chosen = jnp.where(task_row == t, te_ref[t, j], chosen)
        hot.append(lane == chosen)
    level = [jnp.sum(jnp.where(h, logits, 0.0), axis=1, keepdims=True) for h in hot]
    top = jnp.maximum(level[0], level[1])
    weight = [jnp.exp(v - top) for v in level]
    both = weight[0] + weight[1]
    grid = jnp.zeros((tasks, 128), F32)
    for j in range(2):
        grid = jnp.where(hot[j], weight[j] / both, grid)
    grid = jnp.concatenate([grid, jnp.zeros((128 - tasks, 128), F32)], axis=0)
    gates_ref[...] = grid.T[:groups]


def unit_copy(src, dst, send_sem, recv_sem, peer):
    return pltpu.make_async_remote_copy(
        src_ref=src,
        dst_ref=dst,
        send_sem=send_sem,
        recv_sem=recv_sem,
        device_id=peer,
        device_id_type=MESH_ID,
    )


class WeightSpread:
    def __init__(self, up_ref, down_ref, up_all, down_all, sems):
        self.me, self.z = lax.axis_index("dp"), lax.axis_index("fsdp")
        self.core = lax.rem(self.me, 2)
        self.src = (up_ref, down_ref)
        self.dst = (up_all, down_all)
        self.own_send, self.pass_send, self.recv, self.local = sems
        self.side = self.z // 2
        self.near = self.z ^ 1
        self.far = 2 - self.side
        self.inner = (self.z == 1) | (self.z == 2)

    def targets(self):
        chip = self.me - self.core
        return [
            (self.core, self.near),
            (self.core, self.far),
            (1 - self.core, self.near),
            (1 - self.core, self.far),
            (1 - self.core, self.z),
        ], chip

    def copy(self, kind, src, m, p, send_sem, peer):
        return unit_copy(
            src,
            self.dst[kind].at[m, p],
            send_sem,
            self.recv.at[kind * 8 + m * 4 + p],
            peer,
        )

    def own(self):
        targets, chip = self.targets()
        out = []
        for kind in range(2):
            for k, (h, p) in enumerate(targets):
                out.append(
                    self.copy(
                        kind,
                        self.src[kind].at[h],
                        self.core,
                        self.z,
                        self.own_send.at[kind * 5 + k],
                        (chip + h, p),
                    )
                )
        return out

    def mine(self):
        return [
            pltpu.make_async_copy(
                self.src[kind].at[self.core],
                self.dst[kind].at[self.core, self.z],
                self.local.at[kind],
            )
            for kind in range(2)
        ]

    def passed(self, j):
        p = 2 * (1 - self.side) + j
        return [
            self.copy(
                kind,
                self.dst[kind].at[m, p],
                m,
                p,
                self.pass_send.at[kind * 4 + m * 2 + j],
                (self.me, self.near),
            )
            for kind in range(2)
            for m in range(2)
        ]

    def start(self, kind):
        self.mine()[kind].start()
        copies = self.own()[5 * kind : 5 * kind + 5]
        for k, copy in enumerate(copies):
            if k not in (1, 3):
                copy.start()

        @pl.when(self.inner)
        def _():
            for k, copy in enumerate(copies):
                if k in (1, 3):
                    copy.start()

    def start_far(self, kind):
        @pl.when(jnp.logical_not(self.inner))
        def _():
            for k, copy in enumerate(self.own()):
                if k in (5 * kind + 1, 5 * kind + 3):
                    copy.start()

    def pass_on(self, first, kind):
        for side in range(2):

            @pl.when((self.z == 1 + side))
            def _():
                j = side if first else 1 - side
                for copy in self.passed(j)[2 * kind : 2 * kind + 2]:
                    copy.wait_recv()
                    copy.start()

    def finish(self):
        for copy in self.mine():
            copy.wait()
        for copy in self.own():
            copy.wait_send()

        def arrived(kind, m, p):
            self.copy(
                kind, self.dst[kind].at[m, p], m, p, self.own_send.at[0], (self.me, self.near)
            ).wait_recv()

        for kind in range(2):
            arrived(kind, 1 - self.core, self.z)
            for m in range(2):
                arrived(kind, m, self.near)

        @pl.when(self.inner)
        def _():
            for j in range(2):
                for copy in self.passed(j):
                    copy.wait_send()

        @pl.when(jnp.logical_not(self.inner))
        def _():
            for kind in range(2):
                for m in range(2):
                    for j in range(2):
                        arrived(kind, m, 2 * (1 - self.side) + j)


def forward_kernel(
    heads,
    planes,
    capacity,
    sent_ref,
    te_ref,
    seg_ref,
    key_ref,
    logit_ref,
    shard_norms,
    bup_ref,
    bdown_ref,
    tok_ref,
    gm_ref,
    wqkv_ref,
    wproj_ref,
    upw_in,
    downw_in,
    codes_ref,
    marks_ref,
    gates_ref,
    order_ref,
    norm_ref,
    qf_ref,
    kf_ref,
    row_out,
    dense_out,
    qkv_out,
    o_out,
    lse_out,
    hres_out,
    xn2_ref,
    x_all,
    g_all,
    up_all,
    down_all,
    row_ref,
    dense_ref,
    qkv_ref,
    o_ref,
    lse_ref,
    hres_ref,
    kaug,
    vaug,
    w_ref,
    upw_ref,
    downw_ref,
    payload,
    tok_out,
    gm_out,
    p_send,
    p_recv,
    z_send,
    z_recv,
    w_send,
    w_recv,
    x_send,
    x_recv,
    g_send,
    g_recv,
    u_own,
    u_pass,
    u_recv,
    loc_sems,
    out_sems,
    in_sems,
):
    me, z = lax.axis_index("dp"), lax.axis_index("fsdp")
    z_peers = [(me, lax.rem(z + k, planes)) for k in range(1, planes)]
    groups = codes_ref.shape[0]
    d_peers = [(lax.rem(me + k, groups), z) for k in range(1, groups)]
    width = row_ref.shape[2]
    stages = [
        pltpu.make_async_copy(wqkv_ref, w_ref.at[:, pl.ds(0, 3 * width)], in_sems.at[0]),
        pltpu.make_async_copy(wproj_ref, w_ref.at[:, pl.ds(3 * width, width)], in_sems.at[1]),
        pltpu.make_async_copy(downw_in.at[0], downw_ref, in_sems.at[2]),
    ]
    part = upw_ref.shape[2] // planes
    for p in range(planes):
        for h in range(2):
            stages.append(
                pltpu.make_async_copy(
                    upw_in.at[0, :, pl.ds((2 * p + h) * part, part)],
                    upw_ref.at[h, :, pl.ds(p * part, part)],
                    in_sems.at[len(stages)],
                )
            )
    for copy in stages:
        copy.start()
    greet(column_peers(planes) + d_peers)
    rows = qkv_ref.shape[0]
    for copy in stages:
        copy.wait()
    chunk = row_ref.shape[1]
    head = width // heads
    pair = 2 * head
    shard = w_ref.shape[0]
    sender = Sender(z_send, z_recv)
    dense_own = pltpu.make_async_copy(
        w_ref, dense_ref.at[me, pl.ds(z * shard, shard)], loc_sems.at[0]
    )
    dense_own.start()
    make_payload(payload, sent_ref, seg_ref, key_ref, logit_ref, shard_norms, bup_ref, bdown_ref)
    codes_ref[me, z] = payload[...]
    p_sender = Sender(p_send, p_recv)
    codes_z = [p_sender.start(payload, codes_ref.at[me, z], peer) for peer in z_peers]
    dense_z = [
        sender.start(w_ref, dense_ref.at[me, pl.ds(z * shard, shard)], peer) for peer in z_peers
    ]
    spread = WeightSpread(upw_ref, downw_ref, up_all, down_all, (u_own, u_pass, u_recv, loc_sems.at[pl.ds(3, 2)]))
    spread.start(0)
    for copy in codes_z:
        copy.wait_recv()
    order = row_order(codes_ref, me, planes)
    for c in range(planes):
        tok_out[c] = tok_ref[order[c]]
        gm_out[c] = gm_ref[order[c]]
    toks = [sender.start(tok_out.at[peer[1]], row_ref.at[z], peer) for peer in z_peers]
    tok_own = pltpu.make_async_copy(tok_out.at[z], row_ref.at[z], loc_sems.at[1])
    tok_own.start()
    gm_own = pltpu.make_async_copy(gm_out.at[z], g_all.at[me, z], loc_sems.at[2])
    gm_own.start()
    codes_d = [p_sender.start(codes_ref.at[me], codes_ref.at[me], peer) for peer in d_peers]
    dense_own.wait()
    for copy in dense_z:
        copy.wait_recv()
    dense_sender = Sender(w_send, w_recv)
    plane_gather_steps(
        lambda i: dense_ref.at[i], dense_ref.at[me], planes * shard, dense_sender, z
    )
    row_features(codes_ref, me, order, z, planes, qf_ref, kf_ref, order_ref)
    for copy in codes_d:
        copy.wait_recv()
    gather_norms(codes_ref, norm_ref)
    routing_marks(codes_ref, te_ref, marks_ref, gates_ref, me, z, planes, capacity)
    x_gather = PlaneGather(lambda i: x_all.at[i], xn2_ref, x_send, x_recv)
    g_gather = PlaneGather(lambda i: g_all.at[i], g_all.at[me], g_send, g_recv)

    for copy in toks:
        copy.wait_recv()
    tok_own.wait()
    gms = [sender.start(gm_out.at[peer[1]], g_all.at[me, z], peer) for peer in z_peers]

    lane = lax.broadcasted_iota(jnp.int32, (rows, pair), 1)
    lane_c = lax.broadcasted_iota(jnp.int32, (chunk, pair), 1)

    def project(c, carry):
        part = pl.ds(pl.multiple_of(c * chunk, chunk), chunk)
        normal, _ = norm_parts(row_ref[c].astype(F32))
        xn1 = (normal * norm_ref[0:1, :] + norm_ref[1:2, :]).astype(BF16)
        out = dot_nn(xn1, dense_ref[:, :, : 3 * width].reshape(width, 3 * width))
        qkv_ref[part, :width] = (out[:, :width] * 0.125).astype(BF16)
        qkv_ref[part, width:] = out[:, width:].astype(BF16)
        return carry

    lax.fori_loop(0, planes, project, 0)

    def prepare(g, carry):
        k_pair = qkv_ref[:, pl.ds(pl.multiple_of(width + g * pair, pair), pair)]
        v_pair = qkv_ref[:, pl.ds(pl.multiple_of(2 * width + g * pair, pair), pair)]
        zero = jnp.zeros_like(k_pair)
        for side in range(2):
            mine = (lane // head) == side
            kaug[g, side, :, :pair] = jnp.where(mine, k_pair, zero)
            vaug[g, side, :, :pair] = jnp.where(mine, v_pair, zero)
            kaug[g, side, :, pair:] = kf_ref[...]
            vaug[g, side, :, pair:] = jnp.where(mine, 1.0, 0.0).astype(BF16)
        return carry

    lax.fori_loop(0, heads // 2, prepare, 0)

    def attend(c):
        part = pl.ds(c * chunk, chunk)

        def one_pair(g, carry):
            cols = pl.ds(pl.multiple_of(g * pair, pair), pair)
            qa = jnp.concatenate([qkv_ref[part, cols], qf_ref[part, :]], axis=1)
            acc = jnp.zeros((chunk, 2 * pair), F32)
            tops = []
            for side in range(2):
                s = dot_nt(qa, kaug[g, side])
                top = jnp.max(s, axis=-1, keepdims=True)
                acc = acc + dot_nn(jnp.exp(s - top).astype(BF16), vaug[g, side])
                tops.append(top)
            total = acc[:, pair:]
            o_ref[part, cols] = (acc[:, :pair] / total).astype(BF16)
            table = lse_ref[part, :]
            for side in range(2):
                level = tops[side] + jnp.log(total[:, side * head : side * head + 1])
                table = jnp.where(lane_c == 2 * g + side, level, table)
            lse_ref[part, :] = table
            return carry

        lax.fori_loop(0, heads // 2, one_pair, 0)
        w_proj = dense_ref[:, :, 3 * width : 4 * width].reshape(width, width)
        hres = row_ref[c].astype(F32) + dot_nn(o_ref[part, :], w_proj)
        hres_ref[part, :] = hres
        normal, _ = norm_parts(hres)
        xn2_ref[c] = (normal * norm_ref[2:3, :] + norm_ref[3:4, :]).astype(BF16)
        x_gather.start(c)

    attend(0)
    attend(1)
    for copy in gms:
        copy.wait_recv()
    gm_own.wait()
    spread.start(1)
    spread.pass_on(True, 0)
    for c in range(4):
        g_gather.start(c)
    attend(2)
    x_gather.pass_on(0)
    x_gather.pass_on(1)
    spread.start_far(0)
    attend(3)
    spread.start_far(1)
    spread.pass_on(True, 1)
    pairs = (
        (row_ref, row_out),
        (dense_ref, dense_out),
        (qkv_ref, qkv_out),
        (o_ref, o_out),
        (lse_ref, lse_out),
        (hres_ref, hres_out),
    )
    saves = [pltpu.make_async_copy(a, b, out_sems.at[k]) for k, (a, b) in enumerate(pairs)]
    for copy in saves:
        copy.start()
    x_gather.pass_on(2)
    g_gather.pass_on(0)
    g_gather.pass_on(1)
    spread.pass_on(False, 0)
    x_gather.pass_on(3)
    g_gather.pass_on(2)
    spread.pass_on(False, 1)
    g_gather.pass_on(3)
    for c in range(4):
        x_gather.pass_diag(c)
        g_gather.pass_diag(c)
    for copy in saves:
        copy.wait()
    x_gather.finish()
    g_gather.finish()
    spread.finish()
    for sender in (p_sender, sender, dense_sender):
        sender.drain()


def forward(
    sent_task, task_experts, routing, tokens, grads, w_qkv, w_proj, up, down, heads, groups, capacity
):
    planes, piece, width = tokens.shape
    rows = planes * piece
    half = up.shape[2] // 2
    dense = jax.ShapeDtypeStruct((w_qkv.shape[0], 4 * width), BF16)
    up_half = (2, up.shape[1], half)
    down_half = (2, down.shape[1] // 2, width)
    pair = 2 * (width // heads)
    sd = jax.ShapeDtypeStruct
    dma = pltpu.SemaphoreType.DMA
    return pl.pallas_call(
        functools.partial(forward_kernel, heads, planes, capacity),
        out_shape=(
            sd((groups, planes, PAYLOAD, 128), F32),
            sd((2, groups * planes, piece), F32),
            sd((groups, 128), F32),
            sd((8, 128), jnp.int32),
            sd((8, width), F32),
            sd((rows, pair), BF16),
            sd((rows, pair), BF16),
            sd(tokens.shape, BF16),
            sd((groups, planes * dense.shape[0], dense.shape[1]), BF16),
            sd((rows, 3 * width), BF16),
            sd((rows, width), BF16),
            sd((rows, pair), F32),
            sd((rows, width), F32),
            sd(tokens.shape, BF16),
            sd((groups,) + tokens.shape, BF16),
            sd((groups,) + tokens.shape, BF16),
            sd((2, planes) + up_half[1:], BF16),
            sd((2, planes) + down_half[1:], BF16),
        ),
        in_specs=[smem_spec()] * 2
        + [vmem_spec()] * (len(routing) + 2)
        + [any_spec()] * 4,
        out_specs=tuple(
            [vmem_spec()] * 7 + [any_spec()] * 6 + [vmem_spec()] + [any_spec()] * 4
        ),
        scratch_shapes=[
            pltpu.VMEM(tokens.shape, BF16),
            pltpu.VMEM((groups, planes * dense.shape[0], dense.shape[1]), BF16),
            pltpu.VMEM((rows, 3 * width), BF16),
            pltpu.VMEM((rows, width), BF16),
            pltpu.VMEM((rows, pair), F32),
            pltpu.VMEM((rows, width), F32),
            pltpu.VMEM((heads // 2, 2, rows, 2 * pair), BF16),
            pltpu.VMEM((heads // 2, 2, rows, 2 * pair), BF16),
            pltpu.VMEM(dense.shape, BF16),
            pltpu.VMEM(up_half, BF16),
            pltpu.VMEM(down_half, BF16),
            pltpu.VMEM((PAYLOAD, 128), F32),
            pltpu.VMEM(tokens.shape, BF16),
            pltpu.VMEM(tokens.shape, BF16),
            dma((planes + groups,)),
            dma((planes + groups,)),
            dma((3 * planes,)),
            dma((3 * planes,)),
            dma((PLANE_GATHER_COPIES,)),
            dma((PLANE_GATHER_COPIES,)),
            dma((PlaneGather.COPIES,)),
            dma((PlaneGather.COPIES,)),
            dma((PlaneGather.COPIES,)),
            dma((PlaneGather.COPIES,)),
            dma((10,)),
            dma((8,)),
            dma((16,)),
            dma((5,)),
            dma((6,)),
            dma((3 + 2 * planes,)),
        ],
        compiler_params=pltpu.CompilerParams(
            collective_id=2, has_side_effects=True, vmem_limit_bytes=VMEM_MAX
        ),
        cost_estimate=pl.CostEstimate(
            flops=40_000_000_000, bytes_accessed=10_000_000, transcendentals=8_000_000
        ),
        name="attention_forward",
    )(
        sent_task,
        task_experts,
        *routing,
        tokens,
        grads,
        w_qkv,
        w_proj,
        up,
        down.reshape((1,) + down_half),
    )


def split3(values):
    high = values.astype(BF16)
    rest = values - high.astype(F32)
    middle = rest.astype(BF16)
    low = (rest - middle.astype(F32)).astype(BF16)
    return high, middle, low


class GradChain:
    def __init__(self, src, land, out, stage, temp, sems):
        self.me, self.z = lax.axis_index("dp"), lax.axis_index("fsdp")
        self.core = lax.rem(self.me, 2)
        self.src, self.land, self.out, self.stage, self.temp = src, land, out, stage, temp
        self.load_sems, self.send_sems, self.recv_sems, self.last_sems = sems
        self.near = self.z ^ 1
        self.inner = (self.z == 1) | (self.z == 2)
        self.outer = jnp.logical_not(self.inner)

    def load(self, kind, plane, k):
        return pltpu.make_async_copy(
            self.src[kind].at[plane], self.stage[kind].at[k], self.load_sems.at[kind * 4 + k]
        )

    def link(self, kind, src, place, plane):
        return unit_copy(
            src,
            self.land[kind].at[place],
            self.send_sems.at[kind * 5 + place],
            self.recv_sems.at[kind * 5 + place],
            (self.me, plane),
        )

    def loads(self):
        planes = (3 - self.z, 3 - self.near, self.near)
        return [self.load(kind, planes[k], k) for kind in range(2) for k in range(3)]

    def outer_sends(self):
        planes = (3 - self.near, 3 - self.z, self.near)
        return [
            self.link(kind, self.src[kind].at[planes[place]], place, self.near)
            for place in range(3)
            for kind in range(2)
        ]

    def start(self):
        for copy in self.loads():
            copy.start()

        @pl.when(self.outer)
        def _():
            for copy in self.outer_sends():
                copy.start()

    def gather(self, kind, place, k):
        self.link(kind, self.land[kind].at[place], place, self.near).wait_recv()
        fetch = pltpu.make_async_copy(
            self.land[kind].at[place], self.temp[kind], self.load_sems.at[kind * 4 + 3]
        )
        fetch.start()
        fetch.wait()
        self.stage[kind][k] = (
            self.stage[kind][k].astype(F32) + self.temp[kind][...].astype(F32)
        ).astype(BF16)

    def inner_sends(self, step):
        place = (3, 4, 3)[step]
        plane = (3 - self.z, 3 - self.z, self.near)[step]
        out = []
        for kind in range(2):
            copy = pltpu.make_async_remote_copy(
                src_ref=self.stage[kind].at[step],
                dst_ref=self.land[kind].at[place],
                send_sem=self.send_sems.at[kind * 5 + step],
                recv_sem=self.recv_sems.at[kind * 5 + place],
                device_id=(self.me, plane),
                device_id_type=MESH_ID,
            )
            out.append(copy)
        return out

    def step(self, step):
        @pl.when(self.inner)
        def _():
            sends = self.inner_sends(step)
            for kind in range(2):
                self.loads()[kind * 3 + step].wait()
                self.gather(kind, (0, 1, 4)[step], step)
                sends[kind].start()

    def last_copies(self):
        out = []
        chip = self.me - self.core
        for kind in range(2):
            out.append(
                unit_copy(
                    self.stage[kind].at[0, 1 - self.core],
                    self.out[kind].at[self.core],
                    self.last_sems.at[kind],
                    self.last_sems.at[2 + kind],
                    (chip + 1 - self.core, self.z),
                )
            )
        return out

    def keep_copies(self):
        return [
            pltpu.make_async_copy(
                self.stage[kind].at[0, self.core],
                self.out[kind].at[self.core],
                self.last_sems.at[4 + kind],
            )
            for kind in range(2)
        ]

    def total(self):
        @pl.when(self.outer)
        def _():
            for copy in self.loads():
                copy.wait()
            for copy in self.outer_sends():
                copy.wait_send()

        @pl.when(self.inner)
        def _():
            for step in range(3):
                for copy in self.inner_sends(step):
                    copy.wait_send()

        own = [self.load(kind, self.z, 0) for kind in range(2)]
        for copy in own:
            copy.start()
        for copy in own:
            copy.wait()

        @pl.when(self.inner)
        def _():
            for kind in range(2):
                self.gather(kind, 2, 0)

        for kind in range(2):
            self.gather(kind, 3, 0)
        for copy in self.last_copies() + self.keep_copies():
            copy.start()

    def finish(self):
        for copy in self.last_copies():
            copy.wait_recv()
            copy.wait_send()
        for copy in self.keep_copies():
            copy.wait()


def backward_kernel(
    heads,
    planes,
    groups,
    row_in,
    norm_ref,
    dense_in,
    qf_in,
    kf_in,
    qkv_in,
    o_in,
    lse_in,
    hres_in,
    g_all,
    zd_ref,
    zy_ref,
    gu_ref,
    gd_ref,
    small_ref,
    gates_ref,
    out_ref,
    dtok_ref,
    dqkv_out,
    dproj_out,
    ln_out,
    gu_in,
    gd_in,
    dlogit_out,
    dbup_out,
    dbdown_out,
    norm_out,
    gu_land,
    gd_land,
    row_ref,
    dense_ref,
    qf_ref,
    kf_ref,
    qkv_ref,
    o_ref,
    lse_ref,
    hres_ref,
    gm,
    kaug,
    vaug,
    dh,
    db,
    do,
    delta,
    qt,
    dot_t,
    dkt,
    dvt,
    dqkv,
    xn1,
    dw,
    dnorm,
    moved,
    own,
    d_theirs,
    d_deep,
    d_x,
    d_y,
    y_theirs,
    y_deep,
    y_x,
    y_y,
    w_own,
    w_theirs,
    w_deep,
    w_x,
    w_y,
    w_sum,
    w_in,
    small_in,
    small_out,
    norm_part,
    norm_in,
    norm_all,
    n_send,
    n_recv,
    s_send,
    s_recv,
    d_send,
    d_recv,
    y_send,
    y_recv,
    w_send,
    w_recv,
    z_send,
    z_recv,
    gu_stage,
    gd_stage,
    gu_temp,
    gd_temp,
    c_load,
    c_send,
    c_recv,
    c_last,
    loc_sems,
    in_sems,
):
    me, z = lax.axis_index("dp"), lax.axis_index("fsdp")
    core = lax.rem(me, 2)
    chip = me - core
    z_peers = [(me, lax.rem(z + k, planes)) for k in range(1, planes)]
    d_peers = [(lax.rem(me + k, groups), z) for k in range(1, groups)]
    greet(column_peers(planes) + d_peers)
    rows, width = hres_ref.shape
    chunk = row_ref.shape[1]
    head = width // heads
    pair = 2 * head

    gm_load = pltpu.make_async_copy(g_all.at[me], gm, loc_sems.at[4])
    gm_load.start()
    small_sender = Sender(s_send, s_recv)
    small_z = [small_sender.start(small_ref, small_in.at[k], p) for k, p in enumerate(z_peers)]
    d_sender = Sender(d_send, d_recv)
    d_scatter = plane_scatter_steps(
        zd_ref, own, d_theirs, d_deep, d_x, d_y, d_sender, loc_sems, z
    )
    next(d_scatter)
    next(d_scatter)
    pairs = (
        (hres_in, hres_ref),
        (o_in, o_ref),
        (dense_in, dense_ref),
        (row_in, row_ref),
        (qf_in, qf_ref),
        (kf_in, kf_ref),
        (qkv_in, qkv_ref),
        (lse_in, lse_ref),
    )
    fetched = [pltpu.make_async_copy(a, b, in_sems.at[k]) for k, (a, b) in enumerate(pairs)]
    for copy in fetched:
        copy.start()
    chain = GradChain(
        (gu_ref, gd_ref),
        (gu_land, gd_land),
        (gu_in, gd_in),
        (gu_stage, gd_stage),
        (gu_temp, gd_temp),
        (c_load, c_send, c_recv, c_last),
    )
    chain.start()
    for copy in small_z:
        copy.wait_recv()
    small_out[me] = small_ref[...] + jnp.sum(small_in[...], axis=0)
    small_d = [small_sender.start(small_out.at[me], small_out.at[me], p) for p in d_peers]
    y_sender = Sender(y_send, y_recv)
    y_scatter = plane_scatter_steps(
        zy_ref, own, y_theirs, y_deep, y_x, y_y, y_sender, loc_sems, z
    )
    next(y_scatter)
    gm_load.wait()
    for copy in fetched:
        copy.wait()

    next(d_scatter)
    next(d_scatter)
    chain.step(0)
    next(d_scatter)
    dh[...] = next(d_scatter)
    d_sender.drain()
    next(y_scatter)

    lane = lax.broadcasted_iota(jnp.int32, (rows, pair), 1)
    lane_c = lax.broadcasted_iota(jnp.int32, (chunk, pair), 1)
    same = lax.broadcasted_iota(jnp.int32, (width, pair), 0) // head == lax.broadcasted_iota(
        jnp.int32, (width, pair), 1
    )
    ones = jnp.where(same, 1.0, 0.0).astype(BF16)
    dnorm[...] = jnp.zeros_like(dnorm)

    def begin(c, carry):
        part = pl.ds(pl.multiple_of(c * chunk, chunk), chunk)
        normal, scale = norm_parts(hres_ref[part, :])
        grad = dh[part, :]
        dnorm[2] += fold_rows(grad * normal)
        dnorm[3] += fold_rows(grad)
        dh_part = gm[c].astype(F32) + norm_back_parts(grad * norm_ref[2:3, :], normal, scale)
        dh[part, :] = dh_part
        low = dh_part.astype(BF16)
        db[part, :] = low
        do_part = dot_nt(low, dense_ref[:, :, 3 * width : 4 * width].reshape(width, width)).astype(BF16)
        do[part, :] = do_part
        prod = do_part.astype(F32) * o_ref[part, :].astype(F32)
        high = prod.astype(BF16)
        rest = (prod - high.astype(F32)).astype(BF16)
        delta[part, :] = dot_nn(high, ones) + dot_nn(rest, ones)
        normal, _ = norm_parts(row_ref[c].astype(F32))
        xn1[part, :] = (normal * norm_ref[0:1, :] + norm_ref[1:2, :]).astype(BF16)
        return carry

    next(y_scatter)
    lax.fori_loop(0, planes, begin, 0)
    chain.step(1)
    w_rows = w_sum.shape[0]
    w_cols = w_sum.shape[1]
    dw[:, :, 3 * width : 4 * width] = (
        dot_tn(o_ref[...], db[...]).astype(BF16).reshape(groups, w_rows, width)
    )

    mark = (lane >= heads) & (lane < heads + 3)
    for side in range(2):
        kaug[side, :, pair:] = jnp.where(mark, 1.0, kf_ref[...].astype(F32)).astype(BF16)
        vaug[side, :, pair:] = jnp.where(mark, 1.0, 0.0).astype(BF16)

    def put_parts(base, values):
        high, middle, low = split3(-values)
        out = jnp.where(lane_c == heads, high.astype(F32), base)
        out = jnp.where(lane_c == heads + 1, middle.astype(F32), out)
        return jnp.where(lane_c == heads + 2, low.astype(F32), out).astype(BF16)

    def one_pair(g):
        cols = slice(g * pair, (g + 1) * pair)
        k_pair = qkv_ref[:, width + g * pair : width + (g + 1) * pair]
        v_pair = qkv_ref[:, 2 * width + g * pair : 2 * width + (g + 1) * pair]
        zero = jnp.zeros_like(k_pair)
        for side in range(2):
            mine = (lane // head) == side
            kaug[side, :, :pair] = jnp.where(mine, k_pair, zero)
            vaug[side, :, :pair] = jnp.where(mine, v_pair, zero)
        qt[...] = qkv_ref[:, cols].T
        dot_t[...] = do[:, cols].T
        dkt[...] = jnp.zeros_like(dkt)
        dvt[...] = jnp.zeros_like(dvt)

        def one_chunk(c, inner):
            part = pl.ds(pl.multiple_of(c * chunk, chunk), chunk)
            q_pair, do_pair = qkv_ref[part, cols], do[part, cols]
            lse_all, delta_all = lse_ref[part, :], delta[part, :]
            base = qf_ref[part, :].astype(F32)
            acc = jnp.zeros((chunk, pair), F32)
            for side in range(2):
                lse = lse_all[:, 2 * g + side : 2 * g + side + 1]
                qa = jnp.concatenate([q_pair, put_parts(base, lse)], axis=1)
                pr = jnp.exp(dot_nt(qa, kaug[side]))
                dlt = delta_all[:, 2 * g + side : 2 * g + side + 1]
                da = jnp.concatenate([do_pair, put_parts(jnp.zeros_like(base), dlt)], axis=1)
                ds = (pr * dot_nt(da, vaug[side])).astype(BF16)
                acc = acc + dot_nn(ds, kaug[side, :, :pair])
                here = slice(side * head, (side + 1) * head)
                dkt[here, :] += dot_nn(qt[here, part], ds)
                dvt[here, :] += dot_nn(dot_t[here, part], pr.astype(BF16))
            dqkv[part, cols] = (acc * 0.125).astype(BF16)
            return inner

        lax.fori_loop(0, planes, one_chunk, 0)
        dqkv[:, width + g * pair : width + (g + 1) * pair] = dkt[...].T.astype(BF16)
        dqkv[:, 2 * width + g * pair : 2 * width + (g + 1) * pair] = dvt[...].T.astype(BF16)

    out_sender = Sender(z_send, z_recv)
    next(y_scatter)
    one_pair(0)
    for copy in small_d:
        copy.wait_recv()
    dgate = jnp.concatenate(
        [
            small_out[2 * (e // 2), e % 2 : e % 2 + 1] + small_out[2 * (e // 2) + 1, e % 2 : e % 2 + 1]
            for e in range(groups)
        ]
    )
    gates = gates_ref[...]
    dlogit_out[...] = gates * (dgate - jnp.sum(gates * dgate, axis=0, keepdims=True))
    up_part, up_rows = dbup_out.shape[1] // 256, gu_ref.shape[3] // 128
    for h in range(2):
        for q in range(up_part):
            at = 2 + core * up_rows + z * up_part + q
            spot = (h * up_part + q) * 128
            dbup_out[:, spot : spot + 128] = small_out[chip + h, pl.ds(at, 1), :]
    dbdown_out[...] = small_out[me, pl.ds(2 + 2 * up_rows + core * (width // 128) + z, 1), :]
    chain.step(2)
    one_pair(1)
    next(y_scatter)
    mixed = hres_ref[...] + next(y_scatter)
    moved[0] = mixed.astype(BF16).reshape(planes, chunk, width)
    out_keep = pltpu.make_async_copy(moved.at[0, z], out_ref.at[z], loc_sems.at[7])
    out_keep.start()
    sent = [out_sender.start(moved.at[0, p[1]], out_ref.at[z], p) for p in z_peers]
    one_pair(2)
    chain.total()
    one_pair(3)

    for c in range(3):
        cols = slice(c * width, (c + 1) * width)
        dw[:, :, cols] = (
            dot_tn(xn1[...], dqkv[:, cols]).astype(BF16).reshape(groups, w_rows, width)
        )
    lanes = lax.broadcasted_iota(jnp.int32, (8, width), 0)
    table = jnp.zeros((8, width), F32)
    for k in range(2, 4):
        table = jnp.where(lanes == k, jnp.sum(dnorm[k], axis=0, keepdims=True), table)
    table = jnp.concatenate([table, jnp.zeros((w_cols - 4 * width - 8, width), F32)], axis=0)
    dw[:, :, 4 * width :] = table.T.astype(BF16).reshape(groups, w_rows, w_cols - 4 * width)
    w_sender = Sender(w_send, w_recv)
    w_scatter = plane_scatter_steps(
        dw, w_own, w_theirs, w_deep, w_x, w_y, w_sender, loc_sems, z
    )
    next(w_scatter)
    next(w_scatter)

    def finish(c):
        part = pl.ds(pl.multiple_of(c * chunk, chunk), chunk)
        grad = dot_nt(dqkv[part, :], dense_ref[:, :, : 3 * width].reshape(width, 3 * width))
        normal, scale = norm_parts(row_ref[c].astype(F32))
        dnorm[0] += fold_rows(grad * normal)
        dnorm[1] += fold_rows(grad)
        moved[1, c] = (
            dh[part, :] + norm_back_parts(grad * norm_ref[0:1, :], normal, scale)
        ).astype(BF16)

    for k, peer in enumerate(z_peers):
        finish(peer[1])
        sent.append(out_sender.start(moved.at[1, peer[1]], dtok_ref.at[z], peer))
        next(w_scatter)
    finish(z)
    tok_keep = pltpu.make_async_copy(moved.at[1, z], dtok_ref.at[z], loc_sems.at[8])
    tok_keep.start()
    for k in range(2):
        total = jnp.sum(dnorm[k], axis=0, keepdims=True)
        for q in range(width // 128):
            row = k * (width // 128) + q
            norm_part[row : row + 1] = total[:, q * 128 : (q + 1) * 128]
    norm_sender = Sender(n_send, n_recv)
    norm_z = [norm_sender.start(norm_part, norm_in.at[k], p) for k, p in enumerate(z_peers)]
    w_sum[...] = next(w_scatter).astype(BF16)
    shard = dqkv_out.shape[0]
    last = [
        out_sender.start(w_sum.at[pl.ds(p[1] * shard, shard)], w_in.at[k], p)
        for k, p in enumerate(z_peers)
    ]
    for copy in norm_z:
        copy.wait_recv()
    norm_all[me] = norm_part[...] + jnp.sum(norm_in[...], axis=0)
    norm_d = [norm_sender.start(norm_all.at[me], norm_all.at[me], p) for p in d_peers]
    total = w_sum[pl.ds(z * shard, shard)].astype(F32)
    for k, copy in enumerate(last):
        copy.wait_recv()
        total = total + w_in[k].astype(F32)
    dqkv_out[...] = total[:, : 3 * width]
    dproj_out[...] = total[:, 3 * width : 4 * width]
    ln_out[...] = total[:, 4 * width :]
    for copy in norm_d:
        copy.wait_recv()
    norm_out[...] = jnp.sum(norm_all[...], axis=0)
    for copy in sent:
        copy.wait_recv()
    chain.finish()
    out_keep.wait()
    tok_keep.wait()
    for sender in (small_sender, y_sender, w_sender, out_sender, norm_sender):
        sender.drain()


def scatter_scratch(rows, width):
    return [
        pltpu.VMEM((4, rows, width), BF16),
        pltpu.VMEM((2, rows // 2, width), BF16),
        pltpu.VMEM((rows, width), BF16),
        pltpu.VMEM((rows, width), BF16),
    ]


def backward(
    row, norms, dense, qf, kf, qkv, o, lse, hres, g_all, zd, zy, gu, gd, small, gates, heads
):
    planes, piece, width = row.shape
    groups = zd.shape[0]
    rows = planes * piece
    pair = 2 * (width // heads)
    w_rows, w_cols = width // groups, 4 * width + 128
    sd = jax.ShapeDtypeStruct
    dma = pltpu.SemaphoreType.DMA
    return pl.pallas_call(
        functools.partial(backward_kernel, heads, planes, groups),
        out_shape=(
            sd(row.shape, BF16),
            sd(row.shape, BF16),
            sd((w_rows // planes, 3 * width), F32),
            sd((w_rows // planes, width), F32),
            sd((w_rows // planes, 128), F32),
            sd((2,) + gu.shape[2:], BF16),
            sd((2,) + gd.shape[2:], BF16),
            sd((groups, 128), F32),
            sd((1, 2 * gu.shape[3] // planes), F32),
            sd((1, width // planes), F32),
            sd((2 * width // 128, 128), F32),
            sd((5,) + gu.shape[1:], BF16),
            sd((5,) + gd.shape[1:], BF16),
        ),
        in_specs=[any_spec(), vmem_spec()] + [any_spec()] * 12 + [vmem_spec()] * 2,
        out_specs=tuple(
            [any_spec()] * 2
            + [vmem_spec()] * 3
            + [any_spec()] * 2
            + [vmem_spec()] * 4
            + [any_spec()] * 2
        ),
        scratch_shapes=[pltpu.VMEM(a.shape, a.dtype) for a in (row, dense, qf, kf, qkv, o, lse, hres)]
        + [
            pltpu.VMEM(row.shape, BF16),
            pltpu.VMEM((2, rows, 2 * pair), BF16),
            pltpu.VMEM((2, rows, 2 * pair), BF16),
            pltpu.VMEM((rows, width), F32),
            pltpu.VMEM((rows, width), BF16),
            pltpu.VMEM((rows, width), BF16),
            pltpu.VMEM((rows, pair), F32),
            pltpu.VMEM((pair, rows), BF16),
            pltpu.VMEM((pair, rows), BF16),
            pltpu.VMEM((pair, rows), F32),
            pltpu.VMEM((pair, rows), F32),
            pltpu.VMEM((rows, 3 * width), BF16),
            pltpu.VMEM((rows, width), BF16),
            pltpu.VMEM((groups, w_rows, w_cols), BF16),
            pltpu.VMEM((4, 8, width), F32),
            pltpu.VMEM((2,) + row.shape, BF16),
            pltpu.VMEM((4, rows, width), BF16),
        ]
        + scatter_scratch(rows, width)
        + scatter_scratch(rows, width)
        + [pltpu.VMEM((4, w_rows, w_cols), BF16)]
        + scatter_scratch(w_rows, w_cols)
        + [
            pltpu.VMEM((w_rows, w_cols), BF16),
            pltpu.VMEM((planes - 1, w_rows // planes, w_cols), BF16),
            pltpu.VMEM((planes - 1,) + small.shape, F32),
            pltpu.VMEM((groups,) + small.shape, F32),
            pltpu.VMEM((2 * width // 128, 128), F32),
            pltpu.VMEM((planes - 1, 2 * width // 128, 128), F32),
            pltpu.VMEM((groups, 2 * width // 128, 128), F32),
            dma((planes + groups,)),
            dma((planes + groups,)),
            dma((planes + groups,)),
            dma((planes + groups,)),
            dma((PLANE_SCATTER_COPIES,)),
            dma((PLANE_SCATTER_COPIES,)),
            dma((PLANE_SCATTER_COPIES,)),
            dma((PLANE_SCATTER_COPIES,)),
            dma((PLANE_SCATTER_COPIES,)),
            dma((PLANE_SCATTER_COPIES,)),
            dma((3 * planes,)),
            dma((3 * planes,)),
            pltpu.VMEM((3,) + gu.shape[1:], BF16),
            pltpu.VMEM((3,) + gd.shape[1:], BF16),
            pltpu.VMEM(gu.shape[1:], BF16),
            pltpu.VMEM(gd.shape[1:], BF16),
            dma((8,)),
            dma((10,)),
            dma((10,)),
            dma((6,)),
            dma((9,)),
            dma((8,)),
        ],
        compiler_params=pltpu.CompilerParams(
            collective_id=4, has_side_effects=True, vmem_limit_bytes=VMEM_MAX
        ),
        cost_estimate=pl.CostEstimate(
            flops=80_000_000_000, bytes_accessed=20_000_000, transcendentals=8_000_000
        ),
        name="attention_backward",
    )(row, norms, dense, qf, kf, qkv, o, lse, hres, g_all, zd, zy, gu, gd, small, gates)


def make_tile_list(marks, list_ref):
    blocks, piece = marks.shape
    per = piece // TILE
    iota = functools.partial(lax.broadcasted_iota, jnp.int32)

    def table(mask):
        return jnp.where(mask, 1.0, 0.0).astype(BF16)

    kept = table(marks >= 0.0)
    folded = dot_nn(kept, table(iota((piece, 128), 0) // TILE == iota((piece, 128), 1)))
    real = iota((blocks, 128), 1) < per
    hit = jnp.where(folded > 0.0, 1.0, 0.0)
    inside = dot_nn(hit.astype(BF16), table(iota((128, 128), 0) < iota((128, 128), 1)))
    totals = jnp.broadcast_to(jnp.sum(hit, axis=1, keepdims=True), (blocks, 128))
    above = dot_nn(table(iota((blocks, blocks), 1) < iota((blocks, blocks), 0)), totals.astype(BF16))
    count = jnp.sum(hit)
    rank = inside + above
    index = iota((blocks, 128), 0) * per + iota((blocks, 128), 1)
    place = jnp.where(hit > 0.0, rank, count + index.astype(F32) - rank)
    place = jnp.where(real, place, 0.0).astype(jnp.int32)
    tiles = blocks * per
    row = iota((tiles, 128), 0)
    spread = table(iota((tiles, blocks), 0) // per == iota((tiles, blocks), 1))
    mine = lax.rem(row, per) == iota((tiles, 128), 1)
    digits = []
    for digit in (place // per, lax.rem(place, per)):
        full = dot_nn(spread, digit.astype(F32).astype(BF16))
        digits.append(jnp.sum(jnp.where(mine, full, 0.0), axis=1, keepdims=True).astype(jnp.int32))
    to_row = table(digits[0] == iota((tiles, blocks), 1))
    to_column = digits[1] == iota((tiles, 128), 1)
    found = jnp.zeros((blocks, 128), F32)
    for value, scale in ((row // per, per), (lax.rem(row, per), 1)):
        part = jnp.where(to_column, value.astype(F32), 0.0).astype(BF16)
        found = found + scale * dot_tn(to_row, part)
    found = jnp.where(iota((blocks, 128), 1) == per, count, found)
    list_ref[...] = found.astype(jnp.int32)


def expert_kernel(
    marks_ref,
    gates_ref,
    codes_ref,
    own_ref,
    x_ref,
    g_ref,
    up_ref,
    down_ref,
    zd_ref,
    zy_ref,
    gu_ref,
    gd_ref,
    small_ref,
    dbup_ref,
    dbdown_ref,
    dgate_ref,
    xs,
    gs,
    zds,
    zys,
    up,
    down,
    acc_up,
    acc_down,
    xb,
    gb,
    mb,
    dyb,
    xt,
    dyt,
    yacc,
    xacc,
    meta,
    bup,
    bdown,
    list_vmem,
    list_ref,
    list_sem,
    sems,
    upt,
    downt,
):
    me = lax.axis_index("dp")
    groups, rows, width = x_ref.shape
    hidden = up.shape[2]
    planes = gu_ref.shape[0]
    tiles = BLOCK // TILE
    copies = []

    def load(src, dst):
        copy = pltpu.make_async_copy(src, dst, sems.at[len(copies)])
        copy.start()
        copies.append(copy)

    load(up_ref, up)
    load(down_ref, down)
    load(g_ref, gs)
    load(own_ref, xs.at[me])
    for k in range(1, groups):
        load(x_ref.at[me ^ k], xs.at[me ^ k])

    def wipe(k, carry):
        part = pl.ds(pl.multiple_of(k * BLOCK, BLOCK), BLOCK)
        zds[part, :] = jnp.zeros((BLOCK, width), BF16)
        zys[part, :] = jnp.zeros((BLOCK, width), BF16)
        return carry

    lax.fori_loop(0, groups * rows // BLOCK, wipe, 0)
    dbup_ref[...] = jnp.zeros_like(dbup_ref)
    dbdown_ref[...] = jnp.zeros_like(dbdown_ref)
    dgate_ref[...] = jnp.zeros_like(dgate_ref)
    core = lax.rem(me, 2)
    piece = marks_ref.shape[2]
    blocks = marks_ref.shape[1]
    lane = lax.broadcasted_iota(jnp.int32, (piece, 128), 1)
    turned = [marks_ref[e].T for e in range(2)]
    for k in range(blocks):
        meta[k * piece : (k + 1) * piece, :] = jnp.where(
            lane == 0, turned[0][:, k : k + 1], turned[1][:, k : k + 1]
        )
    for e in range(2):
        for p in range(planes):
            for q in range(2):
                at = p * (hidden // planes) + q * 128
                bup[e, :, at : at + 128] = codes_ref[
                    me - core + e, p, pl.ds(BIAS_UP + 2 * core + q, 1), :
                ]
            bdown[e, :, p * 128 : (p + 1) * 128] = jnp.where(
                core == 0, codes_ref[me - core + e, p, BIAS_DOWN : BIAS_DOWN + 1, :], 0.0
            )
        make_tile_list(marks_ref[e], list_vmem.at[e])
    list_copy = pltpu.make_async_copy(list_vmem, list_ref, list_sem)
    list_copy.start()
    list_copy.wait()
    for copy in copies:
        copy.wait()

    def spot(index):
        return pl.ds(pl.multiple_of(index * TILE, TILE), TILE)

    saves = []

    def save(src, dst):
        copy = pltpu.make_async_copy(src, dst, sems.at[len(copies) + len(saves)])
        copy.start()
        saves.append(copy)

    per_row = rows // TILE

    def one_expert(e):
        acc_up[...] = jnp.zeros_like(acc_up)
        acc_down[...] = jnp.zeros_like(acc_down)
        upt[...] = up[e].T
        downt[...] = down[e].T
        n_blocks = lax.div(list_ref[e, 0, 16] + (tiles - 1), tiles)
        gate_row = gates_ref[pl.ds(me - core + e, 1), :]
        lane_b = lax.broadcasted_iota(jnp.int32, (BLOCK, 128), 1).astype(F32)

        def one_block(b, carry):
            def fetch(k, inner):
                index = list_ref[e, b * (tiles // 16) + lax.div(k, 16), lax.rem(k, 16)]
                src, part = lax.div(index, per_row), spot(lax.rem(index, per_row))
                dst = spot(k)
                xb[dst, :] = xs[src, part, :]
                gb[dst, :] = gs[src, part, :]
                mb[dst, :] = meta[spot(index), :]
                return inner

            lax.fori_loop(0, tiles, fetch, 0, unroll=True)
            hot = lane_b == mb[:, e : e + 1]
            gate = jnp.sum(jnp.where(hot, gate_row, 0.0), axis=1, keepdims=True)
            dyb_new = (gb[...].astype(F32) * gate).astype(BF16)
            dyb[...] = dyb_new
            xt[...] = xb[...].T
            dyt[...] = dyb_new.T
            dbdown_ref[e] += fold_rows(dyb_new.astype(F32))

            def one_chunk(f, inner):
                cols = pl.ds(pl.multiple_of(f * FCHUNK, FCHUNK), FCHUNK)
                u = dot_nn(xb[...], up[e, :, cols]) + bup[e, :, cols]
                sq = u * u
                th = jnp.tanh(u * (0.7978845608028654 + 0.035677408136300125 * sq))
                half = 0.5 + 0.5 * th
                slope = half + u * (
                    (0.5 - 0.5 * th * th) * (0.7978845608028654 + 0.10703222440890037 * sq)
                )
                a = (u * half).astype(BF16)
                du = (dot_nn(dyb[...], downt[:, cols]) * slope).astype(BF16)
                y_new = dot_nn(a, down[e, cols, :])
                x_new = dot_nn(du, upt[cols, :])

                @pl.when(f == 0)
                def _():
                    yacc[...] = y_new
                    xacc[...] = x_new

                @pl.when(f > 0)
                def _():
                    yacc[...] += y_new
                    xacc[...] += x_new

                acc_up[:, cols] += dot_nn(xt[...], du)
                acc_down[:, cols] += dot_nn(dyt[...], a)
                dbup_ref[e, :, cols] += fold_rows(du.astype(F32))
                return inner

            lax.fori_loop(0, hidden // FCHUNK, one_chunk, 0)
            y = yacc[...] + bdown[e]
            inner_prod = jnp.sum(y * gb[...].astype(F32), axis=-1, keepdims=True)
            dgate_ref[e] += fold_rows(jnp.where(hot, inner_prod, 0.0))
            gb[...] = (y * gate).astype(BF16)
            xb[...] = xacc[...].astype(BF16)

            def store(k, inner):
                dst = spot(list_ref[e, b * (tiles // 16) + lax.div(k, 16), lax.rem(k, 16)])
                src = spot(k)
                if e == 0:
                    zds[dst, :] = xb[src, :]
                    zys[dst, :] = gb[src, :]
                else:
                    zds[dst, :] = (zds[dst, :].astype(F32) + xb[src, :].astype(F32)).astype(BF16)
                    zys[dst, :] = (zys[dst, :].astype(F32) + gb[src, :].astype(F32)).astype(BF16)
                return inner

            lax.fori_loop(0, tiles, store, 0, unroll=True)
            return carry

        lax.fori_loop(0, n_blocks, one_block, 0)
        up[e] = acc_up[...].astype(BF16)
        for k in range(hidden // FCHUNK):
            cols = slice(k * FCHUNK, (k + 1) * FCHUNK)
            down[e, cols, :] = acc_down[:, cols].T.astype(BF16)
        up_rows, down_rows = width // planes, hidden // planes
        for k in range(planes):
            save(up.at[e, pl.ds(k * up_rows, up_rows)], gu_ref.at[k, e])
            save(down.at[e, pl.ds(k * down_rows, down_rows)], gd_ref.at[k, e])

    one_expert(0)
    one_expert(1)
    save(zds, zd_ref)
    save(zys, zy_ref)
    small_ref[...] = jnp.zeros_like(small_ref)
    up_rows, down_rows = hidden // 128, width // 128
    for e in range(2):
        small_ref[e : e + 1] = jnp.sum(dgate_ref[e], axis=0, keepdims=True)
        for at, acc, count in (
            (2 + e * up_rows, dbup_ref, up_rows),
            (2 + 2 * up_rows + e * down_rows, dbdown_ref, down_rows),
        ):
            sums = jnp.sum(acc[e], axis=0, keepdims=True)
            for k in range(count):
                small_ref[at + k : at + k + 1] = sums[:, k * 128 : (k + 1) * 128]
    for copy in saves:
        copy.wait()


def experts(marks, gates, codes, x_own, x_all, g_all, up, down):
    groups, rows, width = x_all.shape
    hidden = up.shape[2]
    planes = 4
    total = groups * rows
    sd = jax.ShapeDtypeStruct
    return pl.pallas_call(
        expert_kernel,
        out_shape=(
            sd((total, width), BF16),
            sd((total, width), BF16),
            sd((planes, 2, width // planes, hidden), BF16),
            sd((planes, 2, hidden // planes, width), BF16),
            sd((-(-(2 + 2 * (hidden + width) // 128) // 8) * 8, 128), F32),
        ),
        in_specs=[vmem_spec()] * 3 + [any_spec()] * 5,
        out_specs=tuple([any_spec()] * 4 + [vmem_spec()]),
        scratch_shapes=[
            pltpu.VMEM((2, 8, hidden), F32),
            pltpu.VMEM((2, 8, width), F32),
            pltpu.VMEM((2, 8, 128), F32),
            pltpu.VMEM((groups, rows, width), BF16),
            pltpu.VMEM((groups, rows, width), BF16),
            pltpu.VMEM((total, width), BF16),
            pltpu.VMEM((total, width), BF16),
            pltpu.VMEM((2, width, hidden), BF16),
            pltpu.VMEM((2, hidden, width), BF16),
            pltpu.VMEM((width, hidden), F32),
            pltpu.VMEM((width, hidden), F32),
            pltpu.VMEM((BLOCK, width), BF16),
            pltpu.VMEM((BLOCK, width), BF16),
            pltpu.VMEM((BLOCK, 128), F32),
            pltpu.VMEM((BLOCK, width), BF16),
            pltpu.VMEM((width, BLOCK), BF16),
            pltpu.VMEM((width, BLOCK), BF16),
            pltpu.VMEM((BLOCK, width), F32),
            pltpu.VMEM((BLOCK, width), F32),
            pltpu.VMEM((total, 128), F32),
            pltpu.VMEM((2, 1, hidden), F32),
            pltpu.VMEM((2, 1, width), F32),
            pltpu.VMEM((2, marks.shape[1], 128), jnp.int32),
            pltpu.SMEM((2, marks.shape[1], 128), jnp.int32),
            pltpu.SemaphoreType.DMA,
            pltpu.SemaphoreType.DMA((40,)),
            pltpu.VMEM((hidden, width), BF16),
            pltpu.VMEM((width, hidden), BF16),
        ],
        compiler_params=pltpu.CompilerParams(vmem_limit_bytes=VMEM_MAX),
        cost_estimate=pl.CostEstimate(
            flops=60_000_000_000, bytes_accessed=40_000_000, transcendentals=8_000_000
        ),
        name="experts",
    )(marks, gates, codes, x_own, x_all, g_all, up, down)


def fast_shards(
    mesh_sizes,
    tokens,
    out_grad,
    segment_ids,
    key_mask,
    sent_task,
    task_experts,
    ln1_gain,
    ln1_bias,
    w_qkv,
    w_proj,
    ln2_gain,
    ln2_bias,
    task_embed,
    w_gate,
    w_up,
    b_up,
    w_down,
    b_down,
):
    groups, planes = mesh_sizes
    row_count, piece, width = tokens.shape
    length = piece * planes
    total = groups * length
    tasks = task_experts.shape[0]
    n_experts = w_gate.shape[1]
    hidden = w_up.shape[2]
    capacity = 4 * row_count * piece // n_experts
    me, z = lax.axis_index("dp"), lax.axis_index("fsdp")

    core = me % 2
    half = hidden // 2
    shard_norms = jnp.concatenate([ln1_gain, ln1_bias, ln2_gain, ln2_bias]).astype(F32)
    shard_norms = jnp.pad(shard_norms, (0, 128 - shard_norms.shape[0])).reshape(1, 128)
    logits_part = jnp.dot(task_embed, w_gate, preferred_element_type=F32)
    routing = (segment_ids, key_mask, logits_part, shard_norms, b_up, b_down)
    (
        codes,
        marks,
        gates_rows,
        order,
        norms,
        qf,
        kf,
        row,
        dense_full,
        qkv,
        o,
        lse,
        hres,
        xn2,
        x_all,
        g_all,
        up_all,
        down_all,
    ) = forward(
        sent_task,
        task_experts,
        routing,
        tokens,
        out_grad,
        w_qkv,
        w_proj,
        w_up,
        w_down,
        HEADS,
        groups,
        capacity,
    )
    zd, zy, gu, gd, small = experts(
        marks,
        gates_rows,
        codes,
        xn2.reshape(length, width),
        x_all.reshape(groups, length, width),
        g_all.reshape(groups, length, width),
        up_all.reshape(2, width, half),
        down_all.reshape(2, half, width),
    )
    (
        out_pieces,
        tok_pieces,
        d_w_qkv,
        d_w_proj,
        d_ln2,
        gu_in,
        gd_in,
        dlogits,
        d_b_up,
        d_b_down,
        norm_sums,
        _,
        _,
    ) = backward(
        row,
        norms,
        dense_full,
        qf,
        kf,
        qkv,
        o,
        lse,
        hres,
        g_all,
        zd.reshape(groups, length, width),
        zy.reshape(groups, length, width),
        gu,
        gd,
        small,
        gates_rows,
        HEADS,
    )
    d_w_up = gu_in.astype(F32).reshape(2, -1, planes, half // planes)
    d_w_up = d_w_up.transpose(1, 2, 0, 3).reshape(-1, hidden)
    d_w_down = gd_in.astype(F32).reshape(-1, width)
    output, d_tokens = pick_rows(order, (out_pieces, tok_pieces), (BF16, F32))

    features = width // (groups * planes)
    d_ln1 = lax.dynamic_slice_in_dim(
        norm_sums.reshape(2, width), (me * planes + z) * features, features, 1
    )

    dlogits = dlogits[:, :tasks]
    d_task_embed = jnp.dot(dlogits.T, w_gate.astype(F32).T, precision=exact)
    d_w_gate = jnp.dot(task_embed.astype(F32).T, dlogits.T, precision=exact)
    return (
        output,
        d_tokens,
        d_ln1[0],
        d_ln1[1],
        d_w_qkv,
        d_w_proj,
        d_ln2[:, 2],
        d_ln2[:, 3],
        d_task_embed,
        d_w_gate,
        d_w_up[None],
        d_b_up,
        d_w_down[None],
        d_b_down,
    )


def fits_rows(mesh, tokens, w_gate):
    groups, planes = mesh.shape["dp"], mesh.shape["fsdp"]
    return (
        groups == 8
        and planes == 4
        and tokens.shape[1] == planes * 256
        and tokens.shape[0] == groups * planes
        and w_gate.shape[1] == groups
        and tokens.shape[1] % (planes * QCHUNK) == 0
    )


def solution(mesh):
    placed = (
        P("dp", "fsdp", None),
        P("dp", "fsdp", None),
        P("dp", "fsdp"),
        P("dp", "fsdp"),
        P("dp", None),
        P(),
        P(("dp", "fsdp")),
        P(("dp", "fsdp")),
        P(("dp", "fsdp"), None),
        P(("dp", "fsdp"), None),
        P(("dp", "fsdp")),
        P(("dp", "fsdp")),
        P(None, ("dp", "fsdp")),
        P(("dp", "fsdp"), None),
        P("dp", "fsdp", None),
        P("dp", "fsdp"),
        P("dp", "fsdp", None),
        P("dp", "fsdp"),
    )
    placed_out = (
        P("dp", "fsdp", None),
        P("dp", "fsdp", None),
        P(("dp", "fsdp")),
        P(("dp", "fsdp")),
        P(("dp", "fsdp"), None),
        P(("dp", "fsdp"), None),
        P(("dp", "fsdp")),
        P(("dp", "fsdp")),
        P(None, ("dp", "fsdp")),
        P(("dp", "fsdp"), None),
        P("dp", "fsdp", None),
        P("dp", "fsdp"),
        P("dp", "fsdp", None),
        P("dp", "fsdp"),
    )

    def program(*args):
        fast = fits_rows(mesh, args[0], args[13])
        sizes = (mesh.shape["dp"], mesh.shape["fsdp"])
        return jax.shard_map(
            functools.partial(fast_shards, sizes) if fast else shards,
            mesh=mesh,
            in_specs=placed,
            out_specs=placed_out,
            check_vma=False,
        )(*args)

    return program
```

```python
import functools

import jax
import jax.numpy as jnp
from jax import lax
from jax.experimental import pallas as pl
from jax.experimental.pallas import tpu as pltpu
from jax.sharding import PartitionSpec as P

HEADS = 8
HD = 64


exact = lax.Precision.HIGHEST


def layer_norm(values_in, gain_vec, shift_vec):
    centre = values_in - jnp.mean(values_in, axis=-1, keepdims=True)
    spread = jnp.mean(centre * centre, axis=-1, keepdims=True)
    return centre * lax.rsqrt(spread + 1e-05) * gain_vec + shift_vec


def allow_table(query_codes, key_codes):
    query_int = query_codes.astype(jnp.int32)
    key_int = key_codes.astype(jnp.int32)
    same_sentence = (query_int // 2)[:, :, None] == (key_int // 2)[:, None, :]
    return same_sentence & ((key_int % 2)[:, None, :] == 1)


def row_scores(query_row, key_row, allow_row):
    scores = (
        jnp.einsum("qhd,khd->hqk", query_row, key_row, preferred_element_type=jnp.float32) * 0.125
    )
    return jnp.where(allow_row[None], scores, -1000000000.0)


def attend_forward(queries, key_heads, value_heads, allowed):

    def one_row(parts):
        query_row, key_row, value_row, allow_row = parts
        scores = row_scores(query_row, key_row, allow_row)
        biggest = jnp.max(scores, axis=-1, keepdims=True)
        weights = jnp.exp(scores - biggest)
        row_total = jnp.sum(weights, axis=-1, keepdims=True)
        weights_low = (weights / row_total).astype(jnp.bfloat16)
        mixed_row = jnp.einsum(
            "hqk,khd->qhd", weights_low, value_row, preferred_element_type=jnp.float32
        )
        return (mixed_row.astype(jnp.bfloat16), (biggest + jnp.log(row_total))[..., 0])

    return lax.map(one_row, (queries, key_heads, value_heads, allowed))


def attend_backward(queries, key_heads, value_heads, allowed, logsum, grad_out):

    def one_row(parts):
        query_row, key_row, value_row, allow_row, logsum_row, grad_row = parts
        scores = row_scores(query_row, key_row, allow_row)
        weights = jnp.exp(scores - logsum_row[..., None])
        grad_weights = jnp.einsum(
            "qhd,khd->hqk", grad_row, value_row, preferred_element_type=jnp.float32
        )
        inner = jnp.sum(weights * grad_weights, axis=-1, keepdims=True)
        grad_scores = (weights * (grad_weights - inner)).astype(jnp.bfloat16)
        grad_query = (
            jnp.einsum("hqk,khd->qhd", grad_scores, key_row, preferred_element_type=jnp.float32)
            * 0.125
        )
        grad_key = (
            jnp.einsum("hqk,qhd->khd", grad_scores, query_row, preferred_element_type=jnp.float32)
            * 0.125
        )
        grad_value = jnp.einsum(
            "hqk,qhd->khd",
            weights.astype(jnp.bfloat16),
            grad_row,
            preferred_element_type=jnp.float32,
        )
        return (grad_query, grad_key, grad_value)

    return lax.map(one_row, (queries, key_heads, value_heads, allowed, logsum, grad_out))


def shards(
    tokens,
    out_grad,
    segment_ids,
    key_mask,
    sent_task,
    task_experts,
    ln1_gain,
    ln1_bias,
    w_qkv,
    w_proj,
    ln2_gain,
    ln2_bias,
    task_embed,
    w_gate,
    w_up,
    b_up,
    w_down,
    b_down,
):
    row_count, piece_len, model_width = tokens.shape
    tok_count = row_count * piece_len
    gain_one, bias_one, qkv_full, proj_full, gain_two, bias_two, embed_full, router_full = (
        lax.all_gather(ln1_gain, ("dp", "fsdp"), axis=0, tiled=True),
        lax.all_gather(ln1_bias, ("dp", "fsdp"), axis=0, tiled=True),
        lax.all_gather(w_qkv, ("dp", "fsdp"), axis=0, tiled=True),
        lax.all_gather(w_proj, ("dp", "fsdp"), axis=0, tiled=True),
        lax.all_gather(ln2_gain, ("dp", "fsdp"), axis=0, tiled=True),
        lax.all_gather(ln2_bias, ("dp", "fsdp"), axis=0, tiled=True),
        lax.all_gather(task_embed, ("dp", "fsdp"), axis=1, tiled=True),
        lax.all_gather(w_gate, ("dp", "fsdp"), axis=0, tiled=True),
    )
    up_full, up_bias, down_full, down_bias = (
        lax.all_gather(w_up, "fsdp", axis=1, tiled=True),
        lax.all_gather(b_up, "fsdp", axis=1, tiled=True),
        lax.all_gather(w_down, "fsdp", axis=1, tiled=True),
        lax.all_gather(b_down, "fsdp", axis=1, tiled=True),
    )
    up_full = up_full[0]
    down_full = down_full[0]
    up_bias_f = up_bias[0].astype(jnp.float32)
    down_bias_f = down_bias[0].astype(jnp.float32)
    experts_count = router_full.shape[1]
    task_count = embed_full.shape[0]
    capacity = 4 * tok_count // experts_count
    inputs = tokens.astype(jnp.float32).reshape(tok_count, model_width)
    normed, norm_back = jax.vjp(
        layer_norm, inputs, gain_one.astype(jnp.float32), bias_one.astype(jnp.float32)
    )
    normed_low = normed.astype(jnp.bfloat16)
    projected = jnp.dot(normed_low, qkv_full, preferred_element_type=jnp.float32).astype(
        jnp.bfloat16
    )
    projected = projected.reshape(row_count, piece_len, 3, HEADS, HD)
    queries = projected[:, :, 0]
    key_heads = projected[:, :, 1]
    value_heads = projected[:, :, 2]
    row_codes = (2 * segment_ids + key_mask).astype(jnp.bfloat16)
    keys_all, values_all, codes_all = (
        lax.all_gather(key_heads, "fsdp", axis=1, tiled=True),
        lax.all_gather(value_heads, "fsdp", axis=1, tiled=True),
        lax.all_gather(row_codes, "fsdp", axis=1, tiled=True),
    )
    allowed = allow_table(row_codes, codes_all)
    attended, logsum = attend_forward(queries, keys_all, values_all, allowed)
    attended_flat = attended.reshape(tok_count, model_width)
    hidden = inputs + jnp.dot(attended_flat, proj_full, preferred_element_type=jnp.float32)
    normed_two, norm_two_back = jax.vjp(
        layer_norm, hidden, gain_two.astype(jnp.float32), bias_two.astype(jnp.float32)
    )
    normed_two_low = normed_two.astype(jnp.bfloat16)
    choose = (task_experts[:, :, None] == jnp.arange(experts_count)[None, None, :]).astype(
        jnp.float32
    )

    def gate_values(embed_in, router_in):
        logits = jnp.einsum(
            "te,tke->tk", jnp.dot(embed_in, router_in, precision=exact), choose, precision=exact
        )
        return jax.nn.softmax(logits, axis=-1)

    gate_probs, gate_back = jax.vjp(
        gate_values, embed_full.astype(jnp.float32), router_full.astype(jnp.float32)
    )
    segment_hot = (segment_ids[:, :, None] == jnp.arange(sent_task.shape[1])[None, None, :]).astype(
        jnp.int32
    )
    task_tok = jnp.sum(segment_hot * sent_task[:, None, :], axis=-1).reshape(tok_count)
    task_hot = (task_tok[:, None] == jnp.arange(task_count)[None, :]).astype(jnp.float32)
    gate_tok = jnp.dot(task_hot, gate_probs, precision=exact)
    expert_tok = jnp.sum(task_hot.astype(jnp.int32)[:, :, None] * task_experts[None], axis=1)
    copy_expert = expert_tok.T.reshape(-1)
    one_hot = (copy_expert[:, None] == jnp.arange(experts_count)[None, :]).astype(jnp.int32)
    rank = jnp.sum((jnp.cumsum(one_hot, axis=0) - one_hot) * one_hot, axis=-1)
    kept_copy = rank < capacity
    slot_index = jnp.where(kept_copy, copy_expert * capacity + rank, experts_count * capacity)
    send_rows = (
        jnp.zeros((experts_count * capacity + 1, model_width), jnp.bfloat16)
        .at[slot_index]
        .set(jnp.tile(normed_two_low, (2, 1)))
    )
    send_rows = send_rows[:-1].reshape(experts_count, capacity, model_width)
    received = lax.all_to_all(send_rows, "dp", split_axis=0, concat_axis=0, tiled=True)
    slot_total = received.shape[0] * received.shape[1]
    block_rows = min(512, slot_total)
    block_count = slot_total // block_rows
    slot_blocks = received.reshape(block_count, block_rows, model_width)

    def expert_forward(slot_rows):
        pre_act = jnp.dot(slot_rows, up_full, preferred_element_type=jnp.float32) + up_bias_f
        activated = jax.nn.gelu(pre_act, approximate=True).astype(jnp.bfloat16)
        return (
            jnp.dot(activated, down_full, preferred_element_type=jnp.float32) + down_bias_f
        ).astype(jnp.bfloat16)

    produced = lax.map(expert_forward, slot_blocks).reshape(received.shape)
    returned = lax.all_to_all(produced, "dp", split_axis=0, concat_axis=0, tiled=True)
    return_pad = jnp.concatenate(
        [returned.reshape(-1, model_width), jnp.zeros((1, model_width), jnp.bfloat16)], axis=0
    )
    copies = jnp.take(return_pad, slot_index, axis=0).reshape(2, tok_count, model_width)
    kept_float = kept_copy.reshape(2, tok_count).astype(jnp.float32)
    copy_weight = gate_tok.T * kept_float
    mixed_rows = (
        hidden
        + copy_weight[0][:, None] * copies[0].astype(jnp.float32)
        + copy_weight[1][:, None] * copies[1].astype(jnp.float32)
    )
    output = mixed_rows.astype(jnp.bfloat16).reshape(tokens.shape)
    grad_mixed = out_grad.astype(jnp.float32).reshape(tok_count, model_width)
    grad_copies = (copy_weight[:, :, None] * grad_mixed[None]).astype(jnp.bfloat16)
    grad_gate_copy = jnp.sum(copies.astype(jnp.float32) * grad_mixed[None], axis=-1) * kept_float
    grad_send = (
        jnp.zeros((experts_count * capacity + 1, model_width), jnp.bfloat16)
        .at[slot_index]
        .set(grad_copies.reshape(-1, model_width))
    )
    grad_send = grad_send[:-1].reshape(experts_count, capacity, model_width)
    grad_received = lax.all_to_all(grad_send, "dp", split_axis=0, concat_axis=0, tiled=True)

    def expert_backward(totals, parts):
        slot_rows, grad_rows = parts
        pre_act = jnp.dot(slot_rows, up_full, preferred_element_type=jnp.float32) + up_bias_f
        activated, gelu_back = jax.vjp(
            lambda values_in: jax.nn.gelu(values_in, approximate=True), pre_act
        )
        activated_low = activated.astype(jnp.bfloat16)
        grad_act = jnp.dot(grad_rows, down_full.T, preferred_element_type=jnp.float32)
        grad_pre = gelu_back(grad_act)[0].astype(jnp.bfloat16)
        grad_inputs_slot = jnp.dot(grad_pre, up_full.T, preferred_element_type=jnp.float32).astype(
            jnp.bfloat16
        )
        totals = (
            totals[0] + jnp.dot(slot_rows.T, grad_pre, preferred_element_type=jnp.float32),
            totals[1] + jnp.sum(grad_pre.astype(jnp.float32), axis=0),
            totals[2] + jnp.dot(activated_low.T, grad_rows, preferred_element_type=jnp.float32),
            totals[3] + jnp.sum(grad_rows.astype(jnp.float32), axis=0),
        )
        return (totals, grad_inputs_slot)

    start_totals = (
        jnp.zeros(up_full.shape, jnp.float32),
        jnp.zeros(up_bias_f.shape, jnp.float32),
        jnp.zeros(down_full.shape, jnp.float32),
        jnp.zeros(down_bias_f.shape, jnp.float32),
    )
    totals, grad_slots = lax.scan(
        expert_backward,
        start_totals,
        (slot_blocks, grad_received.reshape(block_count, block_rows, model_width)),
    )
    grad_back = lax.all_to_all(
        grad_slots.reshape(received.shape), "dp", split_axis=0, concat_axis=0, tiled=True
    )
    grad_pad = jnp.concatenate(
        [grad_back.reshape(-1, model_width), jnp.zeros((1, model_width), jnp.bfloat16)], axis=0
    )
    grad_taken = (
        jnp.take(grad_pad, slot_index, axis=0)
        .reshape(2, tok_count, model_width)
        .astype(jnp.float32)
    )
    grad_normed_two = grad_taken[0] + grad_taken[1]
    grad_up, grad_up_bias, grad_down, grad_down_bias = (
        lax.psum_scatter(
            totals[0][None].astype(jnp.bfloat16), "fsdp", scatter_dimension=1, tiled=True
        ).astype(jnp.float32),
        lax.psum_scatter(
            totals[1][None].astype(jnp.bfloat16), "fsdp", scatter_dimension=1, tiled=True
        ).astype(jnp.float32),
        lax.psum_scatter(
            totals[2][None].astype(jnp.bfloat16), "fsdp", scatter_dimension=1, tiled=True
        ).astype(jnp.float32),
        lax.psum_scatter(
            totals[3][None].astype(jnp.bfloat16), "fsdp", scatter_dimension=1, tiled=True
        ).astype(jnp.float32),
    )
    grad_hidden_part, grad_gain_two, grad_bias_two = norm_two_back(grad_normed_two)
    grad_hidden = grad_mixed + grad_hidden_part
    grad_branch = grad_hidden.astype(jnp.bfloat16)
    grad_proj = jnp.dot(attended_flat.T, grad_branch, preferred_element_type=jnp.float32)
    grad_attended = jnp.dot(grad_branch, proj_full.T, preferred_element_type=jnp.float32).astype(
        jnp.bfloat16
    )
    grad_attended = grad_attended.reshape(row_count, piece_len, HEADS, HD)
    part_query, part_key, part_value = attend_backward(
        queries, keys_all, values_all, allowed, logsum, grad_attended
    )
    summed_key, summed_value = (
        lax.psum_scatter(
            part_key.astype(jnp.bfloat16), "fsdp", scatter_dimension=1, tiled=True
        ).astype(jnp.float32),
        lax.psum_scatter(
            part_value.astype(jnp.bfloat16), "fsdp", scatter_dimension=1, tiled=True
        ).astype(jnp.float32),
    )
    grad_query = part_query.astype(jnp.bfloat16)
    grad_key = summed_key.astype(jnp.bfloat16)
    grad_value = summed_value.astype(jnp.bfloat16)
    grad_projected = jnp.stack([grad_query, grad_key, grad_value], axis=2).reshape(
        tok_count, 3 * model_width
    )
    grad_qkv_weight = jnp.dot(normed_low.T, grad_projected, preferred_element_type=jnp.float32)
    grad_normed = jnp.dot(grad_projected, qkv_full.T, preferred_element_type=jnp.float32)
    grad_inputs, grad_gain_one, grad_bias_one = norm_back(grad_normed)
    grad_tokens = (grad_hidden + grad_inputs).reshape(tokens.shape)
    grad_gate_task = jnp.dot(task_hot.T, grad_gate_copy.T, precision=exact)
    grad_embed, grad_router = gate_back(grad_gate_task)
    reduced = (
        lax.psum_scatter(grad_gain_one, ("dp", "fsdp"), scatter_dimension=0, tiled=True),
        lax.psum_scatter(grad_bias_one, ("dp", "fsdp"), scatter_dimension=0, tiled=True),
        lax.psum_scatter(grad_qkv_weight, ("dp", "fsdp"), scatter_dimension=0, tiled=True),
        lax.psum_scatter(grad_proj, ("dp", "fsdp"), scatter_dimension=0, tiled=True),
        lax.psum_scatter(grad_gain_two, ("dp", "fsdp"), scatter_dimension=0, tiled=True),
        lax.psum_scatter(grad_bias_two, ("dp", "fsdp"), scatter_dimension=0, tiled=True),
        lax.psum_scatter(grad_embed, ("dp", "fsdp"), scatter_dimension=1, tiled=True),
        lax.psum_scatter(grad_router, ("dp", "fsdp"), scatter_dimension=0, tiled=True),
    )
    return (
        output,
        grad_tokens,
        reduced[0],
        reduced[1],
        reduced[2],
        reduced[3],
        reduced[4],
        reduced[5],
        reduced[6],
        reduced[7],
        grad_up,
        grad_up_bias,
        grad_down,
        grad_down_bias,
    )


MESH_ID = pl.DeviceIdType.MESH
VMEM_MAX = 62 * 1024 * 1024
TILE = 16
BLOCK = 512
FCHUNK = 1024
QCHUNK = 256
FAR = -float(2**30)
F32 = jnp.float32
BF16 = jnp.bfloat16


def dot_nn(lhs, rhs):
    return lax.dot_general(lhs, rhs, (((1,), (0,)), ((), ())), preferred_element_type=F32)


def dot_nt(lhs, rhs):
    return lax.dot_general(lhs, rhs, (((1,), (1,)), ((), ())), preferred_element_type=F32)


def dot_tn(lhs, rhs):
    return lax.dot_general(lhs, rhs, (((0,), (0,)), ((), ())), preferred_element_type=F32)


def vmem_spec():
    return pl.BlockSpec(memory_space=pltpu.VMEM)


def any_spec():
    return pl.BlockSpec(memory_space=pl.ANY)


def smem_spec():
    return pl.BlockSpec(memory_space=pltpu.SMEM)


def norm_parts(values):
    centre = values - jnp.mean(values, axis=-1, keepdims=True)
    spread = jnp.mean(centre * centre, axis=-1, keepdims=True)
    scale = lax.rsqrt(spread + 1e-05)
    return centre * scale, scale


def norm_back_parts(grad, normal, scale):
    mean_grad = jnp.mean(grad, axis=-1, keepdims=True)
    mean_prod = jnp.mean(grad * normal, axis=-1, keepdims=True)
    return (grad - mean_grad - normal * mean_prod) * scale


def fold_rows(values):
    rows, width = values.shape
    return jnp.sum(values.reshape(rows // 8, 8, width), axis=0)


def plane_ids():
    me = lax.axis_index("dp")
    core, xpos, ypos = lax.rem(me, 2), lax.rem(me // 2, 2), me // 4

    def at(ypos, xpos, core):
        return (ypos * 2 + xpos) * 2 + core

    return me, core, xpos, ypos, at


def greet(peers):
    barrier = pltpu.get_barrier_semaphore()
    for peer in peers:
        pl.semaphore_signal(barrier, inc=1, device_id=peer, device_id_type=MESH_ID)
    pl.semaphore_wait(barrier, len(peers))


class Sender:
    def __init__(self, send_sems, recv_sems):
        self.send_sems, self.recv_sems, self.count, self.all = send_sems, recv_sems, 0, []

    def start(self, src, dst, peer):
        copy = pltpu.make_async_remote_copy(
            src_ref=src,
            dst_ref=dst,
            send_sem=self.send_sems.at[self.count],
            recv_sem=self.recv_sems.at[self.count],
            device_id=peer,
            device_id_type=MESH_ID,
        )
        copy.start()
        self.count += 1
        self.all.append(copy)
        return copy

    def drain(self):
        for copy in self.all:
            copy.wait_send()


def plane_gather_steps(block, own, rows, sender, z):
    me, core, xpos, ypos, at = plane_ids()
    sib, xn, yn = at(ypos, xpos, 1 - core), at(ypos, 1 - xpos, core), at(1 - ypos, xpos, core)
    diag = at(1 - ypos, 1 - xpos, core)
    half = rows // 2

    def part(i, k):
        return block(i).at[pl.ds(k * half, half)]

    def send(i, k, peer):
        src = own.at[pl.ds(k * half, half)] if i is me else part(i, k)
        return sender.start(src, part(i, k), (peer, z))

    x_own = [send(me, 0, xn)]
    y_own = [send(me, 1, yn)]
    x_own.append(send(me, 1, xn))
    y_own.insert(0, send(me, 0, yn))
    last = [send(me, 0, sib), send(me, 1, sib)]
    x_own[0].wait_recv()
    to_y = send(xn, 0, yn)
    y_own[1].wait_recv()
    to_x = send(yn, 1, xn)
    last.append(send(xn, 0, sib))
    last.append(send(yn, 1, sib))
    x_own[1].wait_recv()
    last.append(send(xn, 1, sib))
    y_own[0].wait_recv()
    last.append(send(yn, 0, sib))
    to_y.wait_recv()
    last.append(send(diag, 0, sib))
    to_x.wait_recv()
    last.append(send(diag, 1, sib))
    for copy in last:
        copy.wait_recv()


PLANE_GATHER_COPIES = 14


def plane_peers(z):
    me, core, xpos, ypos, at = plane_ids()
    return [
        (at(ypos, xpos, 1 - core), z),
        (at(ypos, 1 - xpos, core), z),
        (at(1 - ypos, xpos, core), z),
    ]


def column_peers(planes):
    me, z = lax.axis_index("dp"), lax.axis_index("fsdp")
    peers = [(me, lax.rem(z + k, planes)) for k in range(1, planes)]
    return peers + [(me ^ 1, lax.rem(z + k, planes)) for k in range(1, planes)]


class PlaneGather:
    COPIES = 28

    def __init__(self, block, own, send_sems, recv_sems):
        me, core, xpos, ypos, at = plane_ids()
        self.z = lax.axis_index("fsdp")
        self.me = me
        self.sib = at(ypos, xpos, 1 - core)
        self.xn, self.yn = at(ypos, 1 - xpos, core), at(1 - ypos, xpos, core)
        self.diag = at(1 - ypos, 1 - xpos, core)
        self.block, self.own = block, own
        self.send_sems, self.recv_sems = send_sems, recv_sems
        self.all = {}

    def send(self, kind, c, src, owner, peer):
        copy = pltpu.make_async_remote_copy(
            src_ref=src,
            dst_ref=self.block(owner).at[c],
            send_sem=self.send_sems.at[kind * 4 + c],
            recv_sem=self.recv_sems.at[kind * 4 + c],
            device_id=(peer, self.z),
            device_id_type=MESH_ID,
        )
        copy.start()
        self.all[kind, c] = copy

    def start(self, c):
        src = self.own.at[c]
        self.send(0, c, src, self.me, self.xn)
        self.send(1, c, src, self.me, self.yn)
        self.send(2, c, src, self.me, self.sib)

    def pass_on(self, c):
        x_part, y_part = self.block(self.xn).at[c], self.block(self.yn).at[c]
        self.all[0, c].wait_recv()
        if c % 2 == 0:
            self.send(3, c, x_part, self.xn, self.yn)
        self.send(4, c, x_part, self.xn, self.sib)
        self.all[1, c].wait_recv()
        if c % 2 == 1:
            self.send(3, c, y_part, self.yn, self.xn)
        self.send(5, c, y_part, self.yn, self.sib)

    def pass_diag(self, c):
        self.all[3, c].wait_recv()
        self.send(6, c, self.block(self.diag).at[c], self.diag, self.sib)

    def finish(self):
        for kind in (2, 4, 5, 6):
            for c in range(4):
                self.all[kind, c].wait_recv()
        for copy in self.all.values():
            copy.wait_send()


def plane_scatter_steps(z_ref, own, theirs, deep, near_x, near_y, sender, loc_sems, z):
    me, core, xpos, ypos, at = plane_ids()
    sib, xn, yn = at(ypos, xpos, 1 - core), at(ypos, 1 - xpos, core), at(1 - ypos, xpos, core)
    chips = [(ypos, xpos), (ypos, 1 - xpos), (1 - ypos, xpos), (1 - ypos, 1 - xpos)]
    rows = z_ref.shape[1]
    half = rows // 2
    first, second = pl.ds(0, half), pl.ds(half, half)
    loads, trades = {}, {}
    for slot in (3, 1, 2, 0):
        pos = chips[slot]
        trades[slot] = sender.start(
            z_ref.at[at(pos[0], pos[1], 1 - core)], theirs.at[slot], (sib, z)
        )

    yield
    for slot in (3, 1, 2, 0):
        pos = chips[slot]
        loads[slot] = pltpu.make_async_copy(
            z_ref.at[at(pos[0], pos[1], core)], own.at[slot], loc_sems.at[slot]
        )
        loads[slot].start()
    yield

    def add(slot, part):
        own[slot, part] = (
            own[slot, part].astype(F32) + theirs[slot, part].astype(F32)
        ).astype(own.dtype)

    loads[3].wait()
    trades[3].wait_recv()
    add(3, first)
    deep_x = sender.start(own.at[3, first], deep.at[0], (xn, z))
    add(3, second)
    deep_y = sender.start(own.at[3, second], deep.at[1], (yn, z))
    loads[1].wait()
    trades[1].wait_recv()
    add(1, first)
    x_first = sender.start(own.at[1, first], near_x.at[first], (xn, z))
    loads[2].wait()
    trades[2].wait_recv()
    add(2, second)
    y_second = sender.start(own.at[2, second], near_y.at[second], (yn, z))
    add(1, second)
    add(2, first)
    yield
    deep_y.wait_recv()
    own[1, second] = (own[1, second].astype(F32) + deep[1].astype(F32)).astype(own.dtype)
    x_second = sender.start(own.at[1, second], near_x.at[second], (xn, z))
    deep_x.wait_recv()
    own[2, first] = (own[2, first].astype(F32) + deep[0].astype(F32)).astype(own.dtype)
    y_first = sender.start(own.at[2, first], near_y.at[first], (yn, z))
    yield
    loads[0].wait()
    trades[0].wait_recv()
    yield
    mine = own[0].astype(F32) + theirs[0].astype(F32)
    x_first.wait_recv()
    y_second.wait_recv()
    x_second.wait_recv()
    y_first.wait_recv()
    yield mine + near_x[...].astype(F32) + near_y[...].astype(F32)


PLANE_SCATTER_COPIES = 10


def pick_rows_kernel(order_ref, *refs):
    count = len(refs) // 2
    for a in range(count):
        for r in range(refs[a].shape[0]):
            refs[count + a][r] = refs[a][order_ref[0, r]].astype(refs[count + a].dtype)


def pick_rows(order, arrays, kinds):
    return pl.pallas_call(
        pick_rows_kernel,
        out_shape=tuple(
            jax.ShapeDtypeStruct(array.shape, kind) for array, kind in zip(arrays, kinds)
        ),
        in_specs=[smem_spec()] + [vmem_spec()] * len(arrays),
        out_specs=tuple(vmem_spec() for _ in arrays),
        compiler_params=pltpu.CompilerParams(vmem_limit_bytes=VMEM_MAX),
        name="row_order",
    )(order, *arrays)


PAYLOAD = 48
CODE_LOW, CODE_HIGH, BIAS_UP, BIAS_DOWN, NORMS, LOGITS = 0, 4, 8, 12, 13, 16


def make_payload(payload, sent_ref, seg_ref, key_ref, logit_ref, norm_ref, bup_ref, bdown_ref):
    seg = seg_ref[...]
    row_count, piece = seg.shape
    row = lax.broadcasted_iota(jnp.int32, seg.shape, 0)
    task = jnp.zeros_like(seg)
    for r in range(row_count):
        for k in range(sent_ref.shape[1]):
            task = jnp.where((row == r) & (seg == k), sent_ref[r, k], task)
    code = (task * 16 + seg * 2 + key_ref[...]).astype(F32)
    payload[...] = jnp.zeros_like(payload)
    payload[CODE_LOW : CODE_LOW + row_count] = code[:, : piece // 2]
    payload[CODE_HIGH : CODE_HIGH + row_count] = code[:, piece // 2 :]
    for k in range(bup_ref.shape[1] // 128):
        payload[BIAS_UP + k : BIAS_UP + k + 1] = bup_ref[:, k * 128 : (k + 1) * 128].astype(F32)
    payload[BIAS_DOWN : BIAS_DOWN + 1] = bdown_ref[...].astype(F32)
    payload[NORMS : NORMS + 1] = norm_ref[...]
    tasks, n_experts = logit_ref.shape
    payload[LOGITS : LOGITS + tasks, :n_experts] = logit_ref[...]


def code_segment(code):
    return lax.shift_right_logical(code.astype(jnp.int32), 1) & 7


def row_order(codes_ref, me, planes):
    single = jnp.int32(0)
    for r in reversed(range(planes)):
        first = jnp.max(code_segment(codes_ref[me, 0, CODE_LOW + r : CODE_LOW + r + 1, :1]))
        last = jnp.max(
            code_segment(codes_ref[me, planes - 1, CODE_HIGH + r : CODE_HIGH + r + 1, 127:])
        )
        single = jnp.where(first == last, r, single)
    target = lax.rem(me, planes)
    return [
        jnp.where(p == target, single, jnp.where(p == single, target, p)) for p in range(planes)
    ]


def row_features(codes_ref, me, order, z, planes, qf_ref, kf_ref, order_ref):
    mine = order[0]
    for p in range(1, planes):
        mine = jnp.where(z == p, order[p], mine)
    parts = []
    for p in range(planes):
        low, high = codes_ref[me, p, CODE_LOW : CODE_LOW + 4], codes_ref[me, p, CODE_HIGH : CODE_HIGH + 4]
        row = lax.broadcasted_iota(jnp.int32, low.shape, 0)
        for half in (low, high):
            parts.append(jnp.sum(jnp.where(row == mine, half, 0.0), axis=0, keepdims=True))
    columns = jnp.concatenate(parts, axis=0).T
    lane = lax.broadcasted_iota(jnp.int32, (128, qf_ref.shape[1]), 1)
    for k in range(2 * planes):
        code = columns[:, k : k + 1].astype(jnp.int32)
        hot = (lax.shift_right_logical(code, 1) & 7) == lane
        part = slice(k * 128, (k + 1) * 128)
        qf_ref[part, :] = jnp.where(hot, 1.0, 0.0).astype(BF16)
        seen = hot & ((code & 1) == 1)
        kf_ref[part, :] = jnp.where((lane < 8) & jnp.logical_not(seen), FAR, 0.0).astype(BF16)
    spot = lax.broadcasted_iota(jnp.int32, order_ref.shape, 1)
    table = jnp.zeros(order_ref.shape, jnp.int32)
    for p in range(planes):
        table = jnp.where(spot == p, order[p], table)
    order_ref[...] = table


def gather_norms(codes_ref, norm_ref):
    devices = codes_ref.shape[0] * codes_ref.shape[1]
    width = norm_ref.shape[1]
    size = width // devices
    shards = codes_ref[:, :, NORMS : NORMS + 1, :].reshape(devices, 128).astype(BF16)
    lane = lax.broadcasted_iota(jnp.int32, (128, width), 0)
    column = lax.broadcasted_iota(jnp.int32, (128, width), 1)
    owner = lax.broadcasted_iota(jnp.int32, (devices, width), 0)
    owned = lax.broadcasted_iota(jnp.int32, (devices, width), 1) // size
    for k in range(4):
        place = jnp.where(lane == k * size + lax.rem(column, size), 1.0, 0.0).astype(BF16)
        full = jnp.where(owner == owned, dot_nn(shards, place), 0.0)
        norm_ref[k : k + 1] = jnp.sum(full, axis=0, keepdims=True)


def routing_marks(codes_ref, te_ref, marks_ref, gates_ref, me, z, planes, capacity):
    groups = codes_ref.shape[0]
    tasks = te_ref.shape[0]
    count = groups * planes * planes
    low = codes_ref[:, :, CODE_LOW : CODE_LOW + planes, :].reshape(count, 128)
    high = codes_ref[:, :, CODE_HIGH : CODE_HIGH + planes, :].reshape(count, 128)
    code = jnp.concatenate([low, high], axis=1).astype(jnp.int32)
    piece = code.shape[1]
    task = lax.shift_right_logical(code, 4)
    one = lax.broadcasted_iota(jnp.int32, (count, count), 0)
    two = lax.broadcasted_iota(jnp.int32, (count, count), 1)
    block_one, block_two = one // planes, two // planes
    row_one, row_two = lax.rem(one, planes), lax.rem(two, planes)

    def table(mask):
        return jnp.where(mask, 1.0, 0.0).astype(BF16)

    whole = table(block_one == block_two)
    ahead_rows = table((block_one == block_two) & (row_two < row_one))
    group_one, group_two = block_one // planes, block_two // planes
    plane_two = lax.rem(block_two, planes)
    same_row = (group_one == group_two) & (row_one == row_two)

    def wide(column):
        return jnp.broadcast_to(column, (count, 128)).astype(BF16)

    seg = lax.shift_right_logical(code, 1) & 7
    first = dot_nn(table(same_row & (plane_two == 0)), wide(seg[:, :1].astype(F32)))
    last = dot_nn(
        table(same_row & (plane_two == planes - 1)), wide(seg[:, piece - 1 :].astype(F32))
    )
    lone = jnp.where(first == last, 1.0, 0.0)
    lone = jnp.where(dot_nn(ahead_rows, lone.astype(BF16)) == 0.0, lone, 0.0)
    row = lax.rem(lax.broadcasted_iota(jnp.int32, (count, 128), 0), planes)
    group = lax.broadcasted_iota(jnp.int32, (count, 128), 0) // (planes * planes)
    single = dot_nn(whole, (lone * row.astype(F32)).astype(BF16)).astype(jnp.int32)
    target = lax.rem(group, planes)
    picked = jnp.where(z == target, single, jnp.where(z == single, target, z))
    here = jnp.where(row == picked, 1.0, 0.0)[:, :1]

    before_table = table(
        lax.broadcasted_iota(jnp.int32, (piece, piece), 0)
        < lax.broadcasted_iota(jnp.int32, (piece, piece), 1)
    )
    gather = table(
        lax.broadcasted_iota(jnp.int32, (count // planes, count), 0)
        == lax.broadcasted_iota(jnp.int32, (count // planes, count), 1) // planes
    )
    chip = me - lax.rem(me, 2)
    for e in range(2):
        hits = []
        for j in range(2):
            bits = jnp.int32(0)
            for t in range(tasks):
                bit = (1 << t) if t < 31 else -(1 << 31)
                bits = bits | jnp.where(te_ref[t, j] == chip + e, jnp.int32(bit), jnp.int32(0))
            hits.append((lax.shift_right_logical(jnp.full(task.shape, bits), task) & 1).astype(F32))
        kept = jnp.zeros(task.shape, F32)
        base = jnp.zeros((count, 128), F32)
        for j in range(2):
            total = wide(jnp.sum(hits[j], axis=1, keepdims=True))
            rank = dot_nn(hits[j].astype(BF16), before_table)
            rank = rank + (base + dot_nn(ahead_rows, total))[:, :1]
            kept = kept + jnp.where(rank < capacity, hits[j], 0.0)
            base = base + dot_nn(whole, total)
        mark = kept * here * (task + 1).astype(F32)
        marks_ref[e] = dot_nn(gather, mark.astype(BF16)) - 1.0

    logits = jnp.sum(
        codes_ref[:, :, LOGITS : LOGITS + tasks, :].reshape(groups * planes, tasks, 128), axis=0
    )
    lane = lax.broadcasted_iota(jnp.int32, (tasks, 128), 1)
    task_row = lax.broadcasted_iota(jnp.int32, (tasks, 128), 0)
    hot = []
    for j in range(2):
        chosen = jnp.zeros((tasks, 128), jnp.int32)
        for t in range(tasks):
            chosen = jnp.where(task_row == t, te_ref[t, j], chosen)
        hot.append(lane == chosen)
    level = [jnp.sum(jnp.where(h, logits, 0.0), axis=1, keepdims=True) for h in hot]
    top = jnp.maximum(level[0], level[1])
    weight = [jnp.exp(v - top) for v in level]
    both = weight[0] + weight[1]
    grid = jnp.zeros((tasks, 128), F32)
    for j in range(2):
        grid = jnp.where(hot[j], weight[j] / both, grid)
    grid = jnp.concatenate([grid, jnp.zeros((128 - tasks, 128), F32)], axis=0)
    gates_ref[...] = grid.T[:groups]


def unit_copy(src, dst, send_sem, recv_sem, peer):
    return pltpu.make_async_remote_copy(
        src_ref=src,
        dst_ref=dst,
        send_sem=send_sem,
        recv_sem=recv_sem,
        device_id=peer,
        device_id_type=MESH_ID,
    )


class WeightSpread:
    def __init__(self, up_ref, down_ref, up_all, down_all, sems):
        self.me, self.z = lax.axis_index("dp"), lax.axis_index("fsdp")
        self.core = lax.rem(self.me, 2)
        self.src = (up_ref, down_ref)
        self.dst = (up_all, down_all)
        self.own_send, self.pass_send, self.recv, self.local = sems
        self.side = self.z // 2
        self.near = self.z ^ 1
        self.far = 2 - self.side
        self.inner = (self.z == 1) | (self.z == 2)

    def targets(self):
        chip = self.me - self.core
        return [
            (self.core, self.near),
            (self.core, self.far),
            (1 - self.core, self.near),
            (1 - self.core, self.far),
            (1 - self.core, self.z),
        ], chip

    def copy(self, kind, src, m, p, send_sem, peer):
        return unit_copy(
            src,
            self.dst[kind].at[m, p],
            send_sem,
            self.recv.at[kind * 8 + m * 4 + p],
            peer,
        )

    def own(self):
        targets, chip = self.targets()
        out = []
        for kind in range(2):
            for k, (h, p) in enumerate(targets):
                out.append(
                    self.copy(
                        kind,
                        self.src[kind].at[h],
                        self.core,
                        self.z,
                        self.own_send.at[kind * 5 + k],
                        (chip + h, p),
                    )
                )
        return out

    def mine(self):
        return [
            pltpu.make_async_copy(
                self.src[kind].at[self.core],
                self.dst[kind].at[self.core, self.z],
                self.local.at[kind],
            )
            for kind in range(2)
        ]

    def passed(self, j):
        p = 2 * (1 - self.side) + j
        return [
            self.copy(
                kind,
                self.dst[kind].at[m, p],
                m,
                p,
                self.pass_send.at[kind * 4 + m * 2 + j],
                (self.me, self.near),
            )
            for kind in range(2)
            for m in range(2)
        ]

    def start(self, kind):
        self.mine()[kind].start()
        copies = self.own()[5 * kind : 5 * kind + 5]
        for k, copy in enumerate(copies):
            if k not in (1, 3):
                copy.start()

        @pl.when(self.inner)
        def _():
            for k, copy in enumerate(copies):
                if k in (1, 3):
                    copy.start()

    def start_far(self, kind):
        @pl.when(jnp.logical_not(self.inner))
        def _():
            for k, copy in enumerate(self.own()):
                if k in (5 * kind + 1, 5 * kind + 3):
                    copy.start()

    def pass_on(self, first, kind):
        for side in range(2):

            @pl.when((self.z == 1 + side))
            def _():
                j = side if first else 1 - side
                for copy in self.passed(j)[2 * kind : 2 * kind + 2]:
                    copy.wait_recv()
                    copy.start()

    def finish(self):
        for copy in self.mine():
            copy.wait()
        for copy in self.own():
            copy.wait_send()

        def arrived(kind, m, p):
            self.copy(
                kind, self.dst[kind].at[m, p], m, p, self.own_send.at[0], (self.me, self.near)
            ).wait_recv()

        for kind in range(2):
            arrived(kind, 1 - self.core, self.z)
            for m in range(2):
                arrived(kind, m, self.near)

        @pl.when(self.inner)
        def _():
            for j in range(2):
                for copy in self.passed(j):
                    copy.wait_send()

        @pl.when(jnp.logical_not(self.inner))
        def _():
            for kind in range(2):
                for m in range(2):
                    for j in range(2):
                        arrived(kind, m, 2 * (1 - self.side) + j)


def forward_kernel(
    heads,
    planes,
    capacity,
    sent_ref,
    te_ref,
    seg_ref,
    key_ref,
    logit_ref,
    shard_norms,
    bup_ref,
    bdown_ref,
    tok_ref,
    gm_ref,
    wqkv_ref,
    wproj_ref,
    upw_in,
    downw_in,
    codes_ref,
    marks_ref,
    gates_ref,
    order_ref,
    norm_ref,
    qf_ref,
    kf_ref,
    row_out,
    dense_out,
    qkv_out,
    o_out,
    lse_out,
    hres_out,
    xn2_ref,
    x_all,
    g_all,
    up_all,
    down_all,
    row_ref,
    dense_ref,
    qkv_ref,
    o_ref,
    lse_ref,
    hres_ref,
    kaug,
    vaug,
    w_ref,
    upw_ref,
    downw_ref,
    payload,
    tok_out,
    gm_out,
    p_send,
    p_recv,
    z_send,
    z_recv,
    w_send,
    w_recv,
    x_send,
    x_recv,
    g_send,
    g_recv,
    u_own,
    u_pass,
    u_recv,
    loc_sems,
    out_sems,
    in_sems,
):
    me, z = lax.axis_index("dp"), lax.axis_index("fsdp")
    z_peers = [(me, lax.rem(z + k, planes)) for k in range(1, planes)]
    groups = codes_ref.shape[0]
    d_peers = [(lax.rem(me + k, groups), z) for k in range(1, groups)]
    width = row_ref.shape[2]
    stages = [
        pltpu.make_async_copy(wqkv_ref, w_ref.at[:, pl.ds(0, 3 * width)], in_sems.at[0]),
        pltpu.make_async_copy(wproj_ref, w_ref.at[:, pl.ds(3 * width, width)], in_sems.at[1]),
        pltpu.make_async_copy(downw_in.at[0], downw_ref, in_sems.at[2]),
    ]
    part = upw_ref.shape[2] // planes
    for p in range(planes):
        for h in range(2):
            stages.append(
                pltpu.make_async_copy(
                    upw_in.at[0, :, pl.ds((2 * p + h) * part, part)],
                    upw_ref.at[h, :, pl.ds(p * part, part)],
                    in_sems.at[len(stages)],
                )
            )
    for copy in stages:
        copy.start()
    greet(column_peers(planes) + d_peers)
    rows = qkv_ref.shape[0]
    for copy in stages:
        copy.wait()
    chunk = row_ref.shape[1]
    head = width // heads
    pair = 2 * head
    shard = w_ref.shape[0]
    sender = Sender(z_send, z_recv)
    dense_own = pltpu.make_async_copy(
        w_ref, dense_ref.at[me, pl.ds(z * shard, shard)], loc_sems.at[0]
    )
    dense_own.start()
    make_payload(payload, sent_ref, seg_ref, key_ref, logit_ref, shard_norms, bup_ref, bdown_ref)
    codes_ref[me, z] = payload[...]
    p_sender = Sender(p_send, p_recv)
    codes_z = [p_sender.start(payload, codes_ref.at[me, z], peer) for peer in z_peers]
    dense_z = [
        sender.start(w_ref, dense_ref.at[me, pl.ds(z * shard, shard)], peer) for peer in z_peers
    ]
    spread = WeightSpread(upw_ref, downw_ref, up_all, down_all, (u_own, u_pass, u_recv, loc_sems.at[pl.ds(3, 2)]))
    spread.start(0)
    for copy in codes_z:
        copy.wait_recv()
    order = row_order(codes_ref, me, planes)
    for c in range(planes):
        tok_out[c] = tok_ref[order[c]]
        gm_out[c] = gm_ref[order[c]]
    toks = [sender.start(tok_out.at[peer[1]], row_ref.at[z], peer) for peer in z_peers]
    tok_own = pltpu.make_async_copy(tok_out.at[z], row_ref.at[z], loc_sems.at[1])
    tok_own.start()
    gm_own = pltpu.make_async_copy(gm_out.at[z], g_all.at[me, z], loc_sems.at[2])
    gm_own.start()
    codes_d = [p_sender.start(codes_ref.at[me], codes_ref.at[me], peer) for peer in d_peers]
    dense_own.wait()
    for copy in dense_z:
        copy.wait_recv()
    dense_sender = Sender(w_send, w_recv)
    plane_gather_steps(
        lambda i: dense_ref.at[i], dense_ref.at[me], planes * shard, dense_sender, z
    )
    row_features(codes_ref, me, order, z, planes, qf_ref, kf_ref, order_ref)
    for copy in codes_d:
        copy.wait_recv()
    gather_norms(codes_ref, norm_ref)
    routing_marks(codes_ref, te_ref, marks_ref, gates_ref, me, z, planes, capacity)
    x_gather = PlaneGather(lambda i: x_all.at[i], xn2_ref, x_send, x_recv)
    g_gather = PlaneGather(lambda i: g_all.at[i], g_all.at[me], g_send, g_recv)

    for copy in toks:
        copy.wait_recv()
    tok_own.wait()
    gms = [sender.start(gm_out.at[peer[1]], g_all.at[me, z], peer) for peer in z_peers]

    lane = lax.broadcasted_iota(jnp.int32, (rows, pair), 1)
    lane_c = lax.broadcasted_iota(jnp.int32, (chunk, pair), 1)

    def project(c, carry):
        part = pl.ds(pl.multiple_of(c * chunk, chunk), chunk)
        normal, _ = norm_parts(row_ref[c].astype(F32))
        xn1 = (normal * norm_ref[0:1, :] + norm_ref[1:2, :]).astype(BF16)
        out = dot_nn(xn1, dense_ref[:, :, : 3 * width].reshape(width, 3 * width))
        qkv_ref[part, :width] = (out[:, :width] * 0.125).astype(BF16)
        qkv_ref[part, width:] = out[:, width:].astype(BF16)
        return carry

    lax.fori_loop(0, planes, project, 0)

    def prepare(g, carry):
        k_pair = qkv_ref[:, pl.ds(pl.multiple_of(width + g * pair, pair), pair)]
        v_pair = qkv_ref[:, pl.ds(pl.multiple_of(2 * width + g * pair, pair), pair)]
        zero = jnp.zeros_like(k_pair)
        for side in range(2):
            mine = (lane // head) == side
            kaug[g, side, :, :pair] = jnp.where(mine, k_pair, zero)
            vaug[g, side, :, :pair] = jnp.where(mine, v_pair, zero)
            kaug[g, side, :, pair:] = kf_ref[...]
            vaug[g, side, :, pair:] = jnp.where(mine, 1.0, 0.0).astype(BF16)
        return carry

    lax.fori_loop(0, heads // 2, prepare, 0)

    def attend(c):
        part = pl.ds(c * chunk, chunk)

        def one_pair(g, carry):
            cols = pl.ds(pl.multiple_of(g * pair, pair), pair)
            qa = jnp.concatenate([qkv_ref[part, cols], qf_ref[part, :]], axis=1)
            acc = jnp.zeros((chunk, 2 * pair), F32)
            tops = []
            for side in range(2):
                s = dot_nt(qa, kaug[g, side])
                top = jnp.max(s, axis=-1, keepdims=True)
                acc = acc + dot_nn(jnp.exp(s - top).astype(BF16), vaug[g, side])
                tops.append(top)
            total = acc[:, pair:]
            o_ref[part, cols] = (acc[:, :pair] / total).astype(BF16)
            table = lse_ref[part, :]
            for side in range(2):
                level = tops[side] + jnp.log(total[:, side * head : side * head + 1])
                table = jnp.where(lane_c == 2 * g + side, level, table)
            lse_ref[part, :] = table
            return carry

        lax.fori_loop(0, heads // 2, one_pair, 0)
        w_proj = dense_ref[:, :, 3 * width : 4 * width].reshape(width, width)
        hres = row_ref[c].astype(F32) + dot_nn(o_ref[part, :], w_proj)
        hres_ref[part, :] = hres
        normal, _ = norm_parts(hres)
        xn2_ref[c] = (normal * norm_ref[2:3, :] + norm_ref[3:4, :]).astype(BF16)
        x_gather.start(c)

    attend(0)
    attend(1)
    for copy in gms:
        copy.wait_recv()
    gm_own.wait()
    spread.start(1)
    spread.pass_on(True, 0)
    for c in range(4):
        g_gather.start(c)
    attend(2)
    x_gather.pass_on(0)
    x_gather.pass_on(1)
    spread.start_far(0)
    attend(3)
    spread.start_far(1)
    spread.pass_on(True, 1)
    pairs = (
        (row_ref, row_out),
        (dense_ref, dense_out),
        (qkv_ref, qkv_out),
        (o_ref, o_out),
        (lse_ref, lse_out),
        (hres_ref, hres_out),
    )
    saves = [pltpu.make_async_copy(a, b, out_sems.at[k]) for k, (a, b) in enumerate(pairs)]
    for copy in saves:
        copy.start()
    x_gather.pass_on(2)
    g_gather.pass_on(0)
    g_gather.pass_on(1)
    spread.pass_on(False, 0)
    x_gather.pass_on(3)
    g_gather.pass_on(2)
    spread.pass_on(False, 1)
    g_gather.pass_on(3)
    for c in range(4):
        x_gather.pass_diag(c)
        g_gather.pass_diag(c)
    for copy in saves:
        copy.wait()
    x_gather.finish()
    g_gather.finish()
    spread.finish()
    for sender in (p_sender, sender, dense_sender):
        sender.drain()


def forward(
    sent_task, task_experts, routing, tokens, grads, w_qkv, w_proj, up, down, heads, groups, capacity
):
    planes, piece, width = tokens.shape
    rows = planes * piece
    half = up.shape[2] // 2
    dense = jax.ShapeDtypeStruct((w_qkv.shape[0], 4 * width), BF16)
    up_half = (2, up.shape[1], half)
    down_half = (2, down.shape[1] // 2, width)
    pair = 2 * (width // heads)
    sd = jax.ShapeDtypeStruct
    dma = pltpu.SemaphoreType.DMA
    return pl.pallas_call(
        functools.partial(forward_kernel, heads, planes, capacity),
        out_shape=(
            sd((groups, planes, PAYLOAD, 128), F32),
            sd((2, groups * planes, piece), F32),
            sd((groups, 128), F32),
            sd((8, 128), jnp.int32),
            sd((8, width), F32),
            sd((rows, pair), BF16),
            sd((rows, pair), BF16),
            sd(tokens.shape, BF16),
            sd((groups, planes * dense.shape[0], dense.shape[1]), BF16),
            sd((rows, 3 * width), BF16),
            sd((rows, width), BF16),
            sd((rows, pair), F32),
            sd((rows, width), F32),
            sd(tokens.shape, BF16),
            sd((groups,) + tokens.shape, BF16),
            sd((groups,) + tokens.shape, BF16),
            sd((2, planes) + up_half[1:], BF16),
            sd((2, planes) + down_half[1:], BF16),
        ),
        in_specs=[smem_spec()] * 2
        + [vmem_spec()] * (len(routing) + 2)
        + [any_spec()] * 4,
        out_specs=tuple(
            [vmem_spec()] * 7 + [any_spec()] * 6 + [vmem_spec()] + [any_spec()] * 4
        ),
        scratch_shapes=[
            pltpu.VMEM(tokens.shape, BF16),
            pltpu.VMEM((groups, planes * dense.shape[0], dense.shape[1]), BF16),
            pltpu.VMEM((rows, 3 * width), BF16),
            pltpu.VMEM((rows, width), BF16),
            pltpu.VMEM((rows, pair), F32),
            pltpu.VMEM((rows, width), F32),
            pltpu.VMEM((heads // 2, 2, rows, 2 * pair), BF16),
            pltpu.VMEM((heads // 2, 2, rows, 2 * pair), BF16),
            pltpu.VMEM(dense.shape, BF16),
            pltpu.VMEM(up_half, BF16),
            pltpu.VMEM(down_half, BF16),
            pltpu.VMEM((PAYLOAD, 128), F32),
            pltpu.VMEM(tokens.shape, BF16),
            pltpu.VMEM(tokens.shape, BF16),
            dma((planes + groups,)),
            dma((planes + groups,)),
            dma((3 * planes,)),
            dma((3 * planes,)),
            dma((PLANE_GATHER_COPIES,)),
            dma((PLANE_GATHER_COPIES,)),
            dma((PlaneGather.COPIES,)),
            dma((PlaneGather.COPIES,)),
            dma((PlaneGather.COPIES,)),
            dma((PlaneGather.COPIES,)),
            dma((10,)),
            dma((8,)),
            dma((16,)),
            dma((5,)),
            dma((6,)),
            dma((3 + 2 * planes,)),
        ],
        compiler_params=pltpu.CompilerParams(
            collective_id=2, has_side_effects=True, vmem_limit_bytes=VMEM_MAX
        ),
        cost_estimate=pl.CostEstimate(
            flops=40_000_000_000, bytes_accessed=10_000_000, transcendentals=8_000_000
        ),
        name="attention_forward",
    )(
        sent_task,
        task_experts,
        *routing,
        tokens,
        grads,
        w_qkv,
        w_proj,
        up,
        down.reshape((1,) + down_half),
    )


def split3(values):
    high = values.astype(BF16)
    rest = values - high.astype(F32)
    middle = rest.astype(BF16)
    low = (rest - middle.astype(F32)).astype(BF16)
    return high, middle, low


class GradChain:
    def __init__(self, src, land, out, stage, temp, sems):
        self.me, self.z = lax.axis_index("dp"), lax.axis_index("fsdp")
        self.core = lax.rem(self.me, 2)
        self.src, self.land, self.out, self.stage, self.temp = src, land, out, stage, temp
        self.load_sems, self.send_sems, self.recv_sems, self.last_sems = sems
        self.near = self.z ^ 1
        self.inner = (self.z == 1) | (self.z == 2)
        self.outer = jnp.logical_not(self.inner)

    def load(self, kind, plane, k):
        return pltpu.make_async_copy(
            self.src[kind].at[plane], self.stage[kind].at[k], self.load_sems.at[kind * 4 + k]
        )

    def link(self, kind, src, place, plane):
        return unit_copy(
            src,
            self.land[kind].at[place],
            self.send_sems.at[kind * 5 + place],
            self.recv_sems.at[kind * 5 + place],
            (self.me, plane),
        )

    def loads(self):
        planes = (3 - self.z, 3 - self.near, self.near)
        return [self.load(kind, planes[k], k) for kind in range(2) for k in range(3)]

    def outer_sends(self):
        planes = (3 - self.near, 3 - self.z, self.near)
        return [
            self.link(kind, self.src[kind].at[planes[place]], place, self.near)
            for place in range(3)
            for kind in range(2)
        ]

    def start(self):
        for copy in self.loads():
            copy.start()

        @pl.when(self.outer)
        def _():
            for copy in self.outer_sends():
                copy.start()

    def gather(self, kind, place, k):
        self.link(kind, self.land[kind].at[place], place, self.near).wait_recv()
        fetch = pltpu.make_async_copy(
            self.land[kind].at[place], self.temp[kind], self.load_sems.at[kind * 4 + 3]
        )
        fetch.start()
        fetch.wait()
        self.stage[kind][k] = (
            self.stage[kind][k].astype(F32) + self.temp[kind][...].astype(F32)
        ).astype(BF16)

    def inner_sends(self, step):
        place = (3, 4, 3)[step]
        plane = (3 - self.z, 3 - self.z, self.near)[step]
        out = []
        for kind in range(2):
            copy = pltpu.make_async_remote_copy(
                src_ref=self.stage[kind].at[step],
                dst_ref=self.land[kind].at[place],
                send_sem=self.send_sems.at[kind * 5 + step],
                recv_sem=self.recv_sems.at[kind * 5 + place],
                device_id=(self.me, plane),
                device_id_type=MESH_ID,
            )
            out.append(copy)
        return out

    def step(self, step):
        @pl.when(self.inner)
        def _():
            sends = self.inner_sends(step)
            for kind in range(2):
                self.loads()[kind * 3 + step].wait()
                self.gather(kind, (0, 1, 4)[step], step)
                sends[kind].start()

    def last_copies(self):
        out = []
        chip = self.me - self.core
        for kind in range(2):
            out.append(
                unit_copy(
                    self.stage[kind].at[0, 1 - self.core],
                    self.out[kind].at[self.core],
                    self.last_sems.at[kind],
                    self.last_sems.at[2 + kind],
                    (chip + 1 - self.core, self.z),
                )
            )
        return out

    def keep_copies(self):
        return [
            pltpu.make_async_copy(
                self.stage[kind].at[0, self.core],
                self.out[kind].at[self.core],
                self.last_sems.at[4 + kind],
            )
            for kind in range(2)
        ]

    def total(self):
        @pl.when(self.outer)
        def _():
            for copy in self.loads():
                copy.wait()
            for copy in self.outer_sends():
                copy.wait_send()

        @pl.when(self.inner)
        def _():
            for step in range(3):
                for copy in self.inner_sends(step):
                    copy.wait_send()

        own = [self.load(kind, self.z, 0) for kind in range(2)]
        for copy in own:
            copy.start()
        for copy in own:
            copy.wait()

        @pl.when(self.inner)
        def _():
            for kind in range(2):
                self.gather(kind, 2, 0)

        for kind in range(2):
            self.gather(kind, 3, 0)
        for copy in self.last_copies() + self.keep_copies():
            copy.start()

    def finish(self):
        for copy in self.last_copies():
            copy.wait_recv()
            copy.wait_send()
        for copy in self.keep_copies():
            copy.wait()


def backward_kernel(
    heads,
    planes,
    groups,
    row_in,
    norm_ref,
    dense_in,
    qf_in,
    kf_in,
    qkv_in,
    o_in,
    lse_in,
    hres_in,
    g_all,
    zd_ref,
    zy_ref,
    gu_ref,
    gd_ref,
    small_ref,
    gates_ref,
    out_ref,
    dtok_ref,
    dqkv_out,
    dproj_out,
    ln_out,
    gu_in,
    gd_in,
    dlogit_out,
    dbup_out,
    dbdown_out,
    norm_out,
    gu_land,
    gd_land,
    row_ref,
    dense_ref,
    qf_ref,
    kf_ref,
    qkv_ref,
    o_ref,
    lse_ref,
    hres_ref,
    gm,
    kaug,
    vaug,
    dh,
    db,
    do,
    delta,
    qt,
    dot_t,
    dkt,
    dvt,
    dqkv,
    xn1,
    dw,
    dnorm,
    moved,
    own,
    d_theirs,
    d_deep,
    d_x,
    d_y,
    y_theirs,
    y_deep,
    y_x,
    y_y,
    w_own,
    w_theirs,
    w_deep,
    w_x,
    w_y,
    w_sum,
    w_in,
    small_in,
    small_out,
    norm_part,
    norm_in,
    norm_all,
    n_send,
    n_recv,
    s_send,
    s_recv,
    d_send,
    d_recv,
    y_send,
    y_recv,
    w_send,
    w_recv,
    z_send,
    z_recv,
    gu_stage,
    gd_stage,
    gu_temp,
    gd_temp,
    c_load,
    c_send,
    c_recv,
    c_last,
    loc_sems,
    in_sems,
):
    me, z = lax.axis_index("dp"), lax.axis_index("fsdp")
    core = lax.rem(me, 2)
    chip = me - core
    z_peers = [(me, lax.rem(z + k, planes)) for k in range(1, planes)]
    d_peers = [(lax.rem(me + k, groups), z) for k in range(1, groups)]
    greet(column_peers(planes) + d_peers)
    rows, width = hres_ref.shape
    chunk = row_ref.shape[1]
    head = width // heads
    pair = 2 * head

    gm_load = pltpu.make_async_copy(g_all.at[me], gm, loc_sems.at[4])
    gm_load.start()
    small_sender = Sender(s_send, s_recv)
    small_z = [small_sender.start(small_ref, small_in.at[k], p) for k, p in enumerate(z_peers)]
    d_sender = Sender(d_send, d_recv)
    d_scatter = plane_scatter_steps(
        zd_ref, own, d_theirs, d_deep, d_x, d_y, d_sender, loc_sems, z
    )
    next(d_scatter)
    next(d_scatter)
    pairs = (
        (hres_in, hres_ref),
        (o_in, o_ref),
        (dense_in, dense_ref),
        (row_in, row_ref),
        (qf_in, qf_ref),
        (kf_in, kf_ref),
        (qkv_in, qkv_ref),
        (lse_in, lse_ref),
    )
    fetched = [pltpu.make_async_copy(a, b, in_sems.at[k]) for k, (a, b) in enumerate(pairs)]
    for copy in fetched:
        copy.start()
    chain = GradChain(
        (gu_ref, gd_ref),
        (gu_land, gd_land),
        (gu_in, gd_in),
        (gu_stage, gd_stage),
        (gu_temp, gd_temp),
        (c_load, c_send, c_recv, c_last),
    )
    chain.start()
    for copy in small_z:
        copy.wait_recv()
    small_out[me] = small_ref[...] + jnp.sum(small_in[...], axis=0)
    small_d = [small_sender.start(small_out.at[me], small_out.at[me], p) for p in d_peers]
    y_sender = Sender(y_send, y_recv)
    y_scatter = plane_scatter_steps(
        zy_ref, own, y_theirs, y_deep, y_x, y_y, y_sender, loc_sems, z
    )
    next(y_scatter)
    gm_load.wait()
    for copy in fetched:
        copy.wait()

    next(d_scatter)

    def again(c, carry):
        part = pl.ds(pl.multiple_of(c * chunk, chunk), chunk)
        normal, _ = norm_parts(row_ref[c].astype(F32))
        xn1[part, :] = (normal * norm_ref[0:1, :] + norm_ref[1:2, :]).astype(BF16)
        return carry

    lax.fori_loop(0, planes, again, 0)
    next(d_scatter)
    chain.step(0)
    next(d_scatter)
    dh[...] = next(d_scatter)
    d_sender.drain()
    next(y_scatter)

    lane = lax.broadcasted_iota(jnp.int32, (rows, pair), 1)
    lane_c = lax.broadcasted_iota(jnp.int32, (chunk, pair), 1)
    same = lax.broadcasted_iota(jnp.int32, (width, pair), 0) // head == lax.broadcasted_iota(
        jnp.int32, (width, pair), 1
    )
    ones = jnp.where(same, 1.0, 0.0).astype(BF16)
    dnorm[...] = jnp.zeros_like(dnorm)

    def begin(c, carry):
        part = pl.ds(pl.multiple_of(c * chunk, chunk), chunk)
        normal, scale = norm_parts(hres_ref[part, :])
        grad = dh[part, :]
        dnorm[2] += fold_rows(grad * normal)
        dnorm[3] += fold_rows(grad)
        dh_part = gm[c].astype(F32) + norm_back_parts(grad * norm_ref[2:3, :], normal, scale)
        dh[part, :] = dh_part
        low = dh_part.astype(BF16)
        db[part, :] = low
        do_part = dot_nt(low, dense_ref[:, :, 3 * width : 4 * width].reshape(width, width)).astype(BF16)
        do[part, :] = do_part
        prod = do_part.astype(F32) * o_ref[part, :].astype(F32)
        high = prod.astype(BF16)
        rest = (prod - high.astype(F32)).astype(BF16)
        delta[part, :] = dot_nn(high, ones) + dot_nn(rest, ones)
        return carry

    next(y_scatter)
    lax.fori_loop(0, planes, begin, 0)
    chain.step(1)
    w_rows = w_sum.shape[0]
    w_cols = w_sum.shape[1]
    dw[:, :, 3 * width : 4 * width] = (
        dot_tn(o_ref[...], db[...]).astype(BF16).reshape(groups, w_rows, width)
    )

    mark = (lane >= heads) & (lane < heads + 3)
    kaug[:, pair:] = jnp.where(mark, 1.0, kf_ref[...].astype(F32)).astype(BF16)
    vaug[:, pair:] = jnp.where(mark, 1.0, 0.0).astype(BF16)

    def put_parts(base, values):
        high, middle, low = split3(-values)
        out = jnp.where(lane_c == heads, high.astype(F32), base)
        out = jnp.where(lane_c == heads + 1, middle.astype(F32), out)
        return jnp.where(lane_c == heads + 2, low.astype(F32), out).astype(BF16)

    def one_pair(g):
        cols = slice(g * pair, (g + 1) * pair)
        kaug[:, :pair] = qkv_ref[:, width + g * pair : width + (g + 1) * pair]
        vaug[:, :pair] = qkv_ref[:, 2 * width + g * pair : 2 * width + (g + 1) * pair]
        qt[...] = qkv_ref[:, cols].T
        dot_t[...] = do[:, cols].T
        dkt[...] = jnp.zeros_like(dkt)
        dvt[...] = jnp.zeros_like(dvt)

        def one_chunk(c, inner):
            part = pl.ds(pl.multiple_of(c * chunk, chunk), chunk)
            q_pair, do_pair = qkv_ref[part, cols], do[part, cols]
            lse_all, delta_all = lse_ref[part, :], delta[part, :]
            base = qf_ref[part, :].astype(F32)
            acc = jnp.zeros((chunk, pair), F32)
            none = jnp.zeros_like(q_pair)
            for side in range(2):
                mine = (lane_c // head) == side
                lse = lse_all[:, 2 * g + side : 2 * g + side + 1]
                qa = jnp.concatenate(
                    [jnp.where(mine, q_pair, none), put_parts(base, lse)], axis=1
                )
                pr = jnp.exp(dot_nt(qa, kaug[...]))
                dlt = delta_all[:, 2 * g + side : 2 * g + side + 1]
                da = jnp.concatenate(
                    [jnp.where(mine, do_pair, none), put_parts(jnp.zeros_like(base), dlt)], axis=1
                )
                ds = (pr * dot_nt(da, vaug[...])).astype(BF16)
                acc = jnp.where(mine, dot_nn(ds, kaug[:, :pair]), acc)
                here = slice(side * head, (side + 1) * head)
                dkt[here, :] += dot_nn(qt[here, part], ds)
                dvt[here, :] += dot_nn(dot_t[here, part], pr.astype(BF16))
            dqkv[part, cols] = (acc * 0.125).astype(BF16)
            return inner

        lax.fori_loop(0, planes, one_chunk, 0)
        dqkv[:, width + g * pair : width + (g + 1) * pair] = dkt[...].T.astype(BF16)
        dqkv[:, 2 * width + g * pair : 2 * width + (g + 1) * pair] = dvt[...].T.astype(BF16)

    out_sender = Sender(z_send, z_recv)
    next(y_scatter)
    one_pair(0)
    for copy in small_d:
        copy.wait_recv()
    dgate = jnp.concatenate(
        [
            small_out[2 * (e // 2), e % 2 : e % 2 + 1] + small_out[2 * (e // 2) + 1, e % 2 : e % 2 + 1]
            for e in range(groups)
        ]
    )
    gates = gates_ref[...]
    dlogit_out[...] = gates * (dgate - jnp.sum(gates * dgate, axis=0, keepdims=True))
    up_part, up_rows = dbup_out.shape[1] // 256, gu_ref.shape[3] // 128
    for h in range(2):
        for q in range(up_part):
            at = 2 + core * up_rows + z * up_part + q
            spot = (h * up_part + q) * 128
            dbup_out[:, spot : spot + 128] = small_out[chip + h, pl.ds(at, 1), :]
    dbdown_out[...] = small_out[me, pl.ds(2 + 2 * up_rows + core * (width // 128) + z, 1), :]
    chain.step(2)
    one_pair(1)
    next(y_scatter)
    mixed = hres_ref[...] + next(y_scatter)
    moved[0] = mixed.astype(BF16).reshape(planes, chunk, width)
    out_keep = pltpu.make_async_copy(moved.at[0, z], out_ref.at[z], loc_sems.at[7])
    out_keep.start()
    sent = [out_sender.start(moved.at[0, p[1]], out_ref.at[z], p) for p in z_peers]
    one_pair(2)
    chain.total()
    one_pair(3)

    def finish(c):
        part = pl.ds(pl.multiple_of(c * chunk, chunk), chunk)
        grad = dot_nt(dqkv[part, :], dense_ref[:, :, : 3 * width].reshape(width, 3 * width))
        normal, scale = norm_parts(row_ref[c].astype(F32))
        dnorm[0] += fold_rows(grad * normal)
        dnorm[1] += fold_rows(grad)
        moved[1, c] = (
            dh[part, :] + norm_back_parts(grad * norm_ref[0:1, :], normal, scale)
        ).astype(BF16)

    for k, peer in enumerate(z_peers):
        finish(peer[1])
        sent.append(out_sender.start(moved.at[1, peer[1]], dtok_ref.at[z], peer))
    finish(z)
    tok_keep = pltpu.make_async_copy(moved.at[1, z], dtok_ref.at[z], loc_sems.at[8])
    tok_keep.start()
    for k in range(2):
        total = jnp.sum(dnorm[k], axis=0, keepdims=True)
        for q in range(width // 128):
            row = k * (width // 128) + q
            norm_part[row : row + 1] = total[:, q * 128 : (q + 1) * 128]
    norm_sender = Sender(n_send, n_recv)
    norm_z = [norm_sender.start(norm_part, norm_in.at[k], p) for k, p in enumerate(z_peers)]
    for c in range(3):
        cols = slice(c * width, (c + 1) * width)
        dw[:, :, cols] = (
            dot_tn(xn1[...], dqkv[:, cols]).astype(BF16).reshape(groups, w_rows, width)
        )
    lanes = lax.broadcasted_iota(jnp.int32, (8, width), 0)
    table = jnp.zeros((8, width), F32)
    for k in range(2, 4):
        table = jnp.where(lanes == k, jnp.sum(dnorm[k], axis=0, keepdims=True), table)
    table = jnp.concatenate([table, jnp.zeros((w_cols - 4 * width - 8, width), F32)], axis=0)
    dw[:, :, 4 * width :] = table.T.astype(BF16).reshape(groups, w_rows, w_cols - 4 * width)
    w_sender = Sender(w_send, w_recv)
    w_scatter = plane_scatter_steps(
        dw, w_own, w_theirs, w_deep, w_x, w_y, w_sender, loc_sems, z
    )
    next(w_scatter)
    next(w_scatter)
    for _ in range(3):
        next(w_scatter)
    w_sum[...] = next(w_scatter).astype(BF16)
    shard = dqkv_out.shape[0]
    last = [
        out_sender.start(w_sum.at[pl.ds(p[1] * shard, shard)], w_in.at[k], p)
        for k, p in enumerate(z_peers)
    ]
    for copy in norm_z:
        copy.wait_recv()
    norm_all[me] = norm_part[...] + jnp.sum(norm_in[...], axis=0)
    norm_d = [norm_sender.start(norm_all.at[me], norm_all.at[me], p) for p in d_peers]
    total = w_sum[pl.ds(z * shard, shard)].astype(F32)
    for k, copy in enumerate(last):
        copy.wait_recv()
        total = total + w_in[k].astype(F32)
    dqkv_out[...] = total[:, : 3 * width]
    dproj_out[...] = total[:, 3 * width : 4 * width]
    ln_out[...] = total[:, 4 * width :]
    for copy in norm_d:
        copy.wait_recv()
    norm_out[...] = jnp.sum(norm_all[...], axis=0)
    for copy in sent:
        copy.wait_recv()
    chain.finish()
    out_keep.wait()
    tok_keep.wait()
    for sender in (small_sender, y_sender, w_sender, out_sender, norm_sender):
        sender.drain()


def scatter_scratch(rows, width):
    return [
        pltpu.VMEM((4, rows, width), BF16),
        pltpu.VMEM((2, rows // 2, width), BF16),
        pltpu.VMEM((rows, width), BF16),
        pltpu.VMEM((rows, width), BF16),
    ]


def backward(
    row, norms, dense, qf, kf, qkv, o, lse, hres, g_all, zd, zy, gu, gd, small, gates, heads
):
    planes, piece, width = row.shape
    groups = zd.shape[0]
    rows = planes * piece
    pair = 2 * (width // heads)
    w_rows, w_cols = width // groups, 4 * width + 128
    sd = jax.ShapeDtypeStruct
    dma = pltpu.SemaphoreType.DMA
    return pl.pallas_call(
        functools.partial(backward_kernel, heads, planes, groups),
        out_shape=(
            sd(row.shape, BF16),
            sd(row.shape, BF16),
            sd((w_rows // planes, 3 * width), F32),
            sd((w_rows // planes, width), F32),
            sd((w_rows // planes, 128), F32),
            sd((2,) + gu.shape[2:], BF16),
            sd((2,) + gd.shape[2:], BF16),
            sd((groups, 128), F32),
            sd((1, 2 * gu.shape[3] // planes), F32),
            sd((1, width // planes), F32),
            sd((2 * width // 128, 128), F32),
            sd((5,) + gu.shape[1:], BF16),
            sd((5,) + gd.shape[1:], BF16),
        ),
        in_specs=[any_spec(), vmem_spec()] + [any_spec()] * 12 + [vmem_spec()] * 2,
        out_specs=tuple(
            [any_spec()] * 2
            + [vmem_spec()] * 3
            + [any_spec()] * 2
            + [vmem_spec()] * 4
            + [any_spec()] * 2
        ),
        scratch_shapes=[pltpu.VMEM(a.shape, a.dtype) for a in (row, dense, qf, kf, qkv, o, lse, hres)]
        + [
            pltpu.VMEM(row.shape, BF16),
            pltpu.VMEM((rows, 2 * pair), BF16),
            pltpu.VMEM((rows, 2 * pair), BF16),
            pltpu.VMEM((rows, width), F32),
            pltpu.VMEM((rows, width), BF16),
            pltpu.VMEM((rows, width), BF16),
            pltpu.VMEM((rows, pair), F32),
            pltpu.VMEM((pair, rows), BF16),
            pltpu.VMEM((pair, rows), BF16),
            pltpu.VMEM((pair, rows), F32),
            pltpu.VMEM((pair, rows), F32),
            pltpu.VMEM((rows, 3 * width), BF16),
            pltpu.VMEM((rows, width), BF16),
            pltpu.VMEM((groups, w_rows, w_cols), BF16),
            pltpu.VMEM((4, 8, width), F32),
            pltpu.VMEM((2,) + row.shape, BF16),
            pltpu.VMEM((4, rows, width), BF16),
        ]
        + scatter_scratch(rows, width)
        + scatter_scratch(rows, width)
        + [pltpu.VMEM((4, w_rows, w_cols), BF16)]
        + scatter_scratch(w_rows, w_cols)
        + [
            pltpu.VMEM((w_rows, w_cols), BF16),
            pltpu.VMEM((planes - 1, w_rows // planes, w_cols), BF16),
            pltpu.VMEM((planes - 1,) + small.shape, F32),
            pltpu.VMEM((groups,) + small.shape, F32),
            pltpu.VMEM((2 * width // 128, 128), F32),
            pltpu.VMEM((planes - 1, 2 * width // 128, 128), F32),
            pltpu.VMEM((groups, 2 * width // 128, 128), F32),
            dma((planes + groups,)),
            dma((planes + groups,)),
            dma((planes + groups,)),
            dma((planes + groups,)),
            dma((PLANE_SCATTER_COPIES,)),
            dma((PLANE_SCATTER_COPIES,)),
            dma((PLANE_SCATTER_COPIES,)),
            dma((PLANE_SCATTER_COPIES,)),
            dma((PLANE_SCATTER_COPIES,)),
            dma((PLANE_SCATTER_COPIES,)),
            dma((3 * planes,)),
            dma((3 * planes,)),
            pltpu.VMEM((3,) + gu.shape[1:], BF16),
            pltpu.VMEM((3,) + gd.shape[1:], BF16),
            pltpu.VMEM(gu.shape[1:], BF16),
            pltpu.VMEM(gd.shape[1:], BF16),
            dma((8,)),
            dma((10,)),
            dma((10,)),
            dma((6,)),
            dma((9,)),
            dma((8,)),
        ],
        compiler_params=pltpu.CompilerParams(
            collective_id=4, has_side_effects=True, vmem_limit_bytes=VMEM_MAX
        ),
        cost_estimate=pl.CostEstimate(
            flops=80_000_000_000, bytes_accessed=20_000_000, transcendentals=8_000_000
        ),
        name="attention_backward",
    )(row, norms, dense, qf, kf, qkv, o, lse, hres, g_all, zd, zy, gu, gd, small, gates)


def make_tile_list(marks, list_ref):
    blocks, piece = marks.shape
    per = piece // TILE
    iota = functools.partial(lax.broadcasted_iota, jnp.int32)

    def table(mask):
        return jnp.where(mask, 1.0, 0.0).astype(BF16)

    kept = table(marks >= 0.0)
    folded = dot_nn(kept, table(iota((piece, 128), 0) // TILE == iota((piece, 128), 1)))
    real = iota((blocks, 128), 1) < per
    hit = jnp.where(folded > 0.0, 1.0, 0.0)
    inside = dot_nn(hit.astype(BF16), table(iota((128, 128), 0) < iota((128, 128), 1)))
    totals = jnp.broadcast_to(jnp.sum(hit, axis=1, keepdims=True), (blocks, 128))
    above = dot_nn(table(iota((blocks, blocks), 1) < iota((blocks, blocks), 0)), totals.astype(BF16))
    count = jnp.sum(hit)
    rank = inside + above
    index = iota((blocks, 128), 0) * per + iota((blocks, 128), 1)
    place = jnp.where(hit > 0.0, rank, count + index.astype(F32) - rank)
    place = jnp.where(real, place, 0.0).astype(jnp.int32)
    tiles = blocks * per
    row = iota((tiles, 128), 0)
    spread = table(iota((tiles, blocks), 0) // per == iota((tiles, blocks), 1))
    mine = lax.rem(row, per) == iota((tiles, 128), 1)
    digits = []
    for digit in (place // per, lax.rem(place, per)):
        full = dot_nn(spread, digit.astype(F32).astype(BF16))
        digits.append(jnp.sum(jnp.where(mine, full, 0.0), axis=1, keepdims=True).astype(jnp.int32))
    to_row = table(digits[0] == iota((tiles, blocks), 1))
    to_column = digits[1] == iota((tiles, 128), 1)
    found = jnp.zeros((blocks, 128), F32)
    for value, scale in ((row // per, per), (lax.rem(row, per), 1)):
        part = jnp.where(to_column, value.astype(F32), 0.0).astype(BF16)
        found = found + scale * dot_tn(to_row, part)
    found = jnp.where(iota((blocks, 128), 1) == per, count, found)
    list_ref[...] = found.astype(jnp.int32)


def expert_kernel(
    marks_ref,
    gates_ref,
    codes_ref,
    own_ref,
    x_ref,
    g_ref,
    up_ref,
    down_ref,
    zd_ref,
    zy_ref,
    gu_ref,
    gd_ref,
    small_ref,
    dbup_ref,
    dbdown_ref,
    dgate_ref,
    xs,
    gs,
    zds,
    zys,
    up,
    down,
    acc_up,
    acc_down,
    xb,
    gb,
    mb,
    dyb,
    xt,
    dyt,
    yacc,
    xacc,
    meta,
    bup,
    bdown,
    list_vmem,
    list_ref,
    list_sem,
    sems,
    upt,
    downt,
    row_sems,
):
    me = lax.axis_index("dp")
    groups, rows, width = x_ref.shape
    hidden = up.shape[2]
    planes = gu_ref.shape[0]
    tiles = BLOCK // TILE
    copies = []

    def load(src, dst):
        copy = pltpu.make_async_copy(src, dst, sems.at[len(copies)])
        copy.start()
        copies.append(copy)

    load(up_ref, up)
    load(down_ref, down)

    def x_copy(source):
        return pltpu.make_async_copy(x_ref.at[source], xs.at[source], row_sems.at[source])

    def g_copy(source):
        return pltpu.make_async_copy(
            g_ref.at[source], gs.at[source], row_sems.at[groups + source]
        )

    for source in range(groups):

        @pl.when(me == source)
        def _():
            pltpu.make_async_copy(own_ref, xs.at[source], row_sems.at[source]).start()

        @pl.when(me != source)
        def _():
            x_copy(source).start()

        g_copy(source).start()

    def wait_rows(source, carry):
        x_copy(source).wait()
        g_copy(source).wait()
        return carry

    def zd_copy(source):
        part = pl.ds(pl.multiple_of(source * rows, rows), rows)
        return pltpu.make_async_copy(
            zds.at[part], zd_ref.at[part], row_sems.at[2 * groups + source]
        )

    def zy_copy(source):
        part = pl.ds(pl.multiple_of(source * rows, rows), rows)
        return pltpu.make_async_copy(
            zys.at[part], zy_ref.at[part], row_sems.at[3 * groups + source]
        )

    def save_rows(source, carry):
        zd_copy(source).start()
        zy_copy(source).start()
        return carry

    def wipe(k, carry):
        part = pl.ds(pl.multiple_of(k * BLOCK, BLOCK), BLOCK)
        zds[part, :] = jnp.zeros((BLOCK, width), BF16)
        zys[part, :] = jnp.zeros((BLOCK, width), BF16)
        return carry

    lax.fori_loop(0, groups * rows // BLOCK, wipe, 0)
    dbup_ref[...] = jnp.zeros_like(dbup_ref)
    dbdown_ref[...] = jnp.zeros_like(dbdown_ref)
    dgate_ref[...] = jnp.zeros_like(dgate_ref)
    core = lax.rem(me, 2)
    piece = marks_ref.shape[2]
    blocks = marks_ref.shape[1]
    lane = lax.broadcasted_iota(jnp.int32, (piece, 128), 1)
    turned = [marks_ref[e].T for e in range(2)]
    for k in range(blocks):
        meta[k * piece : (k + 1) * piece, :] = jnp.where(
            lane == 0, turned[0][:, k : k + 1], turned[1][:, k : k + 1]
        )
    for e in range(2):
        for p in range(planes):
            for q in range(2):
                at = p * (hidden // planes) + q * 128
                bup[e, :, at : at + 128] = codes_ref[
                    me - core + e, p, pl.ds(BIAS_UP + 2 * core + q, 1), :
                ]
            bdown[e, :, p * 128 : (p + 1) * 128] = jnp.where(
                core == 0, codes_ref[me - core + e, p, BIAS_DOWN : BIAS_DOWN + 1, :], 0.0
            )
        make_tile_list(marks_ref[e], list_vmem.at[e])
    list_copy = pltpu.make_async_copy(list_vmem, list_ref, list_sem)
    list_copy.start()
    list_copy.wait()
    for copy in copies:
        copy.wait()

    def spot(index):
        return pl.ds(pl.multiple_of(index * TILE, TILE), TILE)

    saves = []

    def save(src, dst):
        copy = pltpu.make_async_copy(src, dst, sems.at[len(copies) + len(saves)])
        copy.start()
        saves.append(copy)

    per_row = rows // TILE

    def entry(e, position):
        return list_ref[e, lax.div(position, 16), lax.rem(position, 16)]

    def one_expert(e, state):
        acc_up[...] = jnp.zeros_like(acc_up)
        acc_down[...] = jnp.zeros_like(acc_down)
        upt[...] = up[e].T
        downt[...] = down[e].T
        n_tiles = list_ref[e, 0, 16]
        n_blocks = lax.div(n_tiles + (tiles - 1), tiles)
        gate_row = gates_ref[pl.ds(me - core + e, 1), :]
        lane_b = lax.broadcasted_iota(jnp.int32, (BLOCK, 128), 1).astype(F32)

        def one_block(b, state):
            ready, saved = state
            end = (b + 1) * tiles
            need = lax.div(
                jnp.maximum(entry(e, jnp.minimum(end, n_tiles) - 1), entry(e, end - 1)), per_row
            )
            lax.fori_loop(ready, need + 1, wait_rows, 0)
            ready = jnp.maximum(ready, need + 1)

            def fetch(k, inner):
                index = list_ref[e, b * (tiles // 16) + lax.div(k, 16), lax.rem(k, 16)]
                src, part = lax.div(index, per_row), spot(lax.rem(index, per_row))
                dst = spot(k)
                xb[dst, :] = xs[src, part, :]
                gb[dst, :] = gs[src, part, :]
                mb[dst, :] = meta[spot(index), :]
                return inner

            lax.fori_loop(0, tiles, fetch, 0, unroll=True)
            hot = lane_b == mb[:, e : e + 1]
            gate = jnp.sum(jnp.where(hot, gate_row, 0.0), axis=1, keepdims=True)
            dyb_new = (gb[...].astype(F32) * gate).astype(BF16)
            dyb[...] = dyb_new
            xt[...] = xb[...].T
            dyt[...] = dyb_new.T
            dbdown_ref[e] += fold_rows(dyb_new.astype(F32))

            parts = []
            for k in range(2):
                rows_k = slice(k * BLOCK // 2, (k + 1) * BLOCK // 2)
                u = dot_nn(xb[rows_k, :], up[e]) + bup[e]
                sq = u * u
                th = jnp.tanh(u * (0.7978845608028654 + 0.035677408136300125 * sq))
                half = 0.5 + 0.5 * th
                slope = half + u * (
                    (0.5 - 0.5 * th * th) * (0.7978845608028654 + 0.10703222440890037 * sq)
                )
                a = (u * half).astype(BF16)
                du = (dot_nn(dyb[rows_k, :], downt[...]) * slope).astype(BF16)
                parts.append((a, du))
            a = jnp.concatenate([p[0] for p in parts], axis=0)
            du = jnp.concatenate([p[1] for p in parts], axis=0)
            y = dot_nn(a, down[e]) + bdown[e]
            x_new = dot_nn(du, upt[...])
            acc_up[...] += dot_nn(xt[...], du)
            acc_down[...] += dot_nn(dyt[...], a)
            dbup_ref[e] += fold_rows(du.astype(F32))
            inner_prod = jnp.sum(y * gb[...].astype(F32), axis=-1, keepdims=True)
            dgate_ref[e] += fold_rows(jnp.where(hot, inner_prod, 0.0))
            gb[...] = (y * gate).astype(BF16)
            xb[...] = x_new.astype(BF16)

            def store(k, inner):
                real = b * tiles + k < n_tiles
                dst = spot(jnp.where(real, entry(e, b * tiles + k), groups * per_row))
                src = spot(k)
                if e == 0:
                    zds[dst, :] = xb[src, :]
                    zys[dst, :] = gb[src, :]
                else:
                    zds[dst, :] = (zds[dst, :].astype(F32) + xb[src, :].astype(F32)).astype(BF16)
                    zys[dst, :] = (zys[dst, :].astype(F32) + gb[src, :].astype(F32)).astype(BF16)
                return inner

            lax.fori_loop(0, tiles, store, 0, unroll=True)
            if e == 1:
                upto = lax.div(entry(e, jnp.minimum(end, groups * per_row - 1)), per_row)
                upto = jnp.where(end < n_tiles, upto, saved)
                lax.fori_loop(saved, upto, save_rows, 0)
                saved = jnp.maximum(saved, upto)
            return ready, saved

        state = lax.fori_loop(0, n_blocks, one_block, state)
        up[e] = acc_up[...].astype(BF16)
        for k in range(hidden // FCHUNK):
            cols = slice(k * FCHUNK, (k + 1) * FCHUNK)
            down[e, cols, :] = acc_down[:, cols].T.astype(BF16)
        up_rows, down_rows = width // planes, hidden // planes
        for k in range(planes):
            save(up.at[e, pl.ds(k * up_rows, up_rows)], gu_ref.at[k, e])
            save(down.at[e, pl.ds(k * down_rows, down_rows)], gd_ref.at[k, e])
        return state

    state = one_expert(0, (jnp.int32(0), jnp.int32(0)))
    ready, saved = one_expert(1, state)
    lax.fori_loop(saved, groups, save_rows, 0)
    lax.fori_loop(ready, groups, wait_rows, 0)
    small_ref[...] = jnp.zeros_like(small_ref)
    up_rows, down_rows = hidden // 128, width // 128
    for e in range(2):
        small_ref[e : e + 1] = jnp.sum(dgate_ref[e], axis=0, keepdims=True)
        for at, acc, count in (
            (2 + e * up_rows, dbup_ref, up_rows),
            (2 + 2 * up_rows + e * down_rows, dbdown_ref, down_rows),
        ):
            sums = jnp.sum(acc[e], axis=0, keepdims=True)
            for k in range(count):
                small_ref[at + k : at + k + 1] = sums[:, k * 128 : (k + 1) * 128]
    for copy in saves:
        copy.wait()
    for source in range(groups):
        zd_copy(source).wait()
        zy_copy(source).wait()


def experts(marks, gates, codes, x_own, x_all, g_all, up, down):
    groups, rows, width = x_all.shape
    hidden = up.shape[2]
    planes = 4
    total = groups * rows
    sd = jax.ShapeDtypeStruct
    return pl.pallas_call(
        expert_kernel,
        out_shape=(
            sd((total, width), BF16),
            sd((total, width), BF16),
            sd((planes, 2, width // planes, hidden), BF16),
            sd((planes, 2, hidden // planes, width), BF16),
            sd((-(-(2 + 2 * (hidden + width) // 128) // 8) * 8, 128), F32),
        ),
        in_specs=[vmem_spec()] * 3 + [any_spec()] * 5,
        out_specs=tuple([any_spec()] * 4 + [vmem_spec()]),
        scratch_shapes=[
            pltpu.VMEM((2, 8, hidden), F32),
            pltpu.VMEM((2, 8, width), F32),
            pltpu.VMEM((2, 8, 128), F32),
            pltpu.VMEM((groups, rows, width), BF16),
            pltpu.VMEM((groups, rows, width), BF16),
            pltpu.VMEM((total + TILE, width), BF16),
            pltpu.VMEM((total + TILE, width), BF16),
            pltpu.VMEM((2, width, hidden), BF16),
            pltpu.VMEM((2, hidden, width), BF16),
            pltpu.VMEM((width, hidden), F32),
            pltpu.VMEM((width, hidden), F32),
            pltpu.VMEM((BLOCK, width), BF16),
            pltpu.VMEM((BLOCK, width), BF16),
            pltpu.VMEM((BLOCK, 128), F32),
            pltpu.VMEM((BLOCK, width), BF16),
            pltpu.VMEM((width, BLOCK), BF16),
            pltpu.VMEM((width, BLOCK), BF16),
            pltpu.VMEM((BLOCK, width), F32),
            pltpu.VMEM((BLOCK, width), F32),
            pltpu.VMEM((total, 128), F32),
            pltpu.VMEM((2, 1, hidden), F32),
            pltpu.VMEM((2, 1, width), F32),
            pltpu.VMEM((2, marks.shape[1], 128), jnp.int32),
            pltpu.SMEM((2, marks.shape[1], 128), jnp.int32),
            pltpu.SemaphoreType.DMA,
            pltpu.SemaphoreType.DMA((40,)),
            pltpu.VMEM((hidden, width), BF16),
            pltpu.VMEM((width, hidden), BF16),
            pltpu.SemaphoreType.DMA((4 * groups,)),
        ],
        compiler_params=pltpu.CompilerParams(vmem_limit_bytes=VMEM_MAX),
        cost_estimate=pl.CostEstimate(
            flops=60_000_000_000, bytes_accessed=40_000_000, transcendentals=8_000_000
        ),
        name="experts",
    )(marks, gates, codes, x_own, x_all, g_all, up, down)


def fast_shards(
    mesh_sizes,
    tokens,
    out_grad,
    segment_ids,
    key_mask,
    sent_task,
    task_experts,
    ln1_gain,
    ln1_bias,
    w_qkv,
    w_proj,
    ln2_gain,
    ln2_bias,
    task_embed,
    w_gate,
    w_up,
    b_up,
    w_down,
    b_down,
):
    groups, planes = mesh_sizes
    row_count, piece, width = tokens.shape
    length = piece * planes
    total = groups * length
    tasks = task_experts.shape[0]
    n_experts = w_gate.shape[1]
    hidden = w_up.shape[2]
    capacity = 4 * row_count * piece // n_experts
    me, z = lax.axis_index("dp"), lax.axis_index("fsdp")

    core = me % 2
    half = hidden // 2
    shard_norms = jnp.concatenate([ln1_gain, ln1_bias, ln2_gain, ln2_bias]).astype(F32)
    shard_norms = jnp.pad(shard_norms, (0, 128 - shard_norms.shape[0])).reshape(1, 128)
    logits_part = jnp.dot(task_embed, w_gate, preferred_element_type=F32)
    routing = (segment_ids, key_mask, logits_part, shard_norms, b_up, b_down)
    (
        codes,
        marks,
        gates_rows,
        order,
        norms,
        qf,
        kf,
        row,
        dense_full,
        qkv,
        o,
        lse,
        hres,
        xn2,
        x_all,
        g_all,
        up_all,
        down_all,
    ) = forward(
        sent_task,
        task_experts,
        routing,
        tokens,
        out_grad,
        w_qkv,
        w_proj,
        w_up,
        w_down,
        HEADS,
        groups,
        capacity,
    )
    zd, zy, gu, gd, small = experts(
        marks,
        gates_rows,
        codes,
        xn2.reshape(length, width),
        x_all.reshape(groups, length, width),
        g_all.reshape(groups, length, width),
        up_all.reshape(2, width, half),
        down_all.reshape(2, half, width),
    )
    (
        out_pieces,
        tok_pieces,
        d_w_qkv,
        d_w_proj,
        d_ln2,
        gu_in,
        gd_in,
        dlogits,
        d_b_up,
        d_b_down,
        norm_sums,
        _,
        _,
    ) = backward(
        row,
        norms,
        dense_full,
        qf,
        kf,
        qkv,
        o,
        lse,
        hres,
        g_all,
        zd.reshape(groups, length, width),
        zy.reshape(groups, length, width),
        gu,
        gd,
        small,
        gates_rows,
        HEADS,
    )
    d_w_up = gu_in.astype(F32).reshape(2, -1, planes, half // planes)
    d_w_up = d_w_up.transpose(1, 2, 0, 3).reshape(-1, hidden)
    d_w_down = gd_in.astype(F32).reshape(-1, width)
    output, d_tokens = pick_rows(order, (out_pieces, tok_pieces), (BF16, F32))

    features = width // (groups * planes)
    d_ln1 = lax.dynamic_slice_in_dim(
        norm_sums.reshape(2, width), (me * planes + z) * features, features, 1
    )

    dlogits = dlogits[:, :tasks]
    d_task_embed = jnp.dot(dlogits.T, w_gate.astype(F32).T, precision=exact)
    d_w_gate = jnp.dot(task_embed.astype(F32).T, dlogits.T, precision=exact)
    return (
        output,
        d_tokens,
        d_ln1[0],
        d_ln1[1],
        d_w_qkv,
        d_w_proj,
        d_ln2[:, 2],
        d_ln2[:, 3],
        d_task_embed,
        d_w_gate,
        d_w_up[None],
        d_b_up,
        d_w_down[None],
        d_b_down,
    )


def fits_rows(mesh, tokens, w_gate):
    groups, planes = mesh.shape["dp"], mesh.shape["fsdp"]
    return (
        groups == 8
        and planes == 4
        and tokens.shape[1] == planes * 256
        and tokens.shape[0] == groups * planes
        and w_gate.shape[1] == groups
        and tokens.shape[1] % (planes * QCHUNK) == 0
    )


def solution(mesh):
    placed = (
        P("dp", "fsdp", None),
        P("dp", "fsdp", None),
        P("dp", "fsdp"),
        P("dp", "fsdp"),
        P("dp", None),
        P(),
        P(("dp", "fsdp")),
        P(("dp", "fsdp")),
        P(("dp", "fsdp"), None),
        P(("dp", "fsdp"), None),
        P(("dp", "fsdp")),
        P(("dp", "fsdp")),
        P(None, ("dp", "fsdp")),
        P(("dp", "fsdp"), None),
        P("dp", "fsdp", None),
        P("dp", "fsdp"),
        P("dp", "fsdp", None),
        P("dp", "fsdp"),
    )
    placed_out = (
        P("dp", "fsdp", None),
        P("dp", "fsdp", None),
        P(("dp", "fsdp")),
        P(("dp", "fsdp")),
        P(("dp", "fsdp"), None),
        P(("dp", "fsdp"), None),
        P(("dp", "fsdp")),
        P(("dp", "fsdp")),
        P(None, ("dp", "fsdp")),
        P(("dp", "fsdp"), None),
        P("dp", "fsdp", None),
        P("dp", "fsdp"),
        P("dp", "fsdp", None),
        P("dp", "fsdp"),
    )

    def program(*args):
        fast = fits_rows(mesh, args[0], args[13])
        sizes = (mesh.shape["dp"], mesh.shape["fsdp"])
        return jax.shard_map(
            functools.partial(fast_shards, sizes) if fast else shards,
            mesh=mesh,
            in_specs=placed,
            out_specs=placed_out,
            check_vma=False,
        )(*args)

    return program
```

```python
import functools

import jax
import jax.numpy as jnp
from jax import lax
from jax.experimental import pallas as pl
from jax.experimental.pallas import tpu as pltpu
from jax.sharding import PartitionSpec as P

HEADS = 8
HD = 64


exact = lax.Precision.HIGHEST


def layer_norm(values_in, gain_vec, shift_vec):
    centre = values_in - jnp.mean(values_in, axis=-1, keepdims=True)
    spread = jnp.mean(centre * centre, axis=-1, keepdims=True)
    return centre * lax.rsqrt(spread + 1e-05) * gain_vec + shift_vec


def allow_table(query_codes, key_codes):
    query_int = query_codes.astype(jnp.int32)
    key_int = key_codes.astype(jnp.int32)
    same_sentence = (query_int // 2)[:, :, None] == (key_int // 2)[:, None, :]
    return same_sentence & ((key_int % 2)[:, None, :] == 1)


def row_scores(query_row, key_row, allow_row):
    scores = (
        jnp.einsum("qhd,khd->hqk", query_row, key_row, preferred_element_type=jnp.float32) * 0.125
    )
    return jnp.where(allow_row[None], scores, -1000000000.0)


def attend_forward(queries, key_heads, value_heads, allowed):

    def one_row(parts):
        query_row, key_row, value_row, allow_row = parts
        scores = row_scores(query_row, key_row, allow_row)
        biggest = jnp.max(scores, axis=-1, keepdims=True)
        weights = jnp.exp(scores - biggest)
        row_total = jnp.sum(weights, axis=-1, keepdims=True)
        weights_low = (weights / row_total).astype(jnp.bfloat16)
        mixed_row = jnp.einsum(
            "hqk,khd->qhd", weights_low, value_row, preferred_element_type=jnp.float32
        )
        return (mixed_row.astype(jnp.bfloat16), (biggest + jnp.log(row_total))[..., 0])

    return lax.map(one_row, (queries, key_heads, value_heads, allowed))


def attend_backward(queries, key_heads, value_heads, allowed, logsum, grad_out):

    def one_row(parts):
        query_row, key_row, value_row, allow_row, logsum_row, grad_row = parts
        scores = row_scores(query_row, key_row, allow_row)
        weights = jnp.exp(scores - logsum_row[..., None])
        grad_weights = jnp.einsum(
            "qhd,khd->hqk", grad_row, value_row, preferred_element_type=jnp.float32
        )
        inner = jnp.sum(weights * grad_weights, axis=-1, keepdims=True)
        grad_scores = (weights * (grad_weights - inner)).astype(jnp.bfloat16)
        grad_query = (
            jnp.einsum("hqk,khd->qhd", grad_scores, key_row, preferred_element_type=jnp.float32)
            * 0.125
        )
        grad_key = (
            jnp.einsum("hqk,qhd->khd", grad_scores, query_row, preferred_element_type=jnp.float32)
            * 0.125
        )
        grad_value = jnp.einsum(
            "hqk,qhd->khd",
            weights.astype(jnp.bfloat16),
            grad_row,
            preferred_element_type=jnp.float32,
        )
        return (grad_query, grad_key, grad_value)

    return lax.map(one_row, (queries, key_heads, value_heads, allowed, logsum, grad_out))


def shards(
    tokens,
    out_grad,
    segment_ids,
    key_mask,
    sent_task,
    task_experts,
    ln1_gain,
    ln1_bias,
    w_qkv,
    w_proj,
    ln2_gain,
    ln2_bias,
    task_embed,
    w_gate,
    w_up,
    b_up,
    w_down,
    b_down,
):
    row_count, piece_len, model_width = tokens.shape
    tok_count = row_count * piece_len
    gain_one, bias_one, qkv_full, proj_full, gain_two, bias_two, embed_full, router_full = (
        lax.all_gather(ln1_gain, ("dp", "fsdp"), axis=0, tiled=True),
        lax.all_gather(ln1_bias, ("dp", "fsdp"), axis=0, tiled=True),
        lax.all_gather(w_qkv, ("dp", "fsdp"), axis=0, tiled=True),
        lax.all_gather(w_proj, ("dp", "fsdp"), axis=0, tiled=True),
        lax.all_gather(ln2_gain, ("dp", "fsdp"), axis=0, tiled=True),
        lax.all_gather(ln2_bias, ("dp", "fsdp"), axis=0, tiled=True),
        lax.all_gather(task_embed, ("dp", "fsdp"), axis=1, tiled=True),
        lax.all_gather(w_gate, ("dp", "fsdp"), axis=0, tiled=True),
    )
    up_full, up_bias, down_full, down_bias = (
        lax.all_gather(w_up, "fsdp", axis=1, tiled=True),
        lax.all_gather(b_up, "fsdp", axis=1, tiled=True),
        lax.all_gather(w_down, "fsdp", axis=1, tiled=True),
        lax.all_gather(b_down, "fsdp", axis=1, tiled=True),
    )
    up_full = up_full[0]
    down_full = down_full[0]
    up_bias_f = up_bias[0].astype(jnp.float32)
    down_bias_f = down_bias[0].astype(jnp.float32)
    experts_count = router_full.shape[1]
    task_count = embed_full.shape[0]
    capacity = 4 * tok_count // experts_count
    inputs = tokens.astype(jnp.float32).reshape(tok_count, model_width)
    normed, norm_back = jax.vjp(
        layer_norm, inputs, gain_one.astype(jnp.float32), bias_one.astype(jnp.float32)
    )
    normed_low = normed.astype(jnp.bfloat16)
    projected = jnp.dot(normed_low, qkv_full, preferred_element_type=jnp.float32).astype(
        jnp.bfloat16
    )
    projected = projected.reshape(row_count, piece_len, 3, HEADS, HD)
    queries = projected[:, :, 0]
    key_heads = projected[:, :, 1]
    value_heads = projected[:, :, 2]
    row_codes = (2 * segment_ids + key_mask).astype(jnp.bfloat16)
    keys_all, values_all, codes_all = (
        lax.all_gather(key_heads, "fsdp", axis=1, tiled=True),
        lax.all_gather(value_heads, "fsdp", axis=1, tiled=True),
        lax.all_gather(row_codes, "fsdp", axis=1, tiled=True),
    )
    allowed = allow_table(row_codes, codes_all)
    attended, logsum = attend_forward(queries, keys_all, values_all, allowed)
    attended_flat = attended.reshape(tok_count, model_width)
    hidden = inputs + jnp.dot(attended_flat, proj_full, preferred_element_type=jnp.float32)
    normed_two, norm_two_back = jax.vjp(
        layer_norm, hidden, gain_two.astype(jnp.float32), bias_two.astype(jnp.float32)
    )
    normed_two_low = normed_two.astype(jnp.bfloat16)
    choose = (task_experts[:, :, None] == jnp.arange(experts_count)[None, None, :]).astype(
        jnp.float32
    )

    def gate_values(embed_in, router_in):
        logits = jnp.einsum(
            "te,tke->tk", jnp.dot(embed_in, router_in, precision=exact), choose, precision=exact
        )
        return jax.nn.softmax(logits, axis=-1)

    gate_probs, gate_back = jax.vjp(
        gate_values, embed_full.astype(jnp.float32), router_full.astype(jnp.float32)
    )
    segment_hot = (segment_ids[:, :, None] == jnp.arange(sent_task.shape[1])[None, None, :]).astype(
        jnp.int32
    )
    task_tok = jnp.sum(segment_hot * sent_task[:, None, :], axis=-1).reshape(tok_count)
    task_hot = (task_tok[:, None] == jnp.arange(task_count)[None, :]).astype(jnp.float32)
    gate_tok = jnp.dot(task_hot, gate_probs, precision=exact)
    expert_tok = jnp.sum(task_hot.astype(jnp.int32)[:, :, None] * task_experts[None], axis=1)
    copy_expert = expert_tok.T.reshape(-1)
    one_hot = (copy_expert[:, None] == jnp.arange(experts_count)[None, :]).astype(jnp.int32)
    rank = jnp.sum((jnp.cumsum(one_hot, axis=0) - one_hot) * one_hot, axis=-1)
    kept_copy = rank < capacity
    slot_index = jnp.where(kept_copy, copy_expert * capacity + rank, experts_count * capacity)
    send_rows = (
        jnp.zeros((experts_count * capacity + 1, model_width), jnp.bfloat16)
        .at[slot_index]
        .set(jnp.tile(normed_two_low, (2, 1)))
    )
    send_rows = send_rows[:-1].reshape(experts_count, capacity, model_width)
    received = lax.all_to_all(send_rows, "dp", split_axis=0, concat_axis=0, tiled=True)
    slot_total = received.shape[0] * received.shape[1]
    block_rows = min(512, slot_total)
    block_count = slot_total // block_rows
    slot_blocks = received.reshape(block_count, block_rows, model_width)

    def expert_forward(slot_rows):
        pre_act = jnp.dot(slot_rows, up_full, preferred_element_type=jnp.float32) + up_bias_f
        activated = jax.nn.gelu(pre_act, approximate=True).astype(jnp.bfloat16)
        return (
            jnp.dot(activated, down_full, preferred_element_type=jnp.float32) + down_bias_f
        ).astype(jnp.bfloat16)

    produced = lax.map(expert_forward, slot_blocks).reshape(received.shape)
    returned = lax.all_to_all(produced, "dp", split_axis=0, concat_axis=0, tiled=True)
    return_pad = jnp.concatenate(
        [returned.reshape(-1, model_width), jnp.zeros((1, model_width), jnp.bfloat16)], axis=0
    )
    copies = jnp.take(return_pad, slot_index, axis=0).reshape(2, tok_count, model_width)
    kept_float = kept_copy.reshape(2, tok_count).astype(jnp.float32)
    copy_weight = gate_tok.T * kept_float
    mixed_rows = (
        hidden
        + copy_weight[0][:, None] * copies[0].astype(jnp.float32)
        + copy_weight[1][:, None] * copies[1].astype(jnp.float32)
    )
    output = mixed_rows.astype(jnp.bfloat16).reshape(tokens.shape)
    grad_mixed = out_grad.astype(jnp.float32).reshape(tok_count, model_width)
    grad_copies = (copy_weight[:, :, None] * grad_mixed[None]).astype(jnp.bfloat16)
    grad_gate_copy = jnp.sum(copies.astype(jnp.float32) * grad_mixed[None], axis=-1) * kept_float
    grad_send = (
        jnp.zeros((experts_count * capacity + 1, model_width), jnp.bfloat16)
        .at[slot_index]
        .set(grad_copies.reshape(-1, model_width))
    )
    grad_send = grad_send[:-1].reshape(experts_count, capacity, model_width)
    grad_received = lax.all_to_all(grad_send, "dp", split_axis=0, concat_axis=0, tiled=True)

    def expert_backward(totals, parts):
        slot_rows, grad_rows = parts
        pre_act = jnp.dot(slot_rows, up_full, preferred_element_type=jnp.float32) + up_bias_f
        activated, gelu_back = jax.vjp(
            lambda values_in: jax.nn.gelu(values_in, approximate=True), pre_act
        )
        activated_low = activated.astype(jnp.bfloat16)
        grad_act = jnp.dot(grad_rows, down_full.T, preferred_element_type=jnp.float32)
        grad_pre = gelu_back(grad_act)[0].astype(jnp.bfloat16)
        grad_inputs_slot = jnp.dot(grad_pre, up_full.T, preferred_element_type=jnp.float32).astype(
            jnp.bfloat16
        )
        totals = (
            totals[0] + jnp.dot(slot_rows.T, grad_pre, preferred_element_type=jnp.float32),
            totals[1] + jnp.sum(grad_pre.astype(jnp.float32), axis=0),
            totals[2] + jnp.dot(activated_low.T, grad_rows, preferred_element_type=jnp.float32),
            totals[3] + jnp.sum(grad_rows.astype(jnp.float32), axis=0),
        )
        return (totals, grad_inputs_slot)

    start_totals = (
        jnp.zeros(up_full.shape, jnp.float32),
        jnp.zeros(up_bias_f.shape, jnp.float32),
        jnp.zeros(down_full.shape, jnp.float32),
        jnp.zeros(down_bias_f.shape, jnp.float32),
    )
    totals, grad_slots = lax.scan(
        expert_backward,
        start_totals,
        (slot_blocks, grad_received.reshape(block_count, block_rows, model_width)),
    )
    grad_back = lax.all_to_all(
        grad_slots.reshape(received.shape), "dp", split_axis=0, concat_axis=0, tiled=True
    )
    grad_pad = jnp.concatenate(
        [grad_back.reshape(-1, model_width), jnp.zeros((1, model_width), jnp.bfloat16)], axis=0
    )
    grad_taken = (
        jnp.take(grad_pad, slot_index, axis=0)
        .reshape(2, tok_count, model_width)
        .astype(jnp.float32)
    )
    grad_normed_two = grad_taken[0] + grad_taken[1]
    grad_up, grad_up_bias, grad_down, grad_down_bias = (
        lax.psum_scatter(
            totals[0][None].astype(jnp.bfloat16), "fsdp", scatter_dimension=1, tiled=True
        ).astype(jnp.float32),
        lax.psum_scatter(
            totals[1][None].astype(jnp.bfloat16), "fsdp", scatter_dimension=1, tiled=True
        ).astype(jnp.float32),
        lax.psum_scatter(
            totals[2][None].astype(jnp.bfloat16), "fsdp", scatter_dimension=1, tiled=True
        ).astype(jnp.float32),
        lax.psum_scatter(
            totals[3][None].astype(jnp.bfloat16), "fsdp", scatter_dimension=1, tiled=True
        ).astype(jnp.float32),
    )
    grad_hidden_part, grad_gain_two, grad_bias_two = norm_two_back(grad_normed_two)
    grad_hidden = grad_mixed + grad_hidden_part
    grad_branch = grad_hidden.astype(jnp.bfloat16)
    grad_proj = jnp.dot(attended_flat.T, grad_branch, preferred_element_type=jnp.float32)
    grad_attended = jnp.dot(grad_branch, proj_full.T, preferred_element_type=jnp.float32).astype(
        jnp.bfloat16
    )
    grad_attended = grad_attended.reshape(row_count, piece_len, HEADS, HD)
    part_query, part_key, part_value = attend_backward(
        queries, keys_all, values_all, allowed, logsum, grad_attended
    )
    summed_key, summed_value = (
        lax.psum_scatter(
            part_key.astype(jnp.bfloat16), "fsdp", scatter_dimension=1, tiled=True
        ).astype(jnp.float32),
        lax.psum_scatter(
            part_value.astype(jnp.bfloat16), "fsdp", scatter_dimension=1, tiled=True
        ).astype(jnp.float32),
    )
    grad_query = part_query.astype(jnp.bfloat16)
    grad_key = summed_key.astype(jnp.bfloat16)
    grad_value = summed_value.astype(jnp.bfloat16)
    grad_projected = jnp.stack([grad_query, grad_key, grad_value], axis=2).reshape(
        tok_count, 3 * model_width
    )
    grad_qkv_weight = jnp.dot(normed_low.T, grad_projected, preferred_element_type=jnp.float32)
    grad_normed = jnp.dot(grad_projected, qkv_full.T, preferred_element_type=jnp.float32)
    grad_inputs, grad_gain_one, grad_bias_one = norm_back(grad_normed)
    grad_tokens = (grad_hidden + grad_inputs).reshape(tokens.shape)
    grad_gate_task = jnp.dot(task_hot.T, grad_gate_copy.T, precision=exact)
    grad_embed, grad_router = gate_back(grad_gate_task)
    reduced = (
        lax.psum_scatter(grad_gain_one, ("dp", "fsdp"), scatter_dimension=0, tiled=True),
        lax.psum_scatter(grad_bias_one, ("dp", "fsdp"), scatter_dimension=0, tiled=True),
        lax.psum_scatter(grad_qkv_weight, ("dp", "fsdp"), scatter_dimension=0, tiled=True),
        lax.psum_scatter(grad_proj, ("dp", "fsdp"), scatter_dimension=0, tiled=True),
        lax.psum_scatter(grad_gain_two, ("dp", "fsdp"), scatter_dimension=0, tiled=True),
        lax.psum_scatter(grad_bias_two, ("dp", "fsdp"), scatter_dimension=0, tiled=True),
        lax.psum_scatter(grad_embed, ("dp", "fsdp"), scatter_dimension=1, tiled=True),
        lax.psum_scatter(grad_router, ("dp", "fsdp"), scatter_dimension=0, tiled=True),
    )
    return (
        output,
        grad_tokens,
        reduced[0],
        reduced[1],
        reduced[2],
        reduced[3],
        reduced[4],
        reduced[5],
        reduced[6],
        reduced[7],
        grad_up,
        grad_up_bias,
        grad_down,
        grad_down_bias,
    )


MESH_ID = pl.DeviceIdType.MESH
VMEM_MAX = 62 * 1024 * 1024
TILE = 16
BLOCK = 512
FCHUNK = 1024
QCHUNK = 256
FAR = -float(2**30)
F32 = jnp.float32
BF16 = jnp.bfloat16


def dot_nn(lhs, rhs):
    return lax.dot_general(lhs, rhs, (((1,), (0,)), ((), ())), preferred_element_type=F32)


def dot_nt(lhs, rhs):
    return lax.dot_general(lhs, rhs, (((1,), (1,)), ((), ())), preferred_element_type=F32)


def dot_tn(lhs, rhs):
    return lax.dot_general(lhs, rhs, (((0,), (0,)), ((), ())), preferred_element_type=F32)


def vmem_spec():
    return pl.BlockSpec(memory_space=pltpu.VMEM)


def any_spec():
    return pl.BlockSpec(memory_space=pl.ANY)


def smem_spec():
    return pl.BlockSpec(memory_space=pltpu.SMEM)


def norm_parts(values):
    centre = values - jnp.mean(values, axis=-1, keepdims=True)
    spread = jnp.mean(centre * centre, axis=-1, keepdims=True)
    scale = lax.rsqrt(spread + 1e-05)
    return centre * scale, scale


def norm_back_parts(grad, normal, scale):
    mean_grad = jnp.mean(grad, axis=-1, keepdims=True)
    mean_prod = jnp.mean(grad * normal, axis=-1, keepdims=True)
    return (grad - mean_grad - normal * mean_prod) * scale


def fold_rows(values):
    rows, width = values.shape
    return jnp.sum(values.reshape(rows // 8, 8, width), axis=0)


def plane_ids():
    me = lax.axis_index("dp")
    core, xpos, ypos = lax.rem(me, 2), lax.rem(me // 2, 2), me // 4

    def at(ypos, xpos, core):
        return (ypos * 2 + xpos) * 2 + core

    return me, core, xpos, ypos, at


def greet(peers):
    barrier = pltpu.get_barrier_semaphore()
    for peer in peers:
        pl.semaphore_signal(barrier, inc=1, device_id=peer, device_id_type=MESH_ID)
    pl.semaphore_wait(barrier, len(peers))


class Sender:
    def __init__(self, send_sems, recv_sems):
        self.send_sems, self.recv_sems, self.count, self.all = send_sems, recv_sems, 0, []

    def start(self, src, dst, peer):
        copy = pltpu.make_async_remote_copy(
            src_ref=src,
            dst_ref=dst,
            send_sem=self.send_sems.at[self.count],
            recv_sem=self.recv_sems.at[self.count],
            device_id=peer,
            device_id_type=MESH_ID,
        )
        copy.start()
        self.count += 1
        self.all.append(copy)
        return copy

    def drain(self):
        for copy in self.all:
            copy.wait_send()


def plane_gather_steps(block, own, rows, sender, z):
    me, core, xpos, ypos, at = plane_ids()
    sib, xn, yn = at(ypos, xpos, 1 - core), at(ypos, 1 - xpos, core), at(1 - ypos, xpos, core)
    diag = at(1 - ypos, 1 - xpos, core)
    half = rows // 2

    def part(i, k):
        return block(i).at[pl.ds(k * half, half)]

    def send(i, k, peer):
        src = own.at[pl.ds(k * half, half)] if i is me else part(i, k)
        return sender.start(src, part(i, k), (peer, z))

    x_own = [send(me, 0, xn)]
    y_own = [send(me, 1, yn)]
    x_own.append(send(me, 1, xn))
    y_own.insert(0, send(me, 0, yn))
    last = [send(me, 0, sib), send(me, 1, sib)]
    x_own[0].wait_recv()
    to_y = send(xn, 0, yn)
    y_own[1].wait_recv()
    to_x = send(yn, 1, xn)
    last.append(send(xn, 0, sib))
    last.append(send(yn, 1, sib))
    x_own[1].wait_recv()
    last.append(send(xn, 1, sib))
    y_own[0].wait_recv()
    last.append(send(yn, 0, sib))
    to_y.wait_recv()
    last.append(send(diag, 0, sib))
    to_x.wait_recv()
    last.append(send(diag, 1, sib))
    for copy in last:
        copy.wait_recv()


PLANE_GATHER_COPIES = 14


def plane_peers(z):
    me, core, xpos, ypos, at = plane_ids()
    return [
        (at(ypos, xpos, 1 - core), z),
        (at(ypos, 1 - xpos, core), z),
        (at(1 - ypos, xpos, core), z),
    ]


def column_peers(planes):
    me, z = lax.axis_index("dp"), lax.axis_index("fsdp")
    peers = [(me, lax.rem(z + k, planes)) for k in range(1, planes)]
    return peers + [(me ^ 1, lax.rem(z + k, planes)) for k in range(1, planes)]


class PlaneGather:
    COPIES = 28

    def __init__(self, block, own, send_sems, recv_sems):
        me, core, xpos, ypos, at = plane_ids()
        self.z = lax.axis_index("fsdp")
        self.me = me
        self.sib = at(ypos, xpos, 1 - core)
        self.xn, self.yn = at(ypos, 1 - xpos, core), at(1 - ypos, xpos, core)
        self.diag = at(1 - ypos, 1 - xpos, core)
        self.block, self.own = block, own
        self.send_sems, self.recv_sems = send_sems, recv_sems
        self.all = {}

    def send(self, kind, c, src, owner, peer):
        copy = pltpu.make_async_remote_copy(
            src_ref=src,
            dst_ref=self.block(owner).at[c],
            send_sem=self.send_sems.at[kind * 4 + c],
            recv_sem=self.recv_sems.at[kind * 4 + c],
            device_id=(peer, self.z),
            device_id_type=MESH_ID,
        )
        copy.start()
        self.all[kind, c] = copy

    def start(self, c):
        src = self.own.at[c]
        self.send(0, c, src, self.me, self.xn)
        self.send(1, c, src, self.me, self.yn)
        self.send(2, c, src, self.me, self.sib)

    def pass_on(self, c):
        x_part, y_part = self.block(self.xn).at[c], self.block(self.yn).at[c]
        self.all[0, c].wait_recv()
        if c % 2 == 0:
            self.send(3, c, x_part, self.xn, self.yn)
        self.send(4, c, x_part, self.xn, self.sib)
        self.all[1, c].wait_recv()
        if c % 2 == 1:
            self.send(3, c, y_part, self.yn, self.xn)
        self.send(5, c, y_part, self.yn, self.sib)

    def pass_diag(self, c):
        self.all[3, c].wait_recv()
        self.send(6, c, self.block(self.diag).at[c], self.diag, self.sib)

    def finish(self):
        for kind in (2, 4, 5, 6):
            for c in range(4):
                self.all[kind, c].wait_recv()
        for copy in self.all.values():
            copy.wait_send()


def plane_scatter_steps(z_ref, own, theirs, deep, near_x, near_y, sender, loc_sems, z):
    me, core, xpos, ypos, at = plane_ids()
    sib, xn, yn = at(ypos, xpos, 1 - core), at(ypos, 1 - xpos, core), at(1 - ypos, xpos, core)
    chips = [(ypos, xpos), (ypos, 1 - xpos), (1 - ypos, xpos), (1 - ypos, 1 - xpos)]
    rows = z_ref.shape[1]
    half = rows // 2
    first, second = pl.ds(0, half), pl.ds(half, half)
    loads, trades = {}, {}
    for slot in (3, 1, 2, 0):
        pos = chips[slot]
        trades[slot] = sender.start(
            z_ref.at[at(pos[0], pos[1], 1 - core)], theirs.at[slot], (sib, z)
        )

    yield
    for slot in (3, 1, 2, 0):
        pos = chips[slot]
        loads[slot] = pltpu.make_async_copy(
            z_ref.at[at(pos[0], pos[1], core)], own.at[slot], loc_sems.at[slot]
        )
        loads[slot].start()
    yield

    def add(slot, part):
        own[slot, part] = (
            own[slot, part].astype(F32) + theirs[slot, part].astype(F32)
        ).astype(own.dtype)

    loads[3].wait()
    trades[3].wait_recv()
    add(3, first)
    deep_x = sender.start(own.at[3, first], deep.at[0], (xn, z))
    add(3, second)
    deep_y = sender.start(own.at[3, second], deep.at[1], (yn, z))
    loads[1].wait()
    trades[1].wait_recv()
    add(1, first)
    x_first = sender.start(own.at[1, first], near_x.at[first], (xn, z))
    loads[2].wait()
    trades[2].wait_recv()
    add(2, second)
    y_second = sender.start(own.at[2, second], near_y.at[second], (yn, z))
    add(1, second)
    add(2, first)
    yield
    deep_y.wait_recv()
    own[1, second] = (own[1, second].astype(F32) + deep[1].astype(F32)).astype(own.dtype)
    x_second = sender.start(own.at[1, second], near_x.at[second], (xn, z))
    deep_x.wait_recv()
    own[2, first] = (own[2, first].astype(F32) + deep[0].astype(F32)).astype(own.dtype)
    y_first = sender.start(own.at[2, first], near_y.at[first], (yn, z))
    yield
    loads[0].wait()
    trades[0].wait_recv()
    yield
    mine = own[0].astype(F32) + theirs[0].astype(F32)
    x_first.wait_recv()
    y_second.wait_recv()
    x_second.wait_recv()
    y_first.wait_recv()
    yield mine + near_x[...].astype(F32) + near_y[...].astype(F32)


PLANE_SCATTER_COPIES = 10


def pick_rows_kernel(order_ref, *refs):
    count = len(refs) // 2
    for a in range(count):
        for r in range(refs[a].shape[0]):
            refs[count + a][r] = refs[a][order_ref[0, r]].astype(refs[count + a].dtype)


def pick_rows(order, arrays, kinds):
    return pl.pallas_call(
        pick_rows_kernel,
        out_shape=tuple(
            jax.ShapeDtypeStruct(array.shape, kind) for array, kind in zip(arrays, kinds)
        ),
        in_specs=[smem_spec()] + [vmem_spec()] * len(arrays),
        out_specs=tuple(vmem_spec() for _ in arrays),
        compiler_params=pltpu.CompilerParams(vmem_limit_bytes=VMEM_MAX),
        name="row_order",
    )(order, *arrays)


PAYLOAD = 48
CODE_LOW, CODE_HIGH, BIAS_UP, BIAS_DOWN, NORMS, LOGITS = 0, 4, 8, 12, 13, 16


def make_payload(payload, sent_ref, seg_ref, key_ref, logit_ref, norm_ref, bup_ref, bdown_ref):
    seg = seg_ref[...]
    row_count, piece = seg.shape
    row = lax.broadcasted_iota(jnp.int32, seg.shape, 0)
    task = jnp.zeros_like(seg)
    for r in range(row_count):
        for k in range(sent_ref.shape[1]):
            task = jnp.where((row == r) & (seg == k), sent_ref[r, k], task)
    code = (task * 16 + seg * 2 + key_ref[...]).astype(F32)
    payload[...] = jnp.zeros_like(payload)
    payload[CODE_LOW : CODE_LOW + row_count] = code[:, : piece // 2]
    payload[CODE_HIGH : CODE_HIGH + row_count] = code[:, piece // 2 :]
    for k in range(bup_ref.shape[1] // 128):
        payload[BIAS_UP + k : BIAS_UP + k + 1] = bup_ref[:, k * 128 : (k + 1) * 128].astype(F32)
    payload[BIAS_DOWN : BIAS_DOWN + 1] = bdown_ref[...].astype(F32)
    payload[NORMS : NORMS + 1] = norm_ref[...]
    tasks, n_experts = logit_ref.shape
    payload[LOGITS : LOGITS + tasks, :n_experts] = logit_ref[...]


def code_segment(code):
    return lax.shift_right_logical(code.astype(jnp.int32), 1) & 7


def row_order(codes_ref, me, planes):
    single = jnp.int32(0)
    for r in reversed(range(planes)):
        first = jnp.max(code_segment(codes_ref[me, 0, CODE_LOW + r : CODE_LOW + r + 1, :1]))
        last = jnp.max(
            code_segment(codes_ref[me, planes - 1, CODE_HIGH + r : CODE_HIGH + r + 1, 127:])
        )
        single = jnp.where(first == last, r, single)
    target = lax.rem(me, planes)
    return [
        jnp.where(p == target, single, jnp.where(p == single, target, p)) for p in range(planes)
    ]


def row_features(codes_ref, me, order, z, planes, qf_ref, kf_ref, order_ref):
    mine = order[0]
    for p in range(1, planes):
        mine = jnp.where(z == p, order[p], mine)
    parts = []
    for p in range(planes):
        low, high = codes_ref[me, p, CODE_LOW : CODE_LOW + 4], codes_ref[me, p, CODE_HIGH : CODE_HIGH + 4]
        row = lax.broadcasted_iota(jnp.int32, low.shape, 0)
        for half in (low, high):
            parts.append(jnp.sum(jnp.where(row == mine, half, 0.0), axis=0, keepdims=True))
    columns = jnp.concatenate(parts, axis=0).T
    lane = lax.broadcasted_iota(jnp.int32, (128, qf_ref.shape[1]), 1)
    for k in range(2 * planes):
        code = columns[:, k : k + 1].astype(jnp.int32)
        hot = (lax.shift_right_logical(code, 1) & 7) == lane
        part = slice(k * 128, (k + 1) * 128)
        qf_ref[part, :] = jnp.where(hot, 1.0, 0.0).astype(BF16)
        seen = hot & ((code & 1) == 1)
        kf_ref[part, :] = jnp.where((lane < 8) & jnp.logical_not(seen), FAR, 0.0).astype(BF16)
    spot = lax.broadcasted_iota(jnp.int32, order_ref.shape, 1)
    table = jnp.zeros(order_ref.shape, jnp.int32)
    for p in range(planes):
        table = jnp.where(spot == p, order[p], table)
    order_ref[...] = table


def gather_norms(codes_ref, norm_ref):
    devices = codes_ref.shape[0] * codes_ref.shape[1]
    width = norm_ref.shape[1]
    size = width // devices
    shards = codes_ref[:, :, NORMS : NORMS + 1, :].reshape(devices, 128).astype(BF16)
    lane = lax.broadcasted_iota(jnp.int32, (128, width), 0)
    column = lax.broadcasted_iota(jnp.int32, (128, width), 1)
    owner = lax.broadcasted_iota(jnp.int32, (devices, width), 0)
    owned = lax.broadcasted_iota(jnp.int32, (devices, width), 1) // size
    for k in range(4):
        place = jnp.where(lane == k * size + lax.rem(column, size), 1.0, 0.0).astype(BF16)
        full = jnp.where(owner == owned, dot_nn(shards, place), 0.0)
        norm_ref[k : k + 1] = jnp.sum(full, axis=0, keepdims=True)


def routing_marks(codes_ref, te_ref, marks_ref, gates_ref, me, z, planes, capacity):
    groups = codes_ref.shape[0]
    tasks = te_ref.shape[0]
    count = groups * planes * planes
    low = codes_ref[:, :, CODE_LOW : CODE_LOW + planes, :].reshape(count, 128)
    high = codes_ref[:, :, CODE_HIGH : CODE_HIGH + planes, :].reshape(count, 128)
    code = jnp.concatenate([low, high], axis=1).astype(jnp.int32)
    piece = code.shape[1]
    task = lax.shift_right_logical(code, 4)
    one = lax.broadcasted_iota(jnp.int32, (count, count), 0)
    two = lax.broadcasted_iota(jnp.int32, (count, count), 1)
    block_one, block_two = one // planes, two // planes
    row_one, row_two = lax.rem(one, planes), lax.rem(two, planes)

    def table(mask):
        return jnp.where(mask, 1.0, 0.0).astype(BF16)

    whole = table(block_one == block_two)
    ahead_rows = table((block_one == block_two) & (row_two < row_one))
    group_one, group_two = block_one // planes, block_two // planes
    plane_two = lax.rem(block_two, planes)
    same_row = (group_one == group_two) & (row_one == row_two)

    def wide(column):
        return jnp.broadcast_to(column, (count, 128)).astype(BF16)

    seg = lax.shift_right_logical(code, 1) & 7
    first = dot_nn(table(same_row & (plane_two == 0)), wide(seg[:, :1].astype(F32)))
    last = dot_nn(
        table(same_row & (plane_two == planes - 1)), wide(seg[:, piece - 1 :].astype(F32))
    )
    lone = jnp.where(first == last, 1.0, 0.0)
    lone = jnp.where(dot_nn(ahead_rows, lone.astype(BF16)) == 0.0, lone, 0.0)
    row = lax.rem(lax.broadcasted_iota(jnp.int32, (count, 128), 0), planes)
    group = lax.broadcasted_iota(jnp.int32, (count, 128), 0) // (planes * planes)
    single = dot_nn(whole, (lone * row.astype(F32)).astype(BF16)).astype(jnp.int32)
    target = lax.rem(group, planes)
    picked = jnp.where(z == target, single, jnp.where(z == single, target, z))
    here = jnp.where(row == picked, 1.0, 0.0)[:, :1]

    before_table = table(
        lax.broadcasted_iota(jnp.int32, (piece, piece), 0)
        < lax.broadcasted_iota(jnp.int32, (piece, piece), 1)
    )
    gather = table(
        lax.broadcasted_iota(jnp.int32, (count // planes, count), 0)
        == lax.broadcasted_iota(jnp.int32, (count // planes, count), 1) // planes
    )
    chip = me - lax.rem(me, 2)
    for e in range(2):
        hits = []
        for j in range(2):
            bits = jnp.int32(0)
            for t in range(tasks):
                bit = (1 << t) if t < 31 else -(1 << 31)
                bits = bits | jnp.where(te_ref[t, j] == chip + e, jnp.int32(bit), jnp.int32(0))
            hits.append((lax.shift_right_logical(jnp.full(task.shape, bits), task) & 1).astype(F32))
        kept = jnp.zeros(task.shape, F32)
        base = jnp.zeros((count, 128), F32)
        for j in range(2):
            total = wide(jnp.sum(hits[j], axis=1, keepdims=True))
            rank = dot_nn(hits[j].astype(BF16), before_table)
            rank = rank + (base + dot_nn(ahead_rows, total))[:, :1]
            kept = kept + jnp.where(rank < capacity, hits[j], 0.0)
            base = base + dot_nn(whole, total)
        mark = kept * here * (task + 1).astype(F32)
        marks_ref[e] = dot_nn(gather, mark.astype(BF16)) - 1.0

    logits = jnp.sum(
        codes_ref[:, :, LOGITS : LOGITS + tasks, :].reshape(groups * planes, tasks, 128), axis=0
    )
    lane = lax.broadcasted_iota(jnp.int32, (tasks, 128), 1)
    task_row = lax.broadcasted_iota(jnp.int32, (tasks, 128), 0)
    hot = []
    for j in range(2):
        chosen = jnp.zeros((tasks, 128), jnp.int32)
        for t in range(tasks):
            chosen = jnp.where(task_row == t, te_ref[t, j], chosen)
        hot.append(lane == chosen)
    level = [jnp.sum(jnp.where(h, logits, 0.0), axis=1, keepdims=True) for h in hot]
    top = jnp.maximum(level[0], level[1])
    weight = [jnp.exp(v - top) for v in level]
    both = weight[0] + weight[1]
    grid = jnp.zeros((tasks, 128), F32)
    for j in range(2):
        grid = jnp.where(hot[j], weight[j] / both, grid)
    grid = jnp.concatenate([grid, jnp.zeros((128 - tasks, 128), F32)], axis=0)
    gates_ref[...] = grid.T[:groups]


def unit_copy(src, dst, send_sem, recv_sem, peer):
    return pltpu.make_async_remote_copy(
        src_ref=src,
        dst_ref=dst,
        send_sem=send_sem,
        recv_sem=recv_sem,
        device_id=peer,
        device_id_type=MESH_ID,
    )


class WeightSpread:
    def __init__(self, up_ref, down_ref, up_all, down_all, sems):
        self.me, self.z = lax.axis_index("dp"), lax.axis_index("fsdp")
        self.core = lax.rem(self.me, 2)
        self.src = (up_ref, down_ref)
        self.dst = (up_all, down_all)
        self.own_send, self.pass_send, self.recv, self.local = sems
        self.side = self.z // 2
        self.near = self.z ^ 1
        self.far = 2 - self.side
        self.inner = (self.z == 1) | (self.z == 2)

    def targets(self):
        chip = self.me - self.core
        return [
            (self.core, self.near),
            (self.core, self.far),
            (1 - self.core, self.near),
            (1 - self.core, self.far),
            (1 - self.core, self.z),
        ], chip

    def copy(self, kind, src, m, p, send_sem, peer):
        return unit_copy(
            src,
            self.dst[kind].at[m, p],
            send_sem,
            self.recv.at[kind * 8 + m * 4 + p],
            peer,
        )

    def own(self):
        targets, chip = self.targets()
        out = []
        for kind in range(2):
            for k, (h, p) in enumerate(targets):
                out.append(
                    self.copy(
                        kind,
                        self.src[kind].at[h],
                        self.core,
                        self.z,
                        self.own_send.at[kind * 5 + k],
                        (chip + h, p),
                    )
                )
        return out

    def mine(self):
        return [
            pltpu.make_async_copy(
                self.src[kind].at[self.core],
                self.dst[kind].at[self.core, self.z],
                self.local.at[kind],
            )
            for kind in range(2)
        ]

    def passed(self, j):
        p = 2 * (1 - self.side) + j
        return [
            self.copy(
                kind,
                self.dst[kind].at[m, p],
                m,
                p,
                self.pass_send.at[kind * 4 + m * 2 + j],
                (self.me, self.near),
            )
            for kind in range(2)
            for m in range(2)
        ]

    def start(self, kind):
        self.mine()[kind].start()
        copies = self.own()[5 * kind : 5 * kind + 5]
        for k, copy in enumerate(copies):
            if k not in (1, 3):
                copy.start()

        @pl.when(self.inner)
        def _():
            for k, copy in enumerate(copies):
                if k in (1, 3):
                    copy.start()

    def start_far(self, kind):
        @pl.when(jnp.logical_not(self.inner))
        def _():
            for k, copy in enumerate(self.own()):
                if k in (5 * kind + 1, 5 * kind + 3):
                    copy.start()

    def pass_on(self, first, kind):
        for side in range(2):

            @pl.when((self.z == 1 + side))
            def _():
                j = side if first else 1 - side
                for copy in self.passed(j)[2 * kind : 2 * kind + 2]:
                    copy.wait_recv()
                    copy.start()

    def finish(self):
        for copy in self.mine():
            copy.wait()
        for copy in self.own():
            copy.wait_send()

        def arrived(kind, m, p):
            self.copy(
                kind, self.dst[kind].at[m, p], m, p, self.own_send.at[0], (self.me, self.near)
            ).wait_recv()

        for kind in range(2):
            arrived(kind, 1 - self.core, self.z)
            for m in range(2):
                arrived(kind, m, self.near)

        @pl.when(self.inner)
        def _():
            for j in range(2):
                for copy in self.passed(j):
                    copy.wait_send()

        @pl.when(jnp.logical_not(self.inner))
        def _():
            for kind in range(2):
                for m in range(2):
                    for j in range(2):
                        arrived(kind, m, 2 * (1 - self.side) + j)


def forward_kernel(
    heads,
    planes,
    capacity,
    sent_ref,
    te_ref,
    seg_ref,
    key_ref,
    logit_ref,
    shard_norms,
    bup_ref,
    bdown_ref,
    tok_ref,
    gm_ref,
    wqkv_ref,
    wproj_ref,
    upw_in,
    downw_in,
    codes_ref,
    marks_ref,
    gates_ref,
    order_ref,
    norm_ref,
    qf_ref,
    kf_ref,
    row_out,
    dense_out,
    qkv_out,
    o_out,
    lse_out,
    hres_out,
    xn2_ref,
    x_all,
    g_all,
    up_all,
    down_all,
    row_ref,
    dense_ref,
    qkv_ref,
    o_ref,
    lse_ref,
    hres_ref,
    kaug,
    vaug,
    w_ref,
    upw_ref,
    downw_ref,
    payload,
    tok_out,
    gm_out,
    p_send,
    p_recv,
    z_send,
    z_recv,
    w_send,
    w_recv,
    x_send,
    x_recv,
    g_send,
    g_recv,
    u_own,
    u_pass,
    u_recv,
    loc_sems,
    out_sems,
    in_sems,
):
    me, z = lax.axis_index("dp"), lax.axis_index("fsdp")
    z_peers = [(me, lax.rem(z + k, planes)) for k in range(1, planes)]
    groups = codes_ref.shape[0]
    d_peers = [(lax.rem(me + k, groups), z) for k in range(1, groups)]
    width = row_ref.shape[2]
    stages = [
        pltpu.make_async_copy(wqkv_ref, w_ref.at[:, pl.ds(0, 3 * width)], in_sems.at[0]),
        pltpu.make_async_copy(wproj_ref, w_ref.at[:, pl.ds(3 * width, width)], in_sems.at[1]),
        pltpu.make_async_copy(downw_in.at[0], downw_ref, in_sems.at[2]),
    ]
    part = upw_ref.shape[2] // planes
    for p in range(planes):
        for h in range(2):
            stages.append(
                pltpu.make_async_copy(
                    upw_in.at[0, :, pl.ds((2 * p + h) * part, part)],
                    upw_ref.at[h, :, pl.ds(p * part, part)],
                    in_sems.at[len(stages)],
                )
            )
    for copy in stages:
        copy.start()
    make_payload(payload, sent_ref, seg_ref, key_ref, logit_ref, shard_norms, bup_ref, bdown_ref)
    codes_ref[me, z] = payload[...]
    greet(column_peers(planes) + d_peers)
    rows = qkv_ref.shape[0]
    chunk = row_ref.shape[1]
    head = width // heads
    pair = 2 * head
    shard = w_ref.shape[0]
    sender = Sender(z_send, z_recv)
    p_sender = Sender(p_send, p_recv)
    codes_z = [p_sender.start(payload, codes_ref.at[me, z], peer) for peer in z_peers]
    for copy in stages:
        copy.wait()
    dense_own = pltpu.make_async_copy(
        w_ref, dense_ref.at[me, pl.ds(z * shard, shard)], loc_sems.at[0]
    )
    dense_own.start()
    dense_z = [
        sender.start(w_ref, dense_ref.at[me, pl.ds(z * shard, shard)], peer) for peer in z_peers
    ]
    spread = WeightSpread(
        upw_ref, downw_ref, up_all, down_all, (u_own, u_pass, u_recv, loc_sems.at[pl.ds(3, 2)])
    )
    spread.start(0)
    for copy in codes_z:
        copy.wait_recv()
    order = row_order(codes_ref, me, planes)
    for c in range(planes):
        tok_out[c] = tok_ref[order[c]]
    toks = [sender.start(tok_out.at[peer[1]], row_ref.at[z], peer) for peer in z_peers]
    tok_own = pltpu.make_async_copy(tok_out.at[z], row_ref.at[z], loc_sems.at[1])
    tok_own.start()
    for c in range(planes):
        gm_out[c] = gm_ref[order[c]]
    gm_own = pltpu.make_async_copy(gm_out.at[z], g_all.at[me, z], loc_sems.at[2])
    gm_own.start()
    codes_d = [p_sender.start(codes_ref.at[me], codes_ref.at[me], peer) for peer in d_peers]
    dense_own.wait()
    for copy in dense_z:
        copy.wait_recv()
    dense_sender = Sender(w_send, w_recv)
    plane_gather_steps(
        lambda i: dense_ref.at[i], dense_ref.at[me], planes * shard, dense_sender, z
    )
    row_features(codes_ref, me, order, z, planes, qf_ref, kf_ref, order_ref)
    for copy in codes_d:
        copy.wait_recv()
    gather_norms(codes_ref, norm_ref)
    routing_marks(codes_ref, te_ref, marks_ref, gates_ref, me, z, planes, capacity)
    x_gather = PlaneGather(lambda i: x_all.at[i], xn2_ref, x_send, x_recv)
    g_gather = PlaneGather(lambda i: g_all.at[i], g_all.at[me], g_send, g_recv)

    for copy in toks:
        copy.wait_recv()
    tok_own.wait()
    gms = [sender.start(gm_out.at[peer[1]], g_all.at[me, z], peer) for peer in z_peers]

    lane = lax.broadcasted_iota(jnp.int32, (rows, pair), 1)
    lane_c = lax.broadcasted_iota(jnp.int32, (chunk, pair), 1)

    def project(c, carry):
        part = pl.ds(pl.multiple_of(c * chunk, chunk), chunk)
        normal, _ = norm_parts(row_ref[c].astype(F32))
        xn1 = (normal * norm_ref[0:1, :] + norm_ref[1:2, :]).astype(BF16)
        out = dot_nn(xn1, dense_ref[:, :, : 3 * width].reshape(width, 3 * width))
        qkv_ref[part, :width] = (out[:, :width] * 0.125).astype(BF16)
        qkv_ref[part, width:] = out[:, width:].astype(BF16)
        return carry

    lax.fori_loop(0, planes, project, 0)

    def prepare(g, carry):
        k_pair = qkv_ref[:, pl.ds(pl.multiple_of(width + g * pair, pair), pair)]
        v_pair = qkv_ref[:, pl.ds(pl.multiple_of(2 * width + g * pair, pair), pair)]
        zero = jnp.zeros_like(k_pair)
        for side in range(2):
            mine = (lane // head) == side
            kaug[g, side, :, :pair] = jnp.where(mine, k_pair, zero)
            vaug[g, side, :, :pair] = jnp.where(mine, v_pair, zero)
            kaug[g, side, :, pair:] = kf_ref[...]
            vaug[g, side, :, pair:] = jnp.where(mine, 1.0, 0.0).astype(BF16)
        return carry

    lax.fori_loop(0, heads // 2, prepare, 0)

    def attend(c):
        part = pl.ds(c * chunk, chunk)

        def one_pair(g, carry):
            cols = pl.ds(pl.multiple_of(g * pair, pair), pair)
            qa = jnp.concatenate([qkv_ref[part, cols], qf_ref[part, :]], axis=1)
            acc = jnp.zeros((chunk, 2 * pair), F32)
            tops = []
            for side in range(2):
                s = dot_nt(qa, kaug[g, side])
                top = jnp.max(s, axis=-1, keepdims=True)
                acc = acc + dot_nn(jnp.exp(s - top).astype(BF16), vaug[g, side])
                tops.append(top)
            total = acc[:, pair:]
            o_ref[part, cols] = (acc[:, :pair] / total).astype(BF16)
            table = lse_ref[part, :]
            for side in range(2):
                level = tops[side] + jnp.log(total[:, side * head : side * head + 1])
                table = jnp.where(lane_c == 2 * g + side, level, table)
            lse_ref[part, :] = table
            return carry

        lax.fori_loop(0, heads // 2, one_pair, 0)
        w_proj = dense_ref[:, :, 3 * width : 4 * width].reshape(width, width)
        hres = row_ref[c].astype(F32) + dot_nn(o_ref[part, :], w_proj)
        hres_ref[part, :] = hres
        normal, _ = norm_parts(hres)
        xn2_ref[c] = (normal * norm_ref[2:3, :] + norm_ref[3:4, :]).astype(BF16)
        x_gather.start(c)

    attend(0)
    attend(1)
    for copy in gms:
        copy.wait_recv()
    gm_own.wait()
    spread.start(1)
    spread.pass_on(True, 0)
    for c in range(4):
        g_gather.start(c)
    attend(2)
    x_gather.pass_on(0)
    x_gather.pass_on(1)
    spread.start_far(0)
    attend(3)
    spread.start_far(1)
    spread.pass_on(True, 1)
    pairs = (
        (row_ref, row_out),
        (dense_ref, dense_out),
        (qkv_ref, qkv_out),
        (o_ref, o_out),
        (lse_ref, lse_out),
        (hres_ref, hres_out),
    )
    saves = [pltpu.make_async_copy(a, b, out_sems.at[k]) for k, (a, b) in enumerate(pairs)]
    for copy in saves:
        copy.start()
    x_gather.pass_on(2)
    g_gather.pass_on(0)
    g_gather.pass_on(1)
    spread.pass_on(False, 0)
    x_gather.pass_on(3)
    g_gather.pass_on(2)
    spread.pass_on(False, 1)
    g_gather.pass_on(3)
    for c in range(4):
        x_gather.pass_diag(c)
        g_gather.pass_diag(c)
    for copy in saves:
        copy.wait()
    x_gather.finish()
    g_gather.finish()
    spread.finish()
    for sender in (p_sender, sender, dense_sender):
        sender.drain()


def forward(
    sent_task, task_experts, routing, tokens, grads, w_qkv, w_proj, up, down, heads, groups, capacity
):
    planes, piece, width = tokens.shape
    rows = planes * piece
    half = up.shape[2] // 2
    dense = jax.ShapeDtypeStruct((w_qkv.shape[0], 4 * width), BF16)
    up_half = (2, up.shape[1], half)
    down_half = (2, down.shape[1] // 2, width)
    pair = 2 * (width // heads)
    sd = jax.ShapeDtypeStruct
    dma = pltpu.SemaphoreType.DMA
    return pl.pallas_call(
        functools.partial(forward_kernel, heads, planes, capacity),
        out_shape=(
            sd((groups, planes, PAYLOAD, 128), F32),
            sd((2, groups * planes, piece), F32),
            sd((groups, 128), F32),
            sd((8, 128), jnp.int32),
            sd((8, width), F32),
            sd((rows, pair), BF16),
            sd((rows, pair), BF16),
            sd(tokens.shape, BF16),
            sd((groups, planes * dense.shape[0], dense.shape[1]), BF16),
            sd((rows, 3 * width), BF16),
            sd((rows, width), BF16),
            sd((rows, pair), F32),
            sd((rows, width), F32),
            sd(tokens.shape, BF16),
            sd((groups,) + tokens.shape, BF16),
            sd((groups,) + tokens.shape, BF16),
            sd((2, planes) + up_half[1:], BF16),
            sd((2, planes) + down_half[1:], BF16),
        ),
        in_specs=[smem_spec()] * 2
        + [vmem_spec()] * (len(routing) + 2)
        + [any_spec()] * 4,
        out_specs=tuple(
            [vmem_spec()] * 7 + [any_spec()] * 6 + [vmem_spec()] + [any_spec()] * 4
        ),
        scratch_shapes=[
            pltpu.VMEM(tokens.shape, BF16),
            pltpu.VMEM((groups, planes * dense.shape[0], dense.shape[1]), BF16),
            pltpu.VMEM((rows, 3 * width), BF16),
            pltpu.VMEM((rows, width), BF16),
            pltpu.VMEM((rows, pair), F32),
            pltpu.VMEM((rows, width), F32),
            pltpu.VMEM((heads // 2, 2, rows, 2 * pair), BF16),
            pltpu.VMEM((heads // 2, 2, rows, 2 * pair), BF16),
            pltpu.VMEM(dense.shape, BF16),
            pltpu.VMEM(up_half, BF16),
            pltpu.VMEM(down_half, BF16),
            pltpu.VMEM((PAYLOAD, 128), F32),
            pltpu.VMEM(tokens.shape, BF16),
            pltpu.VMEM(tokens.shape, BF16),
            dma((planes + groups,)),
            dma((planes + groups,)),
            dma((3 * planes,)),
            dma((3 * planes,)),
            dma((PLANE_GATHER_COPIES,)),
            dma((PLANE_GATHER_COPIES,)),
            dma((PlaneGather.COPIES,)),
            dma((PlaneGather.COPIES,)),
            dma((PlaneGather.COPIES,)),
            dma((PlaneGather.COPIES,)),
            dma((10,)),
            dma((8,)),
            dma((16,)),
            dma((5,)),
            dma((6,)),
            dma((3 + 2 * planes,)),
        ],
        compiler_params=pltpu.CompilerParams(
            collective_id=2, has_side_effects=True, vmem_limit_bytes=VMEM_MAX
        ),
        cost_estimate=pl.CostEstimate(
            flops=40_000_000_000, bytes_accessed=10_000_000, transcendentals=8_000_000
        ),
        name="attention_forward",
    )(
        sent_task,
        task_experts,
        *routing,
        tokens,
        grads,
        w_qkv,
        w_proj,
        up,
        down.reshape((1,) + down_half),
    )


def split3(values):
    high = values.astype(BF16)
    rest = values - high.astype(F32)
    middle = rest.astype(BF16)
    low = (rest - middle.astype(F32)).astype(BF16)
    return high, middle, low


class GradChain:
    def __init__(self, src, land, out, stage, temp, sems):
        self.me, self.z = lax.axis_index("dp"), lax.axis_index("fsdp")
        self.core = lax.rem(self.me, 2)
        self.src, self.land, self.out, self.stage, self.temp = src, land, out, stage, temp
        self.load_sems, self.send_sems, self.recv_sems, self.last_sems = sems
        self.near = self.z ^ 1
        self.inner = (self.z == 1) | (self.z == 2)
        self.outer = jnp.logical_not(self.inner)

    def load(self, kind, plane, k):
        return pltpu.make_async_copy(
            self.src[kind].at[plane], self.stage[kind].at[k], self.load_sems.at[kind * 4 + k]
        )

    def link(self, kind, src, place, plane):
        return unit_copy(
            src,
            self.land[kind].at[place],
            self.send_sems.at[kind * 5 + place],
            self.recv_sems.at[kind * 5 + place],
            (self.me, plane),
        )

    def loads(self):
        planes = (3 - self.z, 3 - self.near, self.near)
        return [self.load(kind, planes[k], k) for kind in range(2) for k in range(3)]

    def outer_sends(self):
        planes = (3 - self.near, 3 - self.z, self.near)
        return [
            self.link(kind, self.src[kind].at[planes[place]], place, self.near)
            for place in range(3)
            for kind in range(2)
        ]

    def start(self):
        for copy in self.loads():
            copy.start()

        @pl.when(self.outer)
        def _():
            for copy in self.outer_sends():
                copy.start()

    def gather(self, kind, place, k):
        self.link(kind, self.land[kind].at[place], place, self.near).wait_recv()
        fetch = pltpu.make_async_copy(
            self.land[kind].at[place], self.temp[kind], self.load_sems.at[kind * 4 + 3]
        )
        fetch.start()
        fetch.wait()
        self.stage[kind][k] = (
            self.stage[kind][k].astype(F32) + self.temp[kind][...].astype(F32)
        ).astype(BF16)

    def inner_sends(self, step):
        place = (3, 4, 3)[step]
        plane = (3 - self.z, 3 - self.z, self.near)[step]
        out = []
        for kind in range(2):
            copy = pltpu.make_async_remote_copy(
                src_ref=self.stage[kind].at[step],
                dst_ref=self.land[kind].at[place],
                send_sem=self.send_sems.at[kind * 5 + step],
                recv_sem=self.recv_sems.at[kind * 5 + place],
                device_id=(self.me, plane),
                device_id_type=MESH_ID,
            )
            out.append(copy)
        return out

    def step(self, step):
        @pl.when(self.inner)
        def _():
            sends = self.inner_sends(step)
            for kind in range(2):
                self.loads()[kind * 3 + step].wait()
                self.gather(kind, (0, 1, 4)[step], step)
                sends[kind].start()

    def places(self, e):
        blocks = self.land[0].shape[0] - 1
        part = self.stage[0].shape[3] // blocks
        out = [
            (
                self.stage[0].at[0, e, :, pl.ds(p * part, part)],
                self.out[0].at[:, pl.ds(pl.multiple_of((2 * p + self.core) * part, part), part)],
            )
            for p in range(blocks)
        ]
        return out + [(self.stage[1].at[0, e], self.out[1].at[self.core])]

    def last_copies(self):
        peer = (self.me - self.core + 1 - self.core, self.z)
        return [
            unit_copy(src, dst, self.last_sems.at[k], self.last_sems.at[5 + k], peer)
            for k, (src, dst) in enumerate(self.places(1 - self.core))
        ]

    def keep_copies(self):
        return [
            pltpu.make_async_copy(src, dst, self.last_sems.at[10 + k])
            for k, (src, dst) in enumerate(self.places(self.core))
        ]

    def total(self):
        @pl.when(self.outer)
        def _():
            for copy in self.loads():
                copy.wait()
            for copy in self.outer_sends():
                copy.wait_send()

        @pl.when(self.inner)
        def _():
            for step in range(3):
                for copy in self.inner_sends(step):
                    copy.wait_send()

        own = [self.load(kind, self.z, 0) for kind in range(2)]
        for copy in own:
            copy.start()
        for copy in own:
            copy.wait()

        @pl.when(self.inner)
        def _():
            for kind in range(2):
                self.gather(kind, 2, 0)

        for kind in range(2):
            self.gather(kind, 3, 0)
        for copy in self.last_copies() + self.keep_copies():
            copy.start()

    def finish(self):
        for copy in self.last_copies():
            copy.wait_recv()
            copy.wait_send()
        for copy in self.keep_copies():
            copy.wait()


def backward_kernel(
    heads,
    planes,
    groups,
    row_in,
    norm_ref,
    dense_in,
    qf_in,
    kf_in,
    qkv_in,
    o_in,
    lse_in,
    hres_in,
    g_all,
    zd_ref,
    zy_ref,
    gu_ref,
    gd_ref,
    small_ref,
    gates_ref,
    out_ref,
    dtok_ref,
    dqkv_out,
    dproj_out,
    ln_out,
    gu_in,
    gd_in,
    dlogit_out,
    dbup_out,
    dbdown_out,
    norm_out,
    gu_land,
    gd_land,
    row_ref,
    dense_ref,
    qf_ref,
    kf_ref,
    qkv_ref,
    o_ref,
    lse_ref,
    hres_ref,
    gm,
    kaug,
    vaug,
    dh,
    db,
    do,
    delta,
    qt,
    dot_t,
    dkt,
    dvt,
    dqkv,
    xn1,
    dw,
    dnorm,
    moved,
    own,
    d_theirs,
    d_deep,
    d_x,
    d_y,
    y_theirs,
    y_deep,
    y_x,
    y_y,
    w_own,
    w_theirs,
    w_deep,
    w_x,
    w_y,
    w_sum,
    w_in,
    small_in,
    small_out,
    norm_part,
    norm_in,
    norm_all,
    n_send,
    n_recv,
    s_send,
    s_recv,
    d_send,
    d_recv,
    y_send,
    y_recv,
    w_send,
    w_recv,
    z_send,
    z_recv,
    gu_stage,
    gd_stage,
    gu_temp,
    gd_temp,
    c_load,
    c_send,
    c_recv,
    c_last,
    loc_sems,
    in_sems,
):
    me, z = lax.axis_index("dp"), lax.axis_index("fsdp")
    core = lax.rem(me, 2)
    chip = me - core
    z_peers = [(me, lax.rem(z + k, planes)) for k in range(1, planes)]
    d_peers = [(lax.rem(me + k, groups), z) for k in range(1, groups)]
    greet(column_peers(planes) + d_peers)
    rows, width = hres_ref.shape
    chunk = row_ref.shape[1]
    head = width // heads
    pair = 2 * head

    gm_load = pltpu.make_async_copy(g_all.at[me], gm, loc_sems.at[4])
    gm_load.start()
    small_sender = Sender(s_send, s_recv)
    small_z = [small_sender.start(small_ref, small_in.at[k], p) for k, p in enumerate(z_peers)]
    d_sender = Sender(d_send, d_recv)
    d_scatter = plane_scatter_steps(
        zd_ref, own, d_theirs, d_deep, d_x, d_y, d_sender, loc_sems, z
    )
    next(d_scatter)
    next(d_scatter)
    pairs = (
        (hres_in, hres_ref),
        (o_in, o_ref),
        (dense_in, dense_ref),
        (row_in, row_ref),
        (qf_in, qf_ref),
        (kf_in, kf_ref),
        (qkv_in, qkv_ref),
        (lse_in, lse_ref),
    )
    fetched = [pltpu.make_async_copy(a, b, in_sems.at[k]) for k, (a, b) in enumerate(pairs)]
    for copy in fetched:
        copy.start()
    chain = GradChain(
        (gu_ref, gd_ref),
        (gu_land, gd_land),
        (gu_in, gd_in),
        (gu_stage, gd_stage),
        (gu_temp, gd_temp),
        (c_load, c_send, c_recv, c_last),
    )
    chain.start()
    for copy in small_z:
        copy.wait_recv()
    small_out[me] = small_ref[...] + jnp.sum(small_in[...], axis=0)
    small_d = [small_sender.start(small_out.at[me], small_out.at[me], p) for p in d_peers]
    y_sender = Sender(y_send, y_recv)
    y_scatter = plane_scatter_steps(
        zy_ref, own, y_theirs, y_deep, y_x, y_y, y_sender, loc_sems, z
    )
    next(y_scatter)
    gm_load.wait()
    for copy in fetched:
        copy.wait()

    next(d_scatter)

    def again(c, carry):
        part = pl.ds(pl.multiple_of(c * chunk, chunk), chunk)
        normal, _ = norm_parts(row_ref[c].astype(F32))
        xn1[part, :] = (normal * norm_ref[0:1, :] + norm_ref[1:2, :]).astype(BF16)
        return carry

    lax.fori_loop(0, planes, again, 0)
    next(d_scatter)
    chain.step(0)
    next(d_scatter)
    dh[...] = next(d_scatter)
    d_sender.drain()
    next(y_scatter)

    lane = lax.broadcasted_iota(jnp.int32, (rows, pair), 1)
    lane_c = lax.broadcasted_iota(jnp.int32, (chunk, pair), 1)
    same = lax.broadcasted_iota(jnp.int32, (width, pair), 0) // head == lax.broadcasted_iota(
        jnp.int32, (width, pair), 1
    )
    ones = jnp.where(same, 1.0, 0.0).astype(BF16)
    dnorm[...] = jnp.zeros_like(dnorm)

    def begin(c, carry):
        part = pl.ds(pl.multiple_of(c * chunk, chunk), chunk)
        normal, scale = norm_parts(hres_ref[part, :])
        grad = dh[part, :]
        dnorm[2] += fold_rows(grad * normal)
        dnorm[3] += fold_rows(grad)
        dh_part = gm[c].astype(F32) + norm_back_parts(grad * norm_ref[2:3, :], normal, scale)
        dh[part, :] = dh_part
        low = dh_part.astype(BF16)
        db[part, :] = low
        do_part = dot_nt(low, dense_ref[:, :, 3 * width : 4 * width].reshape(width, width)).astype(BF16)
        do[part, :] = do_part
        prod = do_part.astype(F32) * o_ref[part, :].astype(F32)
        high = prod.astype(BF16)
        rest = (prod - high.astype(F32)).astype(BF16)
        delta[part, :] = dot_nn(high, ones) + dot_nn(rest, ones)
        return carry

    next(y_scatter)
    lax.fori_loop(0, planes, begin, 0)
    chain.step(1)
    w_rows = w_sum.shape[0]
    w_cols = w_sum.shape[1]
    dw[:, :, 3 * width : 4 * width] = (
        dot_tn(o_ref[...], db[...]).astype(BF16).reshape(groups, w_rows, width)
    )

    mark = (lane >= heads) & (lane < heads + 3)
    kaug[:, pair:] = jnp.where(mark, 1.0, kf_ref[...].astype(F32)).astype(BF16)
    vaug[:, pair:] = jnp.where(mark, 1.0, 0.0).astype(BF16)

    def put_parts(base, values):
        high, middle, low = split3(-values)
        out = jnp.where(lane_c == heads, high.astype(F32), base)
        out = jnp.where(lane_c == heads + 1, middle.astype(F32), out)
        return jnp.where(lane_c == heads + 2, low.astype(F32), out).astype(BF16)

    def one_pair(g):
        cols = slice(g * pair, (g + 1) * pair)
        kaug[:, :pair] = qkv_ref[:, width + g * pair : width + (g + 1) * pair]
        vaug[:, :pair] = qkv_ref[:, 2 * width + g * pair : 2 * width + (g + 1) * pair]
        qt[...] = qkv_ref[:, cols].T
        dot_t[...] = do[:, cols].T
        dkt[...] = jnp.zeros_like(dkt)
        dvt[...] = jnp.zeros_like(dvt)

        def one_chunk(c, inner):
            part = pl.ds(pl.multiple_of(c * chunk, chunk), chunk)
            q_pair, do_pair = qkv_ref[part, cols], do[part, cols]
            lse_all, delta_all = lse_ref[part, :], delta[part, :]
            base = qf_ref[part, :].astype(F32)
            acc = jnp.zeros((chunk, pair), F32)
            none = jnp.zeros_like(q_pair)
            for side in range(2):
                mine = (lane_c // head) == side
                lse = lse_all[:, 2 * g + side : 2 * g + side + 1]
                qa = jnp.concatenate(
                    [jnp.where(mine, q_pair, none), put_parts(base, lse)], axis=1
                )
                pr = jnp.exp(dot_nt(qa, kaug[...]))
                dlt = delta_all[:, 2 * g + side : 2 * g + side + 1]
                da = jnp.concatenate(
                    [jnp.where(mine, do_pair, none), put_parts(jnp.zeros_like(base), dlt)], axis=1
                )
                ds = (pr * dot_nt(da, vaug[...])).astype(BF16)
                acc = jnp.where(mine, dot_nn(ds, kaug[:, :pair]), acc)
                here = slice(side * head, (side + 1) * head)
                dkt[here, :] += dot_nn(qt[here, part], ds)
                dvt[here, :] += dot_nn(dot_t[here, part], pr.astype(BF16))
            dqkv[part, cols] = (acc * 0.125).astype(BF16)
            return inner

        lax.fori_loop(0, planes, one_chunk, 0, unroll=2)
        dqkv[:, width + g * pair : width + (g + 1) * pair] = dkt[...].T.astype(BF16)
        dqkv[:, 2 * width + g * pair : 2 * width + (g + 1) * pair] = dvt[...].T.astype(BF16)

    out_sender = Sender(z_send, z_recv)
    next(y_scatter)
    one_pair(0)
    for copy in small_d:
        copy.wait_recv()
    dgate = jnp.concatenate(
        [
            small_out[2 * (e // 2), e % 2 : e % 2 + 1] + small_out[2 * (e // 2) + 1, e % 2 : e % 2 + 1]
            for e in range(groups)
        ]
    )
    gates = gates_ref[...]
    dlogit_out[...] = gates * (dgate - jnp.sum(gates * dgate, axis=0, keepdims=True))
    up_part, up_rows = dbup_out.shape[1] // 256, gu_ref.shape[3] // 128
    for h in range(2):
        for q in range(up_part):
            at = 2 + core * up_rows + z * up_part + q
            spot = (h * up_part + q) * 128
            dbup_out[:, spot : spot + 128] = small_out[chip + h, pl.ds(at, 1), :]
    dbdown_out[...] = small_out[me, pl.ds(2 + 2 * up_rows + core * (width // 128) + z, 1), :]
    chain.step(2)
    one_pair(1)
    next(y_scatter)
    mixed = hres_ref[...] + next(y_scatter)
    moved[0] = mixed.astype(BF16).reshape(planes, chunk, width)
    out_keep = pltpu.make_async_copy(moved.at[0, z], out_ref.at[z], loc_sems.at[7])
    out_keep.start()
    sent = [out_sender.start(moved.at[0, p[1]], out_ref.at[z], p) for p in z_peers]
    one_pair(2)
    chain.total()
    one_pair(3)

    def finish(c):
        part = pl.ds(pl.multiple_of(c * chunk, chunk), chunk)
        grad = dot_nt(dqkv[part, :], dense_ref[:, :, : 3 * width].reshape(width, 3 * width))
        normal, scale = norm_parts(row_ref[c].astype(F32))
        dnorm[0] += fold_rows(grad * normal)
        dnorm[1] += fold_rows(grad)
        moved[1, c] = (
            dh[part, :] + norm_back_parts(grad * norm_ref[0:1, :], normal, scale)
        ).astype(BF16)

    for k, peer in enumerate(z_peers):
        finish(peer[1])
        sent.append(out_sender.start(moved.at[1, peer[1]], dtok_ref.at[z], peer))
    finish(z)
    tok_keep = pltpu.make_async_copy(moved.at[1, z], dtok_ref.at[z], loc_sems.at[8])
    tok_keep.start()
    for k in range(2):
        total = jnp.sum(dnorm[k], axis=0, keepdims=True)
        for q in range(width // 128):
            row = k * (width // 128) + q
            norm_part[row : row + 1] = total[:, q * 128 : (q + 1) * 128]
    norm_sender = Sender(n_send, n_recv)
    norm_z = [norm_sender.start(norm_part, norm_in.at[k], p) for k, p in enumerate(z_peers)]
    for c in range(3):
        cols = slice(c * width, (c + 1) * width)
        dw[:, :, cols] = (
            dot_tn(xn1[...], dqkv[:, cols]).astype(BF16).reshape(groups, w_rows, width)
        )
    lanes = lax.broadcasted_iota(jnp.int32, (8, width), 0)
    table = jnp.zeros((8, width), F32)
    for k in range(2, 4):
        table = jnp.where(lanes == k, jnp.sum(dnorm[k], axis=0, keepdims=True), table)
    table = jnp.concatenate([table, jnp.zeros((w_cols - 4 * width - 8, width), F32)], axis=0)
    dw[:, :, 4 * width :] = table.T.astype(BF16).reshape(groups, w_rows, w_cols - 4 * width)
    w_sender = Sender(w_send, w_recv)
    w_scatter = plane_scatter_steps(
        dw, w_own, w_theirs, w_deep, w_x, w_y, w_sender, loc_sems, z
    )
    next(w_scatter)
    next(w_scatter)
    for _ in range(3):
        next(w_scatter)
    w_sum[...] = next(w_scatter).astype(BF16)
    shard = dqkv_out.shape[0]
    last = [
        out_sender.start(w_sum.at[pl.ds(p[1] * shard, shard)], w_in.at[k], p)
        for k, p in enumerate(z_peers)
    ]
    for copy in norm_z:
        copy.wait_recv()
    norm_all[me] = norm_part[...] + jnp.sum(norm_in[...], axis=0)
    norm_d = [norm_sender.start(norm_all.at[me], norm_all.at[me], p) for p in d_peers]
    total = w_sum[pl.ds(z * shard, shard)].astype(F32)
    for k, copy in enumerate(last):
        copy.wait_recv()
        total = total + w_in[k].astype(F32)
    dqkv_out[...] = total[:, : 3 * width]
    dproj_out[...] = total[:, 3 * width : 4 * width]
    ln_out[...] = total[:, 4 * width :]
    for copy in norm_d:
        copy.wait_recv()
    norm_out[...] = jnp.sum(norm_all[...], axis=0)
    for copy in sent:
        copy.wait_recv()
    chain.finish()
    out_keep.wait()
    tok_keep.wait()
    for sender in (small_sender, y_sender, w_sender, out_sender, norm_sender):
        sender.drain()


def scatter_scratch(rows, width):
    return [
        pltpu.VMEM((4, rows, width), BF16),
        pltpu.VMEM((2, rows // 2, width), BF16),
        pltpu.VMEM((rows, width), BF16),
        pltpu.VMEM((rows, width), BF16),
    ]


def backward(
    row, norms, dense, qf, kf, qkv, o, lse, hres, g_all, zd, zy, gu, gd, small, gates, heads
):
    planes, piece, width = row.shape
    groups = zd.shape[0]
    rows = planes * piece
    pair = 2 * (width // heads)
    w_rows, w_cols = width // groups, 4 * width + 128
    sd = jax.ShapeDtypeStruct
    dma = pltpu.SemaphoreType.DMA
    return pl.pallas_call(
        functools.partial(backward_kernel, heads, planes, groups),
        out_shape=(
            sd(row.shape, BF16),
            sd(row.shape, BF16),
            sd((w_rows // planes, 3 * width), F32),
            sd((w_rows // planes, width), F32),
            sd((w_rows // planes, 128), F32),
            sd((gu.shape[2], 2 * gu.shape[3]), BF16),
            sd((2,) + gd.shape[2:], BF16),
            sd((groups, 128), F32),
            sd((1, 2 * gu.shape[3] // planes), F32),
            sd((1, width // planes), F32),
            sd((2 * width // 128, 128), F32),
            sd((5,) + gu.shape[1:], BF16),
            sd((5,) + gd.shape[1:], BF16),
        ),
        in_specs=[any_spec(), vmem_spec()] + [any_spec()] * 12 + [vmem_spec()] * 2,
        out_specs=tuple(
            [any_spec()] * 2
            + [vmem_spec()] * 3
            + [any_spec()] * 2
            + [vmem_spec()] * 4
            + [any_spec()] * 2
        ),
        scratch_shapes=[pltpu.VMEM(a.shape, a.dtype) for a in (row, dense, qf, kf, qkv, o, lse, hres)]
        + [
            pltpu.VMEM(row.shape, BF16),
            pltpu.VMEM((rows, 2 * pair), BF16),
            pltpu.VMEM((rows, 2 * pair), BF16),
            pltpu.VMEM((rows, width), F32),
            pltpu.VMEM((rows, width), BF16),
            pltpu.VMEM((rows, width), BF16),
            pltpu.VMEM((rows, pair), F32),
            pltpu.VMEM((pair, rows), BF16),
            pltpu.VMEM((pair, rows), BF16),
            pltpu.VMEM((pair, rows), F32),
            pltpu.VMEM((pair, rows), F32),
            pltpu.VMEM((rows, 3 * width), BF16),
            pltpu.VMEM((rows, width), BF16),
            pltpu.VMEM((groups, w_rows, w_cols), BF16),
            pltpu.VMEM((4, 8, width), F32),
            pltpu.VMEM((2,) + row.shape, BF16),
            pltpu.VMEM((4, rows, width), BF16),
        ]
        + scatter_scratch(rows, width)
        + scatter_scratch(rows, width)
        + [pltpu.VMEM((4, w_rows, w_cols), BF16)]
        + scatter_scratch(w_rows, w_cols)
        + [
            pltpu.VMEM((w_rows, w_cols), BF16),
            pltpu.VMEM((planes - 1, w_rows // planes, w_cols), BF16),
            pltpu.VMEM((planes - 1,) + small.shape, F32),
            pltpu.VMEM((groups,) + small.shape, F32),
            pltpu.VMEM((2 * width // 128, 128), F32),
            pltpu.VMEM((planes - 1, 2 * width // 128, 128), F32),
            pltpu.VMEM((groups, 2 * width // 128, 128), F32),
            dma((planes + groups,)),
            dma((planes + groups,)),
            dma((planes + groups,)),
            dma((planes + groups,)),
            dma((PLANE_SCATTER_COPIES,)),
            dma((PLANE_SCATTER_COPIES,)),
            dma((PLANE_SCATTER_COPIES,)),
            dma((PLANE_SCATTER_COPIES,)),
            dma((PLANE_SCATTER_COPIES,)),
            dma((PLANE_SCATTER_COPIES,)),
            dma((3 * planes,)),
            dma((3 * planes,)),
            pltpu.VMEM((3,) + gu.shape[1:], BF16),
            pltpu.VMEM((3,) + gd.shape[1:], BF16),
            pltpu.VMEM(gu.shape[1:], BF16),
            pltpu.VMEM(gd.shape[1:], BF16),
            dma((8,)),
            dma((10,)),
            dma((10,)),
            dma((15,)),
            dma((9,)),
            dma((8,)),
        ],
        compiler_params=pltpu.CompilerParams(
            collective_id=4, has_side_effects=True, vmem_limit_bytes=VMEM_MAX
        ),
        cost_estimate=pl.CostEstimate(
            flops=80_000_000_000, bytes_accessed=20_000_000, transcendentals=8_000_000
        ),
        name="attention_backward",
    )(row, norms, dense, qf, kf, qkv, o, lse, hres, g_all, zd, zy, gu, gd, small, gates)


def make_tile_list(marks, list_ref):
    blocks, piece = marks.shape
    per = piece // TILE
    iota = functools.partial(lax.broadcasted_iota, jnp.int32)

    def table(mask):
        return jnp.where(mask, 1.0, 0.0).astype(BF16)

    kept = table(marks >= 0.0)
    folded = dot_nn(kept, table(iota((piece, 128), 0) // TILE == iota((piece, 128), 1)))
    real = iota((blocks, 128), 1) < per
    hit = jnp.where(folded > 0.0, 1.0, 0.0)
    inside = dot_nn(hit.astype(BF16), table(iota((128, 128), 0) < iota((128, 128), 1)))
    totals = jnp.broadcast_to(jnp.sum(hit, axis=1, keepdims=True), (blocks, 128))
    above = dot_nn(table(iota((blocks, blocks), 1) < iota((blocks, blocks), 0)), totals.astype(BF16))
    count = jnp.sum(hit)
    rank = inside + above
    index = iota((blocks, 128), 0) * per + iota((blocks, 128), 1)
    place = jnp.where(hit > 0.0, rank, count + index.astype(F32) - rank)
    place = jnp.where(real, place, 0.0).astype(jnp.int32)
    tiles = blocks * per
    row = iota((tiles, 128), 0)
    spread = table(iota((tiles, blocks), 0) // per == iota((tiles, blocks), 1))
    mine = lax.rem(row, per) == iota((tiles, 128), 1)
    digits = []
    for digit in (place // per, lax.rem(place, per)):
        full = dot_nn(spread, digit.astype(F32).astype(BF16))
        digits.append(jnp.sum(jnp.where(mine, full, 0.0), axis=1, keepdims=True).astype(jnp.int32))
    to_row = table(digits[0] == iota((tiles, blocks), 1))
    to_column = digits[1] == iota((tiles, 128), 1)
    found = jnp.zeros((blocks, 128), F32)
    for value, scale in ((row // per, per), (lax.rem(row, per), 1)):
        part = jnp.where(to_column, value.astype(F32), 0.0).astype(BF16)
        found = found + scale * dot_tn(to_row, part)
    found = jnp.where(iota((blocks, 128), 1) == per, count, found)
    list_ref[...] = found.astype(jnp.int32)


def expert_kernel(
    marks_ref,
    gates_ref,
    codes_ref,
    own_ref,
    x_ref,
    g_ref,
    up_ref,
    down_ref,
    zd_ref,
    zy_ref,
    gu_ref,
    gd_ref,
    small_ref,
    dbup_ref,
    dbdown_ref,
    dgate_ref,
    xs,
    gs,
    zds,
    zys,
    up,
    down,
    acc_up,
    acc_down,
    xb,
    gb,
    mb,
    dyb,
    xt,
    dyt,
    yacc,
    xacc,
    meta,
    bup,
    bdown,
    list_vmem,
    list_ref,
    list_sem,
    sems,
    upt,
    downt,
    row_sems,
):
    me = lax.axis_index("dp")
    groups, rows, width = x_ref.shape
    hidden = up.shape[2]
    planes = gu_ref.shape[0]
    tiles = BLOCK // TILE
    copies = []

    def load(src, dst):
        copy = pltpu.make_async_copy(src, dst, sems.at[len(copies)])
        copy.start()
        copies.append(copy)

    load(up_ref, up)
    load(down_ref, down)

    def x_copy(source):
        return pltpu.make_async_copy(x_ref.at[source], xs.at[source], row_sems.at[source])

    def g_copy(source):
        return pltpu.make_async_copy(
            g_ref.at[source], gs.at[source], row_sems.at[groups + source]
        )

    for source in range(groups):

        @pl.when(me == source)
        def _():
            pltpu.make_async_copy(own_ref, xs.at[source], row_sems.at[source]).start()

        @pl.when(me != source)
        def _():
            x_copy(source).start()

        g_copy(source).start()

    def wait_rows(source, carry):
        x_copy(source).wait()
        g_copy(source).wait()
        return carry

    def zd_copy(source):
        part = pl.ds(pl.multiple_of(source * rows, rows), rows)
        return pltpu.make_async_copy(
            zds.at[part], zd_ref.at[part], row_sems.at[2 * groups + source]
        )

    def zy_copy(source):
        part = pl.ds(pl.multiple_of(source * rows, rows), rows)
        return pltpu.make_async_copy(
            zys.at[part], zy_ref.at[part], row_sems.at[3 * groups + source]
        )

    def save_rows(source, carry):
        zd_copy(source).start()
        zy_copy(source).start()
        return carry

    def wipe(k, carry):
        part = pl.ds(pl.multiple_of(k * BLOCK, BLOCK), BLOCK)
        zds[part, :] = jnp.zeros((BLOCK, width), BF16)
        zys[part, :] = jnp.zeros((BLOCK, width), BF16)
        return carry

    lax.fori_loop(0, groups * rows // BLOCK, wipe, 0)
    dbup_ref[...] = jnp.zeros_like(dbup_ref)
    dbdown_ref[...] = jnp.zeros_like(dbdown_ref)
    dgate_ref[...] = jnp.zeros_like(dgate_ref)
    core = lax.rem(me, 2)
    piece = marks_ref.shape[2]
    blocks = marks_ref.shape[1]
    lane = lax.broadcasted_iota(jnp.int32, (piece, 128), 1)
    turned = [marks_ref[e].T for e in range(2)]
    for k in range(blocks):
        meta[k * piece : (k + 1) * piece, :] = jnp.where(
            lane == 0, turned[0][:, k : k + 1], turned[1][:, k : k + 1]
        )
    for e in range(2):
        for p in range(planes):
            for q in range(2):
                at = p * (hidden // planes) + q * 128
                bup[e, :, at : at + 128] = codes_ref[
                    me - core + e, p, pl.ds(BIAS_UP + 2 * core + q, 1), :
                ]
            bdown[e, :, p * 128 : (p + 1) * 128] = jnp.where(
                core == 0, codes_ref[me - core + e, p, BIAS_DOWN : BIAS_DOWN + 1, :], 0.0
            )
        make_tile_list(marks_ref[e], list_vmem.at[e])
    list_copy = pltpu.make_async_copy(list_vmem, list_ref, list_sem)
    list_copy.start()
    list_copy.wait()
    for copy in copies:
        copy.wait()

    def spot(index):
        return pl.ds(pl.multiple_of(index * TILE, TILE), TILE)

    saves = []

    def save(src, dst):
        copy = pltpu.make_async_copy(src, dst, sems.at[len(copies) + len(saves)])
        copy.start()
        saves.append(copy)

    per_row = rows // TILE

    def entry(e, position):
        return list_ref[e, lax.div(position, 16), lax.rem(position, 16)]

    def one_expert(e, state):
        acc_up[...] = jnp.zeros_like(acc_up)
        acc_down[...] = jnp.zeros_like(acc_down)
        upt[...] = up[e].T
        downt[...] = down[e].T
        n_tiles = list_ref[e, 0, 16]
        n_blocks = lax.div(n_tiles + (tiles - 1), tiles)
        gate_row = gates_ref[pl.ds(me - core + e, 1), :]
        lane_b = lax.broadcasted_iota(jnp.int32, (BLOCK, 128), 1).astype(F32)

        def one_block(b, state):
            ready, saved = state
            end = (b + 1) * tiles
            need = lax.div(
                jnp.maximum(entry(e, jnp.minimum(end, n_tiles) - 1), entry(e, end - 1)), per_row
            )
            lax.fori_loop(ready, need + 1, wait_rows, 0)
            ready = jnp.maximum(ready, need + 1)

            def fetch(k, inner):
                index = list_ref[e, b * (tiles // 16) + lax.div(k, 16), lax.rem(k, 16)]
                src, part = lax.div(index, per_row), spot(lax.rem(index, per_row))
                dst = spot(k)
                xb[dst, :] = xs[src, part, :]
                gb[dst, :] = gs[src, part, :]
                mb[dst, :] = meta[spot(index), :]
                return inner

            lax.fori_loop(0, tiles, fetch, 0, unroll=True)
            hot = lane_b == mb[:, e : e + 1]
            gate = jnp.sum(jnp.where(hot, gate_row, 0.0), axis=1, keepdims=True)
            dyb_new = (gb[...].astype(F32) * gate).astype(BF16)
            dyb[...] = dyb_new
            xt[...] = xb[...].T
            dyt[...] = dyb_new.T
            dbdown_ref[e] += fold_rows(dyb_new.astype(F32))

            parts = []
            for k in range(2):
                rows_k = slice(k * BLOCK // 2, (k + 1) * BLOCK // 2)
                u = dot_nn(xb[rows_k, :], up[e]) + bup[e]
                sq = u * u
                th = jnp.tanh(u * (0.7978845608028654 + 0.035677408136300125 * sq))
                half = 0.5 + 0.5 * th
                slope = half + u * (
                    (0.5 - 0.5 * th * th) * (0.7978845608028654 + 0.10703222440890037 * sq)
                )
                a = (u * half).astype(BF16)
                du = (dot_nn(dyb[rows_k, :], downt[...]) * slope).astype(BF16)
                parts.append((a, du))
            a = jnp.concatenate([p[0] for p in parts], axis=0)
            du = jnp.concatenate([p[1] for p in parts], axis=0)
            y = dot_nn(a, down[e]) + bdown[e]
            x_new = dot_nn(du, upt[...])
            acc_up[...] += dot_nn(xt[...], du)
            acc_down[...] += dot_nn(dyt[...], a)
            dbup_ref[e] += fold_rows(du.astype(F32))
            inner_prod = jnp.sum(y * gb[...].astype(F32), axis=-1, keepdims=True)
            dgate_ref[e] += fold_rows(jnp.where(hot, inner_prod, 0.0))
            gb[...] = (y * gate).astype(BF16)
            xb[...] = x_new.astype(BF16)

            def store(k, inner):
                real = b * tiles + k < n_tiles
                dst = spot(jnp.where(real, entry(e, b * tiles + k), groups * per_row))
                src = spot(k)
                if e == 0:
                    zds[dst, :] = xb[src, :]
                    zys[dst, :] = gb[src, :]
                else:
                    zds[dst, :] = (zds[dst, :].astype(F32) + xb[src, :].astype(F32)).astype(BF16)
                    zys[dst, :] = (zys[dst, :].astype(F32) + gb[src, :].astype(F32)).astype(BF16)
                return inner

            lax.fori_loop(0, tiles, store, 0, unroll=True)
            if e == 1:
                upto = lax.div(entry(e, jnp.minimum(end, groups * per_row - 1)), per_row)
                upto = jnp.where(end < n_tiles, upto, saved)
                lax.fori_loop(saved, upto, save_rows, 0)
                saved = jnp.maximum(saved, upto)
            return ready, saved

        state = lax.fori_loop(0, n_blocks, one_block, state)
        up[e] = acc_up[...].astype(BF16)
        for k in range(hidden // FCHUNK):
            cols = slice(k * FCHUNK, (k + 1) * FCHUNK)
            down[e, cols, :] = acc_down[:, cols].T.astype(BF16)
        up_rows, down_rows = width // planes, hidden // planes
        for k in range(planes):
            save(up.at[e, pl.ds(k * up_rows, up_rows)], gu_ref.at[k, e])
            save(down.at[e, pl.ds(k * down_rows, down_rows)], gd_ref.at[k, e])
        return state

    state = one_expert(0, (jnp.int32(0), jnp.int32(0)))
    ready, saved = one_expert(1, state)
    lax.fori_loop(saved, groups, save_rows, 0)
    lax.fori_loop(ready, groups, wait_rows, 0)
    small_ref[...] = jnp.zeros_like(small_ref)
    up_rows, down_rows = hidden // 128, width // 128
    for e in range(2):
        small_ref[e : e + 1] = jnp.sum(dgate_ref[e], axis=0, keepdims=True)
        for at, acc, count in (
            (2 + e * up_rows, dbup_ref, up_rows),
            (2 + 2 * up_rows + e * down_rows, dbdown_ref, down_rows),
        ):
            sums = jnp.sum(acc[e], axis=0, keepdims=True)
            for k in range(count):
                small_ref[at + k : at + k + 1] = sums[:, k * 128 : (k + 1) * 128]
    for copy in saves:
        copy.wait()
    for source in range(groups):
        zd_copy(source).wait()
        zy_copy(source).wait()


def experts(marks, gates, codes, x_own, x_all, g_all, up, down):
    groups, rows, width = x_all.shape
    hidden = up.shape[2]
    planes = 4
    total = groups * rows
    sd = jax.ShapeDtypeStruct
    return pl.pallas_call(
        expert_kernel,
        out_shape=(
            sd((total, width), BF16),
            sd((total, width), BF16),
            sd((planes, 2, width // planes, hidden), BF16),
            sd((planes, 2, hidden // planes, width), BF16),
            sd((-(-(2 + 2 * (hidden + width) // 128) // 8) * 8, 128), F32),
        ),
        in_specs=[vmem_spec()] * 3 + [any_spec()] * 5,
        out_specs=tuple([any_spec()] * 4 + [vmem_spec()]),
        scratch_shapes=[
            pltpu.VMEM((2, 8, hidden), F32),
            pltpu.VMEM((2, 8, width), F32),
            pltpu.VMEM((2, 8, 128), F32),
            pltpu.VMEM((groups, rows, width), BF16),
            pltpu.VMEM((groups, rows, width), BF16),
            pltpu.VMEM((total + TILE, width), BF16),
            pltpu.VMEM((total + TILE, width), BF16),
            pltpu.VMEM((2, width, hidden), BF16),
            pltpu.VMEM((2, hidden, width), BF16),
            pltpu.VMEM((width, hidden), F32),
            pltpu.VMEM((width, hidden), F32),
            pltpu.VMEM((BLOCK, width), BF16),
            pltpu.VMEM((BLOCK, width), BF16),
            pltpu.VMEM((BLOCK, 128), F32),
            pltpu.VMEM((BLOCK, width), BF16),
            pltpu.VMEM((width, BLOCK), BF16),
            pltpu.VMEM((width, BLOCK), BF16),
            pltpu.VMEM((BLOCK, width), F32),
            pltpu.VMEM((BLOCK, width), F32),
            pltpu.VMEM((total, 128), F32),
            pltpu.VMEM((2, 1, hidden), F32),
            pltpu.VMEM((2, 1, width), F32),
            pltpu.VMEM((2, marks.shape[1], 128), jnp.int32),
            pltpu.SMEM((2, marks.shape[1], 128), jnp.int32),
            pltpu.SemaphoreType.DMA,
            pltpu.SemaphoreType.DMA((40,)),
            pltpu.VMEM((hidden, width), BF16),
            pltpu.VMEM((width, hidden), BF16),
            pltpu.SemaphoreType.DMA((4 * groups,)),
        ],
        compiler_params=pltpu.CompilerParams(vmem_limit_bytes=VMEM_MAX),
        cost_estimate=pl.CostEstimate(
            flops=60_000_000_000, bytes_accessed=40_000_000, transcendentals=8_000_000
        ),
        name="experts",
    )(marks, gates, codes, x_own, x_all, g_all, up, down)


def fast_shards(
    mesh_sizes,
    tokens,
    out_grad,
    segment_ids,
    key_mask,
    sent_task,
    task_experts,
    ln1_gain,
    ln1_bias,
    w_qkv,
    w_proj,
    ln2_gain,
    ln2_bias,
    task_embed,
    w_gate,
    w_up,
    b_up,
    w_down,
    b_down,
):
    groups, planes = mesh_sizes
    row_count, piece, width = tokens.shape
    length = piece * planes
    total = groups * length
    tasks = task_experts.shape[0]
    n_experts = w_gate.shape[1]
    hidden = w_up.shape[2]
    capacity = 4 * row_count * piece // n_experts
    me, z = lax.axis_index("dp"), lax.axis_index("fsdp")

    core = me % 2
    half = hidden // 2
    shard_norms = jnp.concatenate([ln1_gain, ln1_bias, ln2_gain, ln2_bias]).astype(F32)
    shard_norms = jnp.pad(shard_norms, (0, 128 - shard_norms.shape[0])).reshape(1, 128)
    logits_part = jnp.dot(task_embed, w_gate, preferred_element_type=F32)
    routing = (segment_ids, key_mask, logits_part, shard_norms, b_up, b_down)
    (
        codes,
        marks,
        gates_rows,
        order,
        norms,
        qf,
        kf,
        row,
        dense_full,
        qkv,
        o,
        lse,
        hres,
        xn2,
        x_all,
        g_all,
        up_all,
        down_all,
    ) = forward(
        sent_task,
        task_experts,
        routing,
        tokens,
        out_grad,
        w_qkv,
        w_proj,
        w_up,
        w_down,
        HEADS,
        groups,
        capacity,
    )
    zd, zy, gu, gd, small = experts(
        marks,
        gates_rows,
        codes,
        xn2.reshape(length, width),
        x_all.reshape(groups, length, width),
        g_all.reshape(groups, length, width),
        up_all.reshape(2, width, half),
        down_all.reshape(2, half, width),
    )
    (
        out_pieces,
        tok_pieces,
        d_w_qkv,
        d_w_proj,
        d_ln2,
        gu_in,
        gd_in,
        dlogits,
        d_b_up,
        d_b_down,
        norm_sums,
        _,
        _,
    ) = backward(
        row,
        norms,
        dense_full,
        qf,
        kf,
        qkv,
        o,
        lse,
        hres,
        g_all,
        zd.reshape(groups, length, width),
        zy.reshape(groups, length, width),
        gu,
        gd,
        small,
        gates_rows,
        HEADS,
    )
    d_w_up = gu_in.astype(F32)
    d_w_down = gd_in.astype(F32).reshape(-1, width)
    output, d_tokens = pick_rows(order, (out_pieces, tok_pieces), (BF16, F32))

    features = width // (groups * planes)
    d_ln1 = lax.dynamic_slice_in_dim(
        norm_sums.reshape(2, width), (me * planes + z) * features, features, 1
    )

    dlogits = dlogits[:, :tasks]
    d_task_embed = jnp.dot(dlogits.T, w_gate.astype(F32).T, precision=exact)
    d_w_gate = jnp.dot(task_embed.astype(F32).T, dlogits.T, precision=exact)
    return (
        output,
        d_tokens,
        d_ln1[0],
        d_ln1[1],
        d_w_qkv,
        d_w_proj,
        d_ln2[:, 2],
        d_ln2[:, 3],
        d_task_embed,
        d_w_gate,
        d_w_up[None],
        d_b_up,
        d_w_down[None],
        d_b_down,
    )


def fits_rows(mesh, tokens, w_gate):
    groups, planes = mesh.shape["dp"], mesh.shape["fsdp"]
    return (
        groups == 8
        and planes == 4
        and tokens.shape[1] == planes * 256
        and tokens.shape[0] == groups * planes
        and w_gate.shape[1] == groups
        and tokens.shape[1] % (planes * QCHUNK) == 0
    )


def solution(mesh):
    placed = (
        P("dp", "fsdp", None),
        P("dp", "fsdp", None),
        P("dp", "fsdp"),
        P("dp", "fsdp"),
        P("dp", None),
        P(),
        P(("dp", "fsdp")),
        P(("dp", "fsdp")),
        P(("dp", "fsdp"), None),
        P(("dp", "fsdp"), None),
        P(("dp", "fsdp")),
        P(("dp", "fsdp")),
        P(None, ("dp", "fsdp")),
        P(("dp", "fsdp"), None),
        P("dp", "fsdp", None),
        P("dp", "fsdp"),
        P("dp", "fsdp", None),
        P("dp", "fsdp"),
    )
    placed_out = (
        P("dp", "fsdp", None),
        P("dp", "fsdp", None),
        P(("dp", "fsdp")),
        P(("dp", "fsdp")),
        P(("dp", "fsdp"), None),
        P(("dp", "fsdp"), None),
        P(("dp", "fsdp")),
        P(("dp", "fsdp")),
        P(None, ("dp", "fsdp")),
        P(("dp", "fsdp"), None),
        P("dp", "fsdp", None),
        P("dp", "fsdp"),
        P("dp", "fsdp", None),
        P("dp", "fsdp"),
    )

    def program(*args):
        fast = fits_rows(mesh, args[0], args[13])
        sizes = (mesh.shape["dp"], mesh.shape["fsdp"])
        return jax.shard_map(
            functools.partial(fast_shards, sizes) if fast else shards,
            mesh=mesh,
            in_specs=placed,
            out_specs=placed_out,
            check_vma=False,
        )(*args)

    return program
```
